128 devices in a mesh: dp: 4 (over z), seq: 32 (over y, x, core).
Axes of the slice: x: 4, y: 4, z: 4, core: 2. Of those that a mesh axis runs over, the one named last changes fastest.
Arguments:
- hidden: bfloat16 [4, 8192, 1536], P('dp', 'seq'), may hold values from -6 to 6
- cotangent: bfloat16 [4, 8192, 1536], P('dp', 'seq'), may hold values from -6 to 6
- in_w: bfloat16 [1536, 6448], P(('dp', 'seq')), may hold values from -0.15625 to 0.15625
- out_w: bfloat16 [3072, 1536], P(('dp', 'seq')), may hold values from -0.109375 to 0.109375
- conv_w: bfloat16 [4, 3328], P(None, ('dp', 'seq')), may hold values from -3 to 3
- conv_b: bfloat16 [3328], P(('dp', 'seq')), may hold values from -0.5 to 0.5
- norm_gain: bfloat16 [1536], P(('dp', 'seq')), may hold values from 0.5 to 1.5
- gate_gain: bfloat16 [3072], P(('dp', 'seq')), may hold values from 0.5 to 1.5
- dt_bias: float32 [48], replicated, may hold values from -4 to -1
- decay_rates: float32 [48], replicated, may hold values from 3.6621095e-05 to 0.2
- d_skip: float32 [48], replicated, may hold values from 0.5 to 1.5
Outputs:
- out: bfloat16 [4, 8192, 1536], P('dp', 'seq')
- d_hidden: float32 [4, 8192, 1536], P('dp', 'seq')
- d_in_w: float32 [1536, 6448], P(('dp', 'seq'))
- d_out_w: float32 [3072, 1536], P(('dp', 'seq'))
- d_conv_w: float32 [4, 3328], P(None, ('dp', 'seq'))
- d_conv_b: float32 [3328], P(('dp', 'seq'))
- d_norm_gain: float32 [1536], P(('dp', 'seq'))
- d_gate_gain: float32 [3072], P(('dp', 'seq'))
- d_dt_bias: float32 [48], replicated
- d_decay_rates: float32 [48], replicated
- d_d_skip: float32 [48], replicated
The draws below stay inside these ranges and needn't reach their ends.
All inputs are finite; a program needn't handle non-finite values.
Results may differ from the reference program's by a relative error of at most 0.017.
Values may be sent and summed in bfloat16 or wider, within the bound.
A program may use at most 320 MiB of HBM per device.

```python
import math
import jax
import jax.numpy as jnp
from jax import lax

D = 1536
H = 48
P_SIZE = 64
NS = 128
KW = 4
SPAN = 256
DI = 3072
CONVC = 3328
PROJ = 6448
LEN = 8192
SEQS = 4


def levels(key, shape, shards, low, top_value):
    level, own = 1.0, jax.random.fold_in(key, 6)
    for dim, parts in shards:
        draws = jnp.exp(jax.random.uniform(jax.random.fold_in(own, dim), (parts,), jnp.float32, low / len(shards), top_value / len(shards)))
        level = level * jnp.repeat(draws, shape[dim] // parts).reshape([-1 if axis == dim else 1 for axis in range(len(shape))])
    return level


def centred(stream_key, dims, width, limit, cuts=(), dtype=jnp.bfloat16):
    entries = width * jax.random.normal(stream_key, dims, jnp.float32)
    if cuts:
        entries = entries * levels(stream_key, dims, cuts, -0.22, 0.18)
    return jnp.clip(entries, -limit, limit).astype(dtype)


def setup_inputs(seed: int = 0) -> dict:
    key_of = jax.random.split(jax.random.key(seed), 12)
    hidden = centred(key_of[0], (SEQS, LEN, D), 1.0, 6.0, ((0, 4), (1, 32)))
    cotangent = centred(key_of[1], (SEQS, LEN, D), 1.0, 6.0, ((0, 4), (1, 32)))
    in_w = centred(key_of[2], (D, PROJ), D ** -0.5, 0.15625, ((0, 128),))
    out_w = centred(key_of[3], (DI, D), DI ** -0.5, 0.109375, ((0, 128),))
    conv_w = centred(key_of[4], (KW, CONVC), KW ** -0.5, 3.0, ((1, 128),))
    conv_b = jnp.clip(jax.random.uniform(key_of[5], (CONVC,), jnp.float32, -0.5, 0.5) * levels(key_of[5], (CONVC,), ((0, 128),), -0.4, 0.0), -0.5, 0.5).astype(jnp.bfloat16)
    norm_gain = jnp.clip(1.0 + 0.1 * jax.random.normal(key_of[6], (D,), jnp.float32), 0.5, 1.5).astype(jnp.bfloat16)
    gate_gain = jnp.clip(1.0 + 0.1 * jax.random.normal(key_of[7], (DI,), jnp.float32), 0.5, 1.5).astype(jnp.bfloat16)
    dt_bias = jnp.clip(jax.random.uniform(key_of[8], (H,), jnp.float32, -4.0, -1.0), -4.0, -1.0)
    decay_rates = jnp.clip(jnp.exp(jax.random.uniform(key_of[9], (H,), jnp.float32, math.log(3.662109520519152e-05), math.log(0.2))), 3.662109520519152e-05, 0.2)
    d_skip = jnp.clip(jax.random.uniform(key_of[10], (H,), jnp.float32, 0.5, 1.5), 0.5, 1.5)
    return {"hidden": hidden, "cotangent": cotangent, "in_w": in_w, "out_w": out_w, "conv_w": conv_w, "conv_b": conv_b, "norm_gain": norm_gain, "gate_gain": gate_gain, "dt_bias": dt_bias, "decay_rates": decay_rates, "d_skip": d_skip}


epsilon = 1e-05
highest = lax.Precision.HIGHEST

@jax.custom_vjp
def low(v):
    return lax.optimization_barrier(v.astype(jnp.bfloat16)).astype(jnp.float32)

@jax.custom_vjp
def low_back(v):
    return v

def low_keep(v):
    return (low(v), None)

def low_pass(kept, grad):
    return (grad,)

def back_keep(v):
    return (v, None)

def back_low(kept, grad):
    return (low(grad),)
low.defvjp(low_keep, low_pass)
low_back.defvjp(back_keep, back_low)

def rms_scale(values, gain):
    return values * lax.rsqrt(lax.optimization_barrier(jnp.mean(values * values, axis=-1, keepdims=True)) + epsilon) * gain

def span_step(carry_state, heads_x, b_in, c_out, steps_dt, neg_rate):
    block_len = heads_x.shape[0]
    log_decay = steps_dt * neg_rate[None, :]
    cum_decay = jnp.cumsum(log_decay, axis=0)
    position = jnp.arange(block_len)
    causal = (position[:, None] >= position[None, :]).astype(jnp.float32)
    gap_decay = jnp.exp((cum_decay[:, None, :] - cum_decay[None, :, :]) * causal[:, :, None]) * causal[:, :, None]
    scores = jnp.dot(c_out, b_in.T, precision=highest)
    mixing = scores[:, :, None] * gap_decay * steps_dt[None, :, :]
    within = jnp.einsum('trh,rhp->thp', mixing, heads_x, precision=highest)
    carried = jnp.exp(cum_decay)[:, :, None] * jnp.einsum('tn,hpn->thp', c_out, carry_state, precision=highest)
    last_sum = cum_decay[-1]
    toward = jnp.exp(last_sum[None, :] - cum_decay) * steps_dt
    added_in = jnp.einsum('rh,rhp,rn->hpn', toward, heads_x, b_in, precision=highest)
    updated = jnp.exp(last_sum)[:, None, None] * carry_state + added_in
    return (updated, within + carried)

def layer(hidden, in_w, out_w, conv_w, conv_b, norm_gain, gate_gain, dt_bias, decay_rates, d_skip):
    length = hidden.shape[0]
    normed = low(rms_scale(hidden, norm_gain))
    projected = low_back(jnp.dot(normed, in_w, precision=highest))
    gate_z = projected[:, :DI]
    conv_in = low(projected[:, DI:DI + CONVC])
    dt_raw = projected[:, DI + CONVC:]
    padded = jnp.concatenate([jnp.zeros((KW - 1, CONVC), jnp.float32), conv_in], axis=0)
    mixed = jnp.zeros((length, CONVC), jnp.float32) + conv_b[None, :]
    for offset in range(KW):
        mixed = mixed + conv_w[offset][None, :] * padded[offset:offset + length]
    activated = low(jax.nn.silu(mixed))
    heads_x = activated[:, :DI].reshape(length, H, P_SIZE)
    b_in = activated[:, DI:DI + NS]
    c_out = activated[:, DI + NS:]
    steps_dt = jax.nn.softplus(dt_raw + dt_bias[None, :])
    neg_rate = -decay_rates
    blocks_n = length // SPAN
    stacked = (heads_x.reshape(blocks_n, SPAN, H, P_SIZE), b_in.reshape(blocks_n, SPAN, NS), c_out.reshape(blocks_n, SPAN, NS), steps_dt.reshape(blocks_n, SPAN, H))

    def advance(carry_state, pieces):
        return span_step(carry_state, pieces[0], pieces[1], pieces[2], pieces[3], neg_rate)
    final_state, outputs = lax.scan(jax.checkpoint(advance), jnp.zeros((H, P_SIZE, NS), jnp.float32), stacked)
    ssd_out = outputs.reshape(length, H, P_SIZE) + d_skip[None, :, None] * heads_x
    gated = ssd_out.reshape(length, DI) * jax.nn.silu(gate_z)
    branch = low(rms_scale(gated, gate_gain))
    return hidden + jnp.dot(branch, out_w, precision=highest)

def reference(hidden, cotangent, in_w, out_w, conv_w, conv_b, norm_gain, gate_gain, dt_bias, decay_rates, d_skip):
    params = (in_w.astype(jnp.float32), out_w.astype(jnp.float32), conv_w.astype(jnp.float32), conv_b.astype(jnp.float32), norm_gain.astype(jnp.float32), gate_gain.astype(jnp.float32), dt_bias.astype(jnp.float32), decay_rates.astype(jnp.float32), d_skip.astype(jnp.float32))

    def one_sequence(totals, pair):
        seq_in, seq_cot = pair
        result, pull = jax.vjp(layer, seq_in.astype(jnp.float32), *params)
        grads = pull(seq_cot.astype(jnp.float32))
        totals = tuple((total + grad for total, grad in zip(totals, grads[1:])))
        return (totals, (result.astype(jnp.bfloat16), grads[0]))
    zeros = tuple((jnp.zeros_like(param) for param in params))
    totals, (outputs, d_hidden) = lax.scan(one_sequence, zeros, (hidden, cotangent))
    return (outputs, d_hidden, totals[0], totals[1], totals[2], totals[3], totals[4], totals[5], totals[6], totals[7], totals[8])
```

```python
import functools
import jax
import jax.numpy as jnp
from jax import lax
from jax.experimental import pallas as pl
from jax.experimental.pallas import tpu as pltpu
from jax.sharding import PartitionSpec as P, Mesh

MESH = pl.DeviceIdType.MESH
ALL = ("z", "y", "x", "c")
ORDERS = (("z", "y", "x"), ("y", "x", "z"), ("x", "z", "y"))


class Links:
    def __init__(self, send, recv):
        self.send, self.recv, self.used, self.sent = send, recv, 0, []

    def copy(self, src, dst, device):
        k = self.used
        self.used += 1
        made = pltpu.make_async_remote_copy(
            src_ref=src, dst_ref=dst, send_sem=self.send.at[k], recv_sem=self.recv.at[k],
            device_id=device, device_id_type=MESH)
        made.start()
        self.sent.append(made)
        return made

    def finish(self):
        for made in self.sent:
            made.wait_send()


def place():
    return {name: lax.axis_index(name) for name in ALL}


def block(ref, part, core, at, have, half=None):
    z, y, x = at["z"], at["y"], at["x"]
    wide = ref.shape[-1]
    full = slice(None)
    zh, zl = (full, full) if "z" in have else (z // 2, lax.rem(z, 2))
    ys = full if "y" in have else y
    first, count = (0, wide) if "x" in have else (x * (wide // 4), wide // 4)
    if half is not None:
        if "y" in have:
            ys = pl.ds(2 * half, 2)
        elif "z" in have:
            zh = pl.ds(half, 1)
        else:
            near = -(-count // 256) * 128
            first, count = (first, near) if half == 0 else (first + near, count - near)
    cols = full if "x" in have and count == wide else pl.ds(first if isinstance(first, int) else pl.multiple_of(first, 128), count)
    return ref.at[core, zh, ys, zl, part, :, cols]


def moved(at, axis, steps):
    return {**at, axis: lax.rem(at[axis] + steps + 4, 4)}


def gather_kernel(*refs, n, rows):
    shards, fulls, refs = refs[:n], refs[n:2 * n], refs[2 * n:]
    stage, landed, unit, (send, recv, own) = refs[:n], refs[n:2 * n], refs[2 * n:3 * n], refs[3 * n:]
    at = place()
    z, y, x, c = (at[name] for name in ALL)
    to_z, to_c = 2 * lax.rem(z, 2) + x // 2, z // 2
    slot = 2 * lax.rem(x, 2) + c
    from_z = 2 * c + z // 2
    barrier = pltpu.get_barrier_semaphore()
    for axis in ("z", "y", "x"):
        for steps in (1, -1):
            pl.semaphore_signal(barrier, inc=1, device_id={axis: moved(at, axis, steps)[axis]}, device_id_type=MESH)
    pl.semaphore_signal(barrier, inc=1, device_id={"c": 1 - c}, device_id_type=MESH)
    for k in range(4):
        sx, sc = 2 * lax.rem(z, 2) + k // 2, k % 2
        other = jnp.logical_or(jnp.logical_or(sx != x, sc != c), from_z != z)

        @pl.when(other)
        def _():
            pl.semaphore_signal(barrier, inc=1, device_id=(from_z, y, sx, jnp.int32(sc)), device_id_type=MESH)
    home = jnp.logical_and(to_z == z, to_c == c)
    pl.semaphore_wait(barrier, 11 - home.astype(jnp.int32))

    links = Links(send, recv)
    first = []
    for i in range(n):
        wide = shards[i].shape[1] // 4
        for tx in range(4):
            k = links.used
            links.used += 1
            src = shards[i].at[:, pl.ds(tx * wide, wide)]
            remote = pltpu.make_async_remote_copy(
                src_ref=src, dst_ref=landed[i].at[slot], send_sem=send.at[k], recv_sem=recv.at[4 * i + slot],
                device_id=(to_z, y, jnp.int32(tx), to_c), device_id_type=MESH)
            local = pltpu.make_async_copy(src, landed[i].at[slot], recv.at[4 * i + slot])
            mine = jnp.logical_and(home, x == tx)
            pl.when(jnp.logical_not(mine))(remote.start)
            pl.when(mine)(local.start)
            first.append((remote, mine))
    kept = []
    for i in range(n):
        deep, height = rows[i], unit[i].shape[1]
        for k in range(4):
            pltpu.make_async_copy(landed[i].at[k], landed[i].at[k], recv.at[4 * i + k]).wait()
            stage[i][pl.ds(deep * k, deep), :] = landed[i][k, :deep, :].astype(jnp.float32)
        for part in range(3):
            unit[i][part] = stage[i][pl.ds(part * height, height), :].astype(jnp.bfloat16)
        for part in range(3):
            copy = pltpu.make_async_copy(unit[i].at[part], block(fulls[i], part, c, at, ()), own.at[3 * i + part])
            copy.start()
            kept.append(copy)
    sibling = {"c": 1 - c}
    streams = [(i, part) for i in range(n) for part in range(3)]
    for phase in range(3):
        near = {}
        for i, part in streams:
            have, axis = ORDERS[part][:phase], ORDERS[part][phase]
            mine = unit[i].at[part] if phase == 0 else block(fulls[i], part, c, at, have)
            there = block(fulls[i], part, c, at, have)
            near[i, part] = [links.copy(mine, there, {axis: moved(at, axis, steps)[axis]}) for steps in (1, -1)]
            if phase == 0:
                links.copy(mine, there, sibling)
        far = {}
        for i, part in streams:
            have, axis = ORDERS[part][:phase], ORDERS[part][phase]
            far[i, part] = []
            for way, steps in ((0, 1), (1, -1)):
                near[i, part][way].wait_recv()
                behind = moved(at, axis, -steps)
                piece = block(fulls[i], part, c, behind, have, way)
                far[i, part].append(links.copy(piece, piece, {axis: moved(at, axis, steps)[axis]}))
                whole = block(fulls[i], part, c, behind, have)
                links.copy(whole, whole, sibling)
        for i, part in streams:
            have, axis = ORDERS[part][:phase], ORDERS[part][phase]
            for way in (0, 1):
                far[i, part][way].wait_recv()
                piece = block(fulls[i], part, c, moved(at, axis, 2), have, way)
                links.copy(piece, piece, sibling)
        if phase == 0:
            for copy in kept:
                copy.wait()
    for made in links.sent:
        if made.device_id is sibling:
            made.wait_recv()
    links.finish()
    for remote, mine in first:
        pl.when(jnp.logical_not(mine))(remote.wait_send)


def gather(shards, rows):
    n = len(shards)
    heights = [4 * r // 3 for r in rows]
    wides = [s.shape[1] for s in shards]
    fulls = [jax.ShapeDtypeStruct((2, 2, 4, 2, 3, h, w), jnp.bfloat16) for h, w in zip(heights, wides)]
    count = n * (4 + 3 * (3 * 3 * 2 + 1 + 6))
    outs = pl.pallas_call(
        functools.partial(gather_kernel, n=n, rows=tuple(rows)),
        out_shape=fulls,
        in_specs=[pl.BlockSpec(memory_space=pltpu.VMEM)] * n,
        out_specs=[pl.BlockSpec(memory_space=pl.ANY)] * n,
        scratch_shapes=[pltpu.VMEM((3 * h, w // 4), jnp.float32) for h, w in zip(heights, wides)]
        + [pltpu.VMEM((4, s.shape[0], w // 4), jnp.bfloat16) for s, w in zip(shards, wides)]
        + [pltpu.VMEM((3, h, w // 4), jnp.bfloat16) for h, w in zip(heights, wides)]
        + [pltpu.SemaphoreType.DMA((count,)), pltpu.SemaphoreType.DMA((count,)), pltpu.SemaphoreType.DMA((3 * n,))],
        compiler_params=pltpu.CompilerParams(collective_id=0, has_side_effects=True, vmem_limit_bytes=32 << 20),
        name="gather_weights",
    )(*shards)
    return [o.reshape(128 * r, w) for o, r, w in zip(outs, rows, wides)]


def span(shape, axis, at):
    cut = [slice(None)] * 5
    if axis == "y":
        cut[1] = pl.ds(at["y"], 1)
    elif axis == "z":
        cut[0], cut[2] = pl.ds(at["z"] // 2, 1), pl.ds(lax.rem(at["z"], 2), 1)
    else:
        cut[4] = pl.ds(pl.multiple_of(at["x"] * (shape[4] // 4), 128), shape[4] // 4)
    return cut


def without(shape, axis):
    zh, y, zl, rows, wide = shape
    return {"y": (zh, 1, zl, rows, wide), "z": (1, y, 1, rows, wide), "x": (zh, y, zl, rows, wide // 4)}[axis]


def halves(shape):
    if shape[1] == 4:
        return 1, ((0, 2), (2, 2))
    if shape[0] == 2:
        return 0, ((0, 1), (1, 1))
    near = -(-shape[4] // 256) * 128
    return 4, ((0, near), (near, shape[4] - near))


def cut_half(cut, shape, half):
    dim, parts = halves(shape)
    start, size = parts[half]
    cut = list(cut)
    old = cut[dim]
    base = 0 if isinstance(old, slice) else old.start
    cut[dim] = pl.ds(pl.multiple_of(base + start, 128) if dim == 4 and not isinstance(base, int) else base + start, size)
    return cut


def half_shape(shape, half):
    dim, parts = halves(shape)
    return tuple(parts[half][1] if k == dim else size for k, size in enumerate(shape))


def add_up(out, terms, shape):
    na, nb, nc = shape[:3]

    def slab(k, carry):
        a, b, d = k // (nb * nc), lax.rem(k // nc, nb), lax.rem(k, nc)
        total = terms[0](a, b, d).astype(jnp.float32)
        for term in terms[1:]:
            total = total + term(a, b, d).astype(jnp.float32)
        out(a, b, d, total)
        return carry

    lax.fori_loop(0, na * nb * nc, slab, 0)


def start_of(cut):
    return 0 if isinstance(cut, slice) else cut.start


def slab_of(ref, cut, shape):
    z0, y0, l0, _, c0 = (start_of(s) for s in cut)
    lead = ref

    def read(a, b, d):
        return lead[z0 + a, y0 + b, l0 + d, :, pl.ds(c0, shape[4])]

    return read


def slab_to(ref, shape):
    def write(a, b, d, value):
        ref[a, b, d] = value.astype(ref.dtype)

    return write


ALL_CUT = [slice(None)] * 5


def scatter_kernel(*refs, n, rows, shapes, tall):
    parts_in, small_in, refs = refs[:n], refs[n], refs[n + 1:]
    outs, small_out, refs = refs[:n], refs[n], refs[n + 1:]
    take = iter(refs)
    near, relay, acc = {}, {}, {}
    streams = [(i, part) for i in range(n) for part in range(3)]
    for phase in range(3):
        for s in streams:
            near[s, phase] = [next(take), next(take)]
            relay[s, phase] = [next(take), next(take)]
            acc[s, phase] = next(take) if phase < 2 else None
    fin = [next(take) for _ in range(n)]
    staged = [next(take) for _ in range(n)]
    landed = [next(take) for _ in range(n)]
    rounds = [next(take) for _ in range(4)]
    send, recv, last, own = (next(take) for _ in range(4))
    at = place()
    z, y, x, c = (at[name] for name in ALL)
    to_z, to_c = 2 * lax.rem(z, 2) + x // 2, z // 2
    from_z = 2 * c + z // 2
    home = jnp.logical_and(to_z == z, to_c == c)
    barrier = pltpu.get_barrier_semaphore()
    for axis in ("z", "y", "x"):
        for steps in (1, 2, 3):
            pl.semaphore_signal(barrier, inc=1, device_id={axis: moved(at, axis, steps)[axis]}, device_id_type=MESH)
    pl.semaphore_signal(barrier, inc=1, device_id={"c": 1 - c}, device_id_type=MESH)
    for tx in range(4):
        mine = jnp.logical_and(home, x == tx)

        @pl.when(jnp.logical_not(mine))
        def _():
            pl.semaphore_signal(barrier, inc=1, device_id=(to_z, y, jnp.int32(tx), to_c), device_id_type=MESH)
    pl.semaphore_wait(barrier, 14 - home.astype(jnp.int32))

    links = Links(send, recv)

    def small_start(k):
        axis = ("c", "x", "y", "z")[k]
        rounds[k][at[axis]] = small_in[...] if k == 0 else sums[0]
        held = rounds[k].at[at[axis]]
        if k == 0:
            return [links.copy(held, held, {"c": 1 - c})]
        return [links.copy(held, held, {axis: moved(at, axis, steps)[axis]}) for steps in (1, 2, 3)]

    def small_end(k, going):
        for copy in going:
            copy.wait_recv()
        total = rounds[k][0]
        for j in range(1, 2 if k == 0 else 4):
            total = total + rounds[k][j]
        sums[0] = total

    sums = [None]
    size = {s: shapes[s[0]] for s in streams}
    source = {s: parts_in[s[0]].at[:, :, :, s[1]] for s in streams}
    going = small_start(0)
    for phase in range(3):
        sent, lent = {}, {}
        for s in streams:
            axis = ORDERS[s[1]][2 - phase]
            shape = without(size[s], axis)
            cuts = {k: span(size[s], axis, moved(at, axis, k)) for k in (0, 1, 2, 3)}
            to = {k: {axis: moved(at, axis, k)[axis]} for k in (1, 3)}
            lent[s], sent[s] = [], []
            for way, step in ((0, 1), (1, 3)):
                src = source[s].at[tuple(cut_half(cuts[2], shape, way))]
                lent[s].append(links.copy(src, relay[s, phase][way], to[step]))
            for way, step in ((0, 1), (1, 3)):
                src = source[s].at[tuple(cut_half(cuts[step], shape, 1 - way))]
                dst = near[s, phase][way].at[tuple(cut_half(ALL_CUT, shape, 1 - way))]
                sent[s].append(links.copy(src, dst, to[step]))
        small_end(phase, going)
        going = small_start(phase + 1)
        for s in streams:
            axis = ORDERS[s[1]][2 - phase]
            shape = without(size[s], axis)
            for way, step in ((0, 1), (1, 3)):
                lent[s][way].wait_recv()
                hs = half_shape(shape, way)
                cut = cut_half(span(size[s], axis, moved(at, axis, step)), shape, way)
                buf = relay[s, phase][way]
                add_up(slab_to(buf, hs), [slab_of(source[s], cut, hs), slab_of(buf, ALL_CUT, hs)], hs)
                dst = near[s, phase][way].at[tuple(cut_half(ALL_CUT, shape, way))]
                sent[s].append(links.copy(buf, dst, {axis: moved(at, axis, step)[axis]}))
        for s in streams:
            i, part = s
            axis = ORDERS[part][2 - phase]
            shape = without(size[s], axis)
            for copy in sent[s]:
                copy.wait_recv()
            terms = [slab_of(source[s], span(size[s], axis, at), shape)]
            terms += [slab_of(near[s, phase][way], ALL_CUT, shape) for way in (0, 1)]
            if phase < 2:
                add_up(slab_to(acc[s, phase], shape), terms, shape)
                source[s], size[s] = acc[s, phase], shape
            else:
                total = terms[0](0, 0, 0).astype(jnp.float32)
                for term in terms[1:]:
                    total = total + term(0, 0, 0).astype(jnp.float32)
                fin[i][pl.ds(part * shape[3], shape[3]), :] = total
    small_end(3, going)
    small_out[...] = sums[0]
    final = []
    for i in range(n):
        deep, wide = rows[i], fin[i].shape[1]
        for k in range(4):
            sx, sc = 2 * lax.rem(z, 2) + k // 2, k % 2
            staged[i][k] = jnp.zeros(staged[i].shape[1:], jnp.float32)
            staged[i][k, :deep] = fin[i][pl.ds(deep * k, deep), :]
            mine = jnp.logical_and(home, jnp.logical_and(sx == x, sc == c))
            remote = pltpu.make_async_remote_copy(
                src_ref=staged[i].at[k], dst_ref=landed[i].at[x], send_sem=own.at[4 * i + k], recv_sem=last.at[4 * i + x],
                device_id=(from_z, y, sx, jnp.int32(sc)), device_id_type=MESH)
            local = pltpu.make_async_copy(staged[i].at[k], landed[i].at[x], last.at[4 * i + x])
            pl.when(jnp.logical_not(mine))(remote.start)
            pl.when(mine)(local.start)
            final.append((remote, mine))
    for i in range(n):
        wide = fin[i].shape[1]
        for tx in range(4):
            pltpu.make_async_copy(landed[i].at[tx], landed[i].at[tx], last.at[4 * i + tx]).wait()
            outs[i][:, pl.ds(tx * wide, wide)] = landed[i][tx]
    links.finish()
    for remote, mine in final:
        pl.when(jnp.logical_not(mine))(remote.wait_send)


def scatter(halves_in, small, rows):
    n = len(halves_in)
    wides = [h.shape[1] for h in halves_in]
    heights = [4 * r // 3 for r in rows]
    ins = [h.reshape(2, 4, 2, 3, t, w) for h, t, w in zip(halves_in, heights, wides)]
    shapes = [(2, 4, 2, t, w) for t, w in zip(heights, wides)]
    tall = [-(-r // 8) * 8 for r in rows]
    scratch = []
    size = {(i, part): shapes[i] for i in range(n) for part in range(3)}
    for phase in range(3):
        for s in size:
            shape = without(size[s], ORDERS[s[1]][2 - phase])
            scratch += [pltpu.VMEM(shape, jnp.bfloat16)] * 2
            scratch += [pltpu.VMEM(half_shape(shape, way), jnp.bfloat16) for way in (0, 1)]
            if phase < 2:
                scratch += [pltpu.VMEM(shape, jnp.bfloat16)]
            size[s] = shape
    scratch += [pltpu.VMEM((3 * t, w // 4), jnp.float32) for t, w in zip(heights, wides)]
    scratch += [pltpu.VMEM((4, t, w // 4), jnp.float32) for t, w in zip(tall, wides)]
    scratch += [pltpu.VMEM((4, t, w // 4), jnp.float32) for t, w in zip(tall, wides)]
    scratch += [pltpu.VMEM((2 if k == 0 else 4,) + small.shape, jnp.float32) for k in range(4)]
    count = n * 3 * 3 * 6 + 10
    scratch += [pltpu.SemaphoreType.DMA((count,)), pltpu.SemaphoreType.DMA((count,)),
                pltpu.SemaphoreType.DMA((4 * n,)), pltpu.SemaphoreType.DMA((4 * n,))]
    outs = pl.pallas_call(
        functools.partial(scatter_kernel, n=n, rows=tuple(rows), shapes=tuple(shapes), tall=tuple(tall)),
        out_shape=[jax.ShapeDtypeStruct((t, w), jnp.float32) for t, w in zip(tall, wides)] + [jax.ShapeDtypeStruct(small.shape, jnp.float32)],
        in_specs=[pl.BlockSpec(memory_space=pltpu.VMEM)] * (n + 1),
        out_specs=[pl.BlockSpec(memory_space=pltpu.VMEM)] * (n + 1),
        scratch_shapes=scratch,
        compiler_params=pltpu.CompilerParams(collective_id=1, has_side_effects=True, vmem_limit_bytes=56 << 20),
        name="scatter_gradients",
    )(*ins, small)
    return outs


H = 48
P_SIZE = 64
NS = 128
KW = 4
DI = 3072
CONVC = 3328
PROJ = 6448
WIDE = 6656
PARAMS = 6528
SEQ = ("y", "x", "c")
epsilon = 1e-05
highest = lax.Precision.HIGHEST


def from_behind(value, steps):
    return lax.ppermute(value, SEQ, [(k, k + steps) for k in range(max(0, -steps), min(32, 32 - steps))])


def carried_in(decay, state, backward):
    mine = lax.axis_index(SEQ)
    rows = H * P_SIZE // 32
    spread = jnp.repeat(decay, P_SIZE).reshape(32, 1, rows)
    spread = jnp.pad(spread, ((0, 0), (0, 7), (0, 128 - rows)))
    packed = jnp.concatenate([state.reshape(32, rows, NS), spread], axis=1)
    blocks = lax.all_to_all(packed, SEQ, split_axis=0, concat_axis=0, tiled=True)
    decays = blocks[:, rows, :rows]
    states = blocks[:, :rows]

    def lap(carry, piece):
        return piece[0][:, None] * carry + piece[1], carry

    _, before = lax.scan(lap, jnp.zeros((rows, NS), jnp.float32), (decays, states), reverse=backward, unroll=8)
    back = lax.all_to_all(before, SEQ, split_axis=0, concat_axis=0, tiled=True)
    return back.reshape(H, P_SIZE, NS)


def rms_scale(values, gain):
    return values * lax.rsqrt(jnp.mean(values * values, axis=-1, keepdims=True) + epsilon) * gain


def span_step(heads_x, b_in, c_out, steps_dt, neg_rate):
    block_len = heads_x.shape[0]
    log_decay = steps_dt * neg_rate[None, :]
    cum_decay = jnp.cumsum(log_decay, axis=0)
    position = jnp.arange(block_len)
    causal = (position[:, None] >= position[None, :]).astype(jnp.float32)
    gap_decay = (
        jnp.exp((cum_decay[:, None, :] - cum_decay[None, :, :]) * causal[:, :, None])
        * causal[:, :, None]
    )
    scores = jnp.dot(c_out, b_in.T, precision=highest)
    mixing = scores[:, :, None] * gap_decay * steps_dt[None, :, :]
    within = jnp.einsum("trh,rhp->thp", mixing, heads_x, precision=highest)
    last_sum = cum_decay[-1]
    toward = jnp.exp(last_sum[None, :] - cum_decay) * steps_dt
    added_in = jnp.einsum("rh,rhp,rn->hpn", toward, heads_x, b_in, precision=highest)
    return (added_in, within)


def local_core(heads_x, b_in, c_out, steps_dt, neg_rate, d_skip):
    final_state, outputs = span_step(heads_x, b_in, c_out, steps_dt, neg_rate)
    cum_decay = jnp.cumsum(steps_dt * neg_rate[None, :], axis=0)
    local_out = outputs + d_skip[None, :, None] * heads_x
    return (local_out, final_state, jnp.exp(cum_decay[-1]), cum_decay)


def correction(c_out, cum_decay, incoming):
    return jnp.exp(cum_decay)[:, :, None] * jnp.einsum(
        "tn,hpn->thp", c_out, incoming, precision=highest
    )


def full_mixer(heads_x, b_in, c_out, steps_dt, neg_rate, d_skip, incoming):
    local_out, final_state, total_decay, cum_decay = local_core(
        heads_x, b_in, c_out, steps_dt, neg_rate, d_skip
    )
    return (local_out + correction(c_out, cum_decay, incoming), final_state, total_decay)


def conv_section(extended, w_conv, b_conv, dt_raw, dt_bias, decay_rates):
    length = dt_raw.shape[0]
    mixed = jnp.zeros((length, CONVC), jnp.float32) + b_conv[None, :]
    for offset in range(KW):
        mixed = mixed + w_conv[offset][None, :] * extended[offset : offset + length]
    return (jax.nn.silu(mixed), jax.nn.softplus(dt_raw + dt_bias[None, :]), -decay_rates)


def gate_section(ssd_out, gate_z, gain_gate):
    length = gate_z.shape[0]
    gated = ssd_out.reshape(length, DI) * jax.nn.silu(gate_z)
    return rms_scale(gated, gain_gate)


def swap(value):
    return lax.ppermute(value, "c", [(0, 1), (1, 0)])


def my_half(value, core):
    wide = value.shape[1] // 2
    given = swap(lax.dynamic_slice_in_dim(value, (1 - core) * wide, wide, axis=1))
    return jnp.concatenate([lax.dynamic_slice_in_dim(value, core * wide, wide, axis=1), given], axis=0)


def shards(
    hidden,
    cotangent,
    in_w,
    out_w,
    conv_w,
    conv_b,
    norm_gain,
    gate_gain,
    dt_bias,
    decay_rates,
    d_skip,
):
    core = lax.axis_index("c")
    spare = jnp.concatenate([
        jnp.pad(conv_w, ((0, 0), (0, 102))),
        jnp.pad(conv_b, (0, 102))[None],
        jnp.pad(norm_gain, (0, 116))[None],
        jnp.pad(gate_gain, (0, 104))[None],
        jnp.zeros((5, 128), jnp.bfloat16),
    ])
    shard_in = jnp.pad(jnp.concatenate([jnp.pad(in_w, ((0, 0), (0, PARAMS - PROJ))), spare], axis=1), ((0, 4), (0, 0)))
    w_in, w_out = gather([shard_in, jnp.pad(out_w, ((0, 8), (0, 0)))], [12, 24])
    spare = w_in[:, PARAMS:].reshape(128, 12, 128).astype(jnp.float32)
    w_conv_f = spare[:, :4, :26].transpose(1, 0, 2).reshape(KW, CONVC)
    b_conv_f = spare[:, 4, :26].reshape(CONVC)
    gain_norm_f = spare[:, 5, :12].reshape(1536)
    gain_gate_f = spare[:, 6, :24].reshape(DI)
    w_in = w_in * (jnp.arange(WIDE) < PROJ).astype(jnp.bfloat16)[None, :]
    residual = hidden[0].astype(jnp.float32)
    length = residual.shape[0]
    normed = rms_scale(residual, gain_norm_f).astype(jnp.bfloat16)
    projected = jnp.dot(normed, w_in, preferred_element_type=jnp.float32)
    gate_z = projected[:, :DI]
    conv_in = projected[:, DI : DI + CONVC].astype(jnp.bfloat16)
    dt_raw = projected[:, DI + CONVC : PROJ]
    edge_rows = from_behind(conv_in[length - (KW - 1) :], 1)
    extended = jnp.concatenate([edge_rows, conv_in], axis=0).astype(jnp.float32)
    pre_act, steps_dt, neg_rate = conv_section(
        extended, w_conv_f, b_conv_f, dt_raw, dt_bias, decay_rates
    )
    activated = lax.optimization_barrier(pre_act.astype(jnp.bfloat16)).astype(jnp.float32)
    heads_x = activated[:, :DI].reshape(length, H, P_SIZE)
    b_in = activated[:, DI : DI + NS]
    c_out = activated[:, DI + NS :]
    local_out, final_state, total_decay, cum_decay = local_core(
        heads_x, b_in, c_out, steps_dt, neg_rate, d_skip
    )
    incoming = carried_in(total_decay, final_state, False)
    ssd_out = local_out + correction(c_out, cum_decay, incoming)
    branch = gate_section(ssd_out, gate_z, gain_gate_f).astype(jnp.bfloat16)
    result = (residual + jnp.dot(branch, w_out, preferred_element_type=jnp.float32)).astype(
        jnp.bfloat16
    )
    grad_out = cotangent[0]
    both_out = jnp.concatenate([grad_out, swap(grad_out)], axis=0)
    d_branch = jnp.einsum("td,kd->tk", grad_out, w_out, preferred_element_type=jnp.float32)
    d_w_out = jnp.einsum("tk,td->kd", my_half(branch, core), both_out, preferred_element_type=jnp.float32).astype(jnp.bfloat16)
    gate_pull = jax.vjp(gate_section, ssd_out, gate_z, gain_gate_f)[1]
    d_ssd, d_gate_z, d_gain_gate = gate_pull(d_branch)
    d_incoming = jnp.einsum("th,thp,tn->hpn", jnp.exp(cum_decay), d_ssd, c_out, precision=highest)
    carried_back = carried_in(total_decay, d_incoming, True)
    d_total_decay = jnp.sum(carried_back * incoming, axis=(1, 2))
    mixer_pull = jax.vjp(full_mixer, heads_x, b_in, c_out, steps_dt, neg_rate, d_skip, incoming)[1]
    d_heads_x, d_b_in, d_c_out, d_steps, d_rate, d_dskip, unused_grad = mixer_pull(
        (d_ssd, carried_back, d_total_decay)
    )
    d_act = jnp.concatenate([d_heads_x.reshape(length, DI), d_b_in, d_c_out], axis=1)
    conv_pull = jax.vjp(conv_section, extended, w_conv_f, b_conv_f, dt_raw, dt_bias, decay_rates)[1]
    d_ext, d_conv_w, d_conv_b, d_dt_raw, d_dt_bias, d_rates = conv_pull((d_act, d_steps, d_rate))
    back_rows = from_behind(d_ext[: KW - 1].astype(jnp.bfloat16), -1).astype(jnp.float32)
    d_conv_in = d_ext[KW - 1 :] + jnp.pad(back_rows, ((length - (KW - 1), 0), (0, 0)))
    d_projected = jnp.concatenate(
        [d_gate_z, d_conv_in, d_dt_raw, jnp.zeros((length, WIDE - PROJ), jnp.float32)], axis=1
    ).astype(jnp.bfloat16)
    d_normed = jnp.einsum("tj,dj->td", d_projected, w_in, preferred_element_type=jnp.float32)
    both_projected = jnp.concatenate([d_projected, swap(d_projected)], axis=0)
    d_w_in = jnp.einsum("td,tj->dj", my_half(normed, core), both_projected, preferred_element_type=jnp.float32).astype(jnp.bfloat16)
    norm_pull = jax.vjp(rms_scale, residual, gain_norm_f)[1]
    d_from_norm, d_gain_norm = norm_pull(d_normed)
    d_hidden = grad_out.astype(jnp.float32) + d_from_norm
    small = jnp.concatenate([
        d_conv_w.reshape(-1), d_conv_b, d_gain_norm, d_gain_gate,
        jnp.pad(d_dt_bias, (0, 80)), jnp.pad(d_rates, (0, 80)), jnp.pad(d_dskip, (0, 80)),
        jnp.zeros((896,), jnp.float32),
    ]).reshape(176, 128)
    g_in, g_out, total = scatter([d_w_in, d_w_out], small, [12, 24])
    mine = lax.axis_index(ALL)
    d_conv_w = total[:104].reshape(KW, CONVC)
    d_conv_b = total[104:130].reshape(CONVC)
    d_gain_norm = total[130:142].reshape(1536)
    d_gain_gate = total[142:166].reshape(DI)
    return (
        result[None],
        d_hidden[None],
        g_in[:12, :PROJ],
        g_out,
        lax.dynamic_slice_in_dim(d_conv_w, 26 * mine, 26, axis=1),
        lax.dynamic_slice_in_dim(d_conv_b, 26 * mine, 26),
        lax.dynamic_slice_in_dim(d_gain_norm, 12 * mine, 12),
        lax.dynamic_slice_in_dim(d_gain_gate, 24 * mine, 24),
        total[166, :H],
        total[167, :H],
        total[168, :H],
    )


def solution(mesh):
    grid = Mesh(mesh.devices.reshape(4, 4, 4, 2), ALL)
    tokens = P("z", SEQ, None)
    placed = (
        tokens,
        tokens,
        P(ALL, None),
        P(ALL, None),
        P(None, ALL),
        P(ALL),
        P(ALL),
        P(ALL),
        P(),
        P(),
        P(),
    )
    return jax.shard_map(
        shards,
        mesh=grid,
        in_specs=placed,
        out_specs=(tokens, tokens, P(ALL, None), P(ALL, None), P(None, ALL), P(ALL), P(ALL), P(ALL), P(), P(), P()),
        check_vma=False,
    )
```

```python
import functools
import jax
import jax.numpy as jnp
from jax import lax
from jax.experimental import pallas as pl
from jax.experimental.pallas import tpu as pltpu
from jax.sharding import PartitionSpec as P, Mesh

MESH = pl.DeviceIdType.MESH
ALL = ("z", "y", "x", "c")
ORDERS = (("z", "y", "x"), ("y", "x", "z"), ("x", "z", "y"))


class Links:
    def __init__(self, send, recv):
        self.send, self.recv, self.used, self.sent = send, recv, 0, []

    def copy(self, src, dst, device):
        k = self.used
        self.used += 1
        made = pltpu.make_async_remote_copy(
            src_ref=src, dst_ref=dst, send_sem=self.send.at[k], recv_sem=self.recv.at[k],
            device_id=device, device_id_type=MESH)
        made.start()
        self.sent.append(made)
        return made

    def finish(self):
        for made in self.sent:
            made.wait_send()


def place():
    return {name: lax.axis_index(name) for name in ALL}


def block(ref, part, core, at, have, half=None):
    z, y, x = at["z"], at["y"], at["x"]
    wide = ref.shape[-1]
    full = slice(None)
    zh, zl = (full, full) if "z" in have else (z // 2, lax.rem(z, 2))
    ys = full if "y" in have else y
    first, count = (0, wide) if "x" in have else (x * (wide // 4), wide // 4)
    if half is not None:
        if "y" in have:
            ys = pl.ds(2 * half, 2)
        elif "z" in have:
            zh = pl.ds(half, 1)
        else:
            near = -(-count // 256) * 128
            first, count = (first, near) if half == 0 else (first + near, count - near)
    cols = full if "x" in have and count == wide else pl.ds(first if isinstance(first, int) else pl.multiple_of(first, 128), count)
    return ref.at[core, zh, ys, zl, part, :, cols]


def moved(at, axis, steps):
    return {**at, axis: lax.rem(at[axis] + steps + 4, 4)}


def gather_kernel(*refs, n, rows):
    shards, fulls, refs = refs[:n], refs[n:2 * n], refs[2 * n:]
    stage, landed, unit, (send, recv, own) = refs[:n], refs[n:2 * n], refs[2 * n:3 * n], refs[3 * n:]
    at = place()
    z, y, x, c = (at[name] for name in ALL)
    to_z, to_c = 2 * lax.rem(z, 2) + x // 2, z // 2
    slot = 2 * lax.rem(x, 2) + c
    from_z = 2 * c + z // 2
    barrier = pltpu.get_barrier_semaphore()
    for axis in ("z", "y", "x"):
        for steps in (1, -1):
            pl.semaphore_signal(barrier, inc=1, device_id={axis: moved(at, axis, steps)[axis]}, device_id_type=MESH)
    pl.semaphore_signal(barrier, inc=1, device_id={"c": 1 - c}, device_id_type=MESH)
    for k in range(4):
        sx, sc = 2 * lax.rem(z, 2) + k // 2, k % 2
        other = jnp.logical_or(jnp.logical_or(sx != x, sc != c), from_z != z)

        @pl.when(other)
        def _():
            pl.semaphore_signal(barrier, inc=1, device_id=(from_z, y, sx, jnp.int32(sc)), device_id_type=MESH)
    home = jnp.logical_and(to_z == z, to_c == c)
    pl.semaphore_wait(barrier, 11 - home.astype(jnp.int32))

    links = Links(send, recv)
    first = []
    for i in range(n):
        wide = shards[i].shape[1] // 4
        for tx in range(4):
            k = links.used
            links.used += 1
            src = shards[i].at[:, pl.ds(tx * wide, wide)]
            remote = pltpu.make_async_remote_copy(
                src_ref=src, dst_ref=landed[i].at[slot], send_sem=send.at[k], recv_sem=recv.at[4 * i + slot],
                device_id=(to_z, y, jnp.int32(tx), to_c), device_id_type=MESH)
            local = pltpu.make_async_copy(src, landed[i].at[slot], recv.at[4 * i + slot])
            mine = jnp.logical_and(home, x == tx)
            pl.when(jnp.logical_not(mine))(remote.start)
            pl.when(mine)(local.start)
            first.append((remote, mine))
    kept = []
    for i in range(n):
        deep, height = rows[i], unit[i].shape[1]
        for k in range(4):
            pltpu.make_async_copy(landed[i].at[k], landed[i].at[k], recv.at[4 * i + k]).wait()
            stage[i][pl.ds(deep * k, deep), :] = landed[i][k, :deep, :].astype(jnp.float32)
        for part in range(3):
            unit[i][part] = stage[i][pl.ds(part * height, height), :].astype(jnp.bfloat16)
        for part in range(3):
            copy = pltpu.make_async_copy(unit[i].at[part], block(fulls[i], part, c, at, ()), own.at[3 * i + part])
            copy.start()
            kept.append(copy)
    sibling = {"c": 1 - c}
    streams = [(i, part) for i in range(n) for part in range(3)]
    for phase in range(3):
        near = {}
        for i, part in streams:
            have, axis = ORDERS[part][:phase], ORDERS[part][phase]
            mine = unit[i].at[part] if phase == 0 else block(fulls[i], part, c, at, have)
            there = block(fulls[i], part, c, at, have)
            near[i, part] = [links.copy(mine, there, {axis: moved(at, axis, steps)[axis]}) for steps in (1, -1)]
            if phase == 0:
                links.copy(mine, there, sibling)
        far = {}
        for i, part in streams:
            have, axis = ORDERS[part][:phase], ORDERS[part][phase]
            far[i, part] = []
            for way, steps in ((0, 1), (1, -1)):
                near[i, part][way].wait_recv()
                behind = moved(at, axis, -steps)
                piece = block(fulls[i], part, c, behind, have, way)
                far[i, part].append(links.copy(piece, piece, {axis: moved(at, axis, steps)[axis]}))
                whole = block(fulls[i], part, c, behind, have)
                links.copy(whole, whole, sibling)
        for i, part in streams:
            have, axis = ORDERS[part][:phase], ORDERS[part][phase]
            for way in (0, 1):
                far[i, part][way].wait_recv()
                piece = block(fulls[i], part, c, moved(at, axis, 2), have, way)
                links.copy(piece, piece, sibling)
        if phase == 0:
            for copy in kept:
                copy.wait()
    for made in links.sent:
        if made.device_id is sibling:
            made.wait_recv()
    links.finish()
    for remote, mine in first:
        pl.when(jnp.logical_not(mine))(remote.wait_send)


def gather(shards, rows):
    n = len(shards)
    heights = [4 * r // 3 for r in rows]
    wides = [s.shape[1] for s in shards]
    fulls = [jax.ShapeDtypeStruct((2, 2, 4, 2, 3, h, w), jnp.bfloat16) for h, w in zip(heights, wides)]
    count = n * (4 + 3 * (3 * 3 * 2 + 1 + 6))
    outs = pl.pallas_call(
        functools.partial(gather_kernel, n=n, rows=tuple(rows)),
        out_shape=fulls,
        in_specs=[pl.BlockSpec(memory_space=pltpu.VMEM)] * n,
        out_specs=[pl.BlockSpec(memory_space=pl.ANY)] * n,
        scratch_shapes=[pltpu.VMEM((3 * h, w // 4), jnp.float32) for h, w in zip(heights, wides)]
        + [pltpu.VMEM((4, s.shape[0], w // 4), jnp.bfloat16) for s, w in zip(shards, wides)]
        + [pltpu.VMEM((3, h, w // 4), jnp.bfloat16) for h, w in zip(heights, wides)]
        + [pltpu.SemaphoreType.DMA((count,)), pltpu.SemaphoreType.DMA((count,)), pltpu.SemaphoreType.DMA((3 * n,))],
        compiler_params=pltpu.CompilerParams(collective_id=0, has_side_effects=True, vmem_limit_bytes=32 << 20),
        name="gather_weights",
    )(*shards)
    return [o.reshape(128 * r, w) for o, r, w in zip(outs, rows, wides)]


def span(shape, axis, at):
    cut = [slice(None)] * 5
    if axis == "y":
        cut[1] = pl.ds(at["y"], 1)
    elif axis == "z":
        cut[0], cut[2] = pl.ds(at["z"] // 2, 1), pl.ds(lax.rem(at["z"], 2), 1)
    else:
        cut[4] = pl.ds(pl.multiple_of(at["x"] * (shape[4] // 4), 128), shape[4] // 4)
    return cut


def without(shape, axis):
    zh, y, zl, rows, wide = shape
    return {"y": (zh, 1, zl, rows, wide), "z": (1, y, 1, rows, wide), "x": (zh, y, zl, rows, wide // 4)}[axis]


def halves(shape):
    if shape[1] == 4:
        return 1, ((0, 2), (2, 2))
    if shape[0] == 2:
        return 0, ((0, 1), (1, 1))
    near = -(-shape[4] // 256) * 128
    return 4, ((0, near), (near, shape[4] - near))


def cut_half(cut, shape, half):
    dim, parts = halves(shape)
    start, size = parts[half]
    cut = list(cut)
    old = cut[dim]
    base = 0 if isinstance(old, slice) else old.start
    cut[dim] = pl.ds(pl.multiple_of(base + start, 128) if dim == 4 and not isinstance(base, int) else base + start, size)
    return cut


def half_shape(shape, half):
    dim, parts = halves(shape)
    return tuple(parts[half][1] if k == dim else size for k, size in enumerate(shape))


def add_up(out, terms, shape):
    na, nb, nc = shape[:3]

    def slab(k, carry):
        a, b, d = k // (nb * nc), lax.rem(k // nc, nb), lax.rem(k, nc)
        total = terms[0](a, b, d).astype(jnp.float32)
        for term in terms[1:]:
            total = total + term(a, b, d).astype(jnp.float32)
        out(a, b, d, total)
        return carry

    lax.fori_loop(0, na * nb * nc, slab, 0)


def start_of(cut):
    return 0 if isinstance(cut, slice) else cut.start


def slab_of(ref, cut, shape):
    z0, y0, l0, _, c0 = (start_of(s) for s in cut)
    lead = ref

    def read(a, b, d):
        return lead[z0 + a, y0 + b, l0 + d, :, pl.ds(c0, shape[4])]

    return read


def slab_to(ref, shape):
    def write(a, b, d, value):
        ref[a, b, d] = value.astype(ref.dtype)

    return write


ALL_CUT = [slice(None)] * 5


def scatter_kernel(*refs, n, rows, shapes, tall):
    parts_in, small_in, refs = refs[:n], refs[n], refs[n + 1:]
    outs, small_out, refs = refs[:n], refs[n], refs[n + 1:]
    take = iter(refs)
    near, relay, acc = {}, {}, {}
    streams = [(i, part) for i in range(n) for part in range(3)]
    for phase in range(3):
        for s in streams:
            near[s, phase] = [next(take), next(take)]
            relay[s, phase] = [next(take), next(take)]
            acc[s, phase] = next(take) if phase < 2 else None
    fin = [next(take) for _ in range(n)]
    staged = [next(take) for _ in range(n)]
    landed = [next(take) for _ in range(n)]
    rounds = [next(take) for _ in range(4)]
    send, recv, last, own = (next(take) for _ in range(4))
    at = place()
    z, y, x, c = (at[name] for name in ALL)
    to_z, to_c = 2 * lax.rem(z, 2) + x // 2, z // 2
    from_z = 2 * c + z // 2
    home = jnp.logical_and(to_z == z, to_c == c)
    barrier = pltpu.get_barrier_semaphore()
    for axis in ("z", "y", "x"):
        for steps in (1, 2, 3):
            pl.semaphore_signal(barrier, inc=1, device_id={axis: moved(at, axis, steps)[axis]}, device_id_type=MESH)
    pl.semaphore_signal(barrier, inc=1, device_id={"c": 1 - c}, device_id_type=MESH)
    for tx in range(4):
        mine = jnp.logical_and(home, x == tx)

        @pl.when(jnp.logical_not(mine))
        def _():
            pl.semaphore_signal(barrier, inc=1, device_id=(to_z, y, jnp.int32(tx), to_c), device_id_type=MESH)
    pl.semaphore_wait(barrier, 14 - home.astype(jnp.int32))

    links = Links(send, recv)

    def small_start(k):
        axis = ("c", "x", "y", "z")[k]
        rounds[k][at[axis]] = small_in[...] if k == 0 else sums[0]
        held = rounds[k].at[at[axis]]
        if k == 0:
            return [links.copy(held, held, {"c": 1 - c})]
        return [links.copy(held, held, {axis: moved(at, axis, steps)[axis]}) for steps in (1, 2, 3)]

    def small_end(k, going):
        for copy in going:
            copy.wait_recv()
        total = rounds[k][0]
        for j in range(1, 2 if k == 0 else 4):
            total = total + rounds[k][j]
        sums[0] = total

    sums = [None]
    size = {s: shapes[s[0]] for s in streams}
    source = {s: parts_in[s[0]].at[:, :, :, s[1]] for s in streams}
    going = small_start(0)
    for phase in range(3):
        sent, lent = {}, {}
        for s in streams:
            axis = ORDERS[s[1]][2 - phase]
            shape = without(size[s], axis)
            cuts = {k: span(size[s], axis, moved(at, axis, k)) for k in (0, 1, 2, 3)}
            to = {k: {axis: moved(at, axis, k)[axis]} for k in (1, 3)}
            lent[s], sent[s] = [], []
            for way, step in ((0, 1), (1, 3)):
                src = source[s].at[tuple(cut_half(cuts[2], shape, way))]
                lent[s].append(links.copy(src, relay[s, phase][way], to[step]))
            for way, step in ((0, 1), (1, 3)):
                src = source[s].at[tuple(cut_half(cuts[step], shape, 1 - way))]
                dst = near[s, phase][way].at[tuple(cut_half(ALL_CUT, shape, 1 - way))]
                sent[s].append(links.copy(src, dst, to[step]))
        small_end(phase, going)
        going = small_start(phase + 1)
        for s in streams:
            axis = ORDERS[s[1]][2 - phase]
            shape = without(size[s], axis)
            for way, step in ((0, 1), (1, 3)):
                lent[s][way].wait_recv()
                hs = half_shape(shape, way)
                cut = cut_half(span(size[s], axis, moved(at, axis, step)), shape, way)
                buf = relay[s, phase][way]
                add_up(slab_to(buf, hs), [slab_of(source[s], cut, hs), slab_of(buf, ALL_CUT, hs)], hs)
                dst = near[s, phase][way].at[tuple(cut_half(ALL_CUT, shape, way))]
                sent[s].append(links.copy(buf, dst, {axis: moved(at, axis, step)[axis]}))
        for s in streams:
            i, part = s
            axis = ORDERS[part][2 - phase]
            shape = without(size[s], axis)
            for copy in sent[s]:
                copy.wait_recv()
            terms = [slab_of(source[s], span(size[s], axis, at), shape)]
            terms += [slab_of(near[s, phase][way], ALL_CUT, shape) for way in (0, 1)]
            if phase < 2:
                add_up(slab_to(acc[s, phase], shape), terms, shape)
                source[s], size[s] = acc[s, phase], shape
            else:
                total = terms[0](0, 0, 0).astype(jnp.float32)
                for term in terms[1:]:
                    total = total + term(0, 0, 0).astype(jnp.float32)
                fin[i][pl.ds(part * shape[3], shape[3]), :] = total
    small_end(3, going)
    small_out[...] = sums[0]
    final = []
    for i in range(n):
        deep, wide = rows[i], fin[i].shape[1]
        for k in range(4):
            sx, sc = 2 * lax.rem(z, 2) + k // 2, k % 2
            staged[i][k] = jnp.zeros(staged[i].shape[1:], jnp.float32)
            staged[i][k, :deep] = fin[i][pl.ds(deep * k, deep), :]
            mine = jnp.logical_and(home, jnp.logical_and(sx == x, sc == c))
            remote = pltpu.make_async_remote_copy(
                src_ref=staged[i].at[k], dst_ref=landed[i].at[x], send_sem=own.at[4 * i + k], recv_sem=last.at[4 * i + x],
                device_id=(from_z, y, sx, jnp.int32(sc)), device_id_type=MESH)
            local = pltpu.make_async_copy(staged[i].at[k], landed[i].at[x], last.at[4 * i + x])
            pl.when(jnp.logical_not(mine))(remote.start)
            pl.when(mine)(local.start)
            final.append((remote, mine))
    for i in range(n):
        wide = fin[i].shape[1]
        for tx in range(4):
            pltpu.make_async_copy(landed[i].at[tx], landed[i].at[tx], last.at[4 * i + tx]).wait()
            outs[i][:, pl.ds(tx * wide, wide)] = landed[i][tx]
    links.finish()
    for remote, mine in final:
        pl.when(jnp.logical_not(mine))(remote.wait_send)


def scatter(halves_in, small, rows):
    n = len(halves_in)
    wides = [h.shape[1] for h in halves_in]
    heights = [4 * r // 3 for r in rows]
    ins = [h.reshape(2, 4, 2, 3, t, w) for h, t, w in zip(halves_in, heights, wides)]
    shapes = [(2, 4, 2, t, w) for t, w in zip(heights, wides)]
    tall = [-(-r // 8) * 8 for r in rows]
    scratch = []
    size = {(i, part): shapes[i] for i in range(n) for part in range(3)}
    for phase in range(3):
        for s in size:
            shape = without(size[s], ORDERS[s[1]][2 - phase])
            scratch += [pltpu.VMEM(shape, jnp.bfloat16)] * 2
            scratch += [pltpu.VMEM(half_shape(shape, way), jnp.bfloat16) for way in (0, 1)]
            if phase < 2:
                scratch += [pltpu.VMEM(shape, jnp.bfloat16)]
            size[s] = shape
    scratch += [pltpu.VMEM((3 * t, w // 4), jnp.float32) for t, w in zip(heights, wides)]
    scratch += [pltpu.VMEM((4, t, w // 4), jnp.float32) for t, w in zip(tall, wides)]
    scratch += [pltpu.VMEM((4, t, w // 4), jnp.float32) for t, w in zip(tall, wides)]
    scratch += [pltpu.VMEM((2 if k == 0 else 4,) + small.shape, jnp.float32) for k in range(4)]
    count = n * 3 * 3 * 6 + 10
    scratch += [pltpu.SemaphoreType.DMA((count,)), pltpu.SemaphoreType.DMA((count,)),
                pltpu.SemaphoreType.DMA((4 * n,)), pltpu.SemaphoreType.DMA((4 * n,))]
    outs = pl.pallas_call(
        functools.partial(scatter_kernel, n=n, rows=tuple(rows), shapes=tuple(shapes), tall=tuple(tall)),
        out_shape=[jax.ShapeDtypeStruct((t, w), jnp.float32) for t, w in zip(tall, wides)] + [jax.ShapeDtypeStruct(small.shape, jnp.float32)],
        in_specs=[pl.BlockSpec(memory_space=pltpu.VMEM)] * (n + 1),
        out_specs=[pl.BlockSpec(memory_space=pltpu.VMEM)] * (n + 1),
        scratch_shapes=scratch,
        compiler_params=pltpu.CompilerParams(collective_id=1, has_side_effects=True, vmem_limit_bytes=56 << 20),
        name="scatter_gradients",
    )(*ins, small)
    return outs


H = 48
P_SIZE = 64
KW = 4
DI = 3072
CONVC = 3328
PROJ = 6448
WIDE = 6656
PARAMS = 6528
SEQ = ("y", "x", "c")
epsilon = 1e-05


TILES = 24


def dot(a, b):
    return jnp.dot(a, b, preferred_element_type=jnp.float32)


def dot_nt(a, b):
    return lax.dot_general(a, b, (((1,), (1,)), ((), ())), preferred_element_type=jnp.float32)


def dot_tn(a, b):
    return lax.dot_general(a, b, (((0,), (0,)), ((), ())), preferred_element_type=jnp.float32)


def low(v):
    return v.astype(jnp.bfloat16)


def wide(v):
    return v.astype(jnp.float32)


def split3(v):
    a = low(v)
    b = low(v - wide(a))
    return a, b, low(v - wide(a) - wide(b))


def running_sums(v, backward):
    row = lax.broadcasted_iota(jnp.int32, (256, 256), 0)
    col = lax.broadcasted_iota(jnp.int32, (256, 256), 1)
    ones = low(jnp.where(row <= col if backward else row >= col, 1.0, 0.0))
    return sum(dot(ones, part) for part in split3(v))


def sigmoid(v):
    return 1.0 / (1.0 + jnp.exp(-v))


def mixer_kernel(proj, db, taps, gain, skip, heads, branch, dproj, sums, headsums,
                 act, mixed, ys, dys, dxs, shift, halo_out, halo_in, back_out, back_in,
                 cum, ecum, toward, steps, rows_a, scores, dscores, usum, qin, qw, prods, stat, coef, db_in, dc_in,
                 snd, rcv, ret, inc, snd2, rcv2, ret2, inc2,
                 a_send, a_recv, h_sem):
    f32, bf16 = jnp.float32, jnp.bfloat16
    z = lax.axis_index("z")
    me = 8 * lax.axis_index("y") + 2 * lax.axis_index("x") + lax.axis_index("c")
    lane = lax.broadcasted_iota(jnp.int32, (256, 128), 1)
    first_head = lane < 64

    def device(k):
        return (z, k // 8, lax.rem(k // 2, 4), lax.rem(k, 2))

    def others(body):
        def step(k, carry):
            body(lax.rem(me + k, 32))
            return carry
        lax.fori_loop(1, 32, step, 0)

    barrier = pltpu.get_barrier_semaphore()
    others(lambda k: pl.semaphore_signal(barrier, inc=1, device_id=device(k), device_id_type=MESH))
    pl.semaphore_wait(barrier, 31)

    def exchange(e, source, target, own):
        def go(k):
            pltpu.make_async_remote_copy(
                src_ref=source(k), dst_ref=target(me), send_sem=a_send.at[e, k], recv_sem=a_recv.at[e, me],
                device_id=device(k), device_id_type=MESH).start()
        others(go)
        own()

    def arrived(e, target):
        others(lambda k: pltpu.make_async_copy(target(k), target(k), a_recv.at[e, k]).wait())

    def left(e, source):
        others(lambda k: pltpu.make_async_copy(source(k), source(k), a_send.at[e, k]).wait())

    def neighbour(k, src, dst, steps_, on):
        made = pltpu.make_async_remote_copy(
            src_ref=src, dst_ref=dst, send_sem=h_sem.at[2 * k], recv_sem=h_sem.at[2 * k + 1],
            device_id=device(lax.rem(me + steps_ + 32, 32)), device_id_type=MESH)
        pl.when(on)(made.start)
        return made

    halo_out[...] = low(proj[240:256, DI:DI + CONVC])
    front = neighbour(0, halo_out, halo_in, 1, me < 31)

    raw = proj[:, DI + CONVC:DI + CONVC + 128] + heads[0:1, :]
    dt = jnp.maximum(raw, 0.0) + jnp.log1p(jnp.exp(-jnp.abs(raw)))
    total = running_sums(-heads[1:2, :] * dt, False)
    last = total[255:256, :]
    steps[...] = dt
    cum[...] = total
    ecum[...] = jnp.exp(total)
    toward[...] = jnp.exp(last - total) * dt
    rows_a[...] = jnp.transpose(total - jnp.log(dt))

    @pl.when(me == 0)
    def _():
        halo_in[...] = jnp.zeros((16, CONVC), bf16)

    pl.when(me > 0)(front.wait_recv)

    def cols(j):
        return pl.ds(pl.multiple_of(128 * j, 128), 128)

    def conv(j, carry):
        shift[0:8, :] = wide(halo_in[:, cols(j)])[8:16, :]
        shift[8:264, :] = wide(low(proj[:, pl.ds(pl.multiple_of(DI + 128 * j, 128), 128)]))
        total = taps[4:5, cols(j)] + taps[0:1, cols(j)] * shift[5:261, :]
        for k in range(1, 4):
            total = total + taps[k:k + 1, cols(j)] * shift[5 + k:261 + k, :]
        mixed[j] = total
        act[j] = low(total * sigmoid(total))
        return carry

    lax.fori_loop(0, TILES + 2, conv, 0)
    b_in, c_out = act[TILES], act[TILES + 1]
    scores[...] = dot_nt(c_out, b_in)

    def pick(ref, j):
        turned = pltpu.roll(ref[...], lax.rem(128 - 2 * j, 128), 1)
        return jnp.broadcast_to(turned[:, 0:1], (256, 128)), jnp.broadcast_to(turned[:, 1:2], (256, 128))

    def spread(ref, j):
        one, two = pick(ref, j)
        return jnp.where(first_head, one, two)

    def by_head(v):
        zero = jnp.zeros_like(v)
        return jnp.where(first_head[:v.shape[0]], v, zero), jnp.where(first_head[:v.shape[0]], zero, v)

    def fold(acc, prod, j):
        row = lax.broadcasted_iota(jnp.int32, (256, 128), 0)
        col = lax.broadcasted_iota(jnp.int32, (256, 128), 1)
        pickers = low(jnp.where(lax.rem(row, 128) // 64 + 2 * j == col, 1.0, 0.0))
        top = low(prod)
        both = jnp.concatenate([top, low(prod - wide(top))], axis=1)
        acc[...] += dot(both, pickers)

    def give(buf, j, tile):
        for g in range(4):
            q = 4 * j + g
            buf[q // 3, pl.ds(pl.multiple_of(32 * lax.rem(q, 3), 32), 32), :] = tile[32 * g:32 * g + 32]

    def local_state(j, carry):
        give(snd, j, low(dot_tn(low(spread(toward, j) * wide(act[j])), b_in)))
        return carry

    lax.fori_loop(0, TILES, local_state, 0)
    tail = split3(last)
    row16 = lax.broadcasted_iota(jnp.int32, (16, 128), 0)
    decays = jnp.zeros((16, 128), f32)
    for k in range(3):
        decays = jnp.where(row16 == k, wide(tail[k]), decays)
    for k in range(32):
        snd[k, 96:112, :] = low(decays)

    def whole(ref):
        return lambda k: ref.at[k]

    def piece(ref):
        return lambda k: ref.at[pl.ds(pl.multiple_of(96 * k, 32), 96)]

    def keep(dst, src):
        dst[me] = src[me]

    exchange(0, whole(snd), whole(rcv), lambda: keep(rcv, snd))

    row = lax.broadcasted_iota(jnp.int32, (128, 128), 0)
    col = lax.broadcasted_iota(jnp.int32, (128, 128), 1)
    causal = row >= col

    def weights(j):
        out = []
        for k, own in enumerate(pick(cum, j)):
            line = rows_a[pl.ds(2 * j + k, 1), :]
            first, second = own[:128], own[128:]
            out.append((
                jnp.exp(jnp.where(causal, first - line[:, :128], -1e30)),
                jnp.exp(second - line[:, :128]),
                jnp.exp(jnp.where(causal, second - line[:, 128:], -1e30))))
        return out

    places = ((slice(0, 128), slice(0, 128)), (slice(128, 256), slice(0, 128)), (slice(128, 256), slice(128, 256)))

    def mixing(gaps):
        return [[low(scores[r, c] * gap) for (r, c), gap in zip(places, head)] for head in gaps]

    def inside(j, carry):
        m = mixing(weights(j))
        xa, xb = by_head(act[j])
        top = dot(jnp.concatenate([m[0][0], m[1][0]], axis=1), jnp.concatenate([xa[:128], xb[:128]], axis=0))
        low_ = dot(jnp.concatenate([m[0][1], m[0][2], m[1][1], m[1][2]], axis=1), jnp.concatenate([xa, xb], axis=0))
        ys[j, 0:128, :] = top
        ys[j, 128:256, :] = low_
        return carry

    head_a = 3 * me // 2
    edge = jnp.where(lax.rem(me, 2) == 0, 64, 32)
    row96 = lax.broadcasted_iota(jnp.int32, (96, 128), 0)

    def scan(got, out, backward):
        carry = jnp.zeros((96, 128), f32)
        for k in (range(31, -1, -1) if backward else range(32)):
            line = wide(rcv[k, 96:112, :])
            line = jnp.exp(line[0:1] + line[1:2] + line[2:3])
            line = pltpu.roll(jnp.broadcast_to(line, (8, 128)), lax.rem(128 - head_a, 128), 1)
            factor = jnp.where(row96 < edge, jnp.broadcast_to(line[0:1, 0:1], (96, 128)), jnp.broadcast_to(line[0:1, 1:2], (96, 128)))
            out[k] = low(carry)
            carry = factor * carry + wide(got[k, 0:96, :])

    lax.fori_loop(0, TILES // 2, inside, 0)
    arrived(0, whole(rcv))
    scan(rcv, ret, False)

    def keep_flat(dst, src):
        dst[pl.ds(pl.multiple_of(96 * me, 32), 96), :] = src[me]

    exchange(1, whole(ret), piece(inc), lambda: keep_flat(inc, ret))
    lax.fori_loop(TILES // 2, TILES, inside, 0)
    arrived(1, piece(inc))

    def state(ref, j):
        return ref[pl.ds(pl.multiple_of(128 * j, 128), 128), :]

    def gate(j, y):
        gz = proj[:, cols(j)]
        sig = sigmoid(gz)
        full = y + skip[:, cols(j)] * wide(act[j])
        return gz, sig, full, full * gz * sig

    stat[...] = jnp.zeros((256, 128), f32)
    coef[...] = jnp.zeros((256, 128), f32)

    def gate_sums(j, carry):
        y = ys[j] + spread(ecum, j) * dot_nt(c_out, state(inc, j))
        ys[j] = y
        _, _, _, gated = gate(j, y)
        stat[...] += gated * gated
        coef[...] += gated * (gain[:, cols(j)] * db[:, cols(j)])
        return carry

    lax.fori_loop(0, TILES, gate_sums, 0)
    scale = lax.rsqrt(jnp.sum(stat[...], axis=1, keepdims=True) * (1.0 / DI) + epsilon)
    factor = scale * scale * scale * (jnp.sum(coef[...], axis=1, keepdims=True) * (1.0 / DI))
    stat[...] = jnp.broadcast_to(scale, (256, 128))
    coef[...] = jnp.broadcast_to(factor, (256, 128))
    sums[...] = jnp.zeros((8, CONVC), f32)

    def gate_back(j, carry):
        y = ys[j]
        gz, sig, full, gated = gate(j, y)
        scaled = gated * stat[...]
        branch[:, cols(j)] = low(scaled * gain[:, cols(j)])
        given = db[:, cols(j)]
        sums[5:6, cols(j)] = jnp.sum(scaled * given, axis=0, keepdims=True)
        d_gated = stat[...] * gain[:, cols(j)] * given - gated * coef[...]
        dproj[:, cols(j)] = low(d_gated * full * (sig * (1.0 + gz * (1.0 - sig))))
        dy = low(d_gated * gz * sig)
        dys[j] = dy
        dyf = wide(dy)
        sums[6:7, cols(j)] = jnp.sum(dyf * wide(act[j]), axis=0, keepdims=True)
        give(snd2, j, low(dot_tn(low(spread(ecum, j) * dyf), c_out)))
        return carry

    lax.fori_loop(0, TILES, gate_back, 0)
    exchange(2, whole(snd2), whole(rcv2), lambda: keep(rcv2, snd2))
    for ref in (usum, qin, qw):
        ref[...] = jnp.zeros((256, 128), f32)
    dscores[...] = jnp.zeros((256, 256), f32)
    prods[...] = jnp.zeros((128, 128), f32)

    def inside_back(j, carry):
        gaps = weights(j)
        m = mixing(gaps)
        x = act[j]
        dya, dyb = by_head(dys[j])
        for k, dy in enumerate((dya, dyb)):
            near = dot_nt(dy[:128], x[:128])
            far = dot_nt(dy[128:], x)
            part = (near, far[:, :128], far[:, 128:])
            for (r, c), gap, value in zip(places, gaps[k], part):
                dscores[r, c] += gap * value
        top = dot_tn(jnp.concatenate([m[0][0], m[0][1], m[1][0], m[1][1]], axis=0), jnp.concatenate([dya, dyb], axis=0))
        low_ = dot_tn(jnp.concatenate([m[0][2], m[1][2]], axis=0), jnp.concatenate([dya[128:], dyb[128:]], axis=0))
        dx = jnp.concatenate([top, low_], axis=0)
        dxs[j] = dx
        fold(usum, wide(dys[j]) * ys[j], j)
        fold(qin, wide(x) * dx, j)
        return carry

    lax.fori_loop(0, TILES // 2, inside_back, 0)
    arrived(2, whole(rcv2))
    scan(rcv2, ret2, True)
    exchange(3, whole(ret2), piece(inc2), lambda: keep_flat(inc2, ret2))
    lax.fori_loop(TILES // 2, TILES, inside_back, 0)
    arrived(3, piece(inc2))
    db_in[...] = jnp.zeros((256, 128), f32)
    dc_in[...] = jnp.zeros((256, 128), f32)

    def d_mix(j, d_act):
        m = mixed[j]
        sig = sigmoid(m)
        d_m = d_act * (sig * (1.0 + m * (1.0 - sig)))
        mixed[j] = d_m
        back_out[:, cols(j)] = low(d_m[0:16])

    def carry_back(j, carry):
        s_in, d_s = state(inc, j), state(inc2, j)
        x, dyf = wide(act[j]), wide(dys[j])
        w = spread(toward, j)
        d_w = w * dot_nt(b_in, d_s)
        fold(qw, x * d_w, j)
        db_in[...] += dot(low(w * x), d_s)
        dc_in[...] += dot(low(spread(ecum, j) * dyf), s_in)
        pair = wide(s_in) * wide(d_s)
        prods[pl.ds(2 * j, 1), :] = jnp.sum(pair[:64], axis=0, keepdims=True)
        prods[pl.ds(2 * j + 1, 1), :] = jnp.sum(pair[64:], axis=0, keepdims=True)
        d_mix(j, dxs[j] + d_w + skip[:, cols(j)] * dyf)
        return carry

    lax.fori_loop(0, TILES, carry_back, 0)
    ds = low(dscores[...])
    d_mix(TILES, db_in[...] + dot_tn(ds, c_out))
    d_mix(TILES + 1, dc_in[...] + dot(ds, b_in))
    behind = neighbour(1, back_out, back_in, -1, me > 0)

    q = qin[...] + qw[...]
    d_last = ecum[255:256, :] * jnp.sum(jnp.transpose(prods[...]), axis=0, keepdims=True) + jnp.sum(qw[...], axis=0, keepdims=True)
    at_end = lax.broadcasted_iota(jnp.int32, (256, 128), 0) == 255
    d_l = running_sums(usum[...] - q + jnp.where(at_end, d_last, 0.0), True)
    dt = steps[...]
    raw = proj[:, DI + CONVC:DI + CONVC + 128] + heads[0:1, :]
    d_raw = (q / jnp.maximum(dt, 1e-30) - heads[1:2, :] * d_l) * sigmoid(raw)
    d_raw = jnp.where(lane < H, d_raw, 0.0)
    headsums[...] = jnp.zeros((8, 128), f32)
    headsums[0:1, :] = jnp.sum(d_raw, axis=0, keepdims=True)
    headsums[1:2, :] = -jnp.sum(d_l * dt, axis=0, keepdims=True)
    dproj[:, DI + CONVC:DI + CONVC + 128] = low(d_raw)
    dproj[:, DI + CONVC + 128:] = jnp.zeros((256, 128), bf16)

    @pl.when(me == 31)
    def _():
        back_in[...] = jnp.zeros((16, CONVC), bf16)

    pl.when(me < 31)(behind.wait_recv)

    def conv_back(j, carry):
        d_m = mixed[j]
        shift[0:8, :] = wide(halo_in[:, cols(j)])[8:16, :]
        shift[8:264, :] = wide(low(proj[:, pl.ds(pl.multiple_of(DI + 128 * j, 128), 128)]))
        for k in range(4):
            sums[k:k + 1, cols(j)] = jnp.sum(d_m * shift[5 + k:261 + k, :], axis=0, keepdims=True)
        sums[4:5, cols(j)] = jnp.sum(d_m, axis=0, keepdims=True)
        shift[0:256, :] = d_m
        shift[256:264, :] = wide(back_in[:, cols(j)])[0:8, :]
        total = taps[3:4, cols(j)] * d_m
        for k in range(3):
            total = total + taps[k:k + 1, cols(j)] * shift[3 - k:259 - k, :]
        dproj[:, pl.ds(pl.multiple_of(DI + 128 * j, 128), 128)] = low(total)
        return carry

    lax.fori_loop(0, TILES + 2, conv_back, 0)
    pl.when(me < 31)(front.wait_send)
    pl.when(me > 0)(behind.wait_send)
    left(0, whole(snd))
    left(1, whole(ret))
    left(2, whole(snd2))
    left(3, whole(ret2))


def mixer(projected, d_branch, taps, gain, skip, heads):
    f32, bf16 = jnp.float32, jnp.bfloat16
    tile, half = (256, 128), (16, CONVC)
    vm = pltpu.VMEM
    scratch = [
        vm((TILES + 2,) + tile, bf16), vm((TILES + 2,) + tile, f32), vm((TILES,) + tile, f32), vm((TILES,) + tile, bf16),
        vm((TILES,) + tile, f32), vm((264, 128), f32), vm(half, bf16), vm(half, bf16), vm(half, bf16), vm(half, bf16),
        vm(tile, f32), vm(tile, f32), vm(tile, f32), vm(tile, f32), vm((128, 256), f32), vm((256, 256), f32), vm((256, 256), f32),
        vm(tile, f32), vm(tile, f32), vm(tile, f32), vm((128, 128), f32), vm(tile, f32), vm(tile, f32), vm(tile, f32), vm(tile, f32),
    ]
    for _ in range(2):
        scratch += [vm((32, 112, 128), bf16), vm((32, 112, 128), bf16), vm((32, 96, 128), bf16), vm((3072, 128), bf16)]
    scratch += [pltpu.SemaphoreType.DMA((4, 32)), pltpu.SemaphoreType.DMA((4, 32)), pltpu.SemaphoreType.DMA((4,))]
    spec = pl.BlockSpec(memory_space=pltpu.VMEM)
    return pl.pallas_call(
        mixer_kernel,
        out_shape=[jax.ShapeDtypeStruct((256, DI), bf16), jax.ShapeDtypeStruct((256, WIDE), bf16),
                   jax.ShapeDtypeStruct((8, CONVC), f32), jax.ShapeDtypeStruct((8, 128), f32)],
        in_specs=[spec] * 6,
        out_specs=[spec] * 4,
        scratch_shapes=scratch,
        compiler_params=pltpu.CompilerParams(collective_id=2, has_side_effects=True, vmem_limit_bytes=60 << 20),
        name="mixer",
    )(projected, d_branch, taps, gain, skip, heads)

def rms_scale(values, gain):
    return values * lax.rsqrt(jnp.mean(values * values, axis=-1, keepdims=True) + epsilon) * gain


def swap(value):
    return lax.ppermute(value, "c", [(0, 1), (1, 0)])


def my_half(value, core):
    wide = value.shape[1] // 2
    given = swap(lax.dynamic_slice_in_dim(value, (1 - core) * wide, wide, axis=1))
    return jnp.concatenate([lax.dynamic_slice_in_dim(value, core * wide, wide, axis=1), given], axis=0)


def shards(
    hidden,
    cotangent,
    in_w,
    out_w,
    conv_w,
    conv_b,
    norm_gain,
    gate_gain,
    dt_bias,
    decay_rates,
    d_skip,
):
    core = lax.axis_index("c")
    spare = jnp.concatenate([
        jnp.pad(conv_w, ((0, 0), (0, 102))),
        jnp.pad(conv_b, (0, 102))[None],
        jnp.pad(norm_gain, (0, 116))[None],
        jnp.pad(gate_gain, (0, 104))[None],
        jnp.zeros((5, 128), jnp.bfloat16),
    ])
    shard_in = jnp.pad(jnp.concatenate([jnp.pad(in_w, ((0, 0), (0, PARAMS - PROJ))), spare], axis=1), ((0, 4), (0, 0)))
    w_in, w_out = gather([shard_in, jnp.pad(out_w, ((0, 8), (0, 0)))], [12, 24])
    spare = w_in[:, PARAMS:].reshape(128, 12, 128).astype(jnp.float32)
    w_conv_f = spare[:, :4, :26].transpose(1, 0, 2).reshape(KW, CONVC)
    b_conv_f = spare[:, 4, :26].reshape(CONVC)
    gain_norm_f = spare[:, 5, :12].reshape(1536)
    gain_gate_f = spare[:, 6, :24].reshape(DI)
    w_in = w_in * (jnp.arange(WIDE) < PROJ).astype(jnp.bfloat16)[None, :]
    residual = hidden[0].astype(jnp.float32)
    length = residual.shape[0]
    normed = rms_scale(residual, gain_norm_f).astype(jnp.bfloat16)
    projected = jnp.dot(normed, w_in, preferred_element_type=jnp.float32)
    grad_out = cotangent[0]
    both_out = jnp.concatenate([grad_out, swap(grad_out)], axis=0)
    d_branch = jnp.einsum("td,kd->tk", grad_out, w_out, preferred_element_type=jnp.float32)
    taps = jnp.pad(jnp.concatenate([w_conv_f, b_conv_f[None]]), ((0, 3), (0, 0)))
    heads = jnp.pad(jnp.stack([dt_bias, decay_rates]), ((0, 6), (0, 80)))
    branch, d_projected, sums, head_sums = mixer(
        projected, d_branch, taps, gain_gate_f[None], jnp.repeat(d_skip, P_SIZE)[None], heads)
    result = (residual + jnp.dot(branch, w_out, preferred_element_type=jnp.float32)).astype(jnp.bfloat16)
    d_w_out = jnp.einsum("tk,td->kd", my_half(branch, core), both_out, preferred_element_type=jnp.float32).astype(jnp.bfloat16)
    d_normed = jnp.einsum("tj,dj->td", d_projected, w_in, preferred_element_type=jnp.float32)
    both_projected = jnp.concatenate([d_projected, swap(d_projected)], axis=0)
    d_w_in = jnp.einsum("td,tj->dj", my_half(normed, core), both_projected, preferred_element_type=jnp.float32).astype(jnp.bfloat16)
    norm_pull = jax.vjp(rms_scale, residual, gain_norm_f)[1]
    d_from_norm, d_gain_norm = norm_pull(d_normed)
    d_hidden = grad_out.astype(jnp.float32) + d_from_norm
    d_skips = jnp.sum(sums[6, :DI].reshape(H, P_SIZE), axis=1)
    small = jnp.concatenate([
        sums[:5].reshape(-1), d_gain_norm, sums[5, :DI], head_sums[:2].reshape(-1), jnp.pad(d_skips, (0, 80)),
        jnp.zeros((896,), jnp.float32),
    ]).reshape(176, 128)
    g_in, g_out, total = scatter([d_w_in, d_w_out], small, [12, 24])
    mine = lax.axis_index(ALL)
    d_conv_w = total[:104].reshape(KW, CONVC)
    d_conv_b = total[104:130].reshape(CONVC)
    d_gain_norm = total[130:142].reshape(1536)
    d_gain_gate = total[142:166].reshape(DI)
    return (
        result[None],
        d_hidden[None],
        g_in[:12, :PROJ],
        g_out,
        lax.dynamic_slice_in_dim(d_conv_w, 26 * mine, 26, axis=1),
        lax.dynamic_slice_in_dim(d_conv_b, 26 * mine, 26),
        lax.dynamic_slice_in_dim(d_gain_norm, 12 * mine, 12),
        lax.dynamic_slice_in_dim(d_gain_gate, 24 * mine, 24),
        total[166, :H],
        total[167, :H],
        total[168, :H],
    )


def solution(mesh):
    grid = Mesh(mesh.devices.reshape(4, 4, 4, 2), ALL)
    tokens = P("z", SEQ, None)
    placed = (
        tokens,
        tokens,
        P(ALL, None),
        P(ALL, None),
        P(None, ALL),
        P(ALL),
        P(ALL),
        P(ALL),
        P(),
        P(),
        P(),
    )
    return jax.shard_map(
        shards,
        mesh=grid,
        in_specs=placed,
        out_specs=(tokens, tokens, P(ALL, None), P(ALL, None), P(None, ALL), P(ALL), P(ALL), P(ALL), P(), P(), P()),
        check_vma=False,
    )
```

```python
import functools
import jax
import jax.numpy as jnp
from jax import lax
from jax.experimental import pallas as pl
from jax.experimental.pallas import tpu as pltpu
from jax.sharding import PartitionSpec as P, Mesh

MESH = pl.DeviceIdType.MESH
ALL = ("z", "y", "x", "c")
ORDERS = (("z", "y", "x"), ("y", "x", "z"), ("x", "z", "y"))


class Links:
    def __init__(self, send, recv):
        self.send, self.recv, self.used, self.sent = send, recv, 0, []

    def copy(self, src, dst, device):
        k = self.used
        self.used += 1
        made = pltpu.make_async_remote_copy(
            src_ref=src, dst_ref=dst, send_sem=self.send.at[k], recv_sem=self.recv.at[k],
            device_id=device, device_id_type=MESH)
        made.start()
        self.sent.append(made)
        return made

    def finish(self):
        for made in self.sent:
            made.wait_send()


def place():
    return {name: lax.axis_index(name) for name in ALL}


def block(ref, part, core, at, have, half=None):
    z, y, x = at["z"], at["y"], at["x"]
    wide = ref.shape[-1]
    full = slice(None)
    zh, zl = (full, full) if "z" in have else (z // 2, lax.rem(z, 2))
    ys = full if "y" in have else y
    first, count = (0, wide) if "x" in have else (x * (wide // 4), wide // 4)
    if half is not None:
        if "y" in have:
            ys = pl.ds(2 * half, 2)
        elif "z" in have:
            zh = pl.ds(half, 1)
        else:
            near = -(-count // 256) * 128
            first, count = (first, near) if half == 0 else (first + near, count - near)
    cols = full if "x" in have and count == wide else pl.ds(first if isinstance(first, int) else pl.multiple_of(first, 128), count)
    return ref.at[core, zh, ys, zl, part, :, cols]


def moved(at, axis, steps):
    return {**at, axis: lax.rem(at[axis] + steps + 4, 4)}


def gather_kernel(*refs, n, rows):
    shards, fulls, refs = refs[:n], refs[n:2 * n], refs[2 * n:]
    stage, landed, unit, (send, recv, own) = refs[:n], refs[n:2 * n], refs[2 * n:3 * n], refs[3 * n:]
    at = place()
    z, y, x, c = (at[name] for name in ALL)
    to_z, to_c = 2 * lax.rem(z, 2) + x // 2, z // 2
    slot = 2 * lax.rem(x, 2) + c
    from_z = 2 * c + z // 2
    barrier = pltpu.get_barrier_semaphore()
    for axis in ("z", "y", "x"):
        for steps in (1, -1):
            pl.semaphore_signal(barrier, inc=1, device_id={axis: moved(at, axis, steps)[axis]}, device_id_type=MESH)
    pl.semaphore_signal(barrier, inc=1, device_id={"c": 1 - c}, device_id_type=MESH)
    for k in range(4):
        sx, sc = 2 * lax.rem(z, 2) + k // 2, k % 2
        other = jnp.logical_or(jnp.logical_or(sx != x, sc != c), from_z != z)

        @pl.when(other)
        def _():
            pl.semaphore_signal(barrier, inc=1, device_id=(from_z, y, sx, jnp.int32(sc)), device_id_type=MESH)
    home = jnp.logical_and(to_z == z, to_c == c)
    pl.semaphore_wait(barrier, 11 - home.astype(jnp.int32))

    links = Links(send, recv)
    first = []
    for i in range(n):
        wide = shards[i].shape[1] // 4
        for tx in range(4):
            k = links.used
            links.used += 1
            src = shards[i].at[:, pl.ds(tx * wide, wide)]
            remote = pltpu.make_async_remote_copy(
                src_ref=src, dst_ref=landed[i].at[slot], send_sem=send.at[k], recv_sem=recv.at[4 * i + slot],
                device_id=(to_z, y, jnp.int32(tx), to_c), device_id_type=MESH)
            local = pltpu.make_async_copy(src, landed[i].at[slot], recv.at[4 * i + slot])
            mine = jnp.logical_and(home, x == tx)
            pl.when(jnp.logical_not(mine))(remote.start)
            pl.when(mine)(local.start)
            first.append((remote, mine))
    kept = []
    for i in range(n):
        deep, height = rows[i], unit[i].shape[1]
        for k in range(4):
            pltpu.make_async_copy(landed[i].at[k], landed[i].at[k], recv.at[4 * i + k]).wait()
            stage[i][pl.ds(deep * k, deep), :] = landed[i][k, :deep, :].astype(jnp.float32)
        for part in range(3):
            unit[i][part] = stage[i][pl.ds(part * height, height), :].astype(jnp.bfloat16)
        for part in range(3):
            copy = pltpu.make_async_copy(unit[i].at[part], block(fulls[i], part, c, at, ()), own.at[3 * i + part])
            copy.start()
            kept.append(copy)
    sibling = {"c": 1 - c}
    streams = [(i, part) for i in range(n) for part in range(3)]
    for phase in range(3):
        near = {}
        for i, part in streams:
            have, axis = ORDERS[part][:phase], ORDERS[part][phase]
            mine = unit[i].at[part] if phase == 0 else block(fulls[i], part, c, at, have)
            there = block(fulls[i], part, c, at, have)
            near[i, part] = [links.copy(mine, there, {axis: moved(at, axis, steps)[axis]}) for steps in (1, -1)]
            if phase == 0:
                links.copy(mine, there, sibling)
        far = {}
        for i, part in streams:
            have, axis = ORDERS[part][:phase], ORDERS[part][phase]
            far[i, part] = []
            for way, steps in ((0, 1), (1, -1)):
                near[i, part][way].wait_recv()
                behind = moved(at, axis, -steps)
                piece = block(fulls[i], part, c, behind, have, way)
                far[i, part].append(links.copy(piece, piece, {axis: moved(at, axis, steps)[axis]}))
                whole = block(fulls[i], part, c, behind, have)
                links.copy(whole, whole, sibling)
        for i, part in streams:
            have, axis = ORDERS[part][:phase], ORDERS[part][phase]
            for way in (0, 1):
                far[i, part][way].wait_recv()
                piece = block(fulls[i], part, c, moved(at, axis, 2), have, way)
                links.copy(piece, piece, sibling)
        if phase == 0:
            for copy in kept:
                copy.wait()
    for made in links.sent:
        if made.device_id is sibling:
            made.wait_recv()
    links.finish()
    for remote, mine in first:
        pl.when(jnp.logical_not(mine))(remote.wait_send)


def gather(shards, rows):
    n = len(shards)
    heights = [4 * r // 3 for r in rows]
    wides = [s.shape[1] for s in shards]
    fulls = [jax.ShapeDtypeStruct((2, 2, 4, 2, 3, h, w), jnp.bfloat16) for h, w in zip(heights, wides)]
    count = n * (4 + 3 * (3 * 3 * 2 + 1 + 6))
    outs = pl.pallas_call(
        functools.partial(gather_kernel, n=n, rows=tuple(rows)),
        out_shape=fulls,
        in_specs=[pl.BlockSpec(memory_space=pltpu.VMEM)] * n,
        out_specs=[pl.BlockSpec(memory_space=pl.ANY)] * n,
        scratch_shapes=[pltpu.VMEM((3 * h, w // 4), jnp.float32) for h, w in zip(heights, wides)]
        + [pltpu.VMEM((4, s.shape[0], w // 4), jnp.bfloat16) for s, w in zip(shards, wides)]
        + [pltpu.VMEM((3, h, w // 4), jnp.bfloat16) for h, w in zip(heights, wides)]
        + [pltpu.SemaphoreType.DMA((count,)), pltpu.SemaphoreType.DMA((count,)), pltpu.SemaphoreType.DMA((3 * n,))],
        compiler_params=pltpu.CompilerParams(collective_id=0, has_side_effects=True, vmem_limit_bytes=32 << 20),
        name="gather_weights",
    )(*shards)
    return [o.reshape(128 * r, w) for o, r, w in zip(outs, rows, wides)]


def span(shape, axis, at):
    cut = [slice(None)] * 5
    if axis == "y":
        cut[1] = pl.ds(at["y"], 1)
    elif axis == "z":
        cut[0], cut[2] = pl.ds(at["z"] // 2, 1), pl.ds(lax.rem(at["z"], 2), 1)
    else:
        cut[4] = pl.ds(pl.multiple_of(at["x"] * (shape[4] // 4), 128), shape[4] // 4)
    return cut


def without(shape, axis):
    zh, y, zl, rows, wide = shape
    return {"y": (zh, 1, zl, rows, wide), "z": (1, y, 1, rows, wide), "x": (zh, y, zl, rows, wide // 4)}[axis]


def halves(shape):
    if shape[1] == 4:
        return 1, ((0, 2), (2, 2))
    if shape[0] == 2:
        return 0, ((0, 1), (1, 1))
    near = -(-shape[4] // 256) * 128
    return 4, ((0, near), (near, shape[4] - near))


def cut_half(cut, shape, half):
    dim, parts = halves(shape)
    start, size = parts[half]
    cut = list(cut)
    old = cut[dim]
    base = 0 if isinstance(old, slice) else old.start
    cut[dim] = pl.ds(pl.multiple_of(base + start, 128) if dim == 4 and not isinstance(base, int) else base + start, size)
    return cut


def half_shape(shape, half):
    dim, parts = halves(shape)
    return tuple(parts[half][1] if k == dim else size for k, size in enumerate(shape))


def add_up(out, terms, shape):
    na, nb, nc = shape[:3]

    def slab(k, carry):
        a, b, d = k // (nb * nc), lax.rem(k // nc, nb), lax.rem(k, nc)
        total = terms[0](a, b, d).astype(jnp.float32)
        for term in terms[1:]:
            total = total + term(a, b, d).astype(jnp.float32)
        out(a, b, d, total)
        return carry

    lax.fori_loop(0, na * nb * nc, slab, 0)


def start_of(cut):
    return 0 if isinstance(cut, slice) else cut.start


def slab_of(ref, cut, shape):
    z0, y0, l0, _, c0 = (start_of(s) for s in cut)
    lead = ref

    def read(a, b, d):
        return lead[z0 + a, y0 + b, l0 + d, :, pl.ds(c0, shape[4])]

    return read


def slab_to(ref, shape):
    def write(a, b, d, value):
        ref[a, b, d] = value.astype(ref.dtype)

    return write


ALL_CUT = [slice(None)] * 5


def scatter_kernel(*refs, n, rows, shapes, tall):
    parts_in, smalls, refs = refs[:n], refs[n:n + 3], refs[n + 3:]
    outs, small_out, refs = refs[:n], refs[n], refs[n + 1:]
    take = iter(refs)
    near, relay, acc = {}, {}, {}
    streams = [(i, part) for i in range(n) for part in range(3)]
    for phase in range(3):
        for s in streams:
            near[s, phase] = [next(take), next(take)]
            relay[s, phase] = [next(take), next(take)]
            acc[s, phase] = next(take) if phase < 2 else None
    fin = [next(take) for _ in range(n)]
    staged = [next(take) for _ in range(n)]
    landed = [next(take) for _ in range(n)]
    rounds = [next(take) for _ in range(4)]
    send, recv, last, own = (next(take) for _ in range(4))
    at = place()
    z, y, x, c = (at[name] for name in ALL)
    to_z, to_c = 2 * lax.rem(z, 2) + x // 2, z // 2
    from_z = 2 * c + z // 2
    home = jnp.logical_and(to_z == z, to_c == c)
    barrier = pltpu.get_barrier_semaphore()
    for axis in ("z", "y", "x"):
        for steps in (1, 2, 3):
            pl.semaphore_signal(barrier, inc=1, device_id={axis: moved(at, axis, steps)[axis]}, device_id_type=MESH)
    pl.semaphore_signal(barrier, inc=1, device_id={"c": 1 - c}, device_id_type=MESH)
    for tx in range(4):
        mine = jnp.logical_and(home, x == tx)

        @pl.when(jnp.logical_not(mine))
        def _():
            pl.semaphore_signal(barrier, inc=1, device_id=(to_z, y, jnp.int32(tx), to_c), device_id_type=MESH)
    pl.semaphore_wait(barrier, 14 - home.astype(jnp.int32))

    links = Links(send, recv)

    def small_start(k):
        axis = ("c", "x", "y", "z")[k]
        if k == 0:
            start = 0
            for part in smalls:
                rounds[0][c, :, start:start + part.shape[1]] = part[...]
                start += part.shape[1]
        else:
            rounds[k][at[axis]] = sums[0]
        held = rounds[k].at[at[axis]]
        if k == 0:
            return [links.copy(held, held, {"c": 1 - c})]
        return [links.copy(held, held, {axis: moved(at, axis, steps)[axis]}) for steps in (1, 2, 3)]

    def small_end(k, going):
        for copy in going:
            copy.wait_recv()
        total = rounds[k][0]
        for j in range(1, 2 if k == 0 else 4):
            total = total + rounds[k][j]
        sums[0] = total

    sums = [None]
    size = {s: shapes[s[0]] for s in streams}
    source = {s: parts_in[s[0]].at[:, :, :, s[1]] for s in streams}
    going = small_start(0)
    for phase in range(3):
        sent, lent = {}, {}
        for s in streams:
            axis = ORDERS[s[1]][2 - phase]
            shape = without(size[s], axis)
            cuts = {k: span(size[s], axis, moved(at, axis, k)) for k in (0, 1, 2, 3)}
            to = {k: {axis: moved(at, axis, k)[axis]} for k in (1, 3)}
            lent[s], sent[s] = [], []
            for way, step in ((0, 1), (1, 3)):
                src = source[s].at[tuple(cut_half(cuts[2], shape, way))]
                lent[s].append(links.copy(src, relay[s, phase][way], to[step]))
            for way, step in ((0, 1), (1, 3)):
                src = source[s].at[tuple(cut_half(cuts[step], shape, 1 - way))]
                dst = near[s, phase][way].at[tuple(cut_half(ALL_CUT, shape, 1 - way))]
                sent[s].append(links.copy(src, dst, to[step]))
        small_end(phase, going)
        going = small_start(phase + 1)
        for s in streams:
            axis = ORDERS[s[1]][2 - phase]
            shape = without(size[s], axis)
            for way, step in ((0, 1), (1, 3)):
                lent[s][way].wait_recv()
                hs = half_shape(shape, way)
                cut = cut_half(span(size[s], axis, moved(at, axis, step)), shape, way)
                buf = relay[s, phase][way]
                add_up(slab_to(buf, hs), [slab_of(source[s], cut, hs), slab_of(buf, ALL_CUT, hs)], hs)
                dst = near[s, phase][way].at[tuple(cut_half(ALL_CUT, shape, way))]
                sent[s].append(links.copy(buf, dst, {axis: moved(at, axis, step)[axis]}))
        for s in streams:
            i, part = s
            axis = ORDERS[part][2 - phase]
            shape = without(size[s], axis)
            for copy in sent[s]:
                copy.wait_recv()
            terms = [slab_of(source[s], span(size[s], axis, at), shape)]
            terms += [slab_of(near[s, phase][way], ALL_CUT, shape) for way in (0, 1)]
            if phase < 2:
                add_up(slab_to(acc[s, phase], shape), terms, shape)
                source[s], size[s] = acc[s, phase], shape
            else:
                total = terms[0](0, 0, 0).astype(jnp.float32)
                for term in terms[1:]:
                    total = total + term(0, 0, 0).astype(jnp.float32)
                fin[i][pl.ds(part * shape[3], shape[3]), :] = total
    small_end(3, going)
    index = 32 * z + 8 * y + 2 * x + c
    total, start = sums[0], 0
    for part, (each, first, count, to) in zip(smalls, ((26, 0, 8, 0), (0, 0, 8, 8), (12, 0, 1, 6))):
        wide_ = part.shape[1]
        value = total[:, start:start + wide_]
        if each:
            value = pltpu.roll(value, lax.rem(wide_ - each * index, wide_), 1)
        small_out[to:to + count, :] = value[first:first + count, :128]
        start += wide_
    gate = pltpu.roll(total[:, :128 * 24], lax.rem(3072 - 24 * index, 3072), 1)
    small_out[5:6, :] = gate[5:6, :128]
    final = []
    for i in range(n):
        deep, wide = rows[i], fin[i].shape[1]
        for k in range(4):
            sx, sc = 2 * lax.rem(z, 2) + k // 2, k % 2
            staged[i][k] = jnp.zeros(staged[i].shape[1:], jnp.float32)
            staged[i][k, :deep] = fin[i][pl.ds(deep * k, deep), :]
            mine = jnp.logical_and(home, jnp.logical_and(sx == x, sc == c))
            remote = pltpu.make_async_remote_copy(
                src_ref=staged[i].at[k], dst_ref=landed[i].at[x], send_sem=own.at[4 * i + k], recv_sem=last.at[4 * i + x],
                device_id=(from_z, y, sx, jnp.int32(sc)), device_id_type=MESH)
            local = pltpu.make_async_copy(staged[i].at[k], landed[i].at[x], last.at[4 * i + x])
            pl.when(jnp.logical_not(mine))(remote.start)
            pl.when(mine)(local.start)
            final.append((remote, mine))
    for i in range(n):
        wide = fin[i].shape[1]
        for tx in range(4):
            pltpu.make_async_copy(landed[i].at[tx], landed[i].at[tx], last.at[4 * i + tx]).wait()
            outs[i][:, pl.ds(tx * wide, wide)] = landed[i][tx]
    links.finish()
    for remote, mine in final:
        pl.when(jnp.logical_not(mine))(remote.wait_send)


def scatter(halves_in, smalls, rows):
    n = len(halves_in)
    wides = [h.shape[1] for h in halves_in]
    heights = [4 * r // 3 for r in rows]
    ins = [h.reshape(2, 4, 2, 3, t, w) for h, t, w in zip(halves_in, heights, wides)]
    shapes = [(2, 4, 2, t, w) for t, w in zip(heights, wides)]
    tall = [-(-r // 8) * 8 for r in rows]
    scratch = []
    size = {(i, part): shapes[i] for i in range(n) for part in range(3)}
    for phase in range(3):
        for s in size:
            shape = without(size[s], ORDERS[s[1]][2 - phase])
            scratch += [pltpu.VMEM(shape, jnp.bfloat16)] * 2
            scratch += [pltpu.VMEM(half_shape(shape, way), jnp.bfloat16) for way in (0, 1)]
            if phase < 2:
                scratch += [pltpu.VMEM(shape, jnp.bfloat16)]
            size[s] = shape
    scratch += [pltpu.VMEM((3 * t, w // 4), jnp.float32) for t, w in zip(heights, wides)]
    scratch += [pltpu.VMEM((4, t, w // 4), jnp.float32) for t, w in zip(tall, wides)]
    scratch += [pltpu.VMEM((4, t, w // 4), jnp.float32) for t, w in zip(tall, wides)]
    scratch += [pltpu.VMEM((2 if k == 0 else 4, 8, sum(s.shape[1] for s in smalls)), jnp.float32) for k in range(4)]
    count = n * 3 * 3 * 6 + 10
    scratch += [pltpu.SemaphoreType.DMA((count,)), pltpu.SemaphoreType.DMA((count,)),
                pltpu.SemaphoreType.DMA((4 * n,)), pltpu.SemaphoreType.DMA((4 * n,))]
    outs = pl.pallas_call(
        functools.partial(scatter_kernel, n=n, rows=tuple(rows), shapes=tuple(shapes), tall=tuple(tall)),
        out_shape=[jax.ShapeDtypeStruct((t, w), jnp.float32) for t, w in zip(tall, wides)] + [jax.ShapeDtypeStruct((16, 128), jnp.float32)],
        in_specs=[pl.BlockSpec(memory_space=pltpu.VMEM)] * (n + 3),
        out_specs=[pl.BlockSpec(memory_space=pltpu.VMEM)] * (n + 1),
        scratch_shapes=scratch,
        compiler_params=pltpu.CompilerParams(collective_id=1, has_side_effects=True, vmem_limit_bytes=56 << 20),
        name="scatter_gradients",
    )(*ins, *smalls)
    return outs


H = 48
P_SIZE = 64
KW = 4
DI = 3072
CONVC = 3328
PROJ = 6448
WIDE = 6656
PARAMS = 6528
SEQ = ("y", "x", "c")
epsilon = 1e-05


TILES = 24


def dot(a, b):
    return jnp.dot(a, b, preferred_element_type=jnp.float32)


def dot_nt(a, b):
    return lax.dot_general(a, b, (((1,), (1,)), ((), ())), preferred_element_type=jnp.float32)


def dot_tn(a, b):
    return lax.dot_general(a, b, (((0,), (0,)), ((), ())), preferred_element_type=jnp.float32)


def low(v):
    return v.astype(jnp.bfloat16)


def wide(v):
    return v.astype(jnp.float32)


def split3(v):
    a = low(v)
    b = low(v - wide(a))
    return a, b, low(v - wide(a) - wide(b))


def running_sums(v, backward):
    row = lax.broadcasted_iota(jnp.int32, (256, 256), 0)
    col = lax.broadcasted_iota(jnp.int32, (256, 256), 1)
    ones = low(jnp.where(row <= col if backward else row >= col, 1.0, 0.0))
    return sum(dot(ones, part) for part in split3(v))


def sigmoid(v):
    return 1.0 / (1.0 + jnp.exp(-v))


def mixer_kernel(proj, db, taps, gain, skip, heads, branch, dproj, sums, headsums,
                 act, mixed, ys, dys, dxs, shift, halo_out, halo_in, back_out, back_in,
                 cum, ecum, toward, steps, rows_a, scores, dscores, usum, qin, qw, prods, stat, coef, db_in, dc_in, decay,
                 skips, loc, inc, inc2, *rest):
    f32, bf16 = jnp.float32, jnp.bfloat16
    ways, (sib_send, sib_recv, a_send, a_recv, h_sem) = (rest[:5], rest[5:10]), rest[10:]
    z, core = lax.axis_index("z"), lax.axis_index("c")
    chip = 4 * lax.axis_index("y") + lax.axis_index("x")
    me = 2 * chip + core
    lane = lax.broadcasted_iota(jnp.int32, (256, 128), 1)
    first_head = lane < 64

    def device(k):
        return (z, k // 8, lax.rem(k // 2, 4), lax.rem(k, 2))

    def same_core(k):
        return (z, k // 4, lax.rem(k, 4), core)

    def others(body):
        def step(k, carry):
            body(lax.rem(chip + k, 16))
            return carry
        lax.fori_loop(1, 16, step, 0)

    barrier = pltpu.get_barrier_semaphore()
    others(lambda k: pl.semaphore_signal(barrier, inc=1, device_id=same_core(k), device_id_type=MESH))
    pl.semaphore_signal(barrier, inc=1, device_id={"c": 1 - core}, device_id_type=MESH)
    beside = jnp.where(core == 1, me + 1, me - 1)
    inner = jnp.logical_and(beside >= 0, beside < 32)

    @pl.when(inner)
    def _():
        pl.semaphore_signal(barrier, inc=1, device_id=device(beside), device_id_type=MESH)

    pl.semaphore_wait(barrier, 16 + inner.astype(jnp.int32))

    def exchange(e, source, target, own):
        def go(k):
            pltpu.make_async_remote_copy(
                src_ref=source(k), dst_ref=target(chip), send_sem=a_send.at[e, k], recv_sem=a_recv.at[e, chip],
                device_id=same_core(k), device_id_type=MESH).start()
        others(go)
        own()

    def arrived(e, target):
        others(lambda k: pltpu.make_async_copy(target(k), target(k), a_recv.at[e, k]).wait())

    def left(e, source):
        others(lambda k: pltpu.make_async_copy(source(k), source(k), a_send.at[e, k]).wait())

    def to_sibling(e, src, dst):
        made = pltpu.make_async_remote_copy(
            src_ref=src, dst_ref=dst, send_sem=sib_send.at[e], recv_sem=sib_recv.at[e],
            device_id={"c": 1 - core}, device_id_type=MESH)
        made.start()
        return made

    def neighbour(k, src, dst, steps_, on):
        made = pltpu.make_async_remote_copy(
            src_ref=src, dst_ref=dst, send_sem=h_sem.at[2 * k], recv_sem=h_sem.at[2 * k + 1],
            device_id=device(lax.rem(me + steps_ + 32, 32)), device_id_type=MESH)
        pl.when(on)(made.start)
        return made

    halo_out[...] = low(proj[240:256, DI:DI + CONVC])
    front = neighbour(0, halo_out, halo_in, 1, me < 31)

    raw = proj[:, DI + CONVC:DI + CONVC + 128] + heads[0:1, :]
    dt = jnp.maximum(raw, 0.0) + jnp.log1p(jnp.exp(-jnp.abs(raw)))
    total = running_sums(-heads[1:2, :] * dt, False)
    last = total[255:256, :]
    steps[...] = dt
    cum[...] = total
    ecum[...] = jnp.exp(total)
    toward[...] = jnp.exp(last - total) * dt
    rows_a[...] = jnp.transpose(total - jnp.log(dt))

    @pl.when(me == 0)
    def _():
        halo_in[...] = jnp.zeros((16, CONVC), bf16)

    pl.when(me > 0)(front.wait_recv)

    def cols(j):
        return pl.ds(pl.multiple_of(128 * j, 128), 128)

    def conv(j, carry):
        shift[0:8, :] = wide(halo_in[:, cols(j)])[8:16, :]
        shift[8:264, :] = wide(low(proj[:, pl.ds(pl.multiple_of(DI + 128 * j, 128), 128)]))
        total = taps[4:5, cols(j)] + taps[0:1, cols(j)] * shift[5:261, :]
        for k in range(1, 4):
            total = total + taps[k:k + 1, cols(j)] * shift[5 + k:261 + k, :]
        mixed[j] = total
        act[j] = low(total * sigmoid(total))
        return carry

    lax.fori_loop(0, TILES + 2, conv, 0)
    b_in, c_out = act[TILES], act[TILES + 1]
    scores[...] = dot_nt(c_out, b_in)

    def pick(ref, j):
        turned = pltpu.roll(ref[...], lax.rem(128 - 2 * j, 128), 1)
        return jnp.broadcast_to(turned[:, 0:1], (256, 128)), jnp.broadcast_to(turned[:, 1:2], (256, 128))

    def spread(ref, j):
        one, two = pick(ref, j)
        return jnp.where(first_head, one, two)

    def by_head(v):
        zero = jnp.zeros_like(v)
        return jnp.where(first_head[:v.shape[0]], v, zero), jnp.where(first_head[:v.shape[0]], zero, v)

    def fold(acc, prod, j):
        row = lax.broadcasted_iota(jnp.int32, (256, 128), 0)
        col = lax.broadcasted_iota(jnp.int32, (256, 128), 1)
        pickers = low(jnp.where(lax.rem(row, 128) // 64 + 2 * j == col, 1.0, 0.0))
        top = low(prod)
        both = jnp.concatenate([top, low(prod - wide(top))], axis=1)
        acc[...] += dot(both, pickers)

    def rows128(j):
        return pl.ds(pl.multiple_of(128 * j, 128), 128)

    mine, given = 12 * core, 12 * (1 - core)
    row128 = lax.broadcasted_iota(jnp.int32, (128, 128), 0)
    row16 = lax.broadcasted_iota(jnp.int32, (16, 128), 0)
    decay[0:8, :] = jnp.broadcast_to(last, (8, 128))

    def pair_factor(line, j):
        turned = pltpu.roll(jnp.broadcast_to(line, (8, 128)), lax.rem(128 - 2 * j, 128), 1)
        return jnp.where(row128 < 64, jnp.broadcast_to(turned[0:1, 0:1], (128, 128)), jnp.broadcast_to(turned[0:1, 1:2], (128, 128)))

    head_a = 24 * core + 3 * chip // 2
    edge = jnp.where(lax.rem(chip, 2) == 0, 64, 32)
    row96 = lax.broadcasted_iota(jnp.int32, (96, 128), 0)

    class Carry:
        def __init__(self, way, backward, into):
            self.e, self.backward, self.into = 2 * way, backward, into
            self.sib, self.snd, self.rcv, self.ret, self.across = ways[way]

        def swap(self):
            self.first = to_sibling(self.e, loc.at[pl.ds(pl.multiple_of(1536 * (1 - core), 128), 1536)], self.sib)

        def start(self):
            self.first.wait_recv()
            second = core == (0 if self.backward else 1)
            other = decay[8:9, :]
            later = jnp.exp(jnp.where(second, last, other))

            def join(j, carry):
                own, theirs = wide(loc[rows128(mine + j), :]), wide(self.sib[rows128(j), :])
                factor = pair_factor(later, mine + j)
                tile = low(factor * jnp.where(second, theirs, own) + jnp.where(second, own, theirs))
                for g in range(4):
                    q = 4 * j + g
                    self.snd[q // 3, pl.ds(pl.multiple_of(32 * lax.rem(q, 3), 32), 32), :] = tile[32 * g:32 * g + 32]
                return carry

            lax.fori_loop(0, 12, join, 0)
            tail = split3(last + other)
            lines = jnp.zeros((16, 128), f32)
            for k in range(3):
                lines = jnp.where(row16 == k, wide(tail[k]), lines)
            for k in range(16):
                self.snd[k, 96:112, :] = low(lines)

            def own():
                self.rcv[chip] = self.snd[chip]

            exchange(self.e, lambda k: self.snd.at[k], lambda k: self.rcv.at[k], own)

        def turn(self):
            arrived(self.e, lambda k: self.rcv.at[k])
            carry = jnp.zeros((96, 128), f32)
            for k in (range(15, -1, -1) if self.backward else range(16)):
                line = wide(self.rcv[k, 96:112, :])
                line = jnp.exp(line[0:1] + line[1:2] + line[2:3])
                line = pltpu.roll(jnp.broadcast_to(line, (8, 128)), lax.rem(128 - head_a, 128), 1)
                factor = jnp.where(row96 < edge, jnp.broadcast_to(line[0:1, 0:1], (96, 128)), jnp.broadcast_to(line[0:1, 1:2], (96, 128)))
                self.ret[k] = low(carry)
                carry = factor * carry + wide(self.rcv[k, 0:96, :])
            start = pl.multiple_of(1536 * core, 128)

            def place_(k):
                return self.into.at[pl.ds(pl.multiple_of(start + 96 * k, 32), 96)]

            def own():
                self.into[pl.ds(pl.multiple_of(start + 96 * chip, 32), 96), :] = self.ret[chip]

            self.place = place_
            exchange(self.e + 1, lambda k: self.ret.at[k], place_, own)

        def finish(self):
            arrived(self.e + 1, self.place)
            second = core == (0 if self.backward else 1)
            before = jnp.exp(jnp.where(second, decay[8:9, :], last))

            def part(j, carry):
                at_ = rows128(mine + j)
                came = self.into[at_, :]
                passed = low(pair_factor(before, mine + j) * wide(came) + wide(jnp.where(second, self.sib[rows128(j), :], loc[at_, :])))
                self.across[rows128(j), :] = jnp.where(second, came, passed)
                self.into[at_, :] = jnp.where(second, passed, came)
                return carry

            lax.fori_loop(0, 12, part, 0)
            half = pl.ds(pl.multiple_of(1536 * core, 128), 1536)
            self.last = to_sibling(self.e + 1, self.across, self.into.at[half])
            self.last.wait_recv()

        def end(self):
            if self.backward:
                self.first.wait_send()
            self.last.wait_send()
            left(self.e, lambda k: self.snd.at[k])
            left(self.e + 1, lambda k: self.ret.at[k])

    ahead, aback = Carry(0, False, inc), Carry(1, True, inc2)
    decays = to_sibling(4, decay.at[0:8], decay.at[8:16])

    def local_state(j, carry):
        loc[rows128(j), :] = low(dot_tn(low(spread(toward, j) * wide(act[j])), b_in))
        return carry

    lax.fori_loop(given, given + 12, local_state, 0)
    ahead.swap()
    lax.fori_loop(mine, mine + 12, local_state, 0)
    decays.wait_recv()
    ahead.start()

    row = lax.broadcasted_iota(jnp.int32, (128, 128), 0)
    col = lax.broadcasted_iota(jnp.int32, (128, 128), 1)
    causal = row >= col

    def weights(j):
        out = []
        for k, own in enumerate(pick(cum, j)):
            line = rows_a[pl.ds(2 * j + k, 1), :]
            first, second = own[:128], own[128:]
            out.append((
                jnp.exp(jnp.where(causal, first - line[:, :128], -1e30)),
                jnp.exp(second - line[:, :128]),
                jnp.exp(jnp.where(causal, second - line[:, 128:], -1e30))))
        return out

    places = ((slice(0, 128), slice(0, 128)), (slice(128, 256), slice(0, 128)), (slice(128, 256), slice(128, 256)))

    def mixing(gaps):
        return [[low(scores[r, c] * gap) for (r, c), gap in zip(places, head)] for head in gaps]

    def inside(j, carry):
        m = mixing(weights(j))
        xa, xb = by_head(act[j])
        top = dot(jnp.concatenate([m[0][0], m[1][0]], axis=1), jnp.concatenate([xa[:128], xb[:128]], axis=0))
        low_ = dot(jnp.concatenate([m[0][1], m[0][2], m[1][1], m[1][2]], axis=1), jnp.concatenate([xa, xb], axis=0))
        ys[j, 0:128, :] = top
        ys[j, 128:256, :] = low_
        return carry

    lax.fori_loop(0, TILES // 2, inside, 0)
    ahead.turn()
    lax.fori_loop(TILES // 2, TILES, inside, 0)
    ahead.finish()

    def state(ref, j):
        return ref[pl.ds(pl.multiple_of(128 * j, 128), 128), :]

    def gate(j, y):
        gz = proj[:, cols(j)]
        sig = sigmoid(gz)
        full = y + skip[:, cols(j)] * wide(act[j])
        return gz, sig, full, full * gz * sig

    stat[...] = jnp.zeros((256, 128), f32)
    coef[...] = jnp.zeros((256, 128), f32)

    def gate_sums(j, carry):
        y = ys[j] + spread(ecum, j) * dot_nt(c_out, state(inc, j))
        ys[j] = y
        _, _, _, gated = gate(j, y)
        stat[...] += gated * gated
        coef[...] += gated * (gain[:, cols(j)] * db[:, cols(j)])
        return carry

    lax.fori_loop(0, TILES, gate_sums, 0)
    scale = lax.rsqrt(jnp.sum(stat[...], axis=1, keepdims=True) * (1.0 / DI) + epsilon)
    factor = scale * scale * scale * (jnp.sum(coef[...], axis=1, keepdims=True) * (1.0 / DI))
    stat[...] = jnp.broadcast_to(scale, (256, 128))
    coef[...] = jnp.broadcast_to(factor, (256, 128))
    sums[...] = jnp.zeros((8, CONVC), f32)
    skips[...] = jnp.zeros((128, 128), f32)

    def gate_back(j, carry):
        y = ys[j]
        gz, sig, full, gated = gate(j, y)
        scaled = gated * stat[...]
        branch[:, cols(j)] = low(scaled * gain[:, cols(j)])
        given = db[:, cols(j)]
        sums[5:6, cols(j)] = jnp.sum(scaled * given, axis=0, keepdims=True)
        d_gated = stat[...] * gain[:, cols(j)] * given - gated * coef[...]
        dproj[:, cols(j)] = low(d_gated * full * (sig * (1.0 + gz * (1.0 - sig))))
        dy = low(d_gated * gz * sig)
        dys[j] = dy
        dyf = wide(dy)
        skips[pl.ds(j, 1), :] = jnp.sum(dyf * wide(act[j]), axis=0, keepdims=True)
        loc[rows128(j), :] = low(dot_tn(low(spread(ecum, j) * dyf), c_out))
        return carry

    ahead.first.wait_send()
    lax.fori_loop(given, given + 12, gate_back, 0)
    aback.swap()
    lax.fori_loop(mine, mine + 12, gate_back, 0)
    aback.start()
    for ref in (usum, qin, qw):
        ref[...] = jnp.zeros((256, 128), f32)
    dscores[...] = jnp.zeros((256, 256), f32)
    prods[...] = jnp.zeros((128, 128), f32)

    def inside_back(j, carry):
        gaps = weights(j)
        m = mixing(gaps)
        x = act[j]
        dya, dyb = by_head(dys[j])
        for k, dy in enumerate((dya, dyb)):
            near = dot_nt(dy[:128], x[:128])
            far = dot_nt(dy[128:], x)
            part = (near, far[:, :128], far[:, 128:])
            for (r, c), gap, value in zip(places, gaps[k], part):
                dscores[r, c] += gap * value
        top = dot_tn(jnp.concatenate([m[0][0], m[0][1], m[1][0], m[1][1]], axis=0), jnp.concatenate([dya, dyb], axis=0))
        low_ = dot_tn(jnp.concatenate([m[0][2], m[1][2]], axis=0), jnp.concatenate([dya[128:], dyb[128:]], axis=0))
        dx = jnp.concatenate([top, low_], axis=0)
        dxs[j] = dx
        fold(usum, wide(dys[j]) * ys[j], j)
        fold(qin, wide(x) * dx, j)
        return carry

    lax.fori_loop(0, TILES // 2, inside_back, 0)
    aback.turn()
    lax.fori_loop(TILES // 2, TILES, inside_back, 0)
    aback.finish()
    db_in[...] = jnp.zeros((256, 128), f32)
    dc_in[...] = jnp.zeros((256, 128), f32)

    def d_mix(j, d_act):
        m = mixed[j]
        sig = sigmoid(m)
        d_m = d_act * (sig * (1.0 + m * (1.0 - sig)))
        mixed[j] = d_m
        back_out[:, cols(j)] = low(d_m[0:16])

    def carry_back(j, carry):
        s_in, d_s = state(inc, j), state(inc2, j)
        x, dyf = wide(act[j]), wide(dys[j])
        w = spread(toward, j)
        d_w = w * dot_nt(b_in, d_s)
        fold(qw, x * d_w, j)
        db_in[...] += dot(low(w * x), d_s)
        dc_in[...] += dot(low(spread(ecum, j) * dyf), s_in)
        pair = wide(s_in) * wide(d_s)
        prods[pl.ds(2 * j, 1), :] = jnp.sum(pair[:64], axis=0, keepdims=True)
        prods[pl.ds(2 * j + 1, 1), :] = jnp.sum(pair[64:], axis=0, keepdims=True)
        d_mix(j, dxs[j] + d_w + skip[:, cols(j)] * dyf)
        return carry

    lax.fori_loop(0, TILES, carry_back, 0)
    ds = low(dscores[...])
    d_mix(TILES, db_in[...] + dot_tn(ds, c_out))
    d_mix(TILES + 1, dc_in[...] + dot(ds, b_in))
    behind = neighbour(1, back_out, back_in, -1, me > 0)

    q = qin[...] + qw[...]
    d_last = ecum[255:256, :] * jnp.sum(jnp.transpose(prods[...]), axis=0, keepdims=True) + jnp.sum(qw[...], axis=0, keepdims=True)
    at_end = lax.broadcasted_iota(jnp.int32, (256, 128), 0) == 255
    d_l = running_sums(usum[...] - q + jnp.where(at_end, d_last, 0.0), True)
    dt = steps[...]
    raw = proj[:, DI + CONVC:DI + CONVC + 128] + heads[0:1, :]
    d_raw = (q / jnp.maximum(dt, 1e-30) - heads[1:2, :] * d_l) * sigmoid(raw)
    d_raw = jnp.where(lane < H, d_raw, 0.0)
    headsums[...] = jnp.zeros((8, 128), f32)
    by_pair = jnp.transpose(skips[...])
    headsums[2:3, :] = jnp.sum(by_pair[:64], axis=0, keepdims=True)
    headsums[3:4, :] = jnp.sum(by_pair[64:], axis=0, keepdims=True)
    headsums[0:1, :] = jnp.sum(d_raw, axis=0, keepdims=True)
    headsums[1:2, :] = -jnp.sum(d_l * dt, axis=0, keepdims=True)
    dproj[:, DI + CONVC:DI + CONVC + 128] = low(d_raw)
    dproj[:, DI + CONVC + 128:] = jnp.zeros((256, 128), bf16)

    @pl.when(me == 31)
    def _():
        back_in[...] = jnp.zeros((16, CONVC), bf16)

    pl.when(me < 31)(behind.wait_recv)

    def conv_back(j, carry):
        d_m = mixed[j]
        shift[0:8, :] = wide(halo_in[:, cols(j)])[8:16, :]
        shift[8:264, :] = wide(low(proj[:, pl.ds(pl.multiple_of(DI + 128 * j, 128), 128)]))
        for k in range(4):
            sums[k:k + 1, cols(j)] = jnp.sum(d_m * shift[5 + k:261 + k, :], axis=0, keepdims=True)
        sums[4:5, cols(j)] = jnp.sum(d_m, axis=0, keepdims=True)
        shift[0:256, :] = d_m
        shift[256:264, :] = wide(back_in[:, cols(j)])[0:8, :]
        total = taps[3:4, cols(j)] * d_m
        for k in range(3):
            total = total + taps[k:k + 1, cols(j)] * shift[3 - k:259 - k, :]
        dproj[:, pl.ds(pl.multiple_of(DI + 128 * j, 128), 128)] = low(total)
        return carry

    lax.fori_loop(0, TILES + 2, conv_back, 0)
    pl.when(me < 31)(front.wait_send)
    pl.when(me > 0)(behind.wait_send)
    decays.wait_send()
    ahead.end()
    aback.end()


def mixer(projected, d_branch, taps, gain, skip, heads):
    f32, bf16 = jnp.float32, jnp.bfloat16
    tile, half = (256, 128), (16, CONVC)
    vm = pltpu.VMEM
    scratch = [
        vm((TILES + 2,) + tile, bf16), vm((TILES + 2,) + tile, f32), vm((TILES,) + tile, f32), vm((TILES,) + tile, bf16),
        vm((TILES,) + tile, f32), vm((264, 128), f32), vm(half, bf16), vm(half, bf16), vm(half, bf16), vm(half, bf16),
        vm(tile, f32), vm(tile, f32), vm(tile, f32), vm(tile, f32), vm((128, 256), f32), vm((256, 256), f32), vm((256, 256), f32),
        vm(tile, f32), vm(tile, f32), vm(tile, f32), vm((128, 128), f32), vm(tile, f32), vm(tile, f32), vm(tile, f32), vm(tile, f32),
        vm((16, 128), f32),
    ]
    scratch += [vm((128, 128), f32), vm((3072, 128), bf16), vm((3072, 128), bf16), vm((3072, 128), bf16)]
    for _ in range(2):
        scratch += [vm((1536, 128), bf16), vm((16, 112, 128), bf16), vm((16, 112, 128), bf16), vm((16, 96, 128), bf16), vm((1536, 128), bf16)]
    scratch += [pltpu.SemaphoreType.DMA((5,)), pltpu.SemaphoreType.DMA((5,)), pltpu.SemaphoreType.DMA((4, 16)),
                pltpu.SemaphoreType.DMA((4, 16)), pltpu.SemaphoreType.DMA((4,))]
    spec = pl.BlockSpec(memory_space=pltpu.VMEM)
    return pl.pallas_call(
        mixer_kernel,
        out_shape=[jax.ShapeDtypeStruct((256, DI), bf16), jax.ShapeDtypeStruct((256, WIDE), bf16),
                   jax.ShapeDtypeStruct((8, CONVC), f32), jax.ShapeDtypeStruct((8, 128), f32)],
        in_specs=[spec] * 6,
        out_specs=[spec] * 4,
        scratch_shapes=scratch,
        compiler_params=pltpu.CompilerParams(collective_id=2, has_side_effects=True, vmem_limit_bytes=60 << 20),
        name="mixer",
    )(projected, d_branch, taps, gain, skip, heads)


def rms_scale(values, gain):
    return values * lax.rsqrt(jnp.mean(values * values, axis=-1, keepdims=True) + epsilon) * gain


def swap(value):
    return lax.ppermute(value, "c", [(0, 1), (1, 0)])


def my_half(value, core):
    wide = value.shape[1] // 2
    given = swap(lax.dynamic_slice_in_dim(value, (1 - core) * wide, wide, axis=1))
    return jnp.concatenate([lax.dynamic_slice_in_dim(value, core * wide, wide, axis=1), given], axis=0)


def shards(
    hidden,
    cotangent,
    in_w,
    out_w,
    conv_w,
    conv_b,
    norm_gain,
    gate_gain,
    dt_bias,
    decay_rates,
    d_skip,
):
    core = lax.axis_index("c")
    spare = jnp.concatenate([
        jnp.pad(conv_w, ((0, 0), (0, 102))),
        jnp.pad(conv_b, (0, 102))[None],
        jnp.pad(norm_gain, (0, 116))[None],
        jnp.pad(gate_gain, (0, 104))[None],
        jnp.zeros((5, 128), jnp.bfloat16),
    ])
    shard_in = jnp.pad(jnp.concatenate([jnp.pad(in_w, ((0, 0), (0, PARAMS - PROJ))), spare], axis=1), ((0, 4), (0, 0)))
    w_in, w_out = gather([shard_in, jnp.pad(out_w, ((0, 8), (0, 0)))], [12, 24])
    spare = w_in[:, PARAMS:].reshape(128, 12, 128).astype(jnp.float32)
    w_conv_f = spare[:, :4, :26].transpose(1, 0, 2).reshape(KW, CONVC)
    b_conv_f = spare[:, 4, :26].reshape(CONVC)
    gain_norm_f = spare[:, 5, :12].reshape(1536)
    gain_gate_f = spare[:, 6, :24].reshape(DI)
    residual = hidden[0].astype(jnp.float32)
    length = residual.shape[0]
    normed = rms_scale(residual, gain_norm_f).astype(jnp.bfloat16)
    projected = jnp.dot(normed, w_in, preferred_element_type=jnp.float32)
    grad_out = cotangent[0]
    both_out = jnp.concatenate([grad_out, swap(grad_out)], axis=0)
    d_branch = jnp.einsum("td,kd->tk", grad_out, w_out, preferred_element_type=jnp.float32)
    taps = jnp.pad(jnp.concatenate([w_conv_f, b_conv_f[None]]), ((0, 3), (0, 0)))
    heads = jnp.pad(jnp.stack([dt_bias, decay_rates]), ((0, 6), (0, 80)))
    branch, d_projected, sums, head_sums = mixer(
        projected, d_branch, taps, gain_gate_f[None], jnp.repeat(d_skip, P_SIZE)[None], heads)
    result = (residual + jnp.dot(branch, w_out, preferred_element_type=jnp.float32)).astype(jnp.bfloat16)
    d_w_out = jnp.einsum("tk,td->kd", my_half(branch, core), both_out, preferred_element_type=jnp.float32).astype(jnp.bfloat16)
    d_normed = jnp.einsum("tj,dj->td", d_projected, w_in, preferred_element_type=jnp.float32)
    both_projected = jnp.concatenate([d_projected, swap(d_projected)], axis=0)
    d_w_in = jnp.einsum("td,tj->dj", my_half(normed, core), both_projected, preferred_element_type=jnp.float32).astype(jnp.bfloat16)
    norm_pull = jax.vjp(rms_scale, residual, gain_norm_f)[1]
    d_from_norm, d_gain_norm = norm_pull(d_normed)
    d_hidden = grad_out.astype(jnp.float32) + d_from_norm
    g_in, g_out, total = scatter(
        [d_w_in, d_w_out], [sums, head_sums, jnp.pad(d_gain_norm[None], ((0, 7), (0, 0)))], [12, 24])
    return (
        result[None],
        d_hidden[None],
        g_in[:12, :PROJ],
        g_out,
        total[:4, :26],
        total[4, :26],
        total[6, :12],
        total[5, :24],
        total[8, :H],
        total[9, :H],
        jnp.stack([total[10, :H // 2], total[11, :H // 2]], axis=1).reshape(H),
    )


def solution(mesh):
    grid = Mesh(mesh.devices.reshape(4, 4, 4, 2), ALL)
    tokens = P("z", SEQ, None)
    placed = (
        tokens,
        tokens,
        P(ALL, None),
        P(ALL, None),
        P(None, ALL),
        P(ALL),
        P(ALL),
        P(ALL),
        P(),
        P(),
        P(),
    )
    return jax.shard_map(
        shards,
        mesh=grid,
        in_specs=placed,
        out_specs=(tokens, tokens, P(ALL, None), P(ALL, None), P(None, ALL), P(ALL), P(ALL), P(ALL), P(), P(), P()),
        check_vma=False,
    )
```

```python
import functools
import jax
import jax.numpy as jnp
from jax import lax
from jax.experimental import pallas as pl
from jax.experimental.pallas import tpu as pltpu
from jax.sharding import PartitionSpec as P, Mesh

MESH = pl.DeviceIdType.MESH
ALL = ("z", "y", "x", "c")
ORDERS = (("z", "y", "x"), ("y", "x", "z"), ("x", "z", "y"))


class Links:
    def __init__(self, send, recv):
        self.send, self.recv, self.used, self.sent = send, recv, 0, []

    def copy(self, src, dst, device):
        k = self.used
        self.used += 1
        made = pltpu.make_async_remote_copy(
            src_ref=src, dst_ref=dst, send_sem=self.send.at[k], recv_sem=self.recv.at[k],
            device_id=device, device_id_type=MESH)
        made.start()
        self.sent.append(made)
        return made

    def finish(self):
        for made in self.sent:
            made.wait_send()


def place():
    return {name: lax.axis_index(name) for name in ALL}


def block(ref, part, core, at, have, half=None):
    z, y, x = at["z"], at["y"], at["x"]
    wide = ref.shape[-1]
    full = slice(None)
    zh, zl = (full, full) if "z" in have else (z // 2, lax.rem(z, 2))
    ys = full if "y" in have else y
    first, count = (0, wide) if "x" in have else (x * (wide // 4), wide // 4)
    if half is not None:
        if "y" in have:
            ys = pl.ds(2 * half, 2)
        elif "z" in have:
            zh = pl.ds(half, 1)
        else:
            near = -(-count // 256) * 128
            first, count = (first, near) if half == 0 else (first + near, count - near)
    cols = full if "x" in have and count == wide else pl.ds(first if isinstance(first, int) else pl.multiple_of(first, 128), count)
    return ref.at[core, zh, ys, zl, part, :, cols]


def moved(at, axis, steps):
    return {**at, axis: lax.rem(at[axis] + steps + 4, 4)}


def gather_kernel(*refs, n, rows):
    shards, fulls, refs = refs[:n], refs[n:2 * n], refs[2 * n:]
    stage, landed, unit, (send, recv, own) = refs[:n], refs[n:2 * n], refs[2 * n:3 * n], refs[3 * n:]
    at = place()
    z, y, x, c = (at[name] for name in ALL)
    to_z, to_c = 2 * lax.rem(z, 2) + x // 2, z // 2
    slot = 2 * lax.rem(x, 2) + c
    from_z = 2 * c + z // 2
    barrier = pltpu.get_barrier_semaphore()
    for axis in ("z", "y", "x"):
        for steps in (1, -1):
            pl.semaphore_signal(barrier, inc=1, device_id={axis: moved(at, axis, steps)[axis]}, device_id_type=MESH)
    pl.semaphore_signal(barrier, inc=1, device_id={"c": 1 - c}, device_id_type=MESH)
    for k in range(4):
        sx, sc = 2 * lax.rem(z, 2) + k // 2, k % 2
        other = jnp.logical_or(jnp.logical_or(sx != x, sc != c), from_z != z)

        @pl.when(other)
        def _():
            pl.semaphore_signal(barrier, inc=1, device_id=(from_z, y, sx, jnp.int32(sc)), device_id_type=MESH)
    home = jnp.logical_and(to_z == z, to_c == c)
    pl.semaphore_wait(barrier, 11 - home.astype(jnp.int32))

    links = Links(send, recv)
    first = []
    for i in range(n):
        wide = shards[i].shape[1] // 4
        for tx in range(4):
            k = links.used
            links.used += 1
            src = shards[i].at[:, pl.ds(tx * wide, wide)]
            remote = pltpu.make_async_remote_copy(
                src_ref=src, dst_ref=landed[i].at[slot], send_sem=send.at[k], recv_sem=recv.at[4 * i + slot],
                device_id=(to_z, y, jnp.int32(tx), to_c), device_id_type=MESH)
            local = pltpu.make_async_copy(src, landed[i].at[slot], recv.at[4 * i + slot])
            mine = jnp.logical_and(home, x == tx)
            pl.when(jnp.logical_not(mine))(remote.start)
            pl.when(mine)(local.start)
            first.append((remote, mine))
    kept = []
    for i in range(n):
        deep, height = rows[i], unit[i].shape[1]
        for k in range(4):
            pltpu.make_async_copy(landed[i].at[k], landed[i].at[k], recv.at[4 * i + k]).wait()
            stage[i][pl.ds(deep * k, deep), :] = landed[i][k, :deep, :].astype(jnp.float32)
        for part in range(3):
            unit[i][part] = stage[i][pl.ds(part * height, height), :].astype(jnp.bfloat16)
        for part in range(3):
            copy = pltpu.make_async_copy(unit[i].at[part], block(fulls[i], part, c, at, ()), own.at[3 * i + part])
            copy.start()
            kept.append(copy)
    sibling = {"c": 1 - c}
    streams = [(i, part) for i in range(n) for part in range(3)]
    for phase in range(3):
        near = {}
        for i, part in streams:
            have, axis = ORDERS[part][:phase], ORDERS[part][phase]
            mine = unit[i].at[part] if phase == 0 else block(fulls[i], part, c, at, have)
            there = block(fulls[i], part, c, at, have)
            near[i, part] = [links.copy(mine, there, {axis: moved(at, axis, steps)[axis]}) for steps in (1, -1)]
            if phase == 0:
                links.copy(mine, there, sibling)
        far = {}
        for i, part in streams:
            have, axis = ORDERS[part][:phase], ORDERS[part][phase]
            far[i, part] = []
            for way, steps in ((0, 1), (1, -1)):
                near[i, part][way].wait_recv()
                behind = moved(at, axis, -steps)
                piece = block(fulls[i], part, c, behind, have, way)
                far[i, part].append(links.copy(piece, piece, {axis: moved(at, axis, steps)[axis]}))
                whole = block(fulls[i], part, c, behind, have)
                links.copy(whole, whole, sibling)
        for i, part in streams:
            have, axis = ORDERS[part][:phase], ORDERS[part][phase]
            for way in (0, 1):
                far[i, part][way].wait_recv()
                piece = block(fulls[i], part, c, moved(at, axis, 2), have, way)
                links.copy(piece, piece, sibling)
        if phase == 0:
            for copy in kept:
                copy.wait()
    for made in links.sent:
        if made.device_id is sibling:
            made.wait_recv()
    links.finish()
    for remote, mine in first:
        pl.when(jnp.logical_not(mine))(remote.wait_send)


def gather(shards, rows):
    n = len(shards)
    heights = [4 * r // 3 for r in rows]
    wides = [s.shape[1] for s in shards]
    fulls = [jax.ShapeDtypeStruct((2, 2, 4, 2, 3, h, w), jnp.bfloat16) for h, w in zip(heights, wides)]
    count = n * (4 + 3 * (3 * 3 * 2 + 1 + 6))
    outs = pl.pallas_call(
        functools.partial(gather_kernel, n=n, rows=tuple(rows)),
        out_shape=fulls,
        in_specs=[pl.BlockSpec(memory_space=pltpu.VMEM)] * n,
        out_specs=[pl.BlockSpec(memory_space=pl.ANY)] * n,
        scratch_shapes=[pltpu.VMEM((3 * h, w // 4), jnp.float32) for h, w in zip(heights, wides)]
        + [pltpu.VMEM((4, s.shape[0], w // 4), jnp.bfloat16) for s, w in zip(shards, wides)]
        + [pltpu.VMEM((3, h, w // 4), jnp.bfloat16) for h, w in zip(heights, wides)]
        + [pltpu.SemaphoreType.DMA((count,)), pltpu.SemaphoreType.DMA((count,)), pltpu.SemaphoreType.DMA((3 * n,))],
        compiler_params=pltpu.CompilerParams(collective_id=0, has_side_effects=True, vmem_limit_bytes=32 << 20),
        name="gather_weights",
    )(*shards)
    return [o.reshape(128 * r, w) for o, r, w in zip(outs, rows, wides)]


def span(shape, axis, at):
    cut = [slice(None)] * 5
    if axis == "y":
        cut[1] = pl.ds(at["y"], 1)
    elif axis == "z":
        cut[0], cut[2] = pl.ds(at["z"] // 2, 1), pl.ds(lax.rem(at["z"], 2), 1)
    else:
        cut[4] = pl.ds(pl.multiple_of(at["x"] * (shape[4] // 4), 128), shape[4] // 4)
    return cut


def without(shape, axis):
    zh, y, zl, rows, wide = shape
    return {"y": (zh, 1, zl, rows, wide), "z": (1, y, 1, rows, wide), "x": (zh, y, zl, rows, wide // 4)}[axis]


def halves(shape):
    if shape[1] == 4:
        return 1, ((0, 2), (2, 2))
    if shape[0] == 2:
        return 0, ((0, 1), (1, 1))
    near = -(-shape[4] // 256) * 128
    return 4, ((0, near), (near, shape[4] - near))


def cut_half(cut, shape, half):
    dim, parts = halves(shape)
    start, size = parts[half]
    cut = list(cut)
    old = cut[dim]
    base = 0 if isinstance(old, slice) else old.start
    cut[dim] = pl.ds(pl.multiple_of(base + start, 128) if dim == 4 and not isinstance(base, int) else base + start, size)
    return cut


def half_shape(shape, half):
    dim, parts = halves(shape)
    return tuple(parts[half][1] if k == dim else size for k, size in enumerate(shape))


def add_up(out, terms, shape):
    na, nb, nc = shape[:3]

    def slab(k, carry):
        a, b, d = k // (nb * nc), lax.rem(k // nc, nb), lax.rem(k, nc)
        total = terms[0](a, b, d).astype(jnp.float32)
        for term in terms[1:]:
            total = total + term(a, b, d).astype(jnp.float32)
        out(a, b, d, total)
        return carry

    lax.fori_loop(0, na * nb * nc, slab, 0)


def start_of(cut):
    return 0 if isinstance(cut, slice) else cut.start


def slab_of(ref, cut, shape):
    z0, y0, l0, _, c0 = (start_of(s) for s in cut)
    lead = ref

    def read(a, b, d):
        return lead[z0 + a, y0 + b, l0 + d, :, pl.ds(c0, shape[4])]

    return read


def slab_to(ref, shape):
    def write(a, b, d, value):
        ref[a, b, d] = value.astype(ref.dtype)

    return write


ALL_CUT = [slice(None)] * 5


def scatter_scratch(rows, wides):
    heights = [4 * r // 3 for r in rows]
    tall = [-(-r // 8) * 8 for r in rows]
    scratch = []
    size = {(i, part): (2, 4, 2, heights[i], wides[i]) for i in range(len(rows)) for part in range(3)}
    for phase in range(3):
        for s in size:
            shape = without(size[s], ORDERS[s[1]][2 - phase])
            scratch += [pltpu.VMEM(shape, jnp.bfloat16)] * 2
            scratch += [pltpu.VMEM(half_shape(shape, way), jnp.bfloat16) for way in (0, 1)]
            if phase < 2:
                scratch += [pltpu.VMEM(shape, jnp.bfloat16)]
            size[s] = shape
    scratch += [pltpu.VMEM((3 * t, w // 4), jnp.float32) for t, w in zip(heights, wides)]
    scratch += [pltpu.VMEM((4, t, w // 4), jnp.float32) for t, w in zip(tall, wides)] * 2
    scratch += [pltpu.SemaphoreType.DMA((4 * len(rows),))] * 2
    return scratch


class Scatter:
    def __init__(self, at, links, sources, rows, wides, refs):
        n = len(rows)
        take = iter(refs)
        self.at, self.links, self.rows, self.n = at, links, rows, n
        self.streams = [(i, part) for i in range(n) for part in range(3)]
        self.near, self.relay, self.acc = {}, {}, {}
        for phase in range(3):
            for s in self.streams:
                self.near[s, phase] = [next(take), next(take)]
                self.relay[s, phase] = [next(take), next(take)]
                self.acc[s, phase] = next(take) if phase < 2 else None
        self.fin, self.staged, self.landed = ([next(take) for _ in range(n)] for _ in range(3))
        self.last, self.own = next(take), next(take)
        self.size = {s: (2, 4, 2, 4 * rows[s[0]] // 3, wides[s[0]]) for s in self.streams}
        self.source = {s: sources[s[0]].at[:, :, :, s[1]] for s in self.streams}

    def steps(self):
        at, links, size, source = self.at, self.links, self.size, self.source
        for phase in range(3):
            sent, lent = {}, {}
            for s in self.streams:
                axis = ORDERS[s[1]][2 - phase]
                shape = without(size[s], axis)
                cuts = {k: span(size[s], axis, moved(at, axis, k)) for k in (1, 2, 3)}
                to = {k: {axis: moved(at, axis, k)[axis]} for k in (1, 3)}
                lent[s], sent[s] = [], []
                for way, step in ((0, 1), (1, 3)):
                    src = source[s].at[tuple(cut_half(cuts[2], shape, way))]
                    lent[s].append(links.copy(src, self.relay[s, phase][way], to[step]))
                for way, step in ((0, 1), (1, 3)):
                    src = source[s].at[tuple(cut_half(cuts[step], shape, 1 - way))]
                    dst = self.near[s, phase][way].at[tuple(cut_half(ALL_CUT, shape, 1 - way))]
                    sent[s].append(links.copy(src, dst, to[step]))
            yield
            for s in self.streams:
                axis = ORDERS[s[1]][2 - phase]
                shape = without(size[s], axis)
                for way, step in ((0, 1), (1, 3)):
                    lent[s][way].wait_recv()
                    hs = half_shape(shape, way)
                    cut = cut_half(span(size[s], axis, moved(at, axis, step)), shape, way)
                    buf = self.relay[s, phase][way]
                    add_up(slab_to(buf, hs), [slab_of(source[s], cut, hs), slab_of(buf, ALL_CUT, hs)], hs)
                    dst = self.near[s, phase][way].at[tuple(cut_half(ALL_CUT, shape, way))]
                    sent[s].append(links.copy(buf, dst, {axis: moved(at, axis, step)[axis]}))
            yield
            for s in self.streams:
                i, part = s
                axis = ORDERS[part][2 - phase]
                shape = without(size[s], axis)
                for copy in sent[s]:
                    copy.wait_recv()
                terms = [slab_of(source[s], span(size[s], axis, at), shape)]
                terms += [slab_of(self.near[s, phase][way], ALL_CUT, shape) for way in (0, 1)]
                if phase < 2:
                    add_up(slab_to(self.acc[s, phase], shape), terms, shape)
                    source[s], size[s] = self.acc[s, phase], shape
                else:
                    total = terms[0](0, 0, 0).astype(jnp.float32)
                    for term in terms[1:]:
                        total = total + term(0, 0, 0).astype(jnp.float32)
                    self.fin[i][pl.ds(part * shape[3], shape[3]), :] = total
        z, y, x, c = (at[name] for name in ALL)
        from_z = 2 * c + z // 2
        home = jnp.logical_and(2 * lax.rem(z, 2) + x // 2 == z, z // 2 == c)
        final = []
        for i in range(self.n):
            deep = self.rows[i]
            staged, landed = self.staged[i], self.landed[i]
            for k in range(4):
                sx, sc = 2 * lax.rem(z, 2) + k // 2, k % 2
                staged[k] = jnp.zeros(staged.shape[1:], jnp.float32)
                staged[k, :deep] = self.fin[i][pl.ds(deep * k, deep), :]
                mine = jnp.logical_and(home, jnp.logical_and(sx == x, sc == c))
                remote = pltpu.make_async_remote_copy(
                    src_ref=staged.at[k], dst_ref=landed.at[x], send_sem=self.own.at[4 * i + k], recv_sem=self.last.at[4 * i + x],
                    device_id=(from_z, y, sx, jnp.int32(sc)), device_id_type=MESH)
                local = pltpu.make_async_copy(staged.at[k], landed.at[x], self.last.at[4 * i + x])
                pl.when(jnp.logical_not(mine))(remote.start)
                pl.when(mine)(local.start)
                final.append((remote, mine))
        self.final = final
        yield

    def finish(self, outs):
        for i in range(self.n):
            wide_ = self.fin[i].shape[1]
            for tx in range(4):
                pltpu.make_async_copy(self.landed[i].at[tx], self.landed[i].at[tx], self.last.at[4 * i + tx]).wait()
                outs[i][:, pl.ds(tx * wide_, wide_)] = self.landed[i][tx]
        for remote, mine in self.final:
            pl.when(jnp.logical_not(mine))(remote.wait_send)


def targets(at):
    z, x, c = at["z"], at["x"], at["c"]
    to_z, to_c = 2 * lax.rem(z, 2) + x // 2, z // 2
    return to_z, to_c, 2 * c + z // 2, jnp.logical_and(to_z == z, to_c == c)


def scatter_kernel(*refs, rows, wides):
    n = len(rows)
    parts_in, smalls, refs = refs[:n], refs[n:n + 3], refs[n + 3:]
    outs, small_out, refs = refs[:n], refs[n], refs[n + 1:]
    rounds, (send, recv), refs = refs[:4], refs[4:6], refs[6:]
    at = place()
    z, y, x, c = (at[name] for name in ALL)
    to_z, to_c, _, home = targets(at)
    barrier = pltpu.get_barrier_semaphore()
    for axis in ("z", "y", "x"):
        for steps in (1, 2, 3):
            pl.semaphore_signal(barrier, inc=1, device_id={axis: moved(at, axis, steps)[axis]}, device_id_type=MESH)
    pl.semaphore_signal(barrier, inc=1, device_id={"c": 1 - c}, device_id_type=MESH)
    for tx in range(4):
        @pl.when(jnp.logical_not(jnp.logical_and(home, x == tx)))
        def _():
            pl.semaphore_signal(barrier, inc=1, device_id=(to_z, y, jnp.int32(tx), to_c), device_id_type=MESH)
    pl.semaphore_wait(barrier, 14 - home.astype(jnp.int32))

    links = Links(send, recv)
    work = Scatter(at, links, parts_in, rows, wides, refs)
    sums = [None]

    def small_start(k):
        axis = ("c", "x", "y", "z")[k]
        if k == 0:
            start = 0
            for part in smalls:
                rounds[0][c, :, start:start + part.shape[1]] = part[...]
                start += part.shape[1]
        else:
            rounds[k][at[axis]] = sums[0]
        held = rounds[k].at[at[axis]]
        if k == 0:
            return [links.copy(held, held, {"c": 1 - c})]
        return [links.copy(held, held, {axis: moved(at, axis, steps)[axis]}) for steps in (1, 2, 3)]

    def small_end(k, going):
        for copy in going:
            copy.wait_recv()
        total = rounds[k][0]
        for j in range(1, 2 if k == 0 else 4):
            total = total + rounds[k][j]
        sums[0] = total

    going = small_start(0)
    for k, _ in enumerate(work.steps()):
        if k in (0, 2, 4):
            small_end(k // 2, going)
            going = small_start(k // 2 + 1)
    small_end(3, going)
    index = 32 * z + 8 * y + 2 * x + c
    total, start = sums[0], 0
    for part, (each, first, count, to) in zip(smalls, ((26, 0, 8, 0), (0, 0, 8, 8), (12, 0, 1, 6))):
        wide_ = part.shape[1]
        value = total[:, start:start + wide_]
        if each:
            value = pltpu.roll(value, lax.rem(wide_ - each * index, wide_), 1)
        small_out[to:to + count, :] = value[first:first + count, :128]
        start += wide_
    gate = pltpu.roll(total[:, :128 * 24], lax.rem(3072 - 24 * index, 3072), 1)
    small_out[5:6, :] = gate[5:6, :128]
    work.finish(outs)
    links.finish()


def scatter(halves_in, smalls, rows):
    n = len(halves_in)
    wides = [h.shape[1] for h in halves_in]
    ins = [h.reshape(2, 4, 2, 3, 4 * r // 3, w) for h, r, w in zip(halves_in, rows, wides)]
    tall = [-(-r // 8) * 8 for r in rows]
    count = n * 3 * 3 * 6 + 10
    scratch = [pltpu.VMEM((2 if k == 0 else 4, 8, sum(s.shape[1] for s in smalls)), jnp.float32) for k in range(4)]
    scratch += [pltpu.SemaphoreType.DMA((count,))] * 2
    return pl.pallas_call(
        functools.partial(scatter_kernel, rows=tuple(rows), wides=tuple(wides)),
        out_shape=[jax.ShapeDtypeStruct((t, w), jnp.float32) for t, w in zip(tall, wides)] + [jax.ShapeDtypeStruct((16, 128), jnp.float32)],
        in_specs=[pl.BlockSpec(memory_space=pltpu.VMEM)] * (n + 3),
        out_specs=[pl.BlockSpec(memory_space=pltpu.VMEM)] * (n + 1),
        scratch_shapes=scratch + scatter_scratch(rows, wides),
        compiler_params=pltpu.CompilerParams(collective_id=1, has_side_effects=True, vmem_limit_bytes=56 << 20),
        name="scatter_gradients",
    )(*ins, *smalls)


H = 48
P_SIZE = 64
KW = 4
DI = 3072
CONVC = 3328
PROJ = 6448
WIDE = 6656
PARAMS = 6528
SEQ = ("y", "x", "c")
epsilon = 1e-05


TILES = 24


def dot(a, b):
    return jnp.dot(a, b, preferred_element_type=jnp.float32)


def dot_nt(a, b):
    return lax.dot_general(a, b, (((1,), (1,)), ((), ())), preferred_element_type=jnp.float32)


def dot_tn(a, b):
    return lax.dot_general(a, b, (((0,), (0,)), ((), ())), preferred_element_type=jnp.float32)


def low(v):
    return v.astype(jnp.bfloat16)


def wide(v):
    return v.astype(jnp.float32)


def split3(v):
    a = low(v)
    b = low(v - wide(a))
    return a, b, low(v - wide(a) - wide(b))


def running_sums(v, backward):
    row = lax.broadcasted_iota(jnp.int32, (256, 256), 0)
    col = lax.broadcasted_iota(jnp.int32, (256, 256), 1)
    ones = low(jnp.where(row <= col if backward else row >= col, 1.0, 0.0))
    return sum(dot(ones, part) for part in split3(v))


def sigmoid(v):
    return 1.0 / (1.0 + jnp.exp(-v))


def loop(first, count, body, unroll):
    def step(k, carry):
        for u in range(unroll):
            body(first + k * unroll + u, u)
        return carry
    lax.fori_loop(0, count // unroll, step, 0)


def mixer_kernel(gates, conv_in, dt_in, normed, hidden, given_out, db, taps, gain, skip, heads, w_in, w_out,
                 out, dproj, d_norm, sums, headsums, g_z, g_o,
                 branch, dz, sib_normed, sib_given, sib_branch, sib_dz, src_z, src_o, chunk, chunk_sem,
                 act, ys, dys, shift, shift2, halo_out, halo_in, back_out, back_in,
                 cum, ecum, toward, steps, rows_a, scores, dscores, usum, qin, qw, prods, stat, coef, db_in, dc_in, decay,
                 skips, loc, inc, inc2, *rest):
    f32, bf16 = jnp.float32, jnp.bfloat16
    snd, rcv, ret = rest[:3]
    ways, (sib_send, sib_recv, a_send, a_recv, h_sem, rs_send, rs_recv), rest = (rest[3:5], rest[5:7]), rest[7:14], rest[14:]
    at = place()
    z, core = lax.axis_index("z"), lax.axis_index("c")
    chip = 4 * lax.axis_index("y") + lax.axis_index("x")
    me = 2 * chip + core
    lane = lax.broadcasted_iota(jnp.int32, (256, 128), 1)
    first_head = lane < 64

    def device(k):
        return (z, k // 8, lax.rem(k // 2, 4), lax.rem(k, 2))

    def same_core(k):
        return (z, k // 4, lax.rem(k, 4), core)

    def others(body):
        def step(k, carry):
            body(lax.rem(chip + k, 16))
            return carry
        lax.fori_loop(1, 16, step, 0)

    barrier = pltpu.get_barrier_semaphore()
    others(lambda k: pl.semaphore_signal(barrier, inc=1, device_id=same_core(k), device_id_type=MESH))
    pl.semaphore_signal(barrier, inc=1, device_id={"c": 1 - core}, device_id_type=MESH)
    beside = jnp.where(core == 1, me + 1, me - 1)
    inner = jnp.logical_and(beside >= 0, beside < 32)

    @pl.when(inner)
    def _():
        pl.semaphore_signal(barrier, inc=1, device_id=device(beside), device_id_type=MESH)

    for steps_ in (1, -1):
        pl.semaphore_signal(barrier, inc=1, device_id={"z": moved(at, "z", steps_)["z"]}, device_id_type=MESH)
    to_z, to_c, _, home = targets(at)
    for tx in range(4):
        @pl.when(jnp.logical_not(jnp.logical_and(home, at["x"] == tx)))
        def _():
            pl.semaphore_signal(barrier, inc=1, device_id=(to_z, at["y"], jnp.int32(tx), to_c), device_id_type=MESH)
    pl.semaphore_wait(barrier, 22 + inner.astype(jnp.int32) - home.astype(jnp.int32))

    def exchange(e, source, target, own):
        def go(k):
            pltpu.make_async_remote_copy(
                src_ref=source(k), dst_ref=target(chip), send_sem=a_send.at[e, k], recv_sem=a_recv.at[e, chip],
                device_id=same_core(k), device_id_type=MESH).start()
        others(go)
        own()

    def arrived(e, target):
        others(lambda k: pltpu.make_async_copy(target(k), target(k), a_recv.at[e, k]).wait())

    def left(e, source):
        others(lambda k: pltpu.make_async_copy(source(k), source(k), a_send.at[e, k]).wait())

    def to_sibling(e, src, dst):
        made = pltpu.make_async_remote_copy(
            src_ref=src, dst_ref=dst, send_sem=sib_send.at[e], recv_sem=sib_recv.at[e],
            device_id={"c": 1 - core}, device_id_type=MESH)
        made.start()
        return made

    def neighbour(k, src, dst, steps_, on):
        made = pltpu.make_async_remote_copy(
            src_ref=src, dst_ref=dst, send_sem=h_sem.at[2 * k], recv_sem=h_sem.at[2 * k + 1],
            device_id=device(lax.rem(me + steps_ + 32, 32)), device_id_type=MESH)
        pl.when(on)(made.start)
        return made

    def lanes(start, size):
        return pl.ds(pl.multiple_of(start, 128), size)

    halo_out[...] = conv_in[240:256, :]
    front = neighbour(0, halo_out, halo_in, 1, me < 31)
    shared = [to_sibling(5, normed.at[:, lanes(768 * (1 - core), 768)], sib_normed), to_sibling(6, given_out, sib_given)]

    raw = dt_in[...] + heads[0:1, :]
    dt = jnp.maximum(raw, 0.0) + jnp.log1p(jnp.exp(-jnp.abs(raw)))
    total = running_sums(-heads[1:2, :] * dt, False)
    last = total[255:256, :]
    steps[...] = dt
    cum[...] = total
    ecum[...] = jnp.exp(total)
    toward[...] = jnp.exp(last - total) * dt
    rows_a[...] = jnp.transpose(total - jnp.log(dt))

    @pl.when(me == 0)
    def _():
        halo_in[...] = jnp.zeros((16, CONVC), bf16)

    pl.when(me > 0)(front.wait_recv)

    def cols(j):
        return pl.ds(pl.multiple_of(128 * j, 128), 128)

    def convolved(j, u):
        shift[u, 0:8, :] = wide(halo_in[:, cols(j)])[8:16, :]
        shift[u, 8:264, :] = wide(conv_in[:, cols(j)])
        total = taps[4:5, cols(j)] + taps[0:1, cols(j)] * shift[u, 5:261, :]
        for k in range(1, 4):
            total = total + taps[k:k + 1, cols(j)] * shift[u, 5 + k:261 + k, :]
        return total

    def conv(j, u):
        total = convolved(j, u)
        act[j] = low(total * sigmoid(total))

    loop(0, TILES + 2, conv, 2)
    b_in, c_out = act[TILES], act[TILES + 1]
    scores[...] = dot_nt(c_out, b_in)

    def pick(ref, j):
        turned = pltpu.roll(ref[...], lax.rem(128 - 2 * j, 128), 1)
        return jnp.broadcast_to(turned[:, 0:1], (256, 128)), jnp.broadcast_to(turned[:, 1:2], (256, 128))

    def spread(ref, j):
        one, two = pick(ref, j)
        return jnp.where(first_head, one, two)

    def by_head(v):
        zero = jnp.zeros_like(v)
        return jnp.where(first_head[:v.shape[0]], v, zero), jnp.where(first_head[:v.shape[0]], zero, v)

    def fold(acc, prod, j):
        row = lax.broadcasted_iota(jnp.int32, (256, 128), 0)
        col = lax.broadcasted_iota(jnp.int32, (256, 128), 1)
        pickers = low(jnp.where(lax.rem(row, 128) // 64 + 2 * j == col, 1.0, 0.0))
        top = low(prod)
        both = jnp.concatenate([top, low(prod - wide(top))], axis=1)
        acc[...] += dot(both, pickers)

    def rows128(j):
        return pl.ds(pl.multiple_of(128 * j, 128), 128)

    mine, given = 12 * core, 12 * (1 - core)
    row128 = lax.broadcasted_iota(jnp.int32, (128, 128), 0)
    row16 = lax.broadcasted_iota(jnp.int32, (16, 128), 0)
    decay[0:8, :] = jnp.broadcast_to(last, (8, 128))

    def pair_factor(line, j):
        turned = pltpu.roll(jnp.broadcast_to(line, (8, 128)), lax.rem(128 - 2 * j, 128), 1)
        return jnp.where(row128 < 64, jnp.broadcast_to(turned[0:1, 0:1], (128, 128)), jnp.broadcast_to(turned[0:1, 1:2], (128, 128)))

    head_a = 24 * core + 3 * chip // 2
    edge = jnp.where(lax.rem(chip, 2) == 0, 64, 32)
    row96 = lax.broadcasted_iota(jnp.int32, (96, 128), 0)

    class Carry:
        def __init__(self, way, backward, into):
            self.e, self.backward, self.into = 2 * way, backward, into
            self.sib, self.across = ways[way]
            self.snd, self.rcv, self.ret = snd, rcv, ret

        def swap(self):
            self.first = to_sibling(self.e, loc.at[pl.ds(pl.multiple_of(1536 * (1 - core), 128), 1536)], self.sib)

        def start(self):
            self.first.wait_recv()
            second = core == (0 if self.backward else 1)
            other = decay[8:9, :]
            later = jnp.exp(jnp.where(second, last, other))

            def join(j, carry):
                own, theirs = wide(loc[rows128(mine + j), :]), wide(self.sib[rows128(j), :])
                factor = pair_factor(later, mine + j)
                tile = low(factor * jnp.where(second, theirs, own) + jnp.where(second, own, theirs))
                for g in range(4):
                    q = 4 * j + g
                    self.snd[q // 3, pl.ds(pl.multiple_of(32 * lax.rem(q, 3), 32), 32), :] = tile[32 * g:32 * g + 32]
                return carry

            loop(0, 12, join, 12)
            tail = split3(last + other)
            lines = jnp.zeros((16, 128), f32)
            for k in range(3):
                lines = jnp.where(row16 == k, wide(tail[k]), lines)
            for k in range(16):
                self.snd[k, 96:112, :] = low(lines)

            def own():
                self.rcv[chip] = self.snd[chip]

            exchange(self.e, lambda k: self.snd.at[k], lambda k: self.rcv.at[k], own)

        def turn(self):
            arrived(self.e, lambda k: self.rcv.at[k])
            carry = jnp.zeros((96, 128), f32)
            for k in (range(15, -1, -1) if self.backward else range(16)):
                line = wide(self.rcv[k, 96:112, :])
                line = jnp.exp(line[0:1] + line[1:2] + line[2:3])
                line = pltpu.roll(jnp.broadcast_to(line, (8, 128)), lax.rem(128 - head_a, 128), 1)
                factor = jnp.where(row96 < edge, jnp.broadcast_to(line[0:1, 0:1], (96, 128)), jnp.broadcast_to(line[0:1, 1:2], (96, 128)))
                self.ret[k] = low(carry)
                carry = factor * carry + wide(self.rcv[k, 0:96, :])
            start = pl.multiple_of(1536 * core, 128)

            def place_(k):
                return self.into.at[pl.ds(pl.multiple_of(start + 96 * k, 32), 96)]

            def own():
                self.into[pl.ds(pl.multiple_of(start + 96 * chip, 32), 96), :] = self.ret[chip]

            self.place = place_
            exchange(self.e + 1, lambda k: self.ret.at[k], place_, own)

        def finish(self):
            arrived(self.e + 1, self.place)
            second = core == (0 if self.backward else 1)
            before = jnp.exp(jnp.where(second, decay[8:9, :], last))

            def part(j, carry):
                at_ = rows128(mine + j)
                came = self.into[at_, :]
                passed = low(pair_factor(before, mine + j) * wide(came) + wide(jnp.where(second, self.sib[rows128(j), :], loc[at_, :])))
                self.across[rows128(j), :] = jnp.where(second, came, passed)
                self.into[at_, :] = jnp.where(second, passed, came)
                return carry

            loop(0, 12, part, 12)
            half = pl.ds(pl.multiple_of(1536 * core, 128), 1536)
            self.last = to_sibling(self.e + 1, self.across, self.into.at[half])
            self.last.wait_recv()

        def end(self):
            if self.backward:
                self.first.wait_send()
            self.last.wait_send()
            left(self.e, lambda k: self.snd.at[k])
            left(self.e + 1, lambda k: self.ret.at[k])

    ahead, aback = Carry(0, False, inc), Carry(1, True, inc2)
    decays = to_sibling(4, decay.at[0:8], decay.at[8:16])

    def local_state(j, carry):
        loc[rows128(j), :] = low(dot_tn(low(spread(toward, j) * wide(act[j])), b_in))
        return carry

    loop(given, 12, local_state, 6)
    ahead.swap()
    loop(mine, 12, local_state, 6)
    decays.wait_recv()
    ahead.start()

    row = lax.broadcasted_iota(jnp.int32, (128, 128), 0)
    col = lax.broadcasted_iota(jnp.int32, (128, 128), 1)
    causal = row >= col

    def weights(j):
        out = []
        for k, own in enumerate(pick(cum, j)):
            line = rows_a[pl.ds(2 * j + k, 1), :]
            first, second = own[:128], own[128:]
            out.append((
                jnp.exp(jnp.where(causal, first - line[:, :128], -1e30)),
                jnp.exp(second - line[:, :128]),
                jnp.exp(jnp.where(causal, second - line[:, 128:], -1e30))))
        return out

    places = ((slice(0, 128), slice(0, 128)), (slice(128, 256), slice(0, 128)), (slice(128, 256), slice(128, 256)))

    def mixing(gaps):
        return [[low(scores[r, c] * gap) for (r, c), gap in zip(places, head)] for head in gaps]

    def inside(j, carry):
        m = mixing(weights(j))
        xa, xb = by_head(act[j])
        top = dot(jnp.concatenate([m[0][0], m[1][0]], axis=1), jnp.concatenate([xa[:128], xb[:128]], axis=0))
        low_ = dot(jnp.concatenate([m[0][1], m[0][2], m[1][1], m[1][2]], axis=1), jnp.concatenate([xa, xb], axis=0))
        ys[j, 0:128, :] = top
        ys[j, 128:256, :] = low_
        return carry

    loop(0, TILES // 2, inside, 3)
    ahead.turn()
    loop(TILES // 2, TILES // 2, inside, 3)
    ahead.finish()

    def state(ref, j):
        return ref[pl.ds(pl.multiple_of(128 * j, 128), 128), :]

    def gate(j, y):
        gz = gates[:, cols(j)]
        sig = sigmoid(gz)
        full = y + skip[:, cols(j)] * wide(act[j])
        return gz, sig, full, full * gz * sig

    stat[...] = jnp.zeros((256, 128), f32)
    coef[...] = jnp.zeros((256, 128), f32)

    def gate_sums(j, carry):
        y = ys[j] + spread(ecum, j) * dot_nt(c_out, state(inc, j))
        ys[j] = y
        _, _, _, gated = gate(j, y)
        stat[...] += gated * gated
        coef[...] += gated * (gain[:, cols(j)] * db[:, cols(j)])
        return carry

    loop(0, TILES, gate_sums, 4)
    scale = lax.rsqrt(jnp.sum(stat[...], axis=1, keepdims=True) * (1.0 / DI) + epsilon)
    factor = scale * scale * scale * (jnp.sum(coef[...], axis=1, keepdims=True) * (1.0 / DI))
    stat[...] = jnp.broadcast_to(scale, (256, 128))
    coef[...] = jnp.broadcast_to(factor, (256, 128))
    sums[...] = jnp.zeros((8, CONVC), f32)
    skips[...] = jnp.zeros((128, 128), f32)

    def gate_back(j, carry):
        y = ys[j]
        gz, sig, full, gated = gate(j, y)
        scaled = gated * stat[...]
        branch[:, cols(j)] = low(scaled * gain[:, cols(j)])
        given = db[:, cols(j)]
        sums[5:6, cols(j)] = jnp.sum(scaled * given, axis=0, keepdims=True)
        d_gated = stat[...] * gain[:, cols(j)] * given - gated * coef[...]
        dz[:, cols(j)] = low(d_gated * full * (sig * (1.0 + gz * (1.0 - sig))))
        dy = low(d_gated * gz * sig)
        dys[j] = dy
        dyf = wide(dy)
        skips[pl.ds(j, 1), :] = jnp.sum(dyf * wide(act[j]), axis=0, keepdims=True)
        loc[rows128(j), :] = low(dot_tn(low(spread(ecum, j) * dyf), c_out))
        return carry

    ahead.first.wait_send()
    loop(given, 12, gate_back, 4)
    aback.swap()
    theirs, ours = lanes(1536 * (1 - core), 1536), lanes(1536 * core, 1536)
    shared += [to_sibling(7, branch.at[:, theirs], sib_branch), to_sibling(8, dz.at[:, theirs], sib_dz.at[:, theirs])]
    loop(mine, 12, gate_back, 4)
    shared += [to_sibling(9, dz.at[:, ours], sib_dz.at[:, ours])]
    ahead.end()
    aback.start()
    for copy in shared:
        copy.wait_recv()

    def d_w_gates(k, u):
        zh, part = k // 8, lanes(384 * lax.rem(k, 8), 384)
        total = dot_tn(normed[:, lanes(768 * core + 384 * zh, 384)], dz[:, part])
        total = total + dot_tn(sib_normed[:, lanes(384 * zh, 384)], sib_dz[:, part])
        src_z[zh, :, :, :, :, part] = low(total).reshape(4, 2, 3, 16, 384)

    def d_w_out(k, u):
        q, part = k // 4, lanes(384 * lax.rem(k, 4), 384)
        total = dot_tn(branch[:, lanes(1536 * core + 384 * q, 384)], given_out[:, part])
        total = total + dot_tn(sib_branch[:, lanes(384 * q, 384)], sib_given[:, part])
        src_o[q // 2, pl.ds(2 * lax.rem(q, 2), 2), :, :, :, part] = low(total).reshape(2, 2, 3, 32, 384)

    loop(0, 16, d_w_gates, 1)
    loop(0, 16, d_w_out, 1)
    aback.turn()
    links = Links(rs_send, rs_recv)
    work = Scatter(at, links, [src_z, src_o], (12, 24), (DI, 1536), rest)
    reduce = work.steps()
    next(reduce)

    def fetch(k, slot):
        last_ = k >= 12
        part = jnp.minimum(k, 11)
        a_ = pltpu.make_async_copy(
            w_out.at[pl.ds(pl.multiple_of(1536 * lax.rem(part, 2), 128), 1536), lanes(256 * (part // 2), 256)], chunk.at[slot], chunk_sem.at[slot])
        b_ = pltpu.make_async_copy(w_in.at[:, lanes(256 * jnp.maximum(k - 12, 0), 256)], chunk.at[slot], chunk_sem.at[slot])
        pl.when(jnp.logical_not(last_))(a_.start)
        pl.when(last_)(b_.start)

    def fetched(slot):
        pltpu.make_async_copy(chunk.at[slot], chunk.at[slot], chunk_sem.at[slot]).wait()

    def out_part(n, u):
        part = lanes(256 * n, 256)
        total = wide(hidden[:, part])
        for slot in range(2):
            fetched(slot)
            total = total + dot(branch[:, 1536 * slot:1536 * slot + 1536], chunk[slot])
            fetch(2 * n + slot + 2, slot)
        out[:, part] = low(total)

    def norm_part(n, u):
        for slot in range(2):
            fetched(slot)
            k = 2 * n + slot
            for half in range(2):
                rows_ = slice(768 * half, 768 * half + 768)
                d_norm[:, rows_] += dot_nt(dz[:, lanes(256 * k, 256)], chunk[slot, rows_, :])

            @pl.when(k + 2 < 12)
            def _():
                fetch(k + 14, slot)

    fetch(jnp.int32(0), 0)
    fetch(jnp.int32(1), 1)
    d_norm[...] = jnp.zeros((256, 1536), f32)
    for ref in (usum, qin, qw):
        ref[...] = jnp.zeros((256, 128), f32)
    dscores[...] = jnp.zeros((256, 256), f32)
    prods[...] = jnp.zeros((128, 128), f32)

    def inside_back(j, carry):
        gaps = weights(j)
        m = mixing(gaps)
        x = act[j]
        dya, dyb = by_head(dys[j])
        for k, dy in enumerate((dya, dyb)):
            near = dot_nt(dy[:128], x[:128])
            far = dot_nt(dy[128:], x)
            part = (near, far[:, :128], far[:, 128:])
            for (r, c), gap, value in zip(places, gaps[k], part):
                dscores[r, c] += gap * value
        top = dot_tn(jnp.concatenate([m[0][0], m[0][1], m[1][0], m[1][1]], axis=0), jnp.concatenate([dya, dyb], axis=0))
        low_ = dot_tn(jnp.concatenate([m[0][2], m[1][2]], axis=0), jnp.concatenate([dya[128:], dyb[128:]], axis=0))
        dx = jnp.concatenate([top, low_], axis=0)
        fold(usum, wide(dys[j]) * ys[j], j)
        ys[j] = dx
        fold(qin, wide(x) * dx, j)
        return carry

    loop(0, TILES // 2, inside_back, 3)
    next(reduce)
    loop(TILES // 2, TILES // 2, inside_back, 3)
    loop(0, 6, out_part, 1)
    loop(0, 6, norm_part, 1)
    next(reduce)
    aback.finish()
    db_in[...] = jnp.zeros((256, 128), f32)
    dc_in[...] = jnp.zeros((256, 128), f32)

    def d_mix(j, u, d_act):
        m = convolved(j, u)
        sig = sigmoid(m)
        d_m = d_act * (sig * (1.0 + m * (1.0 - sig)))
        ys[j] = d_m
        back_out[:, cols(j)] = low(d_m[0:16])

    def carry_back(j, u):
        s_in, d_s = state(inc, j), state(inc2, j)
        x, dyf = wide(act[j]), wide(dys[j])
        w = spread(toward, j)
        d_w = w * dot_nt(b_in, d_s)
        fold(qw, x * d_w, j)
        db_in[...] += dot(low(w * x), d_s)
        dc_in[...] += dot(low(spread(ecum, j) * dyf), s_in)
        pair = wide(s_in) * wide(d_s)
        prods[pl.ds(2 * j, 1), :] = jnp.sum(pair[:64], axis=0, keepdims=True)
        prods[pl.ds(2 * j + 1, 1), :] = jnp.sum(pair[64:], axis=0, keepdims=True)
        d_mix(j, u, ys[j] + d_w + skip[:, cols(j)] * dyf)

    loop(0, TILES // 2, carry_back, 4)
    next(reduce)
    loop(TILES // 2, TILES // 2, carry_back, 4)
    next(reduce)
    ds = low(dscores[...])
    d_mix(TILES, 0, db_in[...] + dot_tn(ds, c_out))
    d_mix(TILES + 1, 1, dc_in[...] + dot(ds, b_in))
    behind = neighbour(1, back_out, back_in, -1, me > 0)

    q = qin[...] + qw[...]
    d_last = ecum[255:256, :] * jnp.sum(jnp.transpose(prods[...]), axis=0, keepdims=True) + jnp.sum(qw[...], axis=0, keepdims=True)
    at_end = lax.broadcasted_iota(jnp.int32, (256, 128), 0) == 255
    d_l = running_sums(usum[...] - q + jnp.where(at_end, d_last, 0.0), True)
    dt = steps[...]
    raw = dt_in[...] + heads[0:1, :]
    d_raw = (q / jnp.maximum(dt, 1e-30) - heads[1:2, :] * d_l) * sigmoid(raw)
    d_raw = jnp.where(lane < H, d_raw, 0.0)
    headsums[...] = jnp.zeros((8, 128), f32)
    by_pair = jnp.transpose(skips[...])
    headsums[2:3, :] = jnp.sum(by_pair[:64], axis=0, keepdims=True)
    headsums[3:4, :] = jnp.sum(by_pair[64:], axis=0, keepdims=True)
    headsums[0:1, :] = jnp.sum(d_raw, axis=0, keepdims=True)
    headsums[1:2, :] = -jnp.sum(d_l * dt, axis=0, keepdims=True)
    dproj[:, CONVC:CONVC + 128] = low(d_raw)
    dproj[:, CONVC + 128:] = jnp.zeros((256, 128), bf16)
    next(reduce)

    @pl.when(me == 31)
    def _():
        back_in[...] = jnp.zeros((16, CONVC), bf16)

    pl.when(me < 31)(behind.wait_recv)

    def conv_back(j, u):
        d_m = ys[j]
        shift[u, 0:8, :] = wide(halo_in[:, cols(j)])[8:16, :]
        shift[u, 8:264, :] = wide(conv_in[:, cols(j)])
        for k in range(4):
            sums[k:k + 1, cols(j)] = jnp.sum(d_m * shift[u, 5 + k:261 + k, :], axis=0, keepdims=True)
        sums[4:5, cols(j)] = jnp.sum(d_m, axis=0, keepdims=True)
        shift2[u, 0:256, :] = d_m
        shift2[u, 256:264, :] = wide(back_in[:, cols(j)])[0:8, :]
        total = taps[3:4, cols(j)] * d_m
        for k in range(3):
            total = total + taps[k:k + 1, cols(j)] * shift2[u, 3 - k:259 - k, :]
        dproj[:, cols(j)] = low(total)

    loop(0, TILES // 2, conv_back, 2)
    next(reduce)
    loop(TILES // 2, TILES // 2 + 2, conv_back, 2)
    work.finish([g_z, g_o])
    links.finish()
    for copy in shared:
        copy.wait_send()
    pl.when(me < 31)(front.wait_send)
    pl.when(me > 0)(behind.wait_send)
    decays.wait_send()
    aback.end()


def mixer(gates, conv_in, dt_in, normed, hidden, given_out, d_branch, taps, gain, skip, heads, w_in, w_out):
    f32, bf16 = jnp.float32, jnp.bfloat16
    tile, half, late = (256, 128), (16, CONVC), WIDE - DI
    vm = pltpu.VMEM
    dma = pltpu.SemaphoreType.DMA
    scratch = [
        vm((256, DI), bf16), vm((256, DI), bf16), vm((256, 768), bf16), vm((256, 1536), bf16), vm((256, 1536), bf16), vm((256, DI), bf16),
        vm((2, 4, 2, 3, 16, DI), bf16), vm((2, 4, 2, 3, 32, 1536), bf16), vm((2, 1536, 256), bf16), dma((2,)),
        vm((TILES + 2,) + tile, bf16), vm((TILES + 2,) + tile, f32), vm((TILES,) + tile, bf16),
        vm((4, 264, 128), f32), vm((2, 264, 128), f32), vm(half, bf16), vm(half, bf16), vm(half, bf16), vm(half, bf16),
        vm(tile, f32), vm(tile, f32), vm(tile, f32), vm(tile, f32), vm((128, 256), f32), vm((256, 256), f32), vm((256, 256), f32),
        vm(tile, f32), vm(tile, f32), vm(tile, f32), vm((128, 128), f32), vm(tile, f32), vm(tile, f32), vm(tile, f32), vm(tile, f32),
        vm((16, 128), f32), vm((128, 128), f32), vm((3072, 128), bf16), vm((3072, 128), bf16), vm((3072, 128), bf16),
    ]
    scratch += [vm((16, 112, 128), bf16), vm((16, 112, 128), bf16), vm((16, 96, 128), bf16)]
    for _ in range(2):
        scratch += [vm((1536, 128), bf16), vm((1536, 128), bf16)]
    scratch += [dma((10,)), dma((10,)), dma((4, 16)), dma((4, 16)), dma((4,)), dma((108,)), dma((108,))]
    scratch += scatter_scratch((12, 24), (DI, 1536))
    near, far = pl.BlockSpec(memory_space=pltpu.VMEM), pl.BlockSpec(memory_space=pl.ANY)
    return pl.pallas_call(
        mixer_kernel,
        out_shape=[jax.ShapeDtypeStruct((256, 1536), bf16), jax.ShapeDtypeStruct((256, late), bf16),
                   jax.ShapeDtypeStruct((256, 1536), f32), jax.ShapeDtypeStruct((8, CONVC), f32), jax.ShapeDtypeStruct((8, 128), f32),
                   jax.ShapeDtypeStruct((16, DI), f32), jax.ShapeDtypeStruct((24, 1536), f32)],
        in_specs=[near] * 11 + [far] * 2,
        out_specs=[near] * 7,
        scratch_shapes=scratch,
        compiler_params=pltpu.CompilerParams(collective_id=2, has_side_effects=True, vmem_limit_bytes=62 << 20),
        name="mixer",
    )(gates, conv_in, dt_in, normed, hidden, given_out, d_branch, taps, gain, skip, heads, w_in, w_out)


def rms_scale(values, gain):
    return values * lax.rsqrt(jnp.mean(values * values, axis=-1, keepdims=True) + epsilon) * gain


def swap(value):
    return lax.ppermute(value, "c", [(0, 1), (1, 0)])


def my_half(value, core):
    wide = value.shape[1] // 2
    given = swap(lax.dynamic_slice_in_dim(value, (1 - core) * wide, wide, axis=1))
    return jnp.concatenate([lax.dynamic_slice_in_dim(value, core * wide, wide, axis=1), given], axis=0)


def shards(
    hidden,
    cotangent,
    in_w,
    out_w,
    conv_w,
    conv_b,
    norm_gain,
    gate_gain,
    dt_bias,
    decay_rates,
    d_skip,
):
    core = lax.axis_index("c")
    spare = jnp.concatenate([
        jnp.pad(conv_w, ((0, 0), (0, 102))),
        jnp.pad(conv_b, (0, 102))[None],
        jnp.pad(norm_gain, (0, 116))[None],
        jnp.pad(gate_gain, (0, 104))[None],
        jnp.zeros((5, 128), jnp.bfloat16),
    ])
    shard_in = jnp.pad(jnp.concatenate([jnp.pad(in_w, ((0, 0), (0, PARAMS - PROJ))), spare], axis=1), ((0, 4), (0, 0)))
    w_in, w_out = gather([shard_in, jnp.pad(out_w, ((0, 8), (0, 0)))], [12, 24])
    spare = w_in[:, PARAMS:].reshape(128, 12, 128).astype(jnp.float32)
    w_conv_f = spare[:, :4, :26].transpose(1, 0, 2).reshape(KW, CONVC)
    b_conv_f = spare[:, 4, :26].reshape(CONVC)
    gain_norm_f = spare[:, 5, :12].reshape(1536)
    gain_gate_f = spare[:, 6, :24].reshape(DI)
    residual = hidden[0].astype(jnp.float32)
    length = residual.shape[0]
    normed = rms_scale(residual, gain_norm_f).astype(jnp.bfloat16)
    gates = jnp.dot(normed, w_in[:, :DI], preferred_element_type=jnp.float32)
    conv_in = jnp.dot(normed, w_in[:, DI : DI + CONVC], preferred_element_type=jnp.float32).astype(jnp.bfloat16)
    dt_in = jnp.dot(normed, w_in[:, DI + CONVC : PARAMS], preferred_element_type=jnp.float32)
    grad_out = cotangent[0]
    d_branch = jnp.einsum("td,kd->tk", grad_out, w_out, preferred_element_type=jnp.float32)
    taps = jnp.pad(jnp.concatenate([w_conv_f, b_conv_f[None]]), ((0, 3), (0, 0)))
    heads = jnp.pad(jnp.stack([dt_bias, decay_rates]), ((0, 6), (0, 80)))
    result, d_late, d_normed, sums, head_sums, g_gates, g_out = mixer(
        gates, conv_in, dt_in, normed, hidden[0], grad_out, d_branch, taps, gain_gate_f[None],
        jnp.repeat(d_skip, P_SIZE)[None], heads, w_in, w_out)
    d_normed = d_normed + jnp.einsum("tj,dj->td", d_late, w_in[:, DI:], preferred_element_type=jnp.float32)
    both_late = jnp.concatenate([d_late, swap(d_late)], axis=0)
    d_w_late = jnp.einsum("td,tj->dj", my_half(normed, core), both_late, preferred_element_type=jnp.float32).astype(jnp.bfloat16)
    norm_pull = jax.vjp(rms_scale, residual, gain_norm_f)[1]
    d_from_norm, d_gain_norm = norm_pull(d_normed)
    d_hidden = grad_out.astype(jnp.float32) + d_from_norm
    g_late, total = scatter([d_w_late], [sums, head_sums, jnp.pad(d_gain_norm[None], ((0, 7), (0, 0)))], [12])
    return (
        result[None],
        d_hidden[None],
        jnp.concatenate([g_gates[:12], g_late[:12, : PROJ - DI]], axis=1),
        g_out,
        total[:4, :26],
        total[4, :26],
        total[6, :12],
        total[5, :24],
        total[8, :H],
        total[9, :H],
        jnp.stack([total[10, :H // 2], total[11, :H // 2]], axis=1).reshape(H),
    )


def solution(mesh):
    grid = Mesh(mesh.devices.reshape(4, 4, 4, 2), ALL)
    tokens = P("z", SEQ, None)
    placed = (
        tokens,
        tokens,
        P(ALL, None),
        P(ALL, None),
        P(None, ALL),
        P(ALL),
        P(ALL),
        P(ALL),
        P(),
        P(),
        P(),
    )
    return jax.shard_map(
        shards,
        mesh=grid,
        in_specs=placed,
        out_specs=(tokens, tokens, P(ALL, None), P(ALL, None), P(None, ALL), P(ALL), P(ALL), P(ALL), P(), P(), P()),
        check_vma=False,
    )
```

```python
import functools
import jax
import jax.numpy as jnp
from jax import lax
from jax.experimental import pallas as pl
from jax.experimental.pallas import tpu as pltpu
from jax.sharding import PartitionSpec as P, Mesh

MESH = pl.DeviceIdType.MESH
ALL = ("z", "y", "x", "c")
ORDERS = (("z", "y", "x"), ("y", "x", "z"), ("x", "z", "y"))
PARTS = range(3)


class Links:
    def __init__(self, send, recv):
        self.send, self.recv, self.used, self.sent = send, recv, 0, []

    def copy(self, src, dst, device):
        k = self.used
        self.used += 1
        made = pltpu.make_async_remote_copy(
            src_ref=src, dst_ref=dst, send_sem=self.send.at[k], recv_sem=self.recv.at[k],
            device_id=device, device_id_type=MESH)
        made.start()
        self.sent.append(made)
        return made

    def finish(self):
        for made in self.sent:
            made.wait_send()


def place():
    return {name: lax.axis_index(name) for name in ALL}


def block(ref, part, core, at, have, half=None):
    z, y, x = at["z"], at["y"], at["x"]
    wide = ref.shape[-1]
    full = slice(None)
    zh, zl = (full, full) if "z" in have else (z // 2, lax.rem(z, 2))
    ys = full if "y" in have else y
    first, count = (0, wide) if "x" in have else (x * (wide // 4), wide // 4)
    if half is not None:
        if "y" in have:
            ys = pl.ds(2 * half, 2)
        elif "z" in have:
            zh = pl.ds(half, 1)
        else:
            near = -(-count // 256) * 128
            first, count = (first, near) if half == 0 else (first + near, count - near)
    cols = full if "x" in have and count == wide else pl.ds(first if isinstance(first, int) else pl.multiple_of(first, 128), count)
    return ref.at[core, zh, ys, zl, part, :, cols]


def moved(at, axis, steps):
    return {**at, axis: lax.rem(at[axis] + steps + 4, 4)}


def targets(at):
    z, x, c = at["z"], at["x"], at["c"]
    to_z, to_c = 2 * lax.rem(z, 2) + x // 2, z // 2
    return to_z, to_c, 2 * c + z // 2, jnp.logical_and(to_z == z, to_c == c)


class Ring:
    def __init__(self, links, at, full, phase, share):
        self.links, self.at, self.full, self.phase, self.share = links, at, full, phase, share
        self.c = at["c"]
        self.shared = []

    def to_sibling(self, ref):
        if self.share:
            self.shared.append(self.links.copy(ref, ref, {"c": 1 - self.c}))

    def start(self):
        self.near = {}
        for part in PARTS:
            have, axis = ORDERS[part][:self.phase], ORDERS[part][self.phase]
            mine = block(self.full, part, self.c, self.at, have)
            self.near[part] = [self.links.copy(mine, mine, {axis: moved(self.at, axis, steps)[axis]}) for steps in (1, -1)]

    def turn(self):
        self.far = {}
        for part in PARTS:
            have, axis = ORDERS[part][:self.phase], ORDERS[part][self.phase]
            self.far[part] = []
            for way, steps in ((0, 1), (1, -1)):
                self.near[part][way].wait_recv()
                piece = block(self.full, part, self.c, moved(self.at, axis, -steps), have, way)
                self.far[part].append(self.links.copy(piece, piece, {axis: moved(self.at, axis, steps)[axis]}))
        for part in PARTS:
            have, axis = ORDERS[part][:self.phase], ORDERS[part][self.phase]
            for steps in (1, -1):
                self.to_sibling(block(self.full, part, self.c, moved(self.at, axis, -steps), have))

    def finish(self):
        for part in PARTS:
            have, axis = ORDERS[part][:self.phase], ORDERS[part][self.phase]
            for way in (0, 1):
                self.far[part][way].wait_recv()
            self.to_sibling(block(self.full, part, self.c, moved(self.at, axis, 2), have))

    def share_held(self):
        for part in PARTS:
            self.to_sibling(block(self.full, part, self.c, self.at, ORDERS[part][:self.phase]))

    def end(self):
        for copy in self.shared:
            copy.wait_recv()


def gather_kernel(*refs):
    shards, fulls, refs = refs[:2], refs[2:4], refs[4:]
    stages, stage_o, landed, unit, (send, recv, first_recv, own) = refs[:2], refs[2], refs[3:5], refs[5:7], refs[7:]
    at = place()
    z, y, x, c = (at[name] for name in ALL)
    to_z, to_c, from_z, home = targets(at)
    slot = 2 * lax.rem(x, 2) + c
    barrier = pltpu.get_barrier_semaphore()
    for axis in ("z", "y", "x"):
        for steps in (1, 2, 3):
            pl.semaphore_signal(barrier, inc=1, device_id={axis: moved(at, axis, steps)[axis]}, device_id_type=MESH)
    pl.semaphore_signal(barrier, inc=1, device_id={"c": 1 - c}, device_id_type=MESH)
    for k in range(4):
        sx, sc = 2 * lax.rem(z, 2) + k // 2, k % 2

        @pl.when(jnp.logical_not(jnp.logical_and(home, jnp.logical_and(sx == x, sc == c))))
        def _():
            pl.semaphore_signal(barrier, inc=1, device_id=(from_z, y, sx, jnp.int32(sc)), device_id_type=MESH)
    pl.semaphore_wait(barrier, 14 - home.astype(jnp.int32))

    links = Links(send, recv)
    first = []
    for i in range(2):
        wide = shards[i].shape[1] // 4
        for tx in range(4):
            k = links.used
            links.used += 1
            src = shards[i].at[:, pl.ds(tx * wide, wide)]
            remote = pltpu.make_async_remote_copy(
                src_ref=src, dst_ref=landed[i].at[slot], send_sem=send.at[k], recv_sem=first_recv.at[4 * i + slot],
                device_id=(to_z, y, jnp.int32(tx), to_c), device_id_type=MESH)
            local = pltpu.make_async_copy(src, landed[i].at[slot], first_recv.at[4 * i + slot])
            mine = jnp.logical_and(home, x == tx)
            pl.when(jnp.logical_not(mine))(remote.start)
            pl.when(mine)(local.start)
            first.append((remote, mine))
    kept, direct = [], []
    for i in range(2):
        wide = stages[i].shape[1]
        for k in range(4):
            pltpu.make_async_copy(landed[i].at[k], landed[i].at[k], first_recv.at[4 * i + k]).wait()
            stages[i][pl.ds(12 * k, 12), :] = landed[i][k, :12, :wide].astype(jnp.float32)
            for b in range(2 * i):
                stage_o[pl.ds(24 * k + 12 * b, 12), :] = landed[i][k, :12, wide + 384 * b:wide + 384 * b + 384].astype(jnp.float32)
        for part in PARTS:
            unit[i][part, :, :wide] = stages[i][pl.ds(16 * part, 16), :].astype(jnp.bfloat16)
            for b in range(2 * i):
                unit[i][part, :, wide + 384 * b:wide + 384 * b + 384] = stage_o[pl.ds(32 * part + 16 * b, 16), :].astype(jnp.bfloat16)
        for part in PARTS:
            axis = ORDERS[part][0]
            there = block(fulls[i], part, c, at, ())
            for steps in (1, 3, 2):
                direct.append(links.copy(unit[i].at[part], there, {axis: moved(at, axis, steps)[axis]}))
            copy = pltpu.make_async_copy(unit[i].at[part], there, own.at[3 * i + part])
            copy.start()
            kept.append(copy)
    rings = [Ring(links, at, fulls[i], 1, False) for i in range(2)]
    for i in range(2):
        for copy in direct[9 * i:9 * i + 9]:
            copy.wait_recv()
        for copy in kept[3 * i:3 * i + 3]:
            copy.wait()
        rings[i].start()
    for ring in rings:
        ring.turn()
    last = Ring(links, at, fulls[0], 2, True)
    rings[0].finish()
    last.start()
    last.share_held()
    rings[1].finish()
    other = Ring(links, at, fulls[1], 2, True)
    other.share_held()
    last.turn()
    last.finish()
    last.end()
    other.end()
    links.finish()
    for remote, mine in first:
        pl.when(jnp.logical_not(mine))(remote.wait_send)


def gather(late, early):
    shards = (late, early)
    wides = [s.shape[1] for s in shards]
    vm, dma = pltpu.VMEM, pltpu.SemaphoreType.DMA
    return pl.pallas_call(
        gather_kernel,
        out_shape=[jax.ShapeDtypeStruct((2, 2, 4, 2, 3, 16, w), jnp.bfloat16) for w in wides],
        in_specs=[pl.BlockSpec(memory_space=pltpu.VMEM)] * 2,
        out_specs=[pl.BlockSpec(memory_space=pl.ANY)] * 2,
        scratch_shapes=[vm((48, wides[0] // 4), jnp.float32), vm((48, 768), jnp.float32), vm((96, 384), jnp.float32)]
        + [vm((4, 16, w // 4), jnp.bfloat16) for w in wides]
        + [vm((3, 16, w // 4), jnp.bfloat16) for w in wides]
        + [dma((96,)), dma((96,)), dma((8,)), dma((6,))],
        compiler_params=pltpu.CompilerParams(collective_id=0, has_side_effects=True, vmem_limit_bytes=32 << 20),
        name="gather_weights",
    )(*shards)


def span(shape, axis, at):
    cut = [slice(None)] * 5
    if axis == "y":
        cut[1] = pl.ds(at["y"], 1)
    elif axis == "z":
        cut[0], cut[2] = pl.ds(at["z"] // 2, 1), pl.ds(lax.rem(at["z"], 2), 1)
    else:
        cut[4] = pl.ds(pl.multiple_of(at["x"] * (shape[4] // 4), 128), shape[4] // 4)
    return cut


def without(shape, axis):
    zh, y, zl, rows, wide = shape
    return {"y": (zh, 1, zl, rows, wide), "z": (1, y, 1, rows, wide), "x": (zh, y, zl, rows, wide // 4)}[axis]


def halves(shape):
    if shape[1] == 4:
        return 1, ((0, 2), (2, 2))
    if shape[0] == 2:
        return 0, ((0, 1), (1, 1))
    near = -(-shape[4] // 256) * 128
    return 4, ((0, near), (near, shape[4] - near))


def cut_half(cut, shape, half):
    dim, parts = halves(shape)
    start, size = parts[half]
    cut = list(cut)
    old = cut[dim]
    base = 0 if isinstance(old, slice) else old.start
    cut[dim] = pl.ds(pl.multiple_of(base + start, 128) if dim == 4 and not isinstance(base, int) else base + start, size)
    return cut


def half_shape(shape, half):
    dim, parts = halves(shape)
    return tuple(parts[half][1] if k == dim else size for k, size in enumerate(shape))


def add_up(out, terms, shape):
    na, nb, nc = shape[:3]

    def slab(k, carry):
        a, b, d = k // (nb * nc), lax.rem(k // nc, nb), lax.rem(k, nc)
        total = terms[0](a, b, d).astype(jnp.float32)
        for term in terms[1:]:
            total = total + term(a, b, d).astype(jnp.float32)
        out(a, b, d, total)
        return carry

    lax.fori_loop(0, na * nb * nc, slab, 0)


def start_of(cut):
    return 0 if isinstance(cut, slice) else cut.start


def slab_of(ref, cut, shape):
    z0, y0, l0, _, c0 = (start_of(s) for s in cut)
    lead = ref

    def read(a, b, d):
        return lead[z0 + a, y0 + b, l0 + d, :, pl.ds(c0, shape[4])]

    return read


def slab_to(ref, shape):
    def write(a, b, d, value):
        ref[a, b, d] = value.astype(ref.dtype)

    return write


ALL_CUT = [slice(None)] * 5


def scatter_scratch(wide, split):
    vm, f32 = pltpu.VMEM, jnp.float32
    scratch = []
    size = {part: (2, 4, 2, 16, wide) for part in PARTS}
    for phase in range(3):
        for part in PARTS:
            shape = without(size[part], ORDERS[part][2 - phase])
            scratch += [vm(shape, jnp.bfloat16)] * (3 if phase else 2)
            if phase == 0:
                scratch += [vm(half_shape(shape, way), jnp.bfloat16) for way in (0, 1)]
            if phase < 2:
                scratch += [vm(shape, jnp.bfloat16)]
            size[part] = shape
    first = 768 if split else wide // 4
    scratch += [vm((48, first), f32), vm((96, 384), f32), vm((4, 16, wide // 4), f32), vm((4, 16, wide // 4), f32)]
    return scratch + [pltpu.SemaphoreType.DMA((4,))] * 2


class Scatter:
    def __init__(self, at, links, source, wide, split, refs):
        take = iter(refs)
        self.at, self.links, self.split = at, links, split
        self.near, self.relay, self.acc = {}, {}, {}
        for phase in range(3):
            for s in PARTS:
                self.near[s, phase] = [next(take) for _ in range(3 if phase else 2)]
                self.relay[s] = [next(take), next(take)] if phase == 0 else self.relay[s]
                self.acc[s, phase] = next(take) if phase < 2 else None
        self.fin, self.fin_o, self.staged, self.landed, self.last, self.own = (next(take) for _ in range(6))
        self.size = {s: (2, 4, 2, 16, wide) for s in PARTS}
        self.source = {s: source.at[:, :, :, s] for s in PARTS}

    def add(self, phase, s, axis, shape):
        terms = [slab_of(self.source[s], span(self.size[s], axis, self.at), shape)]
        terms += [slab_of(buf, ALL_CUT, shape) for buf in self.near[s, phase]]
        if phase < 2:
            add_up(slab_to(self.acc[s, phase], shape), terms, shape)
            self.source[s], self.size[s] = self.acc[s, phase], shape
            return
        total = terms[0](0, 0, 0).astype(jnp.float32)
        for term in terms[1:]:
            total = total + term(0, 0, 0).astype(jnp.float32)
        first = self.fin.shape[1]
        self.fin[pl.ds(16 * s, 16), :] = total[:, :first]
        if self.split:
            for b in range(2):
                self.fin_o[pl.ds(32 * s + 16 * b, 16), :] = total[:, first + 384 * b:first + 384 * b + 384]

    def steps(self):
        at, links, size, source = self.at, self.links, self.size, self.source
        sent, lent = {}, {}
        for s in PARTS:
            axis = ORDERS[s][2]
            shape = without(size[s], axis)
            lent[s] = []
            for way, step in ((0, 1), (1, 3)):
                src = source[s].at[tuple(cut_half(span(size[s], axis, moved(at, axis, 2)), shape, way))]
                lent[s].append(links.copy(src, self.relay[s][way], {axis: moved(at, axis, step)[axis]}))
        for s in PARTS:
            axis = ORDERS[s][2]
            shape = without(size[s], axis)
            sent[s] = []
            for way, step in ((0, 1), (1, 3)):
                src = source[s].at[tuple(cut_half(span(size[s], axis, moved(at, axis, step)), shape, 1 - way))]
                dst = self.near[s, 0][way].at[tuple(cut_half(ALL_CUT, shape, 1 - way))]
                sent[s].append(links.copy(src, dst, {axis: moved(at, axis, step)[axis]}))
        yield
        for s in PARTS:
            axis = ORDERS[s][2]
            shape = without(size[s], axis)
            for way, step in ((0, 1), (1, 3)):
                lent[s][way].wait_recv()
                hs = half_shape(shape, way)
                cut = cut_half(span(size[s], axis, moved(at, axis, step)), shape, way)
                buf = self.relay[s][way]
                add_up(slab_to(buf, hs), [slab_of(source[s], cut, hs), slab_of(buf, ALL_CUT, hs)], hs)
                dst = self.near[s, 0][way].at[tuple(cut_half(ALL_CUT, shape, way))]
                sent[s].append(links.copy(buf, dst, {axis: moved(at, axis, step)[axis]}))
        yield
        for phase in (1, 2):
            for s in PARTS:
                for copy in sent[s]:
                    copy.wait_recv()
                axis = ORDERS[s][3 - phase]
                self.add(phase - 1, s, axis, without(size[s], axis))
                axis = ORDERS[s][2 - phase]
                sent[s] = []
                for k in (1, 3, 2):
                    src = source[s].at[tuple(span(size[s], axis, moved(at, axis, k)))]
                    sent[s].append(links.copy(src, self.near[s, phase][k - 1], {axis: moved(at, axis, k)[axis]}))
            yield
        for s in PARTS:
            for copy in sent[s]:
                copy.wait_recv()
            axis = ORDERS[s][0]
            self.add(2, s, axis, without(size[s], axis))
        z, y, x, c = (at[name] for name in ALL)
        _, _, from_z, home = targets(at)
        self.final = []
        first, staged, landed = self.fin.shape[1], self.staged, self.landed
        for k in range(4):
            sx, sc = 2 * lax.rem(z, 2) + k // 2, k % 2
            staged[k] = jnp.zeros(staged.shape[1:], jnp.float32)
            staged[k, :12, :first] = self.fin[pl.ds(12 * k, 12), :]
            for b in range(2 if self.split else 0):
                staged[k, :12, first + 384 * b:first + 384 * b + 384] = self.fin_o[pl.ds(24 * k + 12 * b, 12), :]
            mine = jnp.logical_and(home, jnp.logical_and(sx == x, sc == c))
            remote = pltpu.make_async_remote_copy(
                src_ref=staged.at[k], dst_ref=landed.at[x], send_sem=self.own.at[k], recv_sem=self.last.at[x],
                device_id=(from_z, y, sx, jnp.int32(sc)), device_id_type=MESH)
            local = pltpu.make_async_copy(staged.at[k], landed.at[x], self.last.at[x])
            pl.when(jnp.logical_not(mine))(remote.start)
            pl.when(mine)(local.start)
            self.final.append((remote, mine))
        yield

    def finish(self, out, out_o=None):
        first = self.fin.shape[1]
        for tx in range(4):
            pltpu.make_async_copy(self.landed.at[tx], self.landed.at[tx], self.last.at[tx]).wait()
            out[:, pl.ds(tx * first, first)] = self.landed[tx, :, :first]
            for b in range(2 if self.split else 0):
                out_o[pl.ds(12 * b, 12), pl.ds(tx * 384, 384)] = self.landed[tx, :12, first + 384 * b:first + 384 * b + 384]
        for remote, mine in self.final:
            pl.when(jnp.logical_not(mine))(remote.wait_send)


SMALL = 1792


def scatter_kernel(part_in, sums_in, heads_in, gain_in, out, small_out, core_sum, core_other, rounds_x, rounds_y, rounds_z, whole, send, recv, *refs, wide):
    at = place()
    z, y, x, c = (at[name] for name in ALL)
    to_z, to_c, _, home = targets(at)
    barrier = pltpu.get_barrier_semaphore()
    for axis in ("z", "y", "x"):
        for steps in (1, 2, 3):
            pl.semaphore_signal(barrier, inc=1, device_id={axis: moved(at, axis, steps)[axis]}, device_id_type=MESH)
    pl.semaphore_signal(barrier, inc=1, device_id={"c": 1 - c}, device_id_type=MESH)
    for tx in range(4):
        @pl.when(jnp.logical_not(jnp.logical_and(home, x == tx)))
        def _():
            pl.semaphore_signal(barrier, inc=1, device_id=(to_z, y, jnp.int32(tx), to_c), device_id_type=MESH)
    pl.semaphore_wait(barrier, 14 - home.astype(jnp.int32))

    links = Links(send, recv)
    work = Scatter(at, links, part_in, wide, False, refs)

    def side(core):
        return pl.ds(pl.multiple_of(SMALL * core, 128), SMALL)

    def small_steps():
        whole[...] = jnp.zeros((8, 2 * SMALL), jnp.float32)
        whole[:, :CONVC] = sums_in[...]
        whole[7:8, :1536] = gain_in[...]
        whole[:, CONVC:CONVC + 128] = heads_in[...]
        going = [links.copy(whole.at[:, side(1 - c)], core_sum, {"c": 1 - c})]
        yield
        going[0].wait()
        links.sent.remove(going[0])
        total = core_sum[...] + whole[:, side(c)]
        for axis, held in (("x", rounds_x), ("y", rounds_y), ("z", rounds_z)):
            held[at[axis]] = total
            mine = held.at[at[axis]]
            going = [links.copy(mine, mine, {axis: moved(at, axis, steps)[axis]}) for steps in (1, 3, 2)]
            yield
            for copy in going:
                copy.wait_recv()
            total = held[0]
            for j in range(1, 4):
                total = total + held[j]
        whole[:, side(c)] = total
        going = [links.copy(whole.at[:, side(c)], core_other, {"c": 1 - c})]
        yield
        going[0].wait_recv()
        whole[:, side(1 - c)] = core_other[...]
        yield

    small = small_steps()
    next(small)
    for _ in work.steps():
        next(small)
    index = 32 * z + 8 * y + 2 * x + c
    total = whole[...]
    for first, size, each, row, count, to in ((0, CONVC, 26, 0, 5, 0), (0, DI, 24, 5, 1, 5), (0, 1536, 12, 7, 1, 6)):
        value = pltpu.roll(total[:, first:first + size], lax.rem(size - each * index, size), 1)
        small_out[to:to + count, :] = value[row:row + count, :128]
    small_out[8:16, :] = total[:, CONVC:CONVC + 128]
    work.finish(out)
    links.finish()


def scatter(half_in, sums, head_sums, d_gain):
    wide = half_in.shape[-1]
    vm, f32 = pltpu.VMEM, jnp.float32
    spec = pl.BlockSpec(memory_space=pltpu.VMEM)
    scratch = [vm((8, SMALL), f32)] * 2 + [vm((4, 8, SMALL), f32)] * 3 + [vm((8, 2 * SMALL), f32)]
    return pl.pallas_call(
        functools.partial(scatter_kernel, wide=wide),
        out_shape=[jax.ShapeDtypeStruct((16, wide), f32), jax.ShapeDtypeStruct((16, 128), f32)],
        in_specs=[spec] * 4,
        out_specs=[spec] * 2,
        scratch_shapes=scratch + [pltpu.SemaphoreType.DMA((64,))] * 2 + scatter_scratch(wide, False),
        compiler_params=pltpu.CompilerParams(collective_id=1, has_side_effects=True, vmem_limit_bytes=48 << 20),
        name="scatter_gradients",
    )(half_in.reshape(2, 4, 2, 3, 16, wide), sums, head_sums, d_gain)


H = 48
P_SIZE = 64
KW = 4
DI = 3072
CONVC = 3328
PROJ = 6448
WIDE = 6656
PARAMS = 6528
SEQ = ("y", "x", "c")
epsilon = 1e-05


TILES = 24


def dot(a, b):
    return jnp.dot(a, b, preferred_element_type=jnp.float32)


def dot_nt(a, b):
    return lax.dot_general(a, b, (((1,), (1,)), ((), ())), preferred_element_type=jnp.float32)


def dot_tn(a, b):
    return lax.dot_general(a, b, (((0,), (0,)), ((), ())), preferred_element_type=jnp.float32)


def low(v):
    return v.astype(jnp.bfloat16)


def wide(v):
    return v.astype(jnp.float32)


def split3(v):
    a = low(v)
    b = low(v - wide(a))
    return a, b, low(v - wide(a) - wide(b))


def running_sums(v, backward):
    row = lax.broadcasted_iota(jnp.int32, (256, 256), 0)
    col = lax.broadcasted_iota(jnp.int32, (256, 256), 1)
    ones = low(jnp.where(row <= col if backward else row >= col, 1.0, 0.0))
    return sum(dot(ones, part) for part in split3(v))


def sigmoid(v):
    return 1.0 / (1.0 + jnp.exp(-v))


def loop(first, count, body, unroll):
    def step(k, carry):
        for u in range(unroll):
            body(first + k * unroll + u, u)
        return carry
    lax.fori_loop(0, count // unroll, step, 0)


def mixer_kernel(conv_in, dt_in, normed, hidden, given_out, taps, gain, skip, heads, part_w,
                 out, dproj, d_norm, sums, headsums, g_z, g_o, weights_,
                 gates, db, branch, dz, sib_normed, sib_given, sib_branch, sib_dz, src, chunk, chunk_sem,
                 act, ys, dys, shift, shift2, halo_out, halo_in, back_out, back_in,
                 cum, ecum, toward, steps, rows_a, scores, dscores, usum, qin, qw, prods, stat, coef, db_in, dc_in, decay,
                 skips, loc, inc, inc2, *rest):
    f32, bf16 = jnp.float32, jnp.bfloat16
    snd, rcv, ret = rest[:3]
    ways, (sib_send, sib_recv, a_send, a_recv, h_sem, rs_send, rs_recv), rest = (rest[3:5], rest[5:7]), rest[7:14], rest[14:]
    at = place()
    z, core = lax.axis_index("z"), lax.axis_index("c")
    chip = 4 * lax.axis_index("y") + lax.axis_index("x")
    me = 2 * chip + core
    lane = lax.broadcasted_iota(jnp.int32, (256, 128), 1)
    first_head = lane < 64

    def device(k):
        return (z, k // 8, lax.rem(k // 2, 4), lax.rem(k, 2))

    def same_core(k):
        return (z, k // 4, lax.rem(k, 4), core)

    def others(body):
        def step(k, carry):
            body(lax.rem(chip + k, 16))
            return carry
        lax.fori_loop(1, 16, step, 0)

    barrier = pltpu.get_barrier_semaphore()
    others(lambda k: pl.semaphore_signal(barrier, inc=1, device_id=same_core(k), device_id_type=MESH))
    pl.semaphore_signal(barrier, inc=1, device_id={"c": 1 - core}, device_id_type=MESH)
    beside = jnp.where(core == 1, me + 1, me - 1)
    inner = jnp.logical_and(beside >= 0, beside < 32)

    @pl.when(inner)
    def _():
        pl.semaphore_signal(barrier, inc=1, device_id=device(beside), device_id_type=MESH)

    for steps_ in (1, 2, 3):
        pl.semaphore_signal(barrier, inc=1, device_id={"z": moved(at, "z", steps_)["z"]}, device_id_type=MESH)
    to_z, to_c, _, home = targets(at)
    for tx in range(4):
        @pl.when(jnp.logical_not(jnp.logical_and(home, at["x"] == tx)))
        def _():
            pl.semaphore_signal(barrier, inc=1, device_id=(to_z, at["y"], jnp.int32(tx), to_c), device_id_type=MESH)
    pl.semaphore_wait(barrier, 23 + inner.astype(jnp.int32) - home.astype(jnp.int32))

    def exchange(e, source, target, own):
        def go(k):
            pltpu.make_async_remote_copy(
                src_ref=source(k), dst_ref=target(chip), send_sem=a_send.at[e, k], recv_sem=a_recv.at[e, chip],
                device_id=same_core(k), device_id_type=MESH).start()
        others(go)
        own()

    def arrived(e, target):
        others(lambda k: pltpu.make_async_copy(target(k), target(k), a_recv.at[e, k]).wait())

    def left(e, source):
        others(lambda k: pltpu.make_async_copy(source(k), source(k), a_send.at[e, k]).wait())

    def to_sibling(e, src, dst):
        made = pltpu.make_async_remote_copy(
            src_ref=src, dst_ref=dst, send_sem=sib_send.at[e], recv_sem=sib_recv.at[e],
            device_id={"c": 1 - core}, device_id_type=MESH)
        made.start()
        return made

    def neighbour(k, src, dst, steps_, on):
        made = pltpu.make_async_remote_copy(
            src_ref=src, dst_ref=dst, send_sem=h_sem.at[2 * k], recv_sem=h_sem.at[2 * k + 1],
            device_id=device(lax.rem(me + steps_ + 32, 32)), device_id_type=MESH)
        pl.when(on)(made.start)
        return made

    def lanes(start, size):
        return pl.ds(pl.multiple_of(start, 128), size)

    halo_out[...] = conv_in[240:256, :]
    front = neighbour(0, halo_out, halo_in, 1, me < 31)
    shared = [to_sibling(5, normed.at[:, lanes(768 * (1 - core), 768)], sib_normed), to_sibling(6, given_out, sib_given)]

    links = Links(rs_send, rs_recv)
    ring = Ring(links, at, weights_, 2, True)
    ring.start()

    raw = dt_in[...] + heads[0:1, :]
    dt = jnp.maximum(raw, 0.0) + jnp.log1p(jnp.exp(-jnp.abs(raw)))
    total = running_sums(-heads[1:2, :] * dt, False)
    last = total[255:256, :]
    steps[...] = dt
    cum[...] = total
    ecum[...] = jnp.exp(total)
    toward[...] = jnp.exp(last - total) * dt
    rows_a[...] = jnp.transpose(total - jnp.log(dt))

    @pl.when(me == 0)
    def _():
        halo_in[...] = jnp.zeros((16, CONVC), bf16)

    pl.when(me > 0)(front.wait_recv)

    def cols(j):
        return pl.ds(pl.multiple_of(128 * j, 128), 128)

    def convolved(j, u):
        shift[u, 0:8, :] = wide(halo_in[:, cols(j)])[8:16, :]
        shift[u, 8:264, :] = wide(conv_in[:, cols(j)])
        total = taps[4:5, cols(j)] + taps[0:1, cols(j)] * shift[u, 5:261, :]
        for k in range(1, 4):
            total = total + taps[k:k + 1, cols(j)] * shift[u, 5 + k:261 + k, :]
        return total

    def conv(j, u):
        total = convolved(j, u)
        act[j] = low(total * sigmoid(total))

    loop(0, TILES + 2, conv, 2)
    b_in, c_out = act[TILES], act[TILES + 1]
    scores[...] = dot_nt(c_out, b_in)

    def pick(ref, j):
        turned = pltpu.roll(ref[...], lax.rem(128 - 2 * j, 128), 1)
        return jnp.broadcast_to(turned[:, 0:1], (256, 128)), jnp.broadcast_to(turned[:, 1:2], (256, 128))

    def spread(ref, j):
        one, two = pick(ref, j)
        return jnp.where(first_head, one, two)

    def by_head(v):
        zero = jnp.zeros_like(v)
        return jnp.where(first_head[:v.shape[0]], v, zero), jnp.where(first_head[:v.shape[0]], zero, v)

    def fold(acc, prod, j):
        row = lax.broadcasted_iota(jnp.int32, (256, 128), 0)
        col = lax.broadcasted_iota(jnp.int32, (256, 128), 1)
        pickers = low(jnp.where(lax.rem(row, 128) // 64 + 2 * j == col, 1.0, 0.0))
        top = low(prod)
        both = jnp.concatenate([top, low(prod - wide(top))], axis=1)
        acc[...] += dot(both, pickers)

    def rows128(j):
        return pl.ds(pl.multiple_of(128 * j, 128), 128)

    mine, given = 12 * core, 12 * (1 - core)
    row128 = lax.broadcasted_iota(jnp.int32, (128, 128), 0)
    row16 = lax.broadcasted_iota(jnp.int32, (16, 128), 0)
    decay[0:8, :] = jnp.broadcast_to(last, (8, 128))

    def pair_factor(line, j):
        turned = pltpu.roll(jnp.broadcast_to(line, (8, 128)), lax.rem(128 - 2 * j, 128), 1)
        return jnp.where(row128 < 64, jnp.broadcast_to(turned[0:1, 0:1], (128, 128)), jnp.broadcast_to(turned[0:1, 1:2], (128, 128)))

    head_a = 24 * core + 3 * chip // 2
    edge = jnp.where(lax.rem(chip, 2) == 0, 64, 32)
    row96 = lax.broadcasted_iota(jnp.int32, (96, 128), 0)

    class Carry:
        def __init__(self, way, backward, into):
            self.e, self.backward, self.into = 2 * way, backward, into
            self.sib, self.across = ways[way]
            self.snd, self.rcv, self.ret = snd, rcv, ret

        def swap(self):
            self.first = to_sibling(self.e, loc.at[pl.ds(pl.multiple_of(1536 * (1 - core), 128), 1536)], self.sib)

        def start(self):
            self.first.wait_recv()
            second = core == (0 if self.backward else 1)
            other = decay[8:9, :]
            later = jnp.exp(jnp.where(second, last, other))

            def join(j, carry):
                own, theirs = wide(loc[rows128(mine + j), :]), wide(self.sib[rows128(j), :])
                factor = pair_factor(later, mine + j)
                tile = low(factor * jnp.where(second, theirs, own) + jnp.where(second, own, theirs))
                for g in range(4):
                    q = 4 * j + g
                    self.snd[q // 3, pl.ds(pl.multiple_of(32 * lax.rem(q, 3), 32), 32), :] = tile[32 * g:32 * g + 32]
                return carry

            loop(0, 12, join, 12)
            tail = split3(last + other)
            lines = jnp.zeros((16, 128), f32)
            for k in range(3):
                lines = jnp.where(row16 == k, wide(tail[k]), lines)
            for k in range(16):
                self.snd[k, 96:112, :] = low(lines)

            def own():
                self.rcv[chip] = self.snd[chip]

            exchange(self.e, lambda k: self.snd.at[k], lambda k: self.rcv.at[k], own)

        def turn(self):
            arrived(self.e, lambda k: self.rcv.at[k])
            carry = jnp.zeros((96, 128), f32)
            for k in (range(15, -1, -1) if self.backward else range(16)):
                line = wide(self.rcv[k, 96:112, :])
                line = jnp.exp(line[0:1] + line[1:2] + line[2:3])
                line = pltpu.roll(jnp.broadcast_to(line, (8, 128)), lax.rem(128 - head_a, 128), 1)
                factor = jnp.where(row96 < edge, jnp.broadcast_to(line[0:1, 0:1], (96, 128)), jnp.broadcast_to(line[0:1, 1:2], (96, 128)))
                self.ret[k] = low(carry)
                carry = factor * carry + wide(self.rcv[k, 0:96, :])
            start = pl.multiple_of(1536 * core, 128)

            def place_(k):
                return self.into.at[pl.ds(pl.multiple_of(start + 96 * k, 32), 96)]

            def own():
                self.into[pl.ds(pl.multiple_of(start + 96 * chip, 32), 96), :] = self.ret[chip]

            self.place = place_
            exchange(self.e + 1, lambda k: self.ret.at[k], place_, own)

        def finish(self):
            arrived(self.e + 1, self.place)
            second = core == (0 if self.backward else 1)
            before = jnp.exp(jnp.where(second, decay[8:9, :], last))

            def part(j, carry):
                at_ = rows128(mine + j)
                came = self.into[at_, :]
                passed = low(pair_factor(before, mine + j) * wide(came) + wide(jnp.where(second, self.sib[rows128(j), :], loc[at_, :])))
                self.across[rows128(j), :] = jnp.where(second, came, passed)
                self.into[at_, :] = jnp.where(second, passed, came)
                return carry

            loop(0, 12, part, 12)
            half = pl.ds(pl.multiple_of(1536 * core, 128), 1536)
            self.last = to_sibling(self.e + 1, self.across, self.into.at[half])
            self.last.wait_recv()

        def end(self):
            if self.backward:
                self.first.wait_send()
            self.last.wait_send()
            left(self.e, lambda k: self.snd.at[k])
            left(self.e + 1, lambda k: self.ret.at[k])

    ahead, aback = Carry(0, False, inc), Carry(1, True, inc2)
    decays = to_sibling(4, decay.at[0:8], decay.at[8:16])

    def local_state(j, carry):
        loc[rows128(j), :] = low(dot_tn(low(spread(toward, j) * wide(act[j])), b_in))
        return carry

    loop(given, 12, local_state, 6)
    ahead.swap()
    loop(mine, 12, local_state, 6)
    decays.wait_recv()
    ahead.start()

    row = lax.broadcasted_iota(jnp.int32, (128, 128), 0)
    col = lax.broadcasted_iota(jnp.int32, (128, 128), 1)
    causal = row >= col

    def weights(j):
        out = []
        for k, own in enumerate(pick(cum, j)):
            line = rows_a[pl.ds(2 * j + k, 1), :]
            first, second = own[:128], own[128:]
            out.append((
                jnp.exp(jnp.where(causal, first - line[:, :128], -1e30)),
                jnp.exp(second - line[:, :128]),
                jnp.exp(jnp.where(causal, second - line[:, 128:], -1e30))))
        return out

    places = ((slice(0, 128), slice(0, 128)), (slice(128, 256), slice(0, 128)), (slice(128, 256), slice(128, 256)))

    def mixing(gaps):
        return [[low(scores[r, c] * gap) for (r, c), gap in zip(places, head)] for head in gaps]

    def inside(j, carry):
        m = mixing(weights(j))
        xa, xb = by_head(act[j])
        top = dot(jnp.concatenate([m[0][0], m[1][0]], axis=1), jnp.concatenate([xa[:128], xb[:128]], axis=0))
        low_ = dot(jnp.concatenate([m[0][1], m[0][2], m[1][1], m[1][2]], axis=1), jnp.concatenate([xa, xb], axis=0))
        ys[j, 0:128, :] = top
        ys[j, 128:256, :] = low_
        return carry

    loop(0, TILES // 2, inside, 3)
    ahead.turn()
    ring.turn()
    loop(TILES // 2, TILES // 2, inside, 3)
    ahead.finish()
    ring.finish()
    ring.end()

    def fetch(k, slot):
        first = jnp.minimum(k, 7)
        a_ = pltpu.make_async_copy(
            weights_.at[:, :, :, :, :, :, lanes(1536 * (first // 2) + 384 * lax.rem(first, 2), 384)],
            chunk.at[slot].reshape(2, 2, 4, 2, 3, 16, 384), chunk_sem.at[slot])
        pl.when(k < 8)(a_.start)
        later = jnp.maximum(k - 8, 0)
        for b in range(2):
            b_ = pltpu.make_async_copy(
                weights_.at[later // 4, :, :, :, :, :, lanes(1536 * lax.rem(later, 4) + 768 + 384 * b, 384)],
                chunk.at[slot].reshape(2, 4, 2, 3, 32, 384).at[:, :, :, :, pl.ds(16 * b, 16)], chunk_sem.at[slot])
            pl.when(k >= 8)(b_.start)

    def stream(use):
        def two(n, u):
            for slot in range(2):
                k = 2 * n + slot
                pltpu.make_async_copy(chunk.at[slot], chunk.at[slot], chunk_sem.at[slot]).wait()
                use(k, chunk[slot])

                @pl.when(k + 2 < 16)
                def _():
                    fetch(k + 2, slot)

        fetch(jnp.int32(0), 0)
        fetch(jnp.int32(1), 1)
        loop(0, 8, two, 1)

    db[...] = jnp.zeros((256, DI), f32)

    def before_gate(k, w):
        @pl.when(k < 8)
        def _():
            gates[:, lanes(384 * jnp.minimum(k, 7), 384)] = dot(normed[...], w)

        @pl.when(k >= 8)
        def _():
            later = jnp.maximum(k - 8, 0)
            part = lanes(1536 * (later // 4), 1536)
            db[:, part] += dot_nt(given_out[:, lanes(384 * lax.rem(later, 4), 384)], w)

    stream(before_gate)

    def state(ref, j):
        return ref[pl.ds(pl.multiple_of(128 * j, 128), 128), :]

    def gate(j, y):
        gz = gates[:, cols(j)]
        sig = sigmoid(gz)
        full = y + skip[:, cols(j)] * wide(act[j])
        return gz, sig, full, full * gz * sig

    stat[...] = jnp.zeros((256, 128), f32)
    coef[...] = jnp.zeros((256, 128), f32)

    def gate_sums(j, carry):
        y = ys[j] + spread(ecum, j) * dot_nt(c_out, state(inc, j))
        ys[j] = y
        _, _, _, gated = gate(j, y)
        stat[...] += gated * gated
        coef[...] += gated * (gain[:, cols(j)] * db[:, cols(j)])
        return carry

    loop(0, TILES, gate_sums, 4)
    scale = lax.rsqrt(jnp.sum(stat[...], axis=1, keepdims=True) * (1.0 / DI) + epsilon)
    factor = scale * scale * scale * (jnp.sum(coef[...], axis=1, keepdims=True) * (1.0 / DI))
    stat[...] = jnp.broadcast_to(scale, (256, 128))
    coef[...] = jnp.broadcast_to(factor, (256, 128))
    sums[...] = jnp.zeros((8, CONVC), f32)
    skips[...] = jnp.zeros((128, 128), f32)

    def gate_back(j, carry):
        y = ys[j]
        gz, sig, full, gated = gate(j, y)
        scaled = gated * stat[...]
        branch[:, cols(j)] = low(scaled * gain[:, cols(j)])
        given = db[:, cols(j)]
        sums[5:6, cols(j)] = jnp.sum(scaled * given, axis=0, keepdims=True)
        d_gated = stat[...] * gain[:, cols(j)] * given - gated * coef[...]
        dz[:, cols(j)] = low(d_gated * full * (sig * (1.0 + gz * (1.0 - sig))))
        dy = low(d_gated * gz * sig)
        dys[j] = dy
        dyf = wide(dy)
        skips[pl.ds(j, 1), :] = jnp.sum(dyf * wide(act[j]), axis=0, keepdims=True)
        loc[rows128(j), :] = low(dot_tn(low(spread(ecum, j) * dyf), c_out))
        return carry

    ahead.first.wait_send()
    loop(given, 12, gate_back, 4)
    aback.swap()
    theirs, ours = lanes(1536 * (1 - core), 1536), lanes(1536 * core, 1536)
    shared += [to_sibling(7, branch.at[:, theirs], sib_branch), to_sibling(8, dz.at[:, theirs], sib_dz.at[:, theirs])]
    loop(mine, 12, gate_back, 4)
    shared += [to_sibling(9, dz.at[:, ours], sib_dz.at[:, ours])]
    ahead.end()
    aback.start()
    for copy in shared:
        copy.wait_recv()

    def d_w_gates(k, u):
        zh, n = k // 8, lax.rem(k, 8)
        part = lanes(384 * n, 384)
        total = dot_tn(normed[:, lanes(768 * core + 384 * zh, 384)], dz[:, part])
        total = total + dot_tn(sib_normed[:, lanes(384 * zh, 384)], sib_dz[:, part])
        src[zh, :, :, :, :, lanes(1536 * (n // 2) + 384 * lax.rem(n, 2), 384)] = low(total).reshape(4, 2, 3, 16, 384)

    def d_w_out(k, u):
        q, n = k // 4, lax.rem(k, 4)
        part = lanes(384 * n, 384)
        total = dot_tn(branch[:, lanes(1536 * core + 384 * q, 384)], given_out[:, part])
        total = total + dot_tn(sib_branch[:, lanes(384 * q, 384)], sib_given[:, part])
        total = low(total).reshape(2, 2, 3, 2, 16, 384)
        for b in range(2):
            src[q // 2, pl.ds(2 * lax.rem(q, 2), 2), :, :, :, lanes(1536 * n + 768 + 384 * b, 384)] = total[:, :, :, b]

    loop(0, 16, d_w_gates, 1)
    loop(0, 16, d_w_out, 1)
    aback.turn()
    work = Scatter(at, links, src, 2 * DI, True, rest)
    reduce = work.steps()
    next(reduce)
    d_norm[...] = jnp.zeros((256, 1536), f32)
    out_sum = db

    def after_gate(k, w):
        @pl.when(k < 8)
        def _():
            d_norm[...] += dot_nt(dz[:, lanes(384 * jnp.minimum(k, 7), 384)], w)

        @pl.when(k >= 8)
        def _():
            later = jnp.maximum(k - 8, 0)
            part = lanes(384 * lax.rem(later, 4), 384)
            held = jnp.where(later < 4, wide(hidden[:, part]), out_sum[:, part])
            out_sum[:, part] = held + dot(branch[:, lanes(1536 * (later // 4), 1536)], w)

    for ref in (usum, qin, qw):
        ref[...] = jnp.zeros((256, 128), f32)
    dscores[...] = jnp.zeros((256, 256), f32)
    prods[...] = jnp.zeros((128, 128), f32)

    def inside_back(j, carry):
        gaps = weights(j)
        m = mixing(gaps)
        x = act[j]
        dya, dyb = by_head(dys[j])
        for k, dy in enumerate((dya, dyb)):
            near = dot_nt(dy[:128], x[:128])
            far = dot_nt(dy[128:], x)
            part = (near, far[:, :128], far[:, 128:])
            for (r, c), gap, value in zip(places, gaps[k], part):
                dscores[r, c] += gap * value
        top = dot_tn(jnp.concatenate([m[0][0], m[0][1], m[1][0], m[1][1]], axis=0), jnp.concatenate([dya, dyb], axis=0))
        low_ = dot_tn(jnp.concatenate([m[0][2], m[1][2]], axis=0), jnp.concatenate([dya[128:], dyb[128:]], axis=0))
        dx = jnp.concatenate([top, low_], axis=0)
        fold(usum, wide(dys[j]) * ys[j], j)
        ys[j] = dx
        fold(qin, wide(x) * dx, j)
        return carry

    loop(0, TILES // 2, inside_back, 3)
    next(reduce)
    loop(TILES // 2, TILES // 2, inside_back, 3)
    stream(after_gate)
    out[...] = low(out_sum[:, :1536])
    next(reduce)
    aback.finish()
    db_in[...] = jnp.zeros((256, 128), f32)
    dc_in[...] = jnp.zeros((256, 128), f32)

    def d_mix(j, u, d_act):
        m = convolved(j, u)
        sig = sigmoid(m)
        d_m = d_act * (sig * (1.0 + m * (1.0 - sig)))
        ys[j] = d_m
        back_out[:, cols(j)] = low(d_m[0:16])

    def carry_back(j, u):
        s_in, d_s = state(inc, j), state(inc2, j)
        x, dyf = wide(act[j]), wide(dys[j])
        w = spread(toward, j)
        d_w = w * dot_nt(b_in, d_s)
        fold(qw, x * d_w, j)
        db_in[...] += dot(low(w * x), d_s)
        dc_in[...] += dot(low(spread(ecum, j) * dyf), s_in)
        pair = wide(s_in) * wide(d_s)
        prods[pl.ds(2 * j, 1), :] = jnp.sum(pair[:64], axis=0, keepdims=True)
        prods[pl.ds(2 * j + 1, 1), :] = jnp.sum(pair[64:], axis=0, keepdims=True)
        d_mix(j, u, ys[j] + d_w + skip[:, cols(j)] * dyf)

    loop(0, TILES, carry_back, 4)
    next(reduce)
    ds = low(dscores[...])
    d_mix(TILES, 0, db_in[...] + dot_tn(ds, c_out))
    d_mix(TILES + 1, 1, dc_in[...] + dot(ds, b_in))
    behind = neighbour(1, back_out, back_in, -1, me > 0)

    q = qin[...] + qw[...]
    d_last = ecum[255:256, :] * jnp.sum(jnp.transpose(prods[...]), axis=0, keepdims=True) + jnp.sum(qw[...], axis=0, keepdims=True)
    at_end = lax.broadcasted_iota(jnp.int32, (256, 128), 0) == 255
    d_l = running_sums(usum[...] - q + jnp.where(at_end, d_last, 0.0), True)
    dt = steps[...]
    raw = dt_in[...] + heads[0:1, :]
    d_raw = (q / jnp.maximum(dt, 1e-30) - heads[1:2, :] * d_l) * sigmoid(raw)
    d_raw = jnp.where(lane < H, d_raw, 0.0)
    headsums[...] = jnp.zeros((8, 128), f32)
    by_pair = jnp.transpose(skips[...])
    headsums[2:3, :] = jnp.sum(by_pair[:64], axis=0, keepdims=True)
    headsums[3:4, :] = jnp.sum(by_pair[64:], axis=0, keepdims=True)
    headsums[0:1, :] = jnp.sum(d_raw, axis=0, keepdims=True)
    headsums[1:2, :] = -jnp.sum(d_l * dt, axis=0, keepdims=True)
    dproj[:, CONVC:CONVC + 128] = low(d_raw)
    dproj[:, CONVC + 128:] = jnp.zeros((256, 128), bf16)
    next(reduce)

    @pl.when(me == 31)
    def _():
        back_in[...] = jnp.zeros((16, CONVC), bf16)

    pl.when(me < 31)(behind.wait_recv)

    def conv_back(j, u):
        d_m = ys[j]
        shift[u, 0:8, :] = wide(halo_in[:, cols(j)])[8:16, :]
        shift[u, 8:264, :] = wide(conv_in[:, cols(j)])
        for k in range(4):
            sums[k:k + 1, cols(j)] = jnp.sum(d_m * shift[u, 5 + k:261 + k, :], axis=0, keepdims=True)
        sums[4:5, cols(j)] = jnp.sum(d_m, axis=0, keepdims=True)
        shift2[u, 0:256, :] = d_m
        shift2[u, 256:264, :] = wide(back_in[:, cols(j)])[0:8, :]
        total = taps[3:4, cols(j)] * d_m
        for k in range(3):
            total = total + taps[k:k + 1, cols(j)] * shift2[u, 3 - k:259 - k, :]
        dproj[:, cols(j)] = low(total)

    loop(0, TILES + 2, conv_back, 2)
    work.finish(g_z, g_o)
    links.finish()
    for copy in shared:
        copy.wait_send()
    pl.when(me < 31)(front.wait_send)
    pl.when(me > 0)(behind.wait_send)
    decays.wait_send()
    aback.end()


def mixer(conv_in, dt_in, normed, hidden, given_out, taps, gain, skip, heads, part_w):
    f32, bf16 = jnp.float32, jnp.bfloat16
    tile, half, late = (256, 128), (16, CONVC), WIDE - DI
    vm = pltpu.VMEM
    dma = pltpu.SemaphoreType.DMA
    scratch = [
        vm((256, DI), f32), vm((256, DI), f32),
        vm((256, DI), bf16), vm((256, DI), bf16), vm((256, 768), bf16), vm((256, 1536), bf16), vm((256, 1536), bf16), vm((256, DI), bf16),
        vm((2, 4, 2, 3, 16, 2 * DI), bf16), vm((2, 1536, 384), bf16), dma((2,)),
        vm((TILES + 2,) + tile, bf16), vm((TILES + 2,) + tile, f32), vm((TILES,) + tile, bf16),
        vm((4, 264, 128), f32), vm((2, 264, 128), f32), vm(half, bf16), vm(half, bf16), vm(half, bf16), vm(half, bf16),
        vm(tile, f32), vm(tile, f32), vm(tile, f32), vm(tile, f32), vm((128, 256), f32), vm((256, 256), f32), vm((256, 256), f32),
        vm(tile, f32), vm(tile, f32), vm(tile, f32), vm((128, 128), f32), vm(tile, f32), vm(tile, f32), vm(tile, f32), vm(tile, f32),
        vm((16, 128), f32), vm((128, 128), f32), vm((3072, 128), bf16), vm((3072, 128), bf16), vm((3072, 128), bf16),
    ]
    scratch += [vm((16, 112, 128), bf16), vm((16, 112, 128), bf16), vm((16, 96, 128), bf16)]
    for _ in range(2):
        scratch += [vm((1536, 128), bf16), vm((1536, 128), bf16)]
    scratch += [dma((10,)), dma((10,)), dma((4, 16)), dma((4, 16)), dma((4,)), dma((64,)), dma((64,))]
    scratch += scatter_scratch(2 * DI, True)
    near, far = pl.BlockSpec(memory_space=pltpu.VMEM), pl.BlockSpec(memory_space=pl.ANY)
    return pl.pallas_call(
        mixer_kernel,
        out_shape=[jax.ShapeDtypeStruct((256, 1536), bf16), jax.ShapeDtypeStruct((256, late), bf16),
                   jax.ShapeDtypeStruct((256, 1536), f32), jax.ShapeDtypeStruct((8, CONVC), f32), jax.ShapeDtypeStruct((8, 128), f32),
                   jax.ShapeDtypeStruct((16, DI), f32), jax.ShapeDtypeStruct((24, 1536), f32),
                   jax.ShapeDtypeStruct(part_w.shape, bf16)],
        in_specs=[near] * 9 + [far],
        out_specs=[near] * 7 + [far],
        scratch_shapes=scratch,
        input_output_aliases={9: 7},
        compiler_params=pltpu.CompilerParams(collective_id=2, has_side_effects=True, vmem_limit_bytes=62 << 20),
        name="mixer",
    )(conv_in, dt_in, normed, hidden, given_out, taps, gain, skip, heads, part_w)


def rms_scale(values, gain):
    return values * lax.rsqrt(jnp.mean(values * values, axis=-1, keepdims=True) + epsilon) * gain


def swap(value):
    return lax.ppermute(value, "c", [(0, 1), (1, 0)])


def my_half(value, core):
    wide = value.shape[1] // 2
    given = swap(lax.dynamic_slice_in_dim(value, (1 - core) * wide, wide, axis=1))
    return jnp.concatenate([lax.dynamic_slice_in_dim(value, core * wide, wide, axis=1), given], axis=0)


def shards(
    hidden,
    cotangent,
    in_w,
    out_w,
    conv_w,
    conv_b,
    norm_gain,
    gate_gain,
    dt_bias,
    decay_rates,
    d_skip,
):
    core = lax.axis_index("c")
    spare = jnp.concatenate([
        jnp.pad(conv_w, ((0, 0), (0, 102))),
        jnp.pad(conv_b, (0, 102))[None],
        jnp.pad(norm_gain, (0, 116))[None],
        jnp.pad(gate_gain, (0, 104))[None],
        jnp.zeros((5, 128), jnp.bfloat16),
    ])
    late = jnp.pad(jnp.concatenate([jnp.pad(in_w[:, DI:], ((0, 0), (0, PARAMS - PROJ))), spare], axis=1), ((0, 4), (0, 0)))
    early = jnp.concatenate([
        in_w[:, :DI].reshape(12, 4, 768), out_w.reshape(2, 12, 4, 384).transpose(1, 2, 0, 3).reshape(12, 4, 768)
    ], axis=2).reshape(12, 2 * DI)
    w_late, w_early = gather(late, jnp.pad(early, ((0, 4), (0, 0))))
    w_late = w_late.reshape(1536, WIDE - DI)
    spare = w_late[:, PARAMS - DI:].reshape(128, 12, 128).astype(jnp.float32)
    w_conv_f = spare[:, :4, :26].transpose(1, 0, 2).reshape(KW, CONVC)
    b_conv_f = spare[:, 4, :26].reshape(CONVC)
    gain_norm_f = spare[:, 5, :12].reshape(1536)
    gain_gate_f = spare[:, 6, :24].reshape(DI)
    residual = hidden[0].astype(jnp.float32)
    length = residual.shape[0]
    normed = rms_scale(residual, gain_norm_f).astype(jnp.bfloat16)
    conv_in = jnp.dot(normed, w_late[:, :CONVC], preferred_element_type=jnp.float32).astype(jnp.bfloat16)
    dt_in = jnp.dot(normed, w_late[:, CONVC : PARAMS - DI], preferred_element_type=jnp.float32)
    grad_out = cotangent[0]
    taps = jnp.pad(jnp.concatenate([w_conv_f, b_conv_f[None]]), ((0, 3), (0, 0)))
    heads = jnp.pad(jnp.stack([dt_bias, decay_rates]), ((0, 6), (0, 80)))
    result, d_late, d_normed, sums, head_sums, g_gates, g_out, _ = mixer(
        conv_in, dt_in, normed, hidden[0], grad_out, taps, gain_gate_f[None],
        jnp.repeat(d_skip, P_SIZE)[None], heads, w_early)
    d_normed = d_normed + jnp.einsum("tj,dj->td", d_late, w_late, preferred_element_type=jnp.float32)
    both_late = jnp.concatenate([d_late, swap(d_late)], axis=0)
    d_w_late = jnp.einsum("td,tj->dj", my_half(normed, core), both_late, preferred_element_type=jnp.float32).astype(jnp.bfloat16)
    norm_pull = jax.vjp(rms_scale, residual, gain_norm_f)[1]
    d_from_norm, d_gain_norm = norm_pull(d_normed)
    d_hidden = grad_out.astype(jnp.float32) + d_from_norm
    g_late, total = scatter(d_w_late, sums, head_sums, d_gain_norm[None])
    return (
        result[None],
        d_hidden[None],
        jnp.concatenate([g_gates[:12], g_late[:12, : PROJ - DI]], axis=1),
        g_out,
        total[:4, :26],
        total[4, :26],
        total[6, :12],
        total[5, :24],
        total[8, :H],
        total[9, :H],
        jnp.stack([total[10, :H // 2], total[11, :H // 2]], axis=1).reshape(H),
    )


def solution(mesh):
    grid = Mesh(mesh.devices.reshape(4, 4, 4, 2), ALL)
    tokens = P("z", SEQ, None)
    placed = (
        tokens,
        tokens,
        P(ALL, None),
        P(ALL, None),
        P(None, ALL),
        P(ALL),
        P(ALL),
        P(ALL),
        P(),
        P(),
        P(),
    )
    return jax.shard_map(
        shards,
        mesh=grid,
        in_specs=placed,
        out_specs=(tokens, tokens, P(ALL, None), P(ALL, None), P(None, ALL), P(ALL), P(ALL), P(ALL), P(), P(), P()),
        check_vma=False,
    )
```

```python
import functools
import jax
import jax.numpy as jnp
from jax import lax
from jax.experimental import pallas as pl
from jax.experimental.pallas import tpu as pltpu
from jax.sharding import PartitionSpec as P, Mesh

MESH = pl.DeviceIdType.MESH
ALL = ("z", "y", "x", "c")
ORDERS = (("z", "y", "x"), ("y", "x", "z"), ("x", "z", "y"))
PARTS = range(3)


class Links:
    def __init__(self, send, recv):
        self.send, self.recv, self.used, self.sent = send, recv, 0, []

    def copy(self, src, dst, device):
        k = self.used
        self.used += 1
        made = pltpu.make_async_remote_copy(
            src_ref=src, dst_ref=dst, send_sem=self.send.at[k], recv_sem=self.recv.at[k],
            device_id=device, device_id_type=MESH)
        made.start()
        self.sent.append(made)
        return made

    def settle(self):
        for made in self.sent:
            made.wait_send()
        self.sent = []

    finish = settle


def place():
    return {name: lax.axis_index(name) for name in ALL}


def block(ref, part, core, at, have, half=None):
    z, y, x = at["z"], at["y"], at["x"]
    wide = ref.shape[-1]
    full = slice(None)
    zh, zl = (full, full) if "z" in have else (z // 2, lax.rem(z, 2))
    ys = full if "y" in have else y
    first, count = (0, wide) if "x" in have else (x * (wide // 4), wide // 4)
    if half is not None:
        if "y" in have:
            ys = pl.ds(2 * half, 2)
        elif "z" in have:
            zh = pl.ds(half, 1)
        else:
            near = -(-count // 256) * 128
            first, count = (first, near) if half == 0 else (first + near, count - near)
    cols = full if "x" in have and count == wide else pl.ds(first if isinstance(first, int) else pl.multiple_of(first, 128), count)
    return ref.at[core, zh, ys, zl, part, :, cols]


def moved(at, axis, steps):
    return {**at, axis: lax.rem(at[axis] + steps + 4, 4)}


def targets(at):
    z, x, c = at["z"], at["x"], at["c"]
    to_z, to_c = 2 * lax.rem(z, 2) + x // 2, z // 2
    return to_z, to_c, 2 * c + z // 2, jnp.logical_and(to_z == z, to_c == c)


class Ring:
    def __init__(self, links, at, full, phase, share):
        self.links, self.at, self.full, self.phase, self.share = links, at, full, phase, share
        self.c = at["c"]
        self.shared = []

    def to_sibling(self, ref):
        if self.share:
            self.shared.append(self.links.copy(ref, ref, {"c": 1 - self.c}))

    def start(self):
        self.near = {}
        for part in PARTS:
            have, axis = ORDERS[part][:self.phase], ORDERS[part][self.phase]
            mine = block(self.full, part, self.c, self.at, have)
            self.near[part] = [self.links.copy(mine, mine, {axis: moved(self.at, axis, steps)[axis]}) for steps in (1, -1)]

    def turn(self):
        self.far = {}
        for part in PARTS:
            have, axis = ORDERS[part][:self.phase], ORDERS[part][self.phase]
            self.far[part] = []
            for way, steps in ((0, 1), (1, -1)):
                self.near[part][way].wait_recv()
                piece = block(self.full, part, self.c, moved(self.at, axis, -steps), have, way)
                self.far[part].append(self.links.copy(piece, piece, {axis: moved(self.at, axis, steps)[axis]}))
        for part in PARTS:
            have, axis = ORDERS[part][:self.phase], ORDERS[part][self.phase]
            for steps in (1, -1):
                self.to_sibling(block(self.full, part, self.c, moved(self.at, axis, -steps), have))

    def finish(self):
        for part in PARTS:
            have, axis = ORDERS[part][:self.phase], ORDERS[part][self.phase]
            for way in (0, 1):
                self.far[part][way].wait_recv()
            self.to_sibling(block(self.full, part, self.c, moved(self.at, axis, 2), have))

    def share_held(self):
        for part in PARTS:
            self.to_sibling(block(self.full, part, self.c, self.at, ORDERS[part][:self.phase]))

    def end(self):
        for copy in self.shared:
            copy.wait_recv()


def gather_kernel(*refs):
    (in_w, out_w, conv_w, conv_b, norm_gain, gate_gain), fulls, shards, (late, early), refs = refs[:6], refs[6:8], refs[8:10], refs[10:12], refs[12:]
    stages, stage_o, landed, unit, (send, recv, first_recv, own) = refs[:2], refs[2], refs[3:5], refs[5:7], refs[7:]
    at = place()
    z, y, x, c = (at[name] for name in ALL)
    to_z, to_c, from_z, home = targets(at)
    slot = 2 * lax.rem(x, 2) + c
    barrier = pltpu.get_barrier_semaphore()
    for axis in ("z", "y", "x"):
        for steps in (1, 2, 3):
            pl.semaphore_signal(barrier, inc=1, device_id={axis: moved(at, axis, steps)[axis]}, device_id_type=MESH)
    pl.semaphore_signal(barrier, inc=1, device_id={"c": 1 - c}, device_id_type=MESH)
    for k in range(4):
        sx, sc = 2 * lax.rem(z, 2) + k // 2, k % 2

        @pl.when(jnp.logical_not(jnp.logical_and(home, jnp.logical_and(sx == x, sc == c))))
        def _():
            pl.semaphore_signal(barrier, inc=1, device_id=(from_z, y, sx, jnp.int32(sc)), device_id_type=MESH)

    def wide_(ref):
        return ref[...].astype(jnp.float32)

    late[...] = jnp.zeros(late.shape, jnp.float32)
    early[...] = jnp.zeros(early.shape, jnp.float32)
    late[0:12, 0:3376] = in_w[:, 3072:6448].astype(jnp.float32)
    late[0:4, 3456:3482] = wide_(conv_w)
    late[4:5, 3456:3482] = wide_(conv_b)
    late[5:6, 3456:3468] = wide_(norm_gain)
    late[6:7, 3456:3480] = wide_(gate_gain)
    held = wide_(out_w)
    for tx in range(4):
        early[0:12, 1536 * tx:1536 * tx + 768] = in_w[:, 768 * tx:768 * tx + 768].astype(jnp.float32)
        for b in range(2):
            start = 1536 * tx + 768 + 384 * b
            early[0:12, start:start + 384] = held[12 * b:12 * b + 12, 384 * tx:384 * tx + 384]
    shards[0][...] = late[...].astype(jnp.bfloat16)
    shards[1][...] = early[...].astype(jnp.bfloat16)
    pl.semaphore_wait(barrier, 14 - home.astype(jnp.int32))

    links = Links(send, recv)
    first = []
    for i in range(2):
        wide = shards[i].shape[1] // 4
        for tx in range(4):
            k = links.used
            links.used += 1
            src = shards[i].at[:, pl.ds(tx * wide, wide)]
            remote = pltpu.make_async_remote_copy(
                src_ref=src, dst_ref=landed[i].at[slot], send_sem=send.at[k], recv_sem=first_recv.at[4 * i + slot],
                device_id=(to_z, y, jnp.int32(tx), to_c), device_id_type=MESH)
            local = pltpu.make_async_copy(src, landed[i].at[slot], first_recv.at[4 * i + slot])
            mine = jnp.logical_and(home, x == tx)
            pl.when(jnp.logical_not(mine))(remote.start)
            pl.when(mine)(local.start)
            first.append((remote, mine))
    kept, direct = [], []
    for i in range(2):
        wide = stages[i].shape[1]
        for k in range(4):
            pltpu.make_async_copy(landed[i].at[k], landed[i].at[k], first_recv.at[4 * i + k]).wait()
            stages[i][pl.ds(12 * k, 12), :] = landed[i][k, :12, :wide].astype(jnp.float32)
            for b in range(2 * i):
                stage_o[pl.ds(24 * k + 12 * b, 12), :] = landed[i][k, :12, wide + 384 * b:wide + 384 * b + 384].astype(jnp.float32)
        for part in PARTS:
            unit[i][part, :, :wide] = stages[i][pl.ds(16 * part, 16), :].astype(jnp.bfloat16)
            for b in range(2 * i):
                unit[i][part, :, wide + 384 * b:wide + 384 * b + 384] = stage_o[pl.ds(32 * part + 16 * b, 16), :].astype(jnp.bfloat16)
        for part in PARTS:
            axis = ORDERS[part][0]
            there = block(fulls[i], part, c, at, ())
            for steps in (1, 3, 2):
                direct.append(links.copy(unit[i].at[part], there, {axis: moved(at, axis, steps)[axis]}))
            copy = pltpu.make_async_copy(unit[i].at[part], there, own.at[3 * i + part])
            copy.start()
            kept.append(copy)
    rings = [Ring(links, at, fulls[i], 1, False) for i in range(2)]
    for i in range(2):
        for copy in direct[9 * i:9 * i + 9]:
            copy.wait_recv()
        for copy in kept[3 * i:3 * i + 3]:
            copy.wait()
        rings[i].start()
    for ring in rings:
        ring.turn()
    last = Ring(links, at, fulls[0], 2, True)
    rings[0].finish()
    last.start()
    last.share_held()
    rings[1].finish()
    other = Ring(links, at, fulls[1], 2, True)
    other.share_held()
    last.turn()
    last.finish()
    last.end()
    other.end()
    links.finish()
    for remote, mine in first:
        pl.when(jnp.logical_not(mine))(remote.wait_send)


def gather(in_w, out_w, conv_w, conv_b, norm_gain, gate_gain):
    wides = (3584, 6144)
    vm, dma = pltpu.VMEM, pltpu.SemaphoreType.DMA
    return pl.pallas_call(
        gather_kernel,
        out_shape=[jax.ShapeDtypeStruct((2, 2, 4, 2, 3, 16, w), jnp.bfloat16) for w in wides],
        in_specs=[pl.BlockSpec(memory_space=pltpu.VMEM)] * 6,
        out_specs=[pl.BlockSpec(memory_space=pl.ANY)] * 2,
        scratch_shapes=[vm((16, w), jnp.bfloat16) for w in wides] + [vm((16, w), jnp.float32) for w in wides]
        + [vm((48, wides[0] // 4), jnp.float32), vm((48, 768), jnp.float32), vm((96, 384), jnp.float32)]
        + [vm((4, 16, w // 4), jnp.bfloat16) for w in wides]
        + [vm((3, 16, w // 4), jnp.bfloat16) for w in wides]
        + [dma((96,)), dma((96,)), dma((8,)), dma((6,))],
        compiler_params=pltpu.CompilerParams(collective_id=0, has_side_effects=True, vmem_limit_bytes=60 << 20),
        name="gather_weights",
    )(in_w, out_w, conv_w, conv_b[None], norm_gain[None], gate_gain[None])


def span(shape, axis, at):
    cut = [slice(None)] * 5
    if axis == "y":
        cut[1] = pl.ds(at["y"], 1)
    elif axis == "z":
        cut[0], cut[2] = pl.ds(at["z"] // 2, 1), pl.ds(lax.rem(at["z"], 2), 1)
    else:
        cut[4] = pl.ds(pl.multiple_of(at["x"] * (shape[4] // 4), 128), shape[4] // 4)
    return cut


def without(shape, axis):
    zh, y, zl, rows, wide = shape
    return {"y": (zh, 1, zl, rows, wide), "z": (1, y, 1, rows, wide), "x": (zh, y, zl, rows, wide // 4)}[axis]


def halves(shape):
    if shape[1] == 4:
        return 1, ((0, 2), (2, 2))
    if shape[0] == 2:
        return 0, ((0, 1), (1, 1))
    near = -(-shape[4] // 256) * 128
    return 4, ((0, near), (near, shape[4] - near))


def cut_half(cut, shape, half):
    dim, parts = halves(shape)
    start, size = parts[half]
    cut = list(cut)
    old = cut[dim]
    base = 0 if isinstance(old, slice) else old.start
    cut[dim] = pl.ds(pl.multiple_of(base + start, 128) if dim == 4 and not isinstance(base, int) else base + start, size)
    return cut


def half_shape(shape, half):
    dim, parts = halves(shape)
    return tuple(parts[half][1] if k == dim else size for k, size in enumerate(shape))


def add_up(out, terms, shape):
    na, nb, nc = shape[:3]

    def slab(k, carry):
        a, b, d = k // (nb * nc), lax.rem(k // nc, nb), lax.rem(k, nc)
        total = terms[0](a, b, d).astype(jnp.float32)
        for term in terms[1:]:
            total = total + term(a, b, d).astype(jnp.float32)
        out(a, b, d, total)
        return carry

    lax.fori_loop(0, na * nb * nc, slab, 0)


def start_of(cut):
    return 0 if isinstance(cut, slice) else cut.start


def slab_of(ref, cut, shape):
    z0, y0, l0, _, c0 = (start_of(s) for s in cut)
    lead = ref

    def read(a, b, d):
        return lead[z0 + a, y0 + b, l0 + d, :, pl.ds(c0, shape[4])]

    return read


def slab_to(ref, shape):
    def write(a, b, d, value):
        ref[a, b, d] = value.astype(ref.dtype)

    return write


ALL_CUT = [slice(None)] * 5


def scatter_scratch(wide):
    vm, f32 = pltpu.VMEM, jnp.float32
    scratch = []
    size = {part: (2, 4, 2, 16, wide) for part in PARTS}
    for phase in range(3):
        for part in PARTS:
            shape = without(size[part], ORDERS[part][2 - phase])
            scratch += [vm(shape, jnp.bfloat16)] * (3 if phase else 2)
            if phase == 0:
                scratch += [vm(half_shape(shape, way), jnp.bfloat16) for way in (0, 1)]
            size[part] = shape
    return scratch


def last_scratch(wide, first):
    vm, f32 = pltpu.VMEM, jnp.float32
    scratch = [vm((48, first), f32), vm((96, 384) if wide > 4 * first else (8, 128), f32), vm((4, 16, wide // 4), f32), vm((4, 16, wide // 4), f32)]
    return scratch + [pltpu.SemaphoreType.DMA((4,))] * 2


class Scatter:
    def __init__(self, at, links, source, wide, split, refs, last, narrow=None):
        take = iter(refs)
        self.at, self.links, self.split = at, links, split
        self.near, self.relay = {}, {}
        for phase in range(3):
            for s in PARTS:
                self.near[s, phase] = [next(take) for _ in range(3 if phase else 2)]
                self.relay[s] = [next(take), next(take)] if phase == 0 else self.relay[s]
        if narrow:
            def less(ref):
                return ref.at[:, :, :, :, pl.ds(0, ref.shape[4] * wide // narrow)]

            self.near = {key: [less(ref) for ref in held] for key, held in self.near.items()}
            self.relay = {key: [less(ref) for ref in held] for key, held in self.relay.items()}
        self.fin, self.fin_o, self.staged, self.landed, self.last, self.own = last
        self.size = {s: (2, 4, 2, 16, wide) for s in PARTS}
        self.source = {s: source.at[:, :, :, s] for s in PARTS}

    def add(self, phase, s, axis, shape):
        terms = [slab_of(self.source[s], span(self.size[s], axis, self.at), shape)]
        terms += [slab_of(buf, ALL_CUT, shape) for buf in self.near[s, phase]]
        if phase < 2:
            held = self.near[s, phase][0]
            add_up(slab_to(held, shape), terms, shape)
            self.source[s], self.size[s] = held, shape
            return
        total = terms[0](0, 0, 0).astype(jnp.float32)
        for term in terms[1:]:
            total = total + term(0, 0, 0).astype(jnp.float32)
        first = self.fin.shape[1]
        self.fin[pl.ds(16 * s, 16), :] = total[:, :first]
        if self.split:
            for b in range(2):
                self.fin_o[pl.ds(32 * s + 16 * b, 16), :] = total[:, first + 384 * b:first + 384 * b + 384]

    def steps(self):
        at, links, size, source = self.at, self.links, self.size, self.source
        sent, lent = {}, {}
        for s in PARTS:
            axis = ORDERS[s][2]
            shape = without(size[s], axis)
            lent[s] = []
            for way, step in ((0, 1), (1, 3)):
                src = source[s].at[tuple(cut_half(span(size[s], axis, moved(at, axis, 2)), shape, way))]
                lent[s].append(links.copy(src, self.relay[s][way], {axis: moved(at, axis, step)[axis]}))
        for s in PARTS:
            axis = ORDERS[s][2]
            shape = without(size[s], axis)
            sent[s] = []
            for way, step in ((0, 1), (1, 3)):
                src = source[s].at[tuple(cut_half(span(size[s], axis, moved(at, axis, step)), shape, 1 - way))]
                dst = self.near[s, 0][way].at[tuple(cut_half(ALL_CUT, shape, 1 - way))]
                sent[s].append(links.copy(src, dst, {axis: moved(at, axis, step)[axis]}))
        yield
        for s in PARTS:
            axis = ORDERS[s][2]
            shape = without(size[s], axis)
            for way, step in ((0, 1), (1, 3)):
                lent[s][way].wait_recv()
                hs = half_shape(shape, way)
                cut = cut_half(span(size[s], axis, moved(at, axis, step)), shape, way)
                buf = self.relay[s][way]
                add_up(slab_to(buf, hs), [slab_of(source[s], cut, hs), slab_of(buf, ALL_CUT, hs)], hs)
                dst = self.near[s, 0][way].at[tuple(cut_half(ALL_CUT, shape, way))]
                sent[s].append(links.copy(buf, dst, {axis: moved(at, axis, step)[axis]}))
        yield
        for phase in (1, 2):
            for s in PARTS:
                for copy in sent[s]:
                    copy.wait_recv()
                axis = ORDERS[s][3 - phase]
                self.add(phase - 1, s, axis, without(size[s], axis))
                axis = ORDERS[s][2 - phase]
                sent[s] = []
                for k in (1, 3, 2):
                    src = source[s].at[tuple(span(size[s], axis, moved(at, axis, k)))]
                    sent[s].append(links.copy(src, self.near[s, phase][k - 1], {axis: moved(at, axis, k)[axis]}))
            yield
        for s in PARTS:
            for copy in sent[s]:
                copy.wait_recv()
            axis = ORDERS[s][0]
            self.add(2, s, axis, without(size[s], axis))
        z, y, x, c = (at[name] for name in ALL)
        _, _, from_z, home = targets(at)
        self.final = []
        first, staged, landed = self.fin.shape[1], self.staged, self.landed
        for k in range(4):
            sx, sc = 2 * lax.rem(z, 2) + k // 2, k % 2
            staged[k] = jnp.zeros(staged.shape[1:], jnp.float32)
            staged[k, :12, :first] = self.fin[pl.ds(12 * k, 12), :]
            for b in range(2 if self.split else 0):
                staged[k, :12, first + 384 * b:first + 384 * b + 384] = self.fin_o[pl.ds(24 * k + 12 * b, 12), :]
            mine = jnp.logical_and(home, jnp.logical_and(sx == x, sc == c))
            remote = pltpu.make_async_remote_copy(
                src_ref=staged.at[k], dst_ref=landed.at[x], send_sem=self.own.at[k], recv_sem=self.last.at[x],
                device_id=(from_z, y, sx, jnp.int32(sc)), device_id_type=MESH)
            local = pltpu.make_async_copy(staged.at[k], landed.at[x], self.last.at[x])
            pl.when(jnp.logical_not(mine))(remote.start)
            pl.when(mine)(local.start)
            self.final.append((remote, mine))
        yield

    def finish(self, out, base, limit, out_o=None):
        first = self.fin.shape[1]
        for tx in range(4):
            pltpu.make_async_copy(self.landed.at[tx], self.landed.at[tx], self.last.at[tx]).wait()
            count = min(first, limit - tx * first)
            out[:, base + tx * first:base + tx * first + count] = self.landed[tx, :12, :count]
            for b in range(2 if self.split else 0):
                out_o[pl.ds(12 * b, 12), pl.ds(tx * 384, 384)] = self.landed[tx, :12, first + 384 * b:first + 384 * b + 384]
        for remote, mine in self.final:
            pl.when(jnp.logical_not(mine))(remote.wait_send)


SMALL = 1792


def small_steps(at, links, whole, core_sum, core_other, rounds):
    c = at["c"]

    def side(core):
        return pl.ds(pl.multiple_of(SMALL * core, 128), SMALL)

    going = [links.copy(whole.at[:, side(1 - c)], core_sum, {"c": 1 - c})]
    yield
    going[0].wait_recv()
    total = core_sum[...] + whole[:, side(c)]
    for axis, held in zip(("x", "y", "z"), rounds):
        held[at[axis]] = total
        mine = held.at[at[axis]]
        going = [links.copy(mine, mine, {axis: moved(at, axis, steps)[axis]}) for steps in (1, 3, 2)]
        yield
        for copy in going:
            copy.wait_recv()
        total = held[0]
        for j in range(1, 4):
            total = total + held[j]
    whole[:, side(c)] = total
    going = [links.copy(whole.at[:, side(c)], core_other, {"c": 1 - c})]
    yield
    going[0].wait_recv()
    links.settle()
    whole[:, side(1 - c)] = core_other[...]
    yield


def own_slices(at, whole, d_taps, d_bias, d_norm_gain, d_gate_gain, d_dt_bias, d_rates, d_skip):
    index = 32 * at["z"] + 8 * at["y"] + 2 * at["x"] + at["c"]
    total = whole[...]

    def own(size, each):
        return pltpu.roll(total[:, :size], lax.rem(size - each * index, size), 1)

    value = own(CONVC, 26)
    d_taps[...] = value[0:4, :26]
    d_bias[...] = value[4:5, :26]
    d_gate_gain[...] = own(DI, 24)[5:6, :24]
    d_norm_gain[...] = own(1536, 12)[7:8, :12]
    by_head = total[:, CONVC:CONVC + 128]
    d_dt_bias[...] = by_head[0:1, :48]
    d_rates[...] = by_head[1:2, :48]
    row = lax.broadcasted_iota(jnp.int32, (128, 128), 0)
    col = lax.broadcasted_iota(jnp.int32, (128, 128), 1)
    heads = jnp.zeros((8, 128), jnp.float32)
    for b in range(2):
        ones = jnp.where(2 * row + b == col, 1.0, 0.0).astype(jnp.bfloat16)
        for part in split3(jnp.broadcast_to(by_head[2 + b:3 + b], (8, 128))):
            heads = heads + jnp.dot(part, ones, preferred_element_type=jnp.float32)
    d_skip[...] = heads[0:1, :48]


H = 48
P_SIZE = 64
KW = 4
DI = 3072
CONVC = 3328
PROJ = 6448
WIDE = 6656
PARAMS = 6528
SEQ = ("y", "x", "c")
epsilon = 1e-05


TILES = 24
BUFFERS = 3


def dot(a, b):
    return jnp.dot(a, b, preferred_element_type=jnp.float32)


def dot_nt(a, b):
    return lax.dot_general(a, b, (((1,), (1,)), ((), ())), preferred_element_type=jnp.float32)


def dot_tn(a, b):
    return lax.dot_general(a, b, (((0,), (0,)), ((), ())), preferred_element_type=jnp.float32)


def low(v):
    return v.astype(jnp.bfloat16)


def wide(v):
    return v.astype(jnp.float32)


def split3(v):
    a = low(v)
    b = low(v - wide(a))
    return a, b, low(v - wide(a) - wide(b))


def running_sums(v, backward):
    row = lax.broadcasted_iota(jnp.int32, (256, 256), 0)
    col = lax.broadcasted_iota(jnp.int32, (256, 256), 1)
    ones = low(jnp.where(row <= col if backward else row >= col, 1.0, 0.0))
    return sum(dot(ones, part) for part in split3(v))


def sigmoid(v):
    return 1.0 / (1.0 + jnp.exp(-v))


def loop(first, count, body, unroll):
    def step(k, carry):
        for u in range(unroll):
            body(first + k * unroll + u, u)
        return carry
    lax.fori_loop(0, count // unroll, step, 0)


def mixer_kernel(normed, given_out, taps, gain, norm_gain, dt_bias, rates, d_skip, hidden_in, w_late, part_w,
                 out, d_hidden, g_in, g_o, o_taps, o_bias, o_norm, o_gate, o_dt, o_rates, o_skip, weights_,
                 skip, heads,
                 conv_in, dt_in, dproj, sums, headsums,
                 gates, db, branch, dz, sib_normed, sib_given, sib_branch, sib_dz, src, chunk, chunk_sem, flipped, out_sem, ready,
                 act, ys, dys, shift, shift2, halo_out, halo_in, back_out, back_in,
                 cum, ecum, toward, steps, rows_a, scores, dscores, usum, qin, qw, prods, stat, coef, db_in, dc_in, decay,
                 skips, loc, inc, inc2, *rest):
    f32, bf16 = jnp.float32, jnp.bfloat16
    snd, rcv, ret, sib, across = rest[:5]
    (sib_send, sib_recv, a_send, a_recv, h_sem, rs_send, rs_recv, l_send, l_recv, t_send, t_recv), rest = rest[5:16], rest[16:]
    whole, core_sum, core_other, rounds, last_early, last_late, rest = rest[0], rest[1], rest[2], rest[3:6], rest[6:12], rest[12:18], rest[18:]
    at = place()
    z, core = lax.axis_index("z"), lax.axis_index("c")
    chip = 4 * lax.axis_index("y") + lax.axis_index("x")
    me = 2 * chip + core
    lane = lax.broadcasted_iota(jnp.int32, (256, 128), 1)
    first_head = lane < 64

    def device(k):
        return (z, k // 8, lax.rem(k // 2, 4), lax.rem(k, 2))

    def same_core(k):
        return (z, k // 4, lax.rem(k, 4), core)

    def others(body):
        def step(k, carry):
            body(lax.rem(chip + k, 16))
            return carry
        lax.fori_loop(1, 16, step, 0)

    barrier = pltpu.get_barrier_semaphore()
    others(lambda k: pl.semaphore_signal(barrier, inc=1, device_id=same_core(k), device_id_type=MESH))
    pl.semaphore_signal(barrier, inc=1, device_id={"c": 1 - core}, device_id_type=MESH)
    beside = jnp.where(core == 1, me + 1, me - 1)
    inner = jnp.logical_and(beside >= 0, beside < 32)

    @pl.when(inner)
    def _():
        pl.semaphore_signal(barrier, inc=1, device_id=device(beside), device_id_type=MESH)

    for steps_ in (1, 2, 3):
        pl.semaphore_signal(barrier, inc=1, device_id={"z": moved(at, "z", steps_)["z"]}, device_id_type=MESH)
    to_z, to_c, _, home = targets(at)
    for tx in range(4):
        @pl.when(jnp.logical_not(jnp.logical_and(home, at["x"] == tx)))
        def _():
            pl.semaphore_signal(barrier, inc=1, device_id=(to_z, at["y"], jnp.int32(tx), to_c), device_id_type=MESH)
    pl.semaphore_wait(barrier, 23 + inner.astype(jnp.int32) - home.astype(jnp.int32))

    def exchange(e, source, target, own):
        def go(k):
            pltpu.make_async_remote_copy(
                src_ref=source(k), dst_ref=target(chip), send_sem=a_send.at[e, k], recv_sem=a_recv.at[e, chip],
                device_id=same_core(k), device_id_type=MESH).start()
        others(go)
        own()

    def arrived(e, target):
        others(lambda k: pltpu.make_async_copy(target(k), target(k), a_recv.at[e, k]).wait())

    def left(e, source):
        others(lambda k: pltpu.make_async_copy(source(k), source(k), a_send.at[e, k]).wait())

    def to_sibling(e, src, dst):
        made = pltpu.make_async_remote_copy(
            src_ref=src, dst_ref=dst, send_sem=sib_send.at[e], recv_sem=sib_recv.at[e],
            device_id={"c": 1 - core}, device_id_type=MESH)
        made.start()
        return made

    def neighbour(k, src, dst, steps_, on):
        made = pltpu.make_async_remote_copy(
            src_ref=src, dst_ref=dst, send_sem=h_sem.at[2 * k], recv_sem=h_sem.at[2 * k + 1],
            device_id=device(lax.rem(me + steps_ + 32, 32)), device_id_type=MESH)
        pl.when(on)(made.start)
        return made

    def lanes(start, size):
        return pl.ds(pl.multiple_of(start, 128), size)

    links = Links(rs_send, rs_recv)
    ring = Ring(links, at, weights_, 2, True)
    ring.start()

    def from_late(k, slot):
        pltpu.make_async_copy(
            w_late.at[:, :, :, :, :, :, lanes(384 * k, 384)],
            chunk.at[slot].reshape(2, 2, 4, 2, 3, 16, 384), chunk_sem.at[slot]).start()

    def from_gates(k, slot):
        pltpu.make_async_copy(
            weights_.at[:, :, :, :, :, :, lanes(1536 * (k // 2) + 384 * lax.rem(k, 2), 384)],
            chunk.at[slot].reshape(2, 2, 4, 2, 3, 16, 384), chunk_sem.at[slot]).start()

    def from_out(k, slot):
        for b in range(2):
            pltpu.make_async_copy(
                weights_.at[k // 4, :, :, :, :, :, lanes(1536 * lax.rem(k, 4) + 768 + 384 * b, 384)],
                chunk.at[slot].reshape(2, 4, 2, 3, 32, 384).at[:, :, :, :, pl.ds(16 * b, 16)], chunk_sem.at[slot]).start()

    def prefetch(fetch):
        for slot in range(BUFFERS):
            fetch(jnp.int32(slot), slot)

    def stream(fetch, count, use):
        def round_(n, u):
            for slot in range(BUFFERS):
                k = BUFFERS * n + slot

                @pl.when(k < count)
                def _():
                    pltpu.make_async_copy(chunk.at[slot], chunk.at[slot], chunk_sem.at[slot]).wait()
                    use(k, chunk[slot])

                @pl.when(k + BUFFERS < count)
                def _():
                    fetch(k + BUFFERS, slot)

        loop(0, -(-count // BUFFERS), round_, 1)

    prefetch(from_late)

    def project(k, w):
        value = dot(normed[...], w)

        @pl.when(k < 8)
        def _():
            conv_in[:, lanes(384 * jnp.minimum(k, 7), 384)] = low(value)

        @pl.when(k == 8)
        def _():
            conv_in[:, 3072:CONVC] = low(value[:, :256])
            dt_in[...] = value[:, 256:]

    stream(from_late, 9, project)
    halo_out[...] = conv_in[240:256, :]
    front = neighbour(0, halo_out, halo_in, 1, me < 31)
    shared = [to_sibling(5, normed.at[:, lanes(768 * (1 - core), 768)], sib_normed), to_sibling(6, given_out, sib_given)]


    heads[...] = jnp.zeros((8, 128), f32)
    for k, ref in enumerate((dt_bias, rates, d_skip)):
        heads[k:k + 1, :H] = ref[...]
    by_head_ = heads[2:3, :]
    for j in range(TILES):
        skip[:, 128 * j:128 * j + 128] = jnp.where(
            lane[0:1] < 64, jnp.broadcast_to(by_head_[:, 2 * j:2 * j + 1], (1, 128)), jnp.broadcast_to(by_head_[:, 2 * j + 1:2 * j + 2], (1, 128)))

    raw = dt_in[...] + heads[0:1, :]
    dt = jnp.maximum(raw, 0.0) + jnp.log1p(jnp.exp(-jnp.abs(raw)))
    total = running_sums(-heads[1:2, :] * dt, False)
    last = total[255:256, :]
    steps[...] = dt
    cum[...] = total
    ecum[...] = jnp.exp(total)
    toward[...] = jnp.exp(last - total) * dt
    rows_a[...] = jnp.transpose(total - jnp.log(dt))

    @pl.when(me == 0)
    def _():
        halo_in[...] = jnp.zeros((16, CONVC), bf16)

    pl.when(me > 0)(front.wait_recv)

    def cols(j):
        return pl.ds(pl.multiple_of(128 * j, 128), 128)

    def convolved(j, u):
        shift[u, 0:8, :] = wide(halo_in[:, cols(j)])[8:16, :]
        shift[u, 8:264, :] = wide(conv_in[:, cols(j)])
        total = taps[4:5, cols(j)] + taps[0:1, cols(j)] * shift[u, 5:261, :]
        for k in range(1, 4):
            total = total + taps[k:k + 1, cols(j)] * shift[u, 5 + k:261 + k, :]
        return total

    def conv(j, u):
        total = convolved(j, u)
        act[j] = low(total * sigmoid(total))

    loop(0, TILES + 2, conv, 2)
    b_in, c_out = act[TILES], act[TILES + 1]
    scores[...] = dot_nt(c_out, b_in)

    def pick(ref, j):
        turned = pltpu.roll(ref[...], lax.rem(128 - 2 * j, 128), 1)
        return jnp.broadcast_to(turned[:, 0:1], (256, 128)), jnp.broadcast_to(turned[:, 1:2], (256, 128))

    def spread(ref, j):
        one, two = pick(ref, j)
        return jnp.where(first_head, one, two)

    def by_head(v):
        zero = jnp.zeros_like(v)
        return jnp.where(first_head[:v.shape[0]], v, zero), jnp.where(first_head[:v.shape[0]], zero, v)

    def fold(acc, prod, j):
        row = lax.broadcasted_iota(jnp.int32, (256, 128), 0)
        col = lax.broadcasted_iota(jnp.int32, (256, 128), 1)
        pickers = low(jnp.where(lax.rem(row, 128) // 64 + 2 * j == col, 1.0, 0.0))
        top = low(prod)
        both = jnp.concatenate([top, low(prod - wide(top))], axis=1)
        acc[...] += dot(both, pickers)

    def rows128(j):
        return pl.ds(pl.multiple_of(128 * j, 128), 128)

    mine, given = 12 * core, 12 * (1 - core)
    row128 = lax.broadcasted_iota(jnp.int32, (128, 128), 0)
    row16 = lax.broadcasted_iota(jnp.int32, (16, 128), 0)
    decay[0:8, :] = jnp.broadcast_to(last, (8, 128))

    def pair_factor(line, j):
        turned = pltpu.roll(jnp.broadcast_to(line, (8, 128)), lax.rem(128 - 2 * j, 128), 1)
        return jnp.where(row128 < 64, jnp.broadcast_to(turned[0:1, 0:1], (128, 128)), jnp.broadcast_to(turned[0:1, 1:2], (128, 128)))

    head_a = 24 * core + 3 * chip // 2
    edge = jnp.where(lax.rem(chip, 2) == 0, 64, 32)
    row96 = lax.broadcasted_iota(jnp.int32, (96, 128), 0)

    class Carry:
        def __init__(self, way, backward, into):
            self.e, self.backward, self.into = 2 * way, backward, into
            self.sib, self.across = sib, across
            self.snd, self.rcv, self.ret = snd, rcv, ret

        def swap(self):
            self.first = to_sibling(self.e, loc.at[pl.ds(pl.multiple_of(1536 * (1 - core), 128), 1536)], self.sib)

        def start(self):
            self.first.wait_recv()
            second = core == (0 if self.backward else 1)
            other = decay[8:9, :]
            later = jnp.exp(jnp.where(second, last, other))

            def join(j, carry):
                own, theirs = wide(loc[rows128(mine + j), :]), wide(self.sib[rows128(j), :])
                factor = pair_factor(later, mine + j)
                tile = low(factor * jnp.where(second, theirs, own) + jnp.where(second, own, theirs))
                for g in range(4):
                    q = 4 * j + g
                    self.snd[q // 3, pl.ds(pl.multiple_of(32 * lax.rem(q, 3), 32), 32), :] = tile[32 * g:32 * g + 32]
                return carry

            loop(0, 12, join, 12)
            tail = split3(last + other)
            lines = jnp.zeros((16, 128), f32)
            for k in range(3):
                lines = jnp.where(row16 == k, wide(tail[k]), lines)
            for k in range(16):
                self.snd[k, 96:112, :] = low(lines)

            def own():
                self.rcv[chip] = self.snd[chip]

            exchange(self.e, lambda k: self.snd.at[k], lambda k: self.rcv.at[k], own)

        def turn(self):
            arrived(self.e, lambda k: self.rcv.at[k])
            carry = jnp.zeros((96, 128), f32)
            for k in (range(15, -1, -1) if self.backward else range(16)):
                line = wide(self.rcv[k, 96:112, :])
                line = jnp.exp(line[0:1] + line[1:2] + line[2:3])
                line = pltpu.roll(jnp.broadcast_to(line, (8, 128)), lax.rem(128 - head_a, 128), 1)
                factor = jnp.where(row96 < edge, jnp.broadcast_to(line[0:1, 0:1], (96, 128)), jnp.broadcast_to(line[0:1, 1:2], (96, 128)))
                self.ret[k] = low(carry)
                carry = factor * carry + wide(self.rcv[k, 0:96, :])
            start = pl.multiple_of(1536 * core, 128)

            def place_(k):
                return self.into.at[pl.ds(pl.multiple_of(start + 96 * k, 32), 96)]

            def own():
                self.into[pl.ds(pl.multiple_of(start + 96 * chip, 32), 96), :] = self.ret[chip]

            self.place = place_
            exchange(self.e + 1, lambda k: self.ret.at[k], place_, own)

        def finish(self):
            arrived(self.e + 1, self.place)
            second = core == (0 if self.backward else 1)
            before = jnp.exp(jnp.where(second, decay[8:9, :], last))

            def part(j, carry):
                at_ = rows128(mine + j)
                came = self.into[at_, :]
                passed = low(pair_factor(before, mine + j) * wide(came) + wide(jnp.where(second, self.sib[rows128(j), :], loc[at_, :])))
                self.across[rows128(j), :] = jnp.where(second, came, passed)
                self.into[at_, :] = jnp.where(second, passed, came)
                return carry

            loop(0, 12, part, 12)
            half = pl.ds(pl.multiple_of(1536 * core, 128), 1536)
            self.last = to_sibling(self.e + 1, self.across, self.into.at[half])
            self.last.wait_recv()

        def end(self):
            if self.backward:
                self.first.wait_send()
            self.last.wait_send()
            left(self.e, lambda k: self.snd.at[k])
            left(self.e + 1, lambda k: self.ret.at[k])

    ahead, aback = Carry(0, False, inc), Carry(1, True, inc2)
    decays = to_sibling(4, decay.at[0:8], decay.at[8:16])

    def local_state(j, carry):
        loc[rows128(j), :] = low(dot_tn(low(spread(toward, j) * wide(act[j])), b_in))
        return carry

    loop(given, 12, local_state, 6)
    ahead.swap()
    loop(mine, 12, local_state, 6)
    decays.wait_recv()
    ahead.start()

    row = lax.broadcasted_iota(jnp.int32, (128, 128), 0)
    col = lax.broadcasted_iota(jnp.int32, (128, 128), 1)
    causal = row >= col

    def weights(j):
        out = []
        for k, own in enumerate(pick(cum, j)):
            line = rows_a[pl.ds(2 * j + k, 1), :]
            first, second = own[:128], own[128:]
            out.append((
                jnp.exp(jnp.where(causal, first - line[:, :128], -1e30)),
                jnp.exp(second - line[:, :128]),
                jnp.exp(jnp.where(causal, second - line[:, 128:], -1e30))))
        return out

    places = ((slice(0, 128), slice(0, 128)), (slice(128, 256), slice(0, 128)), (slice(128, 256), slice(128, 256)))

    def mixing(gaps):
        return [[low(scores[r, c] * gap) for (r, c), gap in zip(places, head)] for head in gaps]

    def inside(j, carry):
        m = mixing(weights(j))
        xa, xb = by_head(act[j])
        top = dot(jnp.concatenate([m[0][0], m[1][0]], axis=1), jnp.concatenate([xa[:128], xb[:128]], axis=0))
        low_ = dot(jnp.concatenate([m[0][1], m[0][2], m[1][1], m[1][2]], axis=1), jnp.concatenate([xa, xb], axis=0))
        ys[j, 0:128, :] = top
        ys[j, 128:256, :] = low_
        return carry

    loop(0, TILES // 2, inside, 3)
    ahead.turn()
    ring.turn()
    loop(TILES // 2, TILES // 2, inside, 3)
    ahead.finish()
    ring.finish()
    ring.end()

    prefetch(from_gates)
    db[...] = jnp.zeros((256, DI), f32)

    def make_gates(k, w):
        gates[:, lanes(384 * k, 384)] = dot(normed[...], w)

    def make_db(k, w):
        db[:, lanes(1536 * (k // 4), 1536)] += dot_nt(given_out[:, lanes(384 * lax.rem(k, 4), 384)], w)

    stream(from_gates, 8, make_gates)
    prefetch(from_out)
    stream(from_out, 8, make_db)

    def state(ref, j):
        return ref[pl.ds(pl.multiple_of(128 * j, 128), 128), :]

    def gate(j, y):
        gz = gates[:, cols(j)]
        sig = sigmoid(gz)
        full = y + skip[:, cols(j)] * wide(act[j])
        return gz, sig, full, full * gz * sig

    stat[...] = jnp.zeros((256, 128), f32)
    coef[...] = jnp.zeros((256, 128), f32)

    def gate_sums(j, carry):
        y = ys[j] + spread(ecum, j) * dot_nt(c_out, state(inc, j))
        ys[j] = y
        _, _, _, gated = gate(j, y)
        stat[...] += gated * gated
        coef[...] += gated * (gain[:, cols(j)] * db[:, cols(j)])
        return carry

    loop(0, TILES, gate_sums, 4)
    scale = lax.rsqrt(jnp.sum(stat[...], axis=1, keepdims=True) * (1.0 / DI) + epsilon)
    factor = scale * scale * scale * (jnp.sum(coef[...], axis=1, keepdims=True) * (1.0 / DI))
    stat[...] = jnp.broadcast_to(scale, (256, 128))
    coef[...] = jnp.broadcast_to(factor, (256, 128))
    sums[...] = jnp.zeros((8, CONVC), f32)
    skips[...] = jnp.zeros((128, 128), f32)

    def gate_back(j, carry):
        y = ys[j]
        gz, sig, full, gated = gate(j, y)
        scaled = gated * stat[...]
        branch[:, cols(j)] = low(scaled * gain[:, cols(j)])
        given = db[:, cols(j)]
        sums[5:6, cols(j)] = jnp.sum(scaled * given, axis=0, keepdims=True)
        d_gated = stat[...] * gain[:, cols(j)] * given - gated * coef[...]
        dz[:, cols(j)] = low(d_gated * full * (sig * (1.0 + gz * (1.0 - sig))))
        dy = low(d_gated * gz * sig)
        dys[j] = dy
        dyf = wide(dy)
        skips[pl.ds(j, 1), :] = jnp.sum(dyf * wide(act[j]), axis=0, keepdims=True)
        loc[rows128(j), :] = low(dot_tn(low(spread(ecum, j) * dyf), c_out))
        return carry

    ahead.first.wait_send()
    ahead.end()
    loop(given, 12, gate_back, 4)
    aback.swap()
    theirs, ours = lanes(1536 * (1 - core), 1536), lanes(1536 * core, 1536)
    shared += [to_sibling(7, branch.at[:, theirs], sib_branch), to_sibling(8, dz.at[:, theirs], sib_dz.at[:, theirs])]
    loop(mine, 12, gate_back, 4)
    shared += [to_sibling(9, dz.at[:, ours], sib_dz.at[:, ours])]
    aback.start()
    for copy in shared:
        copy.wait_recv()

    def flip(own, theirs):
        flipped[:, :256] = low(jnp.transpose(wide(own)))
        flipped[:, 256:] = low(jnp.transpose(wide(theirs)))

    def flip_normed(zh):
        flip(normed[:, lanes(768 * core + 384 * zh, 384)], sib_normed[:, 384 * zh:384 * zh + 384])

    for zh in range(2):
        flip_normed(zh)

        def d_w_gates(n, u):
            part = lanes(384 * n, 384)
            total = dot(flipped[:, :256], dz[:, part]) + dot(flipped[:, 256:], sib_dz[:, part])
            src[zh, :, :, :, :, lanes(1536 * (n // 2) + 384 * lax.rem(n, 2), 384)] = low(total).reshape(4, 2, 3, 16, 384)

        loop(0, 8, d_w_gates, 2)
    for q in range(4):
        flip(branch[:, lanes(1536 * core + 384 * q, 384)], sib_branch[:, 384 * q:384 * q + 384])

        def d_w_out(n, u):
            part = lanes(384 * n, 384)
            total = dot(flipped[:, :256], given_out[:, part]) + dot(flipped[:, 256:], sib_given[:, part])
            total = low(total).reshape(2, 2, 3, 2, 16, 384)
            for b in range(2):
                src[q // 2, 2 * (q % 2):2 * (q % 2) + 2, :, :, :, lanes(1536 * n + 768 + 384 * b, 384)] = total[:, :, :, b]

        loop(0, 4, d_w_out, 2)
    hidden = sib_given
    hidden_load = pltpu.make_async_copy(hidden_in, hidden, out_sem.at[2])
    hidden_load.start()
    prefetch(from_gates)
    aback.turn()
    work = Scatter(at, links, src, 2 * DI, True, rest, last_early)
    reduce = work.steps()
    next(reduce)
    d_norm = gates
    d_norm[:, :1536] = jnp.zeros((256, 1536), f32)
    out_sum = db

    def norm_gates(k, w):
        d_norm[:, :1536] += dot_nt(dz[:, lanes(384 * k, 384)], w)

    def make_out(k, w):
        part = lanes(384 * lax.rem(k, 4), 384)
        held = jnp.where(k < 4, wide(hidden[:, part]), out_sum[:, part])
        out_sum[:, part] = held + dot(branch[:, lanes(1536 * (k // 4), 1536)], w)

    for ref in (usum, qin, qw):
        ref[...] = jnp.zeros((256, 128), f32)
    dscores[...] = jnp.zeros((256, 256), f32)
    prods[...] = jnp.zeros((128, 128), f32)

    def inside_back(j, carry):
        gaps = weights(j)
        m = mixing(gaps)
        x = act[j]
        dya, dyb = by_head(dys[j])
        for k, dy in enumerate((dya, dyb)):
            near = dot_nt(dy[:128], x[:128])
            far = dot_nt(dy[128:], x)
            part = (near, far[:, :128], far[:, 128:])
            for (r, c), gap, value in zip(places, gaps[k], part):
                dscores[r, c] += gap * value
        top = dot_tn(jnp.concatenate([m[0][0], m[0][1], m[1][0], m[1][1]], axis=0), jnp.concatenate([dya, dyb], axis=0))
        low_ = dot_tn(jnp.concatenate([m[0][2], m[1][2]], axis=0), jnp.concatenate([dya[128:], dyb[128:]], axis=0))
        dx = jnp.concatenate([top, low_], axis=0)
        fold(usum, wide(dys[j]) * ys[j], j)
        ys[j] = dx
        fold(qin, wide(x) * dx, j)
        return carry

    loop(0, TILES // 2, inside_back, 3)
    next(reduce)
    loop(TILES // 2, TILES // 2, inside_back, 3)
    stream(from_gates, 8, norm_gates)
    next(reduce)
    aback.finish()
    db_in[...] = jnp.zeros((256, 128), f32)
    dc_in[...] = jnp.zeros((256, 128), f32)

    def d_mix(j, u, d_act):
        m = convolved(j, u)
        sig = sigmoid(m)
        d_m = d_act * (sig * (1.0 + m * (1.0 - sig)))
        ys[j] = d_m
        back_out[:, cols(j)] = low(d_m[0:16])

    def carry_back(j, u):
        s_in, d_s = state(inc, j), state(inc2, j)
        x, dyf = wide(act[j]), wide(dys[j])
        w = spread(toward, j)
        d_w = w * dot_nt(b_in, d_s)
        fold(qw, x * d_w, j)
        db_in[...] += dot(low(w * x), d_s)
        dc_in[...] += dot(low(spread(ecum, j) * dyf), s_in)
        pair = wide(s_in) * wide(d_s)
        prods[pl.ds(2 * j, 1), :] = jnp.sum(pair[:64], axis=0, keepdims=True)
        prods[pl.ds(2 * j + 1, 1), :] = jnp.sum(pair[64:], axis=0, keepdims=True)
        d_mix(j, u, ys[j] + d_w + skip[:, cols(j)] * dyf)

    loop(0, TILES, carry_back, 3)
    next(reduce)
    ds = low(dscores[...])
    d_mix(TILES, 0, db_in[...] + dot_tn(ds, c_out))
    d_mix(TILES + 1, 1, dc_in[...] + dot(ds, b_in))
    behind = neighbour(1, back_out, back_in, -1, me > 0)

    q = qin[...] + qw[...]
    d_last = ecum[255:256, :] * jnp.sum(jnp.transpose(prods[...]), axis=0, keepdims=True) + jnp.sum(qw[...], axis=0, keepdims=True)
    at_end = lax.broadcasted_iota(jnp.int32, (256, 128), 0) == 255
    d_l = running_sums(usum[...] - q + jnp.where(at_end, d_last, 0.0), True)
    dt = steps[...]
    raw = dt_in[...] + heads[0:1, :]
    d_raw = (q / jnp.maximum(dt, 1e-30) - heads[1:2, :] * d_l) * sigmoid(raw)
    d_raw = jnp.where(lane < H, d_raw, 0.0)
    headsums[...] = jnp.zeros((8, 128), f32)
    by_pair = jnp.transpose(skips[...])
    headsums[2:3, :] = jnp.sum(by_pair[:64], axis=0, keepdims=True)
    headsums[3:4, :] = jnp.sum(by_pair[64:], axis=0, keepdims=True)
    headsums[0:1, :] = jnp.sum(d_raw, axis=0, keepdims=True)
    headsums[1:2, :] = -jnp.sum(d_l * dt, axis=0, keepdims=True)
    dproj[:, CONVC:CONVC + 128] = low(d_raw)
    dproj[:, CONVC + 128:] = jnp.zeros((256, 128), bf16)
    next(reduce)

    @pl.when(me == 31)
    def _():
        back_in[...] = jnp.zeros((16, CONVC), bf16)

    pl.when(me < 31)(behind.wait_recv)

    def conv_back(j, u):
        d_m = ys[j]
        shift[u, 0:8, :] = wide(halo_in[:, cols(j)])[8:16, :]
        shift[u, 8:264, :] = wide(conv_in[:, cols(j)])
        for k in range(4):
            sums[k:k + 1, cols(j)] = jnp.sum(d_m * shift[u, 5 + k:261 + k, :], axis=0, keepdims=True)
        sums[4:5, cols(j)] = jnp.sum(d_m, axis=0, keepdims=True)
        shift2[u, 0:256, :] = d_m
        shift2[u, 256:264, :] = wide(back_in[:, cols(j)])[0:8, :]
        total = taps[3:4, cols(j)] * d_m
        for k in range(3):
            total = total + taps[k:k + 1, cols(j)] * shift2[u, 3 - k:259 - k, :]
        dproj[:, cols(j)] = low(total)

    links.settle()
    for axis in ("z", "y", "x"):
        for steps_ in (1, 2, 3):
            pl.semaphore_signal(ready, inc=1, device_id={axis: moved(at, axis, steps_)[axis]}, device_id_type=MESH)
    loop(0, TILES // 2, conv_back, 2)
    shared += [to_sibling(10, dproj.at[:, :1536], sib_dz.at[:, :1536])]
    loop(TILES // 2, TILES // 2 + 2, conv_back, 2)
    shared += [to_sibling(11, dproj.at[:, 1536:], sib_dz.at[:, 1536:])]
    work.finish(g_in, 0, DI, g_o)
    for copy in shared[-2:]:
        copy.wait_recv()

    prefetch(from_late)
    for zh in range(2):
        flip_normed(zh)

        def d_w_late(n, u):
            part = lanes(384 * n, 384)
            total = dot(flipped[:, :256], dproj[:, part]) + dot(flipped[:, 256:], sib_dz[:, part])
            src[zh, :, :, :, :, part] = low(total).reshape(4, 2, 3, 16, 384)

        loop(0, 9, d_w_late, 3)
    for k in range(2):
        src[k, :, :, :, :, 3456:3584] = jnp.zeros((4, 2, 3, 16, 128), bf16)
    pl.semaphore_wait(ready, 9)
    after = Links(l_send, l_recv)
    width = WIDE - DI
    work = Scatter(at, after, src.at[:, :, :, :, :, pl.ds(0, width)], width, False, rest, last_late, 2 * DI)
    reduce = work.steps()
    next(reduce)

    def norm_late(k, w):
        d_norm[:, :1536] += dot_nt(dproj[:, lanes(384 * k, 384)], w)

    stream(from_late, 9, norm_late)
    prefetch(from_out)

    hidden_load.wait()
    stat[...] = jnp.zeros((256, 128), f32)
    coef[...] = jnp.zeros((256, 128), f32)

    def norm_sums(j, u):
        v = wide(hidden[:, cols(j)])
        stat[...] += v * v
        coef[...] += v * (norm_gain[:, cols(j)] * d_norm[:, cols(j)])

    loop(0, 12, norm_sums, 4)
    scale = lax.rsqrt(jnp.sum(stat[...], axis=1, keepdims=True) * (1.0 / 1536) + epsilon)
    factor = scale * scale * scale * (jnp.sum(coef[...], axis=1, keepdims=True) * (1.0 / 1536))
    stat[...] = jnp.broadcast_to(scale, (256, 128))
    coef[...] = jnp.broadcast_to(factor, (256, 128))

    def norm_back(j, u):
        v, dn = wide(hidden[:, cols(j)]), d_norm[:, cols(j)]
        sums[7:8, cols(j)] = jnp.sum(dn * v * stat[...], axis=0, keepdims=True)
        d_norm[:, cols(j)] = wide(given_out[:, cols(j)]) + stat[...] * norm_gain[:, cols(j)] * dn - v * coef[...]

    loop(0, 12, norm_back, 4)
    hidden_copy = pltpu.make_async_copy(d_norm.at[:, :1536], d_hidden, out_sem.at[1])
    hidden_copy.start()
    whole[:, :CONVC] = sums[...]
    whole[:, CONVC:CONVC + 128] = headsums[...]
    whole[:, CONVC + 128:] = jnp.zeros((8, 128), f32)
    tiny = Links(t_send, t_recv)
    small = small_steps(at, tiny, whole, core_sum, core_other, rounds)
    next(small)
    next(reduce)
    next(small)
    stream(from_out, 8, make_out)
    sib_branch[...] = low(out_sum[:, :1536])
    out_copy = pltpu.make_async_copy(sib_branch, out, out_sem.at[0])
    out_copy.start()
    for _ in reduce:
        next(small)
    next(small)
    own_slices(at, whole, o_taps, o_bias, o_norm, o_gate, o_dt, o_rates, o_skip)
    work.finish(g_in, DI, PROJ - DI)
    after.finish()
    tiny.finish()
    for copy in shared:
        copy.wait_send()
    out_copy.wait()
    hidden_copy.wait()
    pl.when(me < 31)(front.wait_send)
    pl.when(me > 0)(behind.wait_send)
    decays.wait_send()
    aback.end()


def mixer(normed, given_out, taps, gain, norm_gain, dt_bias, rates, d_skip, hidden, w_late, part_w):
    f32, bf16 = jnp.float32, jnp.bfloat16
    tile, half, late = (256, 128), (16, CONVC), WIDE - DI
    vm = pltpu.VMEM
    dma = pltpu.SemaphoreType.DMA
    scratch = [
        vm((1, DI), f32), vm((8, 128), f32),
        vm((256, CONVC), bf16), vm(tile, f32), vm((256, late), bf16), vm((8, CONVC), f32), vm((8, 128), f32),
        vm((256, DI), f32), vm((256, DI), f32),
        vm((256, DI), bf16), vm((256, DI), bf16), vm((256, 768), bf16), vm((256, 1536), bf16), vm((256, 1536), bf16), vm((256, late), bf16),
        vm((2, 4, 2, 3, 16, 2 * DI), bf16), vm((BUFFERS, 1536, 384), bf16), dma((BUFFERS,)), vm((384, 512), bf16), dma((3,)), pltpu.SemaphoreType.REGULAR,
        vm((TILES + 2,) + tile, bf16), vm((TILES + 2,) + tile, f32), vm((TILES,) + tile, bf16),
        vm((3, 264, 128), f32), vm((2, 264, 128), f32), vm(half, bf16), vm(half, bf16), vm(half, bf16), vm(half, bf16),
        vm(tile, f32), vm(tile, f32), vm(tile, f32), vm(tile, f32), vm((128, 256), f32), vm((256, 256), f32), vm((256, 256), f32),
        vm(tile, f32), vm(tile, f32), vm(tile, f32), vm((128, 128), f32), vm(tile, f32), vm(tile, f32), vm(tile, f32), vm(tile, f32),
        vm((16, 128), f32), vm((128, 128), f32), vm((3072, 128), bf16), vm((3072, 128), bf16), vm((3072, 128), bf16),
    ]
    scratch += [vm((16, 112, 128), bf16), vm((16, 112, 128), bf16), vm((16, 96, 128), bf16)]
    scratch += [vm((1536, 128), bf16), vm((1536, 128), bf16)]
    scratch += [dma((12,)), dma((12,)), dma((4, 16)), dma((4, 16)), dma((4,)), dma((64,)), dma((64,)), dma((40,)), dma((40,)), dma((12,)), dma((12,))]
    scratch += [vm((8, 2 * SMALL), f32), vm((8, SMALL), f32), vm((8, SMALL), f32)] + [vm((4, 8, SMALL), f32)] * 3
    scratch += last_scratch(2 * DI, 768) + last_scratch(late, late // 4) + scatter_scratch(2 * DI)
    near, far = pl.BlockSpec(memory_space=pltpu.VMEM), pl.BlockSpec(memory_space=pl.ANY)
    return pl.pallas_call(
        mixer_kernel,
        out_shape=[jax.ShapeDtypeStruct((256, 1536), bf16), jax.ShapeDtypeStruct((256, 1536), f32),
                   jax.ShapeDtypeStruct((12, PROJ), f32), jax.ShapeDtypeStruct((24, 1536), f32)]
        + [jax.ShapeDtypeStruct(size, f32) for size in ((4, 26), (1, 26), (1, 12), (1, 24), (1, H), (1, H), (1, H))]
        + [jax.ShapeDtypeStruct(part_w.shape, bf16)],
        in_specs=[near] * 8 + [far] * 3,
        out_specs=[far] * 2 + [near] * 9 + [far],
        scratch_shapes=scratch,
        input_output_aliases={10: 11},
        compiler_params=pltpu.CompilerParams(collective_id=2, has_side_effects=True, vmem_limit_bytes=63 << 20),
        name="mixer",
    )(normed, given_out, taps, gain, norm_gain, dt_bias, rates, d_skip, hidden, w_late, part_w)


def rms_scale(values, gain):
    return values * lax.rsqrt(jnp.mean(values * values, axis=-1, keepdims=True) + epsilon) * gain


def shards(
    hidden,
    cotangent,
    in_w,
    out_w,
    conv_w,
    conv_b,
    norm_gain,
    gate_gain,
    dt_bias,
    decay_rates,
    d_skip,
):
    w_late, w_early = gather(in_w, out_w, conv_w, conv_b, norm_gain, gate_gain)
    spare = w_late[:, :, :, :, :, :, PARAMS - DI:].reshape(128, 12, 128).astype(jnp.float32)
    w_conv_f = spare[:, :4, :26].transpose(1, 0, 2).reshape(KW, CONVC)
    b_conv_f = spare[:, 4, :26].reshape(CONVC)
    gain_norm_f = spare[:, 5, :12].reshape(1536)
    gain_gate_f = spare[:, 6, :24].reshape(DI)
    residual = hidden[0].astype(jnp.float32)
    normed = rms_scale(residual, gain_norm_f).astype(jnp.bfloat16)
    taps = jnp.pad(jnp.concatenate([w_conv_f, b_conv_f[None]]), ((0, 3), (0, 0)))
    result, d_hidden, g_in, g_out, d_taps, d_bias, d_norm_gain, d_gate_gain, d_dt, d_rates, d_skips, _ = mixer(
        normed, cotangent[0], taps, gain_gate_f[None], gain_norm_f[None],
        dt_bias[None], decay_rates[None], d_skip[None], hidden[0], w_late, w_early)
    return (
        result[None],
        d_hidden[None],
        g_in,
        g_out,
        d_taps,
        d_bias[0],
        d_norm_gain[0],
        d_gate_gain[0],
        d_dt[0],
        d_rates[0],
        d_skips[0],
    )


def solution(mesh):
    grid = Mesh(mesh.devices.reshape(4, 4, 4, 2), ALL)
    tokens = P("z", SEQ, None)
    placed = (
        tokens,
        tokens,
        P(ALL, None),
        P(ALL, None),
        P(None, ALL),
        P(ALL),
        P(ALL),
        P(ALL),
        P(),
        P(),
        P(),
    )
    return jax.shard_map(
        shards,
        mesh=grid,
        in_specs=placed,
        out_specs=(tokens, tokens, P(ALL, None), P(ALL, None), P(None, ALL), P(ALL), P(ALL), P(ALL), P(), P(), P()),
        check_vma=False,
    )
```

```python
import functools
import jax
import jax.numpy as jnp
from jax import lax
from jax.experimental import pallas as pl
from jax.experimental.pallas import tpu as pltpu
from jax.sharding import PartitionSpec as P, Mesh

MESH = pl.DeviceIdType.MESH
ALL = ("z", "y", "x", "c")
ORDERS = (("z", "y", "x"), ("y", "x", "z"), ("x", "z", "y"))
PARTS = range(3)


class Links:
    def __init__(self, send, recv):
        self.send, self.recv, self.used, self.sent = send, recv, 0, []

    def copy(self, src, dst, device):
        k = self.used
        self.used += 1
        made = pltpu.make_async_remote_copy(
            src_ref=src, dst_ref=dst, send_sem=self.send.at[k], recv_sem=self.recv.at[k],
            device_id=device, device_id_type=MESH)
        made.start()
        self.sent.append(made)
        return made

    def settle(self):
        for made in self.sent:
            made.wait_send()
        self.sent = []

    finish = settle


def place():
    return {name: lax.axis_index(name) for name in ALL}


def block(ref, part, core, at, have, half=None):
    z, y, x = at["z"], at["y"], at["x"]
    wide = ref.shape[-1]
    full = slice(None)
    zh, zl = (full, full) if "z" in have else (z // 2, lax.rem(z, 2))
    ys = full if "y" in have else y
    first, count = (0, wide) if "x" in have else (x * (wide // 4), wide // 4)
    if half is not None:
        if "y" in have:
            ys = pl.ds(2 * half, 2)
        elif "z" in have:
            zh = pl.ds(half, 1)
        else:
            near = -(-count // 256) * 128
            first, count = (first, near) if half == 0 else (first + near, count - near)
    cols = full if "x" in have and count == wide else pl.ds(first if isinstance(first, int) else pl.multiple_of(first, 128), count)
    return ref.at[core, zh, ys, zl, part, :, cols]


def moved(at, axis, steps):
    return {**at, axis: lax.rem(at[axis] + steps + 4, 4)}


def targets(at):
    z, x, c = at["z"], at["x"], at["c"]
    to_z, to_c = 2 * lax.rem(z, 2) + x // 2, z // 2
    return to_z, to_c, 2 * c + z // 2, jnp.logical_and(to_z == z, to_c == c)


class Ring:
    def __init__(self, links, at, full, phase, share):
        self.links, self.at, self.full, self.phase, self.share = links, at, full, phase, share
        self.c = at["c"]
        self.shared = []

    def to_sibling(self, ref):
        if self.share:
            self.shared.append(self.links.copy(ref, ref, {"c": 1 - self.c}))

    def start(self):
        self.near = {}
        for part in PARTS:
            have, axis = ORDERS[part][:self.phase], ORDERS[part][self.phase]
            mine = block(self.full, part, self.c, self.at, have)
            self.near[part] = [self.links.copy(mine, mine, {axis: moved(self.at, axis, steps)[axis]}) for steps in (1, -1)]

    def turn(self):
        self.far = {}
        for part in PARTS:
            have, axis = ORDERS[part][:self.phase], ORDERS[part][self.phase]
            self.far[part] = []
            for way, steps in ((0, 1), (1, -1)):
                self.near[part][way].wait_recv()
                piece = block(self.full, part, self.c, moved(self.at, axis, -steps), have, way)
                self.far[part].append(self.links.copy(piece, piece, {axis: moved(self.at, axis, steps)[axis]}))
        for part in PARTS:
            have, axis = ORDERS[part][:self.phase], ORDERS[part][self.phase]
            for steps in (1, -1):
                self.to_sibling(block(self.full, part, self.c, moved(self.at, axis, -steps), have))

    def finish(self):
        for part in PARTS:
            have, axis = ORDERS[part][:self.phase], ORDERS[part][self.phase]
            for way in (0, 1):
                self.far[part][way].wait_recv()
            self.to_sibling(block(self.full, part, self.c, moved(self.at, axis, 2), have))

    def share_held(self):
        for part in PARTS:
            self.to_sibling(block(self.full, part, self.c, self.at, ORDERS[part][:self.phase]))

    def end(self):
        for copy in self.shared:
            copy.wait_recv()


def gather_kernel(*refs):
    (in_w, out_w, conv_w, conv_b, norm_gain, gate_gain), fulls, shards, (late, early), refs = refs[:6], refs[6:8], refs[8:10], refs[10:12], refs[12:]
    stages, stage_o, landed, unit, (send, recv, first_recv, own) = refs[:2], refs[2], refs[3:5], refs[5:7], refs[7:]
    at = place()
    z, y, x, c = (at[name] for name in ALL)
    to_z, to_c, from_z, home = targets(at)
    slot = 2 * lax.rem(x, 2) + c
    barrier = pltpu.get_barrier_semaphore()
    for axis in ("z", "y", "x"):
        for steps in (1, 2, 3):
            pl.semaphore_signal(barrier, inc=1, device_id={axis: moved(at, axis, steps)[axis]}, device_id_type=MESH)
    pl.semaphore_signal(barrier, inc=1, device_id={"c": 1 - c}, device_id_type=MESH)
    for k in range(4):
        sx, sc = 2 * lax.rem(z, 2) + k // 2, k % 2

        @pl.when(jnp.logical_not(jnp.logical_and(home, jnp.logical_and(sx == x, sc == c))))
        def _():
            pl.semaphore_signal(barrier, inc=1, device_id=(from_z, y, sx, jnp.int32(sc)), device_id_type=MESH)

    def wide_(ref):
        return ref[...].astype(jnp.float32)

    late[...] = jnp.zeros(late.shape, jnp.float32)
    early[...] = jnp.zeros(early.shape, jnp.float32)
    late[0:12, 0:3376] = in_w[:, 3072:6448].astype(jnp.float32)
    late[0:4, 3456:3482] = wide_(conv_w)
    late[4:5, 3456:3482] = wide_(conv_b)
    late[5:6, 3456:3468] = wide_(norm_gain)
    late[6:7, 3456:3480] = wide_(gate_gain)
    held = wide_(out_w)
    for tx in range(4):
        early[0:12, 1536 * tx:1536 * tx + 768] = in_w[:, 768 * tx:768 * tx + 768].astype(jnp.float32)
        for b in range(2):
            start = 1536 * tx + 768 + 384 * b
            early[0:12, start:start + 384] = held[12 * b:12 * b + 12, 384 * tx:384 * tx + 384]
    shards[0][...] = late[...].astype(jnp.bfloat16)
    shards[1][...] = early[...].astype(jnp.bfloat16)
    pl.semaphore_wait(barrier, 14 - home.astype(jnp.int32))

    links = Links(send, recv)
    first = []
    for i in range(2):
        wide = shards[i].shape[1] // 4
        for tx in range(4):
            k = links.used
            links.used += 1
            src = shards[i].at[:, pl.ds(tx * wide, wide)]
            remote = pltpu.make_async_remote_copy(
                src_ref=src, dst_ref=landed[i].at[slot], send_sem=send.at[k], recv_sem=first_recv.at[4 * i + slot],
                device_id=(to_z, y, jnp.int32(tx), to_c), device_id_type=MESH)
            local = pltpu.make_async_copy(src, landed[i].at[slot], first_recv.at[4 * i + slot])
            mine = jnp.logical_and(home, x == tx)
            pl.when(jnp.logical_not(mine))(remote.start)
            pl.when(mine)(local.start)
            first.append((remote, mine))
    kept, direct = [], []
    for i in range(2):
        wide = stages[i].shape[1]
        for k in range(4):
            pltpu.make_async_copy(landed[i].at[k], landed[i].at[k], first_recv.at[4 * i + k]).wait()
            stages[i][pl.ds(12 * k, 12), :] = landed[i][k, :12, :wide].astype(jnp.float32)
            for b in range(2 * i):
                stage_o[pl.ds(24 * k + 12 * b, 12), :] = landed[i][k, :12, wide + 384 * b:wide + 384 * b + 384].astype(jnp.float32)
        for part in PARTS:
            unit[i][part, :, :wide] = stages[i][pl.ds(16 * part, 16), :].astype(jnp.bfloat16)
            for b in range(2 * i):
                unit[i][part, :, wide + 384 * b:wide + 384 * b + 384] = stage_o[pl.ds(32 * part + 16 * b, 16), :].astype(jnp.bfloat16)
        for part in PARTS:
            axis = ORDERS[part][0]
            there = block(fulls[i], part, c, at, ())
            for steps in (1, 3, 2):
                direct.append(links.copy(unit[i].at[part], there, {axis: moved(at, axis, steps)[axis]}))
            copy = pltpu.make_async_copy(unit[i].at[part], there, own.at[3 * i + part])
            copy.start()
            kept.append(copy)
    rings = [Ring(links, at, fulls[i], 1, False) for i in range(2)]
    for i in range(2):
        for copy in direct[9 * i:9 * i + 9]:
            copy.wait_recv()
        for copy in kept[3 * i:3 * i + 3]:
            copy.wait()
        rings[i].start()
    for ring in rings:
        ring.turn()
    last = Ring(links, at, fulls[0], 2, True)
    rings[0].finish()
    last.start()
    last.share_held()
    rings[1].finish()
    other = Ring(links, at, fulls[1], 2, True)
    other.share_held()
    last.turn()
    last.finish()
    last.end()
    other.end()
    links.finish()
    for remote, mine in first:
        pl.when(jnp.logical_not(mine))(remote.wait_send)


def gather(in_w, out_w, conv_w, conv_b, norm_gain, gate_gain):
    wides = (3584, 6144)
    vm, dma = pltpu.VMEM, pltpu.SemaphoreType.DMA
    return pl.pallas_call(
        gather_kernel,
        out_shape=[jax.ShapeDtypeStruct((2, 2, 4, 2, 3, 16, w), jnp.bfloat16) for w in wides],
        in_specs=[pl.BlockSpec(memory_space=pltpu.VMEM)] * 6,
        out_specs=[pl.BlockSpec(memory_space=pl.ANY)] * 2,
        scratch_shapes=[vm((16, w), jnp.bfloat16) for w in wides] + [vm((16, w), jnp.float32) for w in wides]
        + [vm((48, wides[0] // 4), jnp.float32), vm((48, 768), jnp.float32), vm((96, 384), jnp.float32)]
        + [vm((4, 16, w // 4), jnp.bfloat16) for w in wides]
        + [vm((3, 16, w // 4), jnp.bfloat16) for w in wides]
        + [dma((96,)), dma((96,)), dma((8,)), dma((6,))],
        compiler_params=pltpu.CompilerParams(collective_id=0, has_side_effects=True, vmem_limit_bytes=60 << 20),
        name="gather_weights",
    )(in_w, out_w, conv_w, conv_b[None], norm_gain[None], gate_gain[None])


def span(shape, axis, at):
    cut = [slice(None)] * 5
    if axis == "y":
        cut[1] = pl.ds(at["y"], 1)
    elif axis == "z":
        cut[0], cut[2] = pl.ds(at["z"] // 2, 1), pl.ds(lax.rem(at["z"], 2), 1)
    else:
        cut[4] = pl.ds(pl.multiple_of(at["x"] * (shape[4] // 4), 128), shape[4] // 4)
    return cut


def without(shape, axis):
    zh, y, zl, rows, wide = shape
    return {"y": (zh, 1, zl, rows, wide), "z": (1, y, 1, rows, wide), "x": (zh, y, zl, rows, wide // 4)}[axis]


def halves(shape):
    if shape[1] == 4:
        return 1, ((0, 2), (2, 2))
    if shape[0] == 2:
        return 0, ((0, 1), (1, 1))
    near = -(-shape[4] // 256) * 128
    return 4, ((0, near), (near, shape[4] - near))


def cut_half(cut, shape, half):
    dim, parts = halves(shape)
    start, size = parts[half]
    cut = list(cut)
    old = cut[dim]
    base = 0 if isinstance(old, slice) else old.start
    cut[dim] = pl.ds(pl.multiple_of(base + start, 128) if dim == 4 and not isinstance(base, int) else base + start, size)
    return cut


def half_shape(shape, half):
    dim, parts = halves(shape)
    return tuple(parts[half][1] if k == dim else size for k, size in enumerate(shape))


def add_up(out, terms, shape):
    na, nb, nc = shape[:3]

    def slab(k, carry):
        a, b, d = k // (nb * nc), lax.rem(k // nc, nb), lax.rem(k, nc)
        total = terms[0](a, b, d).astype(jnp.float32)
        for term in terms[1:]:
            total = total + term(a, b, d).astype(jnp.float32)
        out(a, b, d, total)
        return carry

    lax.fori_loop(0, na * nb * nc, slab, 0)


def start_of(cut):
    return 0 if isinstance(cut, slice) else cut.start


def slab_of(ref, cut, shape):
    z0, y0, l0, _, c0 = (start_of(s) for s in cut)
    lead = ref

    def read(a, b, d):
        return lead[z0 + a, y0 + b, l0 + d, :, pl.ds(c0, shape[4])]

    return read


def slab_to(ref, shape):
    def write(a, b, d, value):
        ref[a, b, d] = value.astype(ref.dtype)

    return write


ALL_CUT = [slice(None)] * 5


def scatter_scratch(wide):
    vm, f32 = pltpu.VMEM, jnp.float32
    scratch = []
    size = {part: (2, 4, 2, 16, wide) for part in PARTS}
    for phase in range(3):
        for part in PARTS:
            shape = without(size[part], ORDERS[part][2 - phase])
            scratch += [vm(shape, jnp.bfloat16)] * (3 if phase else 2)
            if phase == 0:
                scratch += [vm(half_shape(shape, way), jnp.bfloat16) for way in (0, 1)]
            size[part] = shape
    return scratch


def last_scratch(wide, first):
    vm, f32 = pltpu.VMEM, jnp.float32
    scratch = [vm((48, first), f32), vm((96, 384) if wide > 4 * first else (8, 128), f32), vm((4, 16, wide // 4), f32), vm((4, 16, wide // 4), f32)]
    return scratch + [pltpu.SemaphoreType.DMA((4,))] * 2


class Scatter:
    def __init__(self, at, links, source, wide, split, refs, last, narrow=None):
        take = iter(refs)
        self.at, self.links, self.split = at, links, split
        self.near, self.relay = {}, {}
        for phase in range(3):
            for s in PARTS:
                self.near[s, phase] = [next(take) for _ in range(3 if phase else 2)]
                self.relay[s] = [next(take), next(take)] if phase == 0 else self.relay[s]
        if narrow:
            def less(ref):
                return ref.at[:, :, :, :, pl.ds(0, ref.shape[4] * wide // narrow)]

            self.near = {key: [less(ref) for ref in held] for key, held in self.near.items()}
            self.relay = {key: [less(ref) for ref in held] for key, held in self.relay.items()}
        self.fin, self.fin_o, self.staged, self.landed, self.last, self.own = last
        self.size = {s: (2, 4, 2, 16, wide) for s in PARTS}
        self.source = {s: source.at[:, :, :, s] for s in PARTS}

    def add(self, phase, s, axis, shape):
        terms = [slab_of(self.source[s], span(self.size[s], axis, self.at), shape)]
        terms += [slab_of(buf, ALL_CUT, shape) for buf in self.near[s, phase]]
        if phase < 2:
            held = self.near[s, phase][0]
            add_up(slab_to(held, shape), terms, shape)
            self.source[s], self.size[s] = held, shape
            return
        total = terms[0](0, 0, 0).astype(jnp.float32)
        for term in terms[1:]:
            total = total + term(0, 0, 0).astype(jnp.float32)
        first = self.fin.shape[1]
        self.fin[pl.ds(16 * s, 16), :] = total[:, :first]
        if self.split:
            for b in range(2):
                self.fin_o[pl.ds(32 * s + 16 * b, 16), :] = total[:, first + 384 * b:first + 384 * b + 384]

    def steps(self):
        at, links, size, source = self.at, self.links, self.size, self.source
        sent, lent = {}, {}
        for s in PARTS:
            axis = ORDERS[s][2]
            shape = without(size[s], axis)
            lent[s] = []
            for way, step in ((0, 1), (1, 3)):
                src = source[s].at[tuple(cut_half(span(size[s], axis, moved(at, axis, 2)), shape, way))]
                lent[s].append(links.copy(src, self.relay[s][way], {axis: moved(at, axis, step)[axis]}))
        for s in PARTS:
            axis = ORDERS[s][2]
            shape = without(size[s], axis)
            sent[s] = []
            for way, step in ((0, 1), (1, 3)):
                src = source[s].at[tuple(cut_half(span(size[s], axis, moved(at, axis, step)), shape, 1 - way))]
                dst = self.near[s, 0][way].at[tuple(cut_half(ALL_CUT, shape, 1 - way))]
                sent[s].append(links.copy(src, dst, {axis: moved(at, axis, step)[axis]}))
        yield
        for s in PARTS:
            axis = ORDERS[s][2]
            shape = without(size[s], axis)
            for way, step in ((0, 1), (1, 3)):
                lent[s][way].wait_recv()
                hs = half_shape(shape, way)
                cut = cut_half(span(size[s], axis, moved(at, axis, step)), shape, way)
                buf = self.relay[s][way]
                add_up(slab_to(buf, hs), [slab_of(source[s], cut, hs), slab_of(buf, ALL_CUT, hs)], hs)
                dst = self.near[s, 0][way].at[tuple(cut_half(ALL_CUT, shape, way))]
                sent[s].append(links.copy(buf, dst, {axis: moved(at, axis, step)[axis]}))
        yield
        for phase in (1, 2):
            for s in PARTS:
                for copy in sent[s]:
                    copy.wait_recv()
                axis = ORDERS[s][3 - phase]
                self.add(phase - 1, s, axis, without(size[s], axis))
                axis = ORDERS[s][2 - phase]
                sent[s] = []
                for k in (1, 3, 2):
                    src = source[s].at[tuple(span(size[s], axis, moved(at, axis, k)))]
                    sent[s].append(links.copy(src, self.near[s, phase][k - 1], {axis: moved(at, axis, k)[axis]}))
            yield
        for s in PARTS:
            for copy in sent[s]:
                copy.wait_recv()
            axis = ORDERS[s][0]
            self.add(2, s, axis, without(size[s], axis))
        z, y, x, c = (at[name] for name in ALL)
        _, _, from_z, home = targets(at)
        self.final = []
        first, staged, landed = self.fin.shape[1], self.staged, self.landed
        for k in range(4):
            sx, sc = 2 * lax.rem(z, 2) + k // 2, k % 2
            staged[k] = jnp.zeros(staged.shape[1:], jnp.float32)
            staged[k, :12, :first] = self.fin[pl.ds(12 * k, 12), :]
            for b in range(2 if self.split else 0):
                staged[k, :12, first + 384 * b:first + 384 * b + 384] = self.fin_o[pl.ds(24 * k + 12 * b, 12), :]
            mine = jnp.logical_and(home, jnp.logical_and(sx == x, sc == c))
            remote = pltpu.make_async_remote_copy(
                src_ref=staged.at[k], dst_ref=landed.at[x], send_sem=self.own.at[k], recv_sem=self.last.at[x],
                device_id=(from_z, y, sx, jnp.int32(sc)), device_id_type=MESH)
            local = pltpu.make_async_copy(staged.at[k], landed.at[x], self.last.at[x])
            pl.when(jnp.logical_not(mine))(remote.start)
            pl.when(mine)(local.start)
            self.final.append((remote, mine))
        yield

    def finish(self, out, base, limit, out_o=None):
        first = self.fin.shape[1]
        for tx in range(4):
            pltpu.make_async_copy(self.landed.at[tx], self.landed.at[tx], self.last.at[tx]).wait()
            count = min(first, limit - tx * first)
            out[:, base + tx * first:base + tx * first + count] = self.landed[tx, :12, :count]
            for b in range(2 if self.split else 0):
                out_o[pl.ds(12 * b, 12), pl.ds(tx * 384, 384)] = self.landed[tx, :12, first + 384 * b:first + 384 * b + 384]
        for remote, mine in self.final:
            pl.when(jnp.logical_not(mine))(remote.wait_send)


SMALL = 1792


def small_steps(at, links, whole, core_sum, core_other, rounds):
    c = at["c"]

    def side(core):
        return pl.ds(pl.multiple_of(SMALL * core, 128), SMALL)

    going = [links.copy(whole.at[:, side(1 - c)], core_sum, {"c": 1 - c})]
    yield
    going[0].wait_recv()
    total = core_sum[...] + whole[:, side(c)]
    for axis, held in zip(("x", "y", "z"), rounds):
        held[at[axis]] = total
        mine = held.at[at[axis]]
        going = [links.copy(mine, mine, {axis: moved(at, axis, steps)[axis]}) for steps in (1, 3, 2)]
        yield
        for copy in going:
            copy.wait_recv()
        total = held[0]
        for j in range(1, 4):
            total = total + held[j]
    whole[:, side(c)] = total
    going = [links.copy(whole.at[:, side(c)], core_other, {"c": 1 - c})]
    yield
    going[0].wait_recv()
    links.settle()
    whole[:, side(1 - c)] = core_other[...]
    yield


def own_slices(at, whole, d_taps, d_bias, d_norm_gain, d_gate_gain, d_dt_bias, d_rates, d_skip):
    index = 32 * at["z"] + 8 * at["y"] + 2 * at["x"] + at["c"]
    total = whole[...]

    def own(size, each):
        return pltpu.roll(total[:, :size], lax.rem(size - each * index, size), 1)

    value = own(CONVC, 26)
    d_taps[...] = value[0:4, :26]
    d_bias[...] = value[4:5, :26]
    d_gate_gain[...] = own(DI, 24)[5:6, :24]
    d_norm_gain[...] = own(1536, 12)[7:8, :12]
    by_head = total[:, CONVC:CONVC + 128]
    d_dt_bias[...] = by_head[0:1, :48]
    d_rates[...] = by_head[1:2, :48]
    row = lax.broadcasted_iota(jnp.int32, (128, 128), 0)
    col = lax.broadcasted_iota(jnp.int32, (128, 128), 1)
    heads = jnp.zeros((8, 128), jnp.float32)
    for b in range(2):
        ones = jnp.where(2 * row + b == col, 1.0, 0.0).astype(jnp.bfloat16)
        for part in split3(jnp.broadcast_to(by_head[2 + b:3 + b], (8, 128))):
            heads = heads + jnp.dot(part, ones, preferred_element_type=jnp.float32)
    d_skip[...] = heads[0:1, :48]


H = 48
P_SIZE = 64
KW = 4
DI = 3072
CONVC = 3328
PROJ = 6448
WIDE = 6656
PARAMS = 6528
SEQ = ("y", "x", "c")
epsilon = 1e-05


TILES = 24
BUFFERS = 3


def dot(a, b):
    return jnp.dot(a, b, preferred_element_type=jnp.float32)


def dot_nt(a, b):
    return lax.dot_general(a, b, (((1,), (1,)), ((), ())), preferred_element_type=jnp.float32)


def dot_tn(a, b):
    return lax.dot_general(a, b, (((0,), (0,)), ((), ())), preferred_element_type=jnp.float32)


def low(v):
    return v.astype(jnp.bfloat16)


def wide(v):
    return v.astype(jnp.float32)


def split3(v):
    a = low(v)
    b = low(v - wide(a))
    return a, b, low(v - wide(a) - wide(b))


def running_sums(v, backward):
    row = lax.broadcasted_iota(jnp.int32, (256, 256), 0)
    col = lax.broadcasted_iota(jnp.int32, (256, 256), 1)
    ones = low(jnp.where(row <= col if backward else row >= col, 1.0, 0.0))
    return sum(dot(ones, part) for part in split3(v))


def sigmoid(v):
    return 1.0 / (1.0 + jnp.exp(-v))


def loop(first, count, body, unroll):
    def step(k, carry):
        for u in range(unroll):
            body(first + k * unroll + u, u)
        return carry
    lax.fori_loop(0, count // unroll, step, 0)


def mixer_kernel(normed, given_out, taps, gain, norm_gain, dt_bias, rates, d_skip, hidden_in, w_late, part_w,
                 out, d_hidden, g_in, g_o, o_taps, o_bias, o_norm, o_gate, o_dt, o_rates, o_skip, weights_,
                 skip, heads,
                 conv_in, dt_in, dproj, sums, headsums,
                 gates, db, branch, dz, sib_normed, sib_given, sib_branch, sib_dz, src, chunk, chunk_sem, flipped, out_sem, ready,
                 act, ys, dys, shift, shift2, halo_out, halo_in, back_out, back_in,
                 cum, ecum, toward, steps, rows_a, scores, dscores, usum, qin, qw, prods, stat, coef, db_in, dc_in, decay,
                 skips, loc, inc, inc2, *rest):
    f32, bf16 = jnp.float32, jnp.bfloat16
    snd, rcv, ret, sib, across = rest[:5]
    (sib_send, sib_recv, a_send, a_recv, h_sem, rs_send, rs_recv, l_send, l_recv, t_send, t_recv), rest = rest[5:16], rest[16:]
    whole, core_sum, core_other, rounds, last_early, last_late, rest = rest[0], rest[1], rest[2], rest[3:6], rest[6:12], rest[12:18], rest[18:]
    at = place()
    z, core = lax.axis_index("z"), lax.axis_index("c")
    chip = 4 * lax.axis_index("y") + lax.axis_index("x")
    me = 2 * chip + core
    lane = lax.broadcasted_iota(jnp.int32, (256, 128), 1)
    first_head = lane < 64

    def device(k):
        return (z, k // 8, lax.rem(k // 2, 4), lax.rem(k, 2))

    def same_core(k):
        return (z, k // 4, lax.rem(k, 4), core)

    def others(body):
        def step(k, carry):
            body(lax.rem(chip + k, 16))
            return carry
        lax.fori_loop(1, 16, step, 0)

    barrier = pltpu.get_barrier_semaphore()
    others(lambda k: pl.semaphore_signal(barrier, inc=1, device_id=same_core(k), device_id_type=MESH))
    pl.semaphore_signal(barrier, inc=1, device_id={"c": 1 - core}, device_id_type=MESH)
    beside = jnp.where(core == 1, me + 1, me - 1)
    inner = jnp.logical_and(beside >= 0, beside < 32)

    @pl.when(inner)
    def _():
        pl.semaphore_signal(barrier, inc=1, device_id=device(beside), device_id_type=MESH)

    for steps_ in (1, 2, 3):
        pl.semaphore_signal(barrier, inc=1, device_id={"z": moved(at, "z", steps_)["z"]}, device_id_type=MESH)
    to_z, to_c, _, home = targets(at)
    for tx in range(4):
        @pl.when(jnp.logical_not(jnp.logical_and(home, at["x"] == tx)))
        def _():
            pl.semaphore_signal(barrier, inc=1, device_id=(to_z, at["y"], jnp.int32(tx), to_c), device_id_type=MESH)
    pl.semaphore_wait(barrier, 23 + inner.astype(jnp.int32) - home.astype(jnp.int32))

    def exchange(e, source, target, own):
        def go(k):
            pltpu.make_async_remote_copy(
                src_ref=source(k), dst_ref=target(chip), send_sem=a_send.at[e, k], recv_sem=a_recv.at[e, chip],
                device_id=same_core(k), device_id_type=MESH).start()
        others(go)
        own()

    def arrived(e, target):
        others(lambda k: pltpu.make_async_copy(target(k), target(k), a_recv.at[e, k]).wait())

    def left(e, source):
        others(lambda k: pltpu.make_async_copy(source(k), source(k), a_send.at[e, k]).wait())

    def to_sibling(e, src, dst):
        made = pltpu.make_async_remote_copy(
            src_ref=src, dst_ref=dst, send_sem=sib_send.at[e], recv_sem=sib_recv.at[e],
            device_id={"c": 1 - core}, device_id_type=MESH)
        made.start()
        return made

    def neighbour(k, src, dst, steps_, on):
        made = pltpu.make_async_remote_copy(
            src_ref=src, dst_ref=dst, send_sem=h_sem.at[2 * k], recv_sem=h_sem.at[2 * k + 1],
            device_id=device(lax.rem(me + steps_ + 32, 32)), device_id_type=MESH)
        pl.when(on)(made.start)
        return made

    def lanes(start, size):
        return pl.ds(pl.multiple_of(start, 128), size)

    links = Links(rs_send, rs_recv)
    ring = Ring(links, at, weights_, 2, True)
    ring.start()

    def from_late(k, slot):
        pltpu.make_async_copy(
            w_late.at[:, :, :, :, :, :, lanes(384 * k, 384)],
            chunk.at[slot].reshape(2, 2, 4, 2, 3, 16, 384), chunk_sem.at[slot]).start()

    def from_gates(k, slot):
        pltpu.make_async_copy(
            weights_.at[:, :, :, :, :, :, lanes(1536 * (k // 2) + 384 * lax.rem(k, 2), 384)],
            chunk.at[slot].reshape(2, 2, 4, 2, 3, 16, 384), chunk_sem.at[slot]).start()

    def from_out(k, slot):
        for b in range(2):
            pltpu.make_async_copy(
                weights_.at[k // 4, :, :, :, :, :, lanes(1536 * lax.rem(k, 4) + 768 + 384 * b, 384)],
                chunk.at[slot].reshape(2, 4, 2, 3, 32, 384).at[:, :, :, :, pl.ds(16 * b, 16)], chunk_sem.at[slot]).start()

    def prefetch(fetch):
        for slot in range(BUFFERS):
            fetch(jnp.int32(slot), slot)

    def stream(fetch, count, use):
        def round_(n, u):
            for slot in range(BUFFERS):
                k = BUFFERS * n + slot

                @pl.when(k < count)
                def _():
                    pltpu.make_async_copy(chunk.at[slot], chunk.at[slot], chunk_sem.at[slot]).wait()
                    use(k, chunk[slot])

                @pl.when(k + BUFFERS < count)
                def _():
                    fetch(k + BUFFERS, slot)

        loop(0, -(-count // BUFFERS), round_, 1)

    prefetch(from_late)

    def project(k, w):
        value = dot(normed[...], w)

        @pl.when(k < 8)
        def _():
            conv_in[:, lanes(384 * jnp.minimum(k, 7), 384)] = low(value)

        @pl.when(k == 8)
        def _():
            conv_in[:, 3072:CONVC] = low(value[:, :256])
            dt_in[...] = value[:, 256:]

    stream(from_late, 9, project)
    halo_out[...] = conv_in[240:256, :]
    front = neighbour(0, halo_out, halo_in, 1, me < 31)
    shared = [to_sibling(5, normed.at[:, lanes(768 * (1 - core), 768)], sib_normed), to_sibling(6, given_out, sib_given)]


    heads[...] = jnp.zeros((8, 128), f32)
    for k, ref in enumerate((dt_bias, rates, d_skip)):
        heads[k:k + 1, :H] = ref[...]
    by_head_ = heads[2:3, :]
    for j in range(TILES):
        skip[:, 128 * j:128 * j + 128] = jnp.where(
            lane[0:1] < 64, jnp.broadcast_to(by_head_[:, 2 * j:2 * j + 1], (1, 128)), jnp.broadcast_to(by_head_[:, 2 * j + 1:2 * j + 2], (1, 128)))

    raw = dt_in[...] + heads[0:1, :]
    dt = jnp.maximum(raw, 0.0) + jnp.log1p(jnp.exp(-jnp.abs(raw)))
    total = running_sums(-heads[1:2, :] * dt, False)
    last = total[255:256, :]
    steps[...] = dt
    cum[...] = total
    ecum[...] = jnp.exp(total)
    toward[...] = jnp.exp(last - total) * dt
    rows_a[...] = jnp.transpose(total - jnp.log(dt))

    @pl.when(me == 0)
    def _():
        halo_in[...] = jnp.zeros((16, CONVC), bf16)

    pl.when(me > 0)(front.wait_recv)

    def cols(j):
        return pl.ds(pl.multiple_of(128 * j, 128), 128)

    def convolved(j, u):
        shift[u, 0:8, :] = wide(halo_in[:, cols(j)])[8:16, :]
        shift[u, 8:264, :] = wide(conv_in[:, cols(j)])
        total = taps[4:5, cols(j)] + taps[0:1, cols(j)] * shift[u, 5:261, :]
        for k in range(1, 4):
            total = total + taps[k:k + 1, cols(j)] * shift[u, 5 + k:261 + k, :]
        return total

    def conv(j, u):
        total = convolved(j, u)
        act[j] = low(total * sigmoid(total))

    loop(0, TILES + 2, conv, 2)
    b_in, c_out = act[TILES], act[TILES + 1]
    scores[...] = dot_nt(c_out, b_in)

    def pick(ref, j):
        turned = pltpu.roll(ref[...], lax.rem(128 - 2 * j, 128), 1)
        return jnp.broadcast_to(turned[:, 0:1], (256, 128)), jnp.broadcast_to(turned[:, 1:2], (256, 128))

    def spread(ref, j):
        one, two = pick(ref, j)
        return jnp.where(first_head, one, two)

    def by_head(v):
        zero = jnp.zeros_like(v)
        return jnp.where(first_head[:v.shape[0]], v, zero), jnp.where(first_head[:v.shape[0]], zero, v)

    def fold(acc, prod, j):
        row = lax.broadcasted_iota(jnp.int32, (256, 128), 0)
        col = lax.broadcasted_iota(jnp.int32, (256, 128), 1)
        pickers = low(jnp.where(lax.rem(row, 128) // 64 + 2 * j == col, 1.0, 0.0))
        top = low(prod)
        both = jnp.concatenate([top, low(prod - wide(top))], axis=1)
        acc[...] += dot(both, pickers)

    def rows128(j):
        return pl.ds(pl.multiple_of(128 * j, 128), 128)

    mine, given = 12 * core, 12 * (1 - core)
    row128 = lax.broadcasted_iota(jnp.int32, (128, 128), 0)
    row16 = lax.broadcasted_iota(jnp.int32, (16, 128), 0)
    decay[0:8, :] = jnp.broadcast_to(last, (8, 128))

    def pair_factor(line, j):
        turned = pltpu.roll(jnp.broadcast_to(line, (8, 128)), lax.rem(128 - 2 * j, 128), 1)
        return jnp.where(row128 < 64, jnp.broadcast_to(turned[0:1, 0:1], (128, 128)), jnp.broadcast_to(turned[0:1, 1:2], (128, 128)))

    head_a = 24 * core + 3 * chip // 2
    edge = jnp.where(lax.rem(chip, 2) == 0, 64, 32)
    row96 = lax.broadcasted_iota(jnp.int32, (96, 128), 0)

    class Carry:
        def __init__(self, way, backward, into):
            self.e, self.backward, self.into = 2 * way, backward, into
            self.sib, self.across = sib, across
            self.snd, self.rcv, self.ret = snd, rcv, ret

        def swap(self):
            self.first = to_sibling(self.e, loc.at[pl.ds(pl.multiple_of(1536 * (1 - core), 128), 1536)], self.sib)

        def start(self):
            self.first.wait_recv()
            second = core == (0 if self.backward else 1)
            other = decay[8:9, :]
            later = jnp.exp(jnp.where(second, last, other))

            def join(j, carry):
                own, theirs = wide(loc[rows128(mine + j), :]), wide(self.sib[rows128(j), :])
                factor = pair_factor(later, mine + j)
                tile = low(factor * jnp.where(second, theirs, own) + jnp.where(second, own, theirs))
                for g in range(4):
                    q = 4 * j + g
                    self.snd[q // 3, pl.ds(pl.multiple_of(32 * lax.rem(q, 3), 32), 32), :] = tile[32 * g:32 * g + 32]
                return carry

            loop(0, 12, join, 12)
            tail = split3(last + other)
            lines = jnp.zeros((16, 128), f32)
            for k in range(3):
                lines = jnp.where(row16 == k, wide(tail[k]), lines)
            for k in range(16):
                self.snd[k, 96:112, :] = low(lines)

            def own():
                self.rcv[chip] = self.snd[chip]

            exchange(self.e, lambda k: self.snd.at[k], lambda k: self.rcv.at[k], own)

        def turn(self):
            arrived(self.e, lambda k: self.rcv.at[k])
            carry = jnp.zeros((96, 128), f32)
            for k in (range(15, -1, -1) if self.backward else range(16)):
                line = wide(self.rcv[k, 96:112, :])
                line = jnp.exp(line[0:1] + line[1:2] + line[2:3])
                line = pltpu.roll(jnp.broadcast_to(line, (8, 128)), lax.rem(128 - head_a, 128), 1)
                factor = jnp.where(row96 < edge, jnp.broadcast_to(line[0:1, 0:1], (96, 128)), jnp.broadcast_to(line[0:1, 1:2], (96, 128)))
                self.ret[k] = low(carry)
                carry = factor * carry + wide(self.rcv[k, 0:96, :])
            start = pl.multiple_of(1536 * core, 128)

            def place_(k):
                return self.into.at[pl.ds(pl.multiple_of(start + 96 * k, 32), 96)]

            def own():
                self.into[pl.ds(pl.multiple_of(start + 96 * chip, 32), 96), :] = self.ret[chip]

            self.place = place_
            exchange(self.e + 1, lambda k: self.ret.at[k], place_, own)

        def finish(self):
            arrived(self.e + 1, self.place)
            second = core == (0 if self.backward else 1)
            before = jnp.exp(jnp.where(second, decay[8:9, :], last))

            def part(j, carry):
                at_ = rows128(mine + j)
                came = self.into[at_, :]
                passed = low(pair_factor(before, mine + j) * wide(came) + wide(jnp.where(second, self.sib[rows128(j), :], loc[at_, :])))
                self.across[rows128(j), :] = jnp.where(second, came, passed)
                self.into[at_, :] = jnp.where(second, passed, came)
                return carry

            loop(0, 12, part, 12)
            half = pl.ds(pl.multiple_of(1536 * core, 128), 1536)
            self.last = to_sibling(self.e + 1, self.across, self.into.at[half])
            self.last.wait_recv()

        def end(self):
            if self.backward:
                self.first.wait_send()
            self.last.wait_send()
            left(self.e, lambda k: self.snd.at[k])
            left(self.e + 1, lambda k: self.ret.at[k])

    ahead, aback = Carry(0, False, inc), Carry(1, True, inc2)
    decays = to_sibling(4, decay.at[0:8], decay.at[8:16])

    def local_state(j, carry):
        loc[rows128(j), :] = low(dot_tn(low(spread(toward, j) * wide(act[j])), b_in))
        return carry

    loop(given, 12, local_state, 6)
    ahead.swap()
    loop(mine, 12, local_state, 6)
    decays.wait_recv()
    ahead.start()

    row = lax.broadcasted_iota(jnp.int32, (128, 128), 0)
    col = lax.broadcasted_iota(jnp.int32, (128, 128), 1)
    causal = row >= col

    def weights(j):
        out = []
        for k, own in enumerate(pick(cum, j)):
            line = rows_a[pl.ds(2 * j + k, 1), :]
            first, second = own[:128], own[128:]
            out.append((
                jnp.exp(jnp.where(causal, first - line[:, :128], -1e30)),
                jnp.exp(second - line[:, :128]),
                jnp.exp(jnp.where(causal, second - line[:, 128:], -1e30))))
        return out

    places = ((slice(0, 128), slice(0, 128)), (slice(128, 256), slice(0, 128)), (slice(128, 256), slice(128, 256)))

    def mixing(gaps):
        return [[low(scores[r, c] * gap) for (r, c), gap in zip(places, head)] for head in gaps]

    def inside(j, carry):
        m = mixing(weights(j))
        xa, xb = by_head(act[j])
        top = dot(jnp.concatenate([m[0][0], m[1][0]], axis=1), jnp.concatenate([xa[:128], xb[:128]], axis=0))
        low_ = dot(jnp.concatenate([m[0][1], m[0][2], m[1][1], m[1][2]], axis=1), jnp.concatenate([xa, xb], axis=0))
        ys[j, 0:128, :] = top
        ys[j, 128:256, :] = low_
        return carry

    loop(0, TILES // 2, inside, 3)
    ring.turn()
    ahead.turn()
    loop(TILES // 2, TILES // 2, inside, 3)
    ring.finish()
    ahead.finish()
    ring.end()

    prefetch(from_gates)
    db[...] = jnp.zeros((256, DI), f32)

    def make_gates(k, w):
        gates[:, lanes(384 * k, 384)] = dot(normed[...], w)

    def make_db(k, w):
        db[:, lanes(1536 * (k // 4), 1536)] += dot_nt(given_out[:, lanes(384 * lax.rem(k, 4), 384)], w)

    stream(from_gates, 8, make_gates)
    prefetch(from_out)
    stream(from_out, 8, make_db)

    def state(ref, j):
        return ref[pl.ds(pl.multiple_of(128 * j, 128), 128), :]

    def gate(j, y):
        gz = gates[:, cols(j)]
        sig = sigmoid(gz)
        full = y + skip[:, cols(j)] * wide(act[j])
        return gz, sig, full, full * gz * sig

    stat[...] = jnp.zeros((256, 128), f32)
    coef[...] = jnp.zeros((256, 128), f32)

    def gate_sums(j, carry):
        y = ys[j] + spread(ecum, j) * dot_nt(c_out, state(inc, j))
        ys[j] = y
        _, _, _, gated = gate(j, y)
        stat[...] += gated * gated
        coef[...] += gated * (gain[:, cols(j)] * db[:, cols(j)])
        return carry

    loop(0, TILES, gate_sums, 4)
    scale = lax.rsqrt(jnp.sum(stat[...], axis=1, keepdims=True) * (1.0 / DI) + epsilon)
    factor = scale * scale * scale * (jnp.sum(coef[...], axis=1, keepdims=True) * (1.0 / DI))
    stat[...] = jnp.broadcast_to(scale, (256, 128))
    coef[...] = jnp.broadcast_to(factor, (256, 128))
    sums[...] = jnp.zeros((8, CONVC), f32)
    skips[...] = jnp.zeros((128, 128), f32)

    def gate_back(j, carry):
        y = ys[j]
        gz, sig, full, gated = gate(j, y)
        scaled = gated * stat[...]
        branch[:, cols(j)] = low(scaled * gain[:, cols(j)])
        given = db[:, cols(j)]
        sums[5:6, cols(j)] = jnp.sum(scaled * given, axis=0, keepdims=True)
        d_gated = stat[...] * gain[:, cols(j)] * given - gated * coef[...]
        dz[:, cols(j)] = low(d_gated * full * (sig * (1.0 + gz * (1.0 - sig))))
        dy = low(d_gated * gz * sig)
        dys[j] = dy
        dyf = wide(dy)
        skips[pl.ds(j, 1), :] = jnp.sum(dyf * wide(act[j]), axis=0, keepdims=True)
        loc[rows128(j), :] = low(dot_tn(low(spread(ecum, j) * dyf), c_out))
        return carry

    ahead.first.wait_send()
    ahead.end()
    loop(given, 12, gate_back, 4)
    aback.swap()
    theirs, ours = lanes(1536 * (1 - core), 1536), lanes(1536 * core, 1536)
    shared += [to_sibling(7, branch.at[:, theirs], sib_branch), to_sibling(8, dz.at[:, theirs], sib_dz.at[:, theirs])]
    loop(mine, 12, gate_back, 4)
    shared += [to_sibling(9, dz.at[:, ours], sib_dz.at[:, ours])]
    aback.start()
    for copy in shared:
        copy.wait_recv()

    def flip(own, theirs):
        flipped[:, :256] = low(jnp.transpose(wide(own)))
        flipped[:, 256:] = low(jnp.transpose(wide(theirs)))

    def flip_normed(zh):
        flip(normed[:, lanes(768 * core + 384 * zh, 384)], sib_normed[:, 384 * zh:384 * zh + 384])

    for zh in range(2):
        flip_normed(zh)

        def d_w_gates(n, u):
            part = lanes(384 * n, 384)
            total = dot(flipped[:, :256], dz[:, part]) + dot(flipped[:, 256:], sib_dz[:, part])
            src[zh, :, :, :, :, lanes(1536 * (n // 2) + 384 * lax.rem(n, 2), 384)] = low(total).reshape(4, 2, 3, 16, 384)

        loop(0, 8, d_w_gates, 2)
    for q in range(4):
        flip(branch[:, lanes(1536 * core + 384 * q, 384)], sib_branch[:, 384 * q:384 * q + 384])

        def d_w_out(n, u):
            part = lanes(384 * n, 384)
            total = dot(flipped[:, :256], given_out[:, part]) + dot(flipped[:, 256:], sib_given[:, part])
            total = low(total).reshape(2, 2, 3, 2, 16, 384)
            for b in range(2):
                src[q // 2, 2 * (q % 2):2 * (q % 2) + 2, :, :, :, lanes(1536 * n + 768 + 384 * b, 384)] = total[:, :, :, b]

        loop(0, 4, d_w_out, 2)
    hidden = sib_given
    hidden_load = pltpu.make_async_copy(hidden_in, hidden, out_sem.at[2])
    hidden_load.start()
    prefetch(from_gates)
    aback.turn()
    work = Scatter(at, links, src, 2 * DI, True, rest, last_early)
    reduce = work.steps()
    next(reduce)
    d_norm = gates
    d_norm[:, :1536] = jnp.zeros((256, 1536), f32)
    out_sum = db

    def norm_gates(k, w):
        d_norm[:, :1536] += dot_nt(dz[:, lanes(384 * k, 384)], w)

    def make_out(k, w):
        part = lanes(384 * lax.rem(k, 4), 384)
        held = jnp.where(k < 4, wide(hidden[:, part]), out_sum[:, part])
        out_sum[:, part] = held + dot(branch[:, lanes(1536 * (k // 4), 1536)], w)

    for ref in (usum, qin, qw):
        ref[...] = jnp.zeros((256, 128), f32)
    dscores[...] = jnp.zeros((256, 256), f32)
    prods[...] = jnp.zeros((128, 128), f32)

    def inside_back(j, carry):
        gaps = weights(j)
        m = mixing(gaps)
        x = act[j]
        dya, dyb = by_head(dys[j])
        for k, dy in enumerate((dya, dyb)):
            near = dot_nt(dy[:128], x[:128])
            far = dot_nt(dy[128:], x)
            part = (near, far[:, :128], far[:, 128:])
            for (r, c), gap, value in zip(places, gaps[k], part):
                dscores[r, c] += gap * value
        top = dot_tn(jnp.concatenate([m[0][0], m[0][1], m[1][0], m[1][1]], axis=0), jnp.concatenate([dya, dyb], axis=0))
        low_ = dot_tn(jnp.concatenate([m[0][2], m[1][2]], axis=0), jnp.concatenate([dya[128:], dyb[128:]], axis=0))
        dx = jnp.concatenate([top, low_], axis=0)
        fold(usum, wide(dys[j]) * ys[j], j)
        ys[j] = dx
        fold(qin, wide(x) * dx, j)
        return carry

    loop(0, TILES, inside_back, 3)
    stream(from_gates, 8, norm_gates)
    next(reduce)
    aback.finish()
    db_in[...] = jnp.zeros((256, 128), f32)
    dc_in[...] = jnp.zeros((256, 128), f32)

    def d_mix(j, u, d_act):
        m = convolved(j, u)
        sig = sigmoid(m)
        d_m = d_act * (sig * (1.0 + m * (1.0 - sig)))
        ys[j] = d_m
        back_out[:, cols(j)] = low(d_m[0:16])

    def carry_back(j, u):
        s_in, d_s = state(inc, j), state(inc2, j)
        x, dyf = wide(act[j]), wide(dys[j])
        w = spread(toward, j)
        d_w = w * dot_nt(b_in, d_s)
        fold(qw, x * d_w, j)
        db_in[...] += dot(low(w * x), d_s)
        dc_in[...] += dot(low(spread(ecum, j) * dyf), s_in)
        pair = wide(s_in) * wide(d_s)
        prods[pl.ds(2 * j, 1), :] = jnp.sum(pair[:64], axis=0, keepdims=True)
        prods[pl.ds(2 * j + 1, 1), :] = jnp.sum(pair[64:], axis=0, keepdims=True)
        d_mix(j, u, ys[j] + d_w + skip[:, cols(j)] * dyf)

    loop(0, 15, carry_back, 3)
    next(reduce)
    loop(15, 9, carry_back, 3)
    ds = low(dscores[...])
    d_mix(TILES, 0, db_in[...] + dot_tn(ds, c_out))
    d_mix(TILES + 1, 1, dc_in[...] + dot(ds, b_in))
    behind = neighbour(1, back_out, back_in, -1, me > 0)

    q = qin[...] + qw[...]
    d_last = ecum[255:256, :] * jnp.sum(jnp.transpose(prods[...]), axis=0, keepdims=True) + jnp.sum(qw[...], axis=0, keepdims=True)
    at_end = lax.broadcasted_iota(jnp.int32, (256, 128), 0) == 255
    d_l = running_sums(usum[...] - q + jnp.where(at_end, d_last, 0.0), True)
    dt = steps[...]
    raw = dt_in[...] + heads[0:1, :]
    d_raw = (q / jnp.maximum(dt, 1e-30) - heads[1:2, :] * d_l) * sigmoid(raw)
    d_raw = jnp.where(lane < H, d_raw, 0.0)
    headsums[...] = jnp.zeros((8, 128), f32)
    by_pair = jnp.transpose(skips[...])
    headsums[2:3, :] = jnp.sum(by_pair[:64], axis=0, keepdims=True)
    headsums[3:4, :] = jnp.sum(by_pair[64:], axis=0, keepdims=True)
    headsums[0:1, :] = jnp.sum(d_raw, axis=0, keepdims=True)
    headsums[1:2, :] = -jnp.sum(d_l * dt, axis=0, keepdims=True)
    dproj[:, CONVC:CONVC + 128] = low(d_raw)
    dproj[:, CONVC + 128:] = jnp.zeros((256, 128), bf16)
    next(reduce)

    @pl.when(me == 31)
    def _():
        back_in[...] = jnp.zeros((16, CONVC), bf16)

    pl.when(me < 31)(behind.wait_recv)

    def conv_back(j, u):
        d_m = ys[j]
        shift[u, 0:8, :] = wide(halo_in[:, cols(j)])[8:16, :]
        shift[u, 8:264, :] = wide(conv_in[:, cols(j)])
        for k in range(4):
            sums[k:k + 1, cols(j)] = jnp.sum(d_m * shift[u, 5 + k:261 + k, :], axis=0, keepdims=True)
        sums[4:5, cols(j)] = jnp.sum(d_m, axis=0, keepdims=True)
        shift2[u, 0:256, :] = d_m
        shift2[u, 256:264, :] = wide(back_in[:, cols(j)])[0:8, :]
        total = taps[3:4, cols(j)] * d_m
        for k in range(3):
            total = total + taps[k:k + 1, cols(j)] * shift2[u, 3 - k:259 - k, :]
        dproj[:, cols(j)] = low(total)

    loop(0, TILES // 2, conv_back, 2)
    shared += [to_sibling(10, dproj.at[:, :1536], sib_dz.at[:, :1536])]
    loop(TILES // 2, TILES // 2 + 2, conv_back, 2)
    shared += [to_sibling(11, dproj.at[:, 1536:], sib_dz.at[:, 1536:])]
    next(reduce)
    links.settle()
    for axis in ("z", "y", "x"):
        for steps_ in (1, 2, 3):
            pl.semaphore_signal(ready, inc=1, device_id={axis: moved(at, axis, steps_)[axis]}, device_id_type=MESH)
    for copy in shared[-2:]:
        copy.wait_recv()

    prefetch(from_late)
    for zh in range(2):
        flip_normed(zh)

        def d_w_late(n, u):
            part = lanes(384 * n, 384)
            total = dot(flipped[:, :256], dproj[:, part]) + dot(flipped[:, 256:], sib_dz[:, part])
            src[zh, :, :, :, :, part] = low(total).reshape(4, 2, 3, 16, 384)

        loop(0, 9, d_w_late, 3)
    for k in range(2):
        src[k, :, :, :, :, 3456:3584] = jnp.zeros((4, 2, 3, 16, 128), bf16)
    work.finish(g_in, 0, DI, g_o)
    pl.semaphore_wait(ready, 9)
    after = Links(l_send, l_recv)
    width = WIDE - DI
    work = Scatter(at, after, src.at[:, :, :, :, :, pl.ds(0, width)], width, False, rest, last_late, 2 * DI)
    reduce = work.steps()
    next(reduce)

    def norm_late(k, w):
        d_norm[:, :1536] += dot_nt(dproj[:, lanes(384 * k, 384)], w)

    stream(from_late, 9, norm_late)
    prefetch(from_out)

    hidden_load.wait()
    stat[...] = jnp.zeros((256, 128), f32)
    coef[...] = jnp.zeros((256, 128), f32)

    def norm_sums(j, u):
        v = wide(hidden[:, cols(j)])
        stat[...] += v * v
        coef[...] += v * (norm_gain[:, cols(j)] * d_norm[:, cols(j)])

    loop(0, 12, norm_sums, 4)
    scale = lax.rsqrt(jnp.sum(stat[...], axis=1, keepdims=True) * (1.0 / 1536) + epsilon)
    factor = scale * scale * scale * (jnp.sum(coef[...], axis=1, keepdims=True) * (1.0 / 1536))
    stat[...] = jnp.broadcast_to(scale, (256, 128))
    coef[...] = jnp.broadcast_to(factor, (256, 128))

    def norm_back(j, u):
        v, dn = wide(hidden[:, cols(j)]), d_norm[:, cols(j)]
        sums[7:8, cols(j)] = jnp.sum(dn * v * stat[...], axis=0, keepdims=True)
        d_norm[:, cols(j)] = wide(given_out[:, cols(j)]) + stat[...] * norm_gain[:, cols(j)] * dn - v * coef[...]

    loop(0, 12, norm_back, 4)
    hidden_copy = pltpu.make_async_copy(d_norm.at[:, :1536], d_hidden, out_sem.at[1])
    hidden_copy.start()
    whole[:, :CONVC] = sums[...]
    whole[:, CONVC:CONVC + 128] = headsums[...]
    whole[:, CONVC + 128:] = jnp.zeros((8, 128), f32)
    tiny = Links(t_send, t_recv)
    small = small_steps(at, tiny, whole, core_sum, core_other, rounds)
    next(small)
    next(reduce)
    next(small)
    stream(from_out, 8, make_out)
    sib_branch[...] = low(out_sum[:, :1536])
    out_copy = pltpu.make_async_copy(sib_branch, out, out_sem.at[0])
    out_copy.start()
    for _ in reduce:
        next(small)
    next(small)
    own_slices(at, whole, o_taps, o_bias, o_norm, o_gate, o_dt, o_rates, o_skip)
    work.finish(g_in, DI, PROJ - DI)
    after.finish()
    tiny.finish()
    for copy in shared:
        copy.wait_send()
    out_copy.wait()
    hidden_copy.wait()
    pl.when(me < 31)(front.wait_send)
    pl.when(me > 0)(behind.wait_send)
    decays.wait_send()
    aback.end()


def mixer(normed, given_out, taps, gain, norm_gain, dt_bias, rates, d_skip, hidden, w_late, part_w):
    f32, bf16 = jnp.float32, jnp.bfloat16
    tile, half, late = (256, 128), (16, CONVC), WIDE - DI
    vm = pltpu.VMEM
    dma = pltpu.SemaphoreType.DMA
    scratch = [
        vm((1, DI), f32), vm((8, 128), f32),
        vm((256, CONVC), bf16), vm(tile, f32), vm((256, late), bf16), vm((8, CONVC), f32), vm((8, 128), f32),
        vm((256, DI), f32), vm((256, DI), f32),
        vm((256, DI), bf16), vm((256, DI), bf16), vm((256, 768), bf16), vm((256, 1536), bf16), vm((256, 1536), bf16), vm((256, late), bf16),
        vm((2, 4, 2, 3, 16, 2 * DI), bf16), vm((BUFFERS, 1536, 384), bf16), dma((BUFFERS,)), vm((384, 512), bf16), dma((3,)), pltpu.SemaphoreType.REGULAR,
        vm((TILES + 2,) + tile, bf16), vm((TILES + 2,) + tile, f32), vm((TILES,) + tile, bf16),
        vm((3, 264, 128), f32), vm((2, 264, 128), f32), vm(half, bf16), vm(half, bf16), vm(half, bf16), vm(half, bf16),
        vm(tile, f32), vm(tile, f32), vm(tile, f32), vm(tile, f32), vm((128, 256), f32), vm((256, 256), f32), vm((256, 256), f32),
        vm(tile, f32), vm(tile, f32), vm(tile, f32), vm((128, 128), f32), vm(tile, f32), vm(tile, f32), vm(tile, f32), vm(tile, f32),
        vm((16, 128), f32), vm((128, 128), f32), vm((3072, 128), bf16), vm((3072, 128), bf16), vm((3072, 128), bf16),
    ]
    scratch += [vm((16, 112, 128), bf16), vm((16, 112, 128), bf16), vm((16, 96, 128), bf16)]
    scratch += [vm((1536, 128), bf16), vm((1536, 128), bf16)]
    scratch += [dma((12,)), dma((12,)), dma((4, 16)), dma((4, 16)), dma((4,)), dma((64,)), dma((64,)), dma((40,)), dma((40,)), dma((12,)), dma((12,))]
    scratch += [vm((8, 2 * SMALL), f32), vm((8, SMALL), f32), vm((8, SMALL), f32)] + [vm((4, 8, SMALL), f32)] * 3
    scratch += last_scratch(2 * DI, 768) + last_scratch(late, late // 4) + scatter_scratch(2 * DI)
    near, far = pl.BlockSpec(memory_space=pltpu.VMEM), pl.BlockSpec(memory_space=pl.ANY)
    return pl.pallas_call(
        mixer_kernel,
        out_shape=[jax.ShapeDtypeStruct((256, 1536), bf16), jax.ShapeDtypeStruct((256, 1536), f32),
                   jax.ShapeDtypeStruct((12, PROJ), f32), jax.ShapeDtypeStruct((24, 1536), f32)]
        + [jax.ShapeDtypeStruct(size, f32) for size in ((4, 26), (1, 26), (1, 12), (1, 24), (1, H), (1, H), (1, H))]
        + [jax.ShapeDtypeStruct(part_w.shape, bf16)],
        in_specs=[near] * 8 + [far] * 3,
        out_specs=[far] * 2 + [near] * 9 + [far],
        scratch_shapes=scratch,
        input_output_aliases={10: 11},
        compiler_params=pltpu.CompilerParams(collective_id=2, has_side_effects=True, vmem_limit_bytes=63 << 20),
        name="mixer",
    )(normed, given_out, taps, gain, norm_gain, dt_bias, rates, d_skip, hidden, w_late, part_w)


def rms_scale(values, gain):
    return values * lax.rsqrt(jnp.mean(values * values, axis=-1, keepdims=True) + epsilon) * gain


def shards(
    hidden,
    cotangent,
    in_w,
    out_w,
    conv_w,
    conv_b,
    norm_gain,
    gate_gain,
    dt_bias,
    decay_rates,
    d_skip,
):
    w_late, w_early = gather(in_w, out_w, conv_w, conv_b, norm_gain, gate_gain)
    spare = w_late[:, :, :, :, :, :, PARAMS - DI:].reshape(128, 12, 128).astype(jnp.float32)
    w_conv_f = spare[:, :4, :26].transpose(1, 0, 2).reshape(KW, CONVC)
    b_conv_f = spare[:, 4, :26].reshape(CONVC)
    gain_norm_f = spare[:, 5, :12].reshape(1536)
    gain_gate_f = spare[:, 6, :24].reshape(DI)
    residual = hidden[0].astype(jnp.float32)
    normed = rms_scale(residual, gain_norm_f).astype(jnp.bfloat16)
    taps = jnp.pad(jnp.concatenate([w_conv_f, b_conv_f[None]]), ((0, 3), (0, 0)))
    result, d_hidden, g_in, g_out, d_taps, d_bias, d_norm_gain, d_gate_gain, d_dt, d_rates, d_skips, _ = mixer(
        normed, cotangent[0], taps, gain_gate_f[None], gain_norm_f[None],
        dt_bias[None], decay_rates[None], d_skip[None], hidden[0], w_late, w_early)
    return (
        result[None],
        d_hidden[None],
        g_in,
        g_out,
        d_taps,
        d_bias[0],
        d_norm_gain[0],
        d_gate_gain[0],
        d_dt[0],
        d_rates[0],
        d_skips[0],
    )


def solution(mesh):
    grid = Mesh(mesh.devices.reshape(4, 4, 4, 2), ALL)
    tokens = P("z", SEQ, None)
    placed = (
        tokens,
        tokens,
        P(ALL, None),
        P(ALL, None),
        P(None, ALL),
        P(ALL),
        P(ALL),
        P(ALL),
        P(),
        P(),
        P(),
    )
    return jax.shard_map(
        shards,
        mesh=grid,
        in_specs=placed,
        out_specs=(tokens, tokens, P(ALL, None), P(ALL, None), P(None, ALL), P(ALL), P(ALL), P(ALL), P(), P(), P()),
        check_vma=False,
    )
```

```python
import functools
import jax
import jax.numpy as jnp
from jax import lax
from jax.experimental import pallas as pl
from jax.experimental.pallas import tpu as pltpu
from jax.sharding import PartitionSpec as P, Mesh

MESH = pl.DeviceIdType.MESH
ALL = ("z", "y", "x", "c")
ORDERS = (("z", "y", "x"), ("y", "x", "z"), ("x", "z", "y"))
PARTS = range(3)


class Links:
    def __init__(self, send, recv):
        self.send, self.recv, self.used, self.sent = send, recv, 0, []

    def copy(self, src, dst, device):
        k = self.used
        self.used += 1
        made = pltpu.make_async_remote_copy(
            src_ref=src, dst_ref=dst, send_sem=self.send.at[k], recv_sem=self.recv.at[k],
            device_id=device, device_id_type=MESH)
        made.start()
        self.sent.append(made)
        return made

    def settle(self):
        for made in self.sent:
            made.wait_send()
        self.sent = []

    finish = settle


def place():
    return {name: lax.axis_index(name) for name in ALL}


def block(ref, part, core, at, have, half=None):
    z, y, x = at["z"], at["y"], at["x"]
    wide = ref.shape[-1]
    full = slice(None)
    zh, zl = (full, full) if "z" in have else (z // 2, lax.rem(z, 2))
    ys = full if "y" in have else y
    first, count = (0, wide) if "x" in have else (x * (wide // 4), wide // 4)
    if half is not None:
        if "y" in have:
            ys = pl.ds(2 * half, 2)
        elif "z" in have:
            zh = pl.ds(half, 1)
        else:
            near = -(-count // 256) * 128
            first, count = (first, near) if half == 0 else (first + near, count - near)
    cols = full if "x" in have and count == wide else pl.ds(first if isinstance(first, int) else pl.multiple_of(first, 128), count)
    return ref.at[core, zh, ys, zl, part, :, cols]


def moved(at, axis, steps):
    return {**at, axis: lax.rem(at[axis] + steps + 4, 4)}


def targets(at):
    z, x, c = at["z"], at["x"], at["c"]
    to_z, to_c = 2 * lax.rem(z, 2) + x // 2, z // 2
    return to_z, to_c, 2 * c + z // 2, jnp.logical_and(to_z == z, to_c == c)


class Ring:
    def __init__(self, links, at, full, phase, share):
        self.links, self.at, self.full, self.phase, self.share = links, at, full, phase, share
        self.c = at["c"]
        self.shared = []

    def to_sibling(self, ref):
        if self.share:
            self.shared.append(self.links.copy(ref, ref, {"c": 1 - self.c}))

    def start(self):
        self.near = {}
        for part in PARTS:
            have, axis = ORDERS[part][:self.phase], ORDERS[part][self.phase]
            mine = block(self.full, part, self.c, self.at, have)
            self.near[part] = [self.links.copy(mine, mine, {axis: moved(self.at, axis, steps)[axis]}) for steps in (1, -1)]

    def turn(self):
        self.far = {}
        for part in PARTS:
            have, axis = ORDERS[part][:self.phase], ORDERS[part][self.phase]
            self.far[part] = []
            for way, steps in ((0, 1), (1, -1)):
                self.near[part][way].wait_recv()
                piece = block(self.full, part, self.c, moved(self.at, axis, -steps), have, way)
                self.far[part].append(self.links.copy(piece, piece, {axis: moved(self.at, axis, steps)[axis]}))
        for part in PARTS:
            have, axis = ORDERS[part][:self.phase], ORDERS[part][self.phase]
            for steps in (1, -1):
                self.to_sibling(block(self.full, part, self.c, moved(self.at, axis, -steps), have))

    def finish(self):
        for part in PARTS:
            have, axis = ORDERS[part][:self.phase], ORDERS[part][self.phase]
            for way in (0, 1):
                self.far[part][way].wait_recv()
            self.to_sibling(block(self.full, part, self.c, moved(self.at, axis, 2), have))

    def share_held(self):
        for part in PARTS:
            self.to_sibling(block(self.full, part, self.c, self.at, ORDERS[part][:self.phase]))

    def end(self):
        for copy in self.shared:
            copy.wait_recv()


def gather_kernel(*refs):
    (in_w, out_w, conv_w, conv_b, norm_gain, gate_gain), fulls, shards, (late, early), refs = refs[:6], refs[6:8], refs[8:10], refs[10:12], refs[12:]
    stages, stage_o, landed, unit, (send, recv, first_recv, own) = refs[:2], refs[2], refs[3:5], refs[5:7], refs[7:]
    at = place()
    z, y, x, c = (at[name] for name in ALL)
    to_z, to_c, from_z, home = targets(at)
    slot = 2 * lax.rem(x, 2) + c
    barrier = pltpu.get_barrier_semaphore()
    for axis in ("z", "y", "x"):
        for steps in (1, 2, 3):
            pl.semaphore_signal(barrier, inc=1, device_id={axis: moved(at, axis, steps)[axis]}, device_id_type=MESH)
    pl.semaphore_signal(barrier, inc=1, device_id={"c": 1 - c}, device_id_type=MESH)
    for k in range(4):
        sx, sc = 2 * lax.rem(z, 2) + k // 2, k % 2

        @pl.when(jnp.logical_not(jnp.logical_and(home, jnp.logical_and(sx == x, sc == c))))
        def _():
            pl.semaphore_signal(barrier, inc=1, device_id=(from_z, y, sx, jnp.int32(sc)), device_id_type=MESH)

    def wide_(ref):
        return ref[...].astype(jnp.float32)

    late[...] = jnp.zeros(late.shape, jnp.float32)
    early[...] = jnp.zeros(early.shape, jnp.float32)
    late[0:12, 0:3376] = in_w[:, 3072:6448].astype(jnp.float32)
    late[0:4, 3456:3482] = wide_(conv_w)
    late[4:5, 3456:3482] = wide_(conv_b)
    late[5:6, 3456:3468] = wide_(norm_gain)
    late[6:7, 3456:3480] = wide_(gate_gain)
    held = wide_(out_w)
    for tx in range(4):
        early[0:12, 1536 * tx:1536 * tx + 768] = in_w[:, 768 * tx:768 * tx + 768].astype(jnp.float32)
        for b in range(2):
            start = 1536 * tx + 768 + 384 * b
            early[0:12, start:start + 384] = held[12 * b:12 * b + 12, 384 * tx:384 * tx + 384]
    shards[0][...] = late[...].astype(jnp.bfloat16)
    shards[1][...] = early[...].astype(jnp.bfloat16)
    pl.semaphore_wait(barrier, 14 - home.astype(jnp.int32))

    links = Links(send, recv)
    first = []
    for i in range(2):
        wide = shards[i].shape[1] // 4
        for tx in range(4):
            k = links.used
            links.used += 1
            src = shards[i].at[:, pl.ds(tx * wide, wide)]
            remote = pltpu.make_async_remote_copy(
                src_ref=src, dst_ref=landed[i].at[slot], send_sem=send.at[k], recv_sem=first_recv.at[4 * i + slot],
                device_id=(to_z, y, jnp.int32(tx), to_c), device_id_type=MESH)
            local = pltpu.make_async_copy(src, landed[i].at[slot], first_recv.at[4 * i + slot])
            mine = jnp.logical_and(home, x == tx)
            pl.when(jnp.logical_not(mine))(remote.start)
            pl.when(mine)(local.start)
            first.append((remote, mine))
    kept, direct = [], []
    for i in range(2):
        wide = stages[i].shape[1]
        for k in range(4):
            pltpu.make_async_copy(landed[i].at[k], landed[i].at[k], first_recv.at[4 * i + k]).wait()
            stages[i][pl.ds(12 * k, 12), :] = landed[i][k, :12, :wide].astype(jnp.float32)
            for b in range(2 * i):
                stage_o[pl.ds(24 * k + 12 * b, 12), :] = landed[i][k, :12, wide + 384 * b:wide + 384 * b + 384].astype(jnp.float32)
        for part in PARTS:
            unit[i][part, :, :wide] = stages[i][pl.ds(16 * part, 16), :].astype(jnp.bfloat16)
            for b in range(2 * i):
                unit[i][part, :, wide + 384 * b:wide + 384 * b + 384] = stage_o[pl.ds(32 * part + 16 * b, 16), :].astype(jnp.bfloat16)
        for part in PARTS:
            axis = ORDERS[part][0]
            there = block(fulls[i], part, c, at, ())
            for steps in (1, 3, 2):
                direct.append(links.copy(unit[i].at[part], there, {axis: moved(at, axis, steps)[axis]}))
            copy = pltpu.make_async_copy(unit[i].at[part], there, own.at[3 * i + part])
            copy.start()
            kept.append(copy)
    rings = [Ring(links, at, fulls[i], 1, False) for i in range(2)]
    for i in range(2):
        for copy in direct[9 * i:9 * i + 9]:
            copy.wait_recv()
        for copy in kept[3 * i:3 * i + 3]:
            copy.wait()
        rings[i].start()
    for ring in rings:
        ring.turn()
    last = Ring(links, at, fulls[0], 2, True)
    rings[0].finish()
    last.start()
    last.share_held()
    rings[1].finish()
    other = Ring(links, at, fulls[1], 2, True)
    other.share_held()
    last.turn()
    last.finish()
    last.end()
    other.end()
    links.finish()
    for remote, mine in first:
        pl.when(jnp.logical_not(mine))(remote.wait_send)


def gather(in_w, out_w, conv_w, conv_b, norm_gain, gate_gain):
    wides = (3584, 6144)
    vm, dma = pltpu.VMEM, pltpu.SemaphoreType.DMA
    return pl.pallas_call(
        gather_kernel,
        out_shape=[jax.ShapeDtypeStruct((2, 2, 4, 2, 3, 16, w), jnp.bfloat16) for w in wides],
        in_specs=[pl.BlockSpec(memory_space=pltpu.VMEM)] * 6,
        out_specs=[pl.BlockSpec(memory_space=pl.ANY)] * 2,
        scratch_shapes=[vm((16, w), jnp.bfloat16) for w in wides] + [vm((16, w), jnp.float32) for w in wides]
        + [vm((48, wides[0] // 4), jnp.float32), vm((48, 768), jnp.float32), vm((96, 384), jnp.float32)]
        + [vm((4, 16, w // 4), jnp.bfloat16) for w in wides]
        + [vm((3, 16, w // 4), jnp.bfloat16) for w in wides]
        + [dma((96,)), dma((96,)), dma((8,)), dma((6,))],
        compiler_params=pltpu.CompilerParams(collective_id=0, has_side_effects=True, vmem_limit_bytes=60 << 20),
        name="gather_weights",
    )(in_w, out_w, conv_w, conv_b[None], norm_gain[None], gate_gain[None])


def span(shape, axis, at):
    cut = [slice(None)] * 5
    if axis == "y":
        cut[1] = pl.ds(at["y"], 1)
    elif axis == "z":
        cut[0], cut[2] = pl.ds(at["z"] // 2, 1), pl.ds(lax.rem(at["z"], 2), 1)
    else:
        cut[4] = pl.ds(pl.multiple_of(at["x"] * (shape[4] // 4), 128), shape[4] // 4)
    return cut


def without(shape, axis):
    zh, y, zl, rows, wide = shape
    return {"y": (zh, 1, zl, rows, wide), "z": (1, y, 1, rows, wide), "x": (zh, y, zl, rows, wide // 4)}[axis]


def halves(shape):
    if shape[1] == 4:
        return 1, ((0, 2), (2, 2))
    if shape[0] == 2:
        return 0, ((0, 1), (1, 1))
    near = -(-shape[4] // 256) * 128
    return 4, ((0, near), (near, shape[4] - near))


def cut_half(cut, shape, half):
    dim, parts = halves(shape)
    start, size = parts[half]
    cut = list(cut)
    old = cut[dim]
    base = 0 if isinstance(old, slice) else old.start
    cut[dim] = pl.ds(pl.multiple_of(base + start, 128) if dim == 4 and not isinstance(base, int) else base + start, size)
    return cut


def half_shape(shape, half):
    dim, parts = halves(shape)
    return tuple(parts[half][1] if k == dim else size for k, size in enumerate(shape))


def add_up(out, terms, shape):
    na, nb, nc = shape[:3]

    def slab(k, carry):
        a, b, d = k // (nb * nc), lax.rem(k // nc, nb), lax.rem(k, nc)
        total = terms[0](a, b, d).astype(jnp.float32)
        for term in terms[1:]:
            total = total + term(a, b, d).astype(jnp.float32)
        out(a, b, d, total)
        return carry

    lax.fori_loop(0, na * nb * nc, slab, 0)


def start_of(cut):
    return 0 if isinstance(cut, slice) else cut.start


def slab_of(ref, cut, shape):
    z0, y0, l0, _, c0 = (start_of(s) for s in cut)
    lead = ref

    def read(a, b, d):
        return lead[z0 + a, y0 + b, l0 + d, :, pl.ds(c0, shape[4])]

    return read


def slab_to(ref, shape):
    def write(a, b, d, value):
        ref[a, b, d] = value.astype(ref.dtype)

    return write


ALL_CUT = [slice(None)] * 5


def scatter_scratch(wide):
    vm, f32 = pltpu.VMEM, jnp.float32
    scratch = []
    size = {part: (2, 4, 2, 16, wide) for part in PARTS}
    for phase in range(3):
        for part in PARTS:
            shape = without(size[part], ORDERS[part][2 - phase])
            scratch += [vm(shape, jnp.bfloat16)] * (3 if phase else 2)
            if phase == 0:
                scratch += [vm(half_shape(shape, way), jnp.bfloat16) for way in (0, 1)]
            size[part] = shape
    return scratch


def last_scratch(wide, first):
    vm, f32 = pltpu.VMEM, jnp.float32
    scratch = [vm((48, first), f32), vm((96, 384) if wide > 4 * first else (8, 128), f32), vm((4, 16, wide // 4), f32), vm((4, 16, wide // 4), f32)]
    return scratch + [pltpu.SemaphoreType.DMA((4,))] * 2


class Scatter:
    def __init__(self, at, links, source, wide, split, refs, last, narrow=None):
        take = iter(refs)
        self.at, self.links, self.split = at, links, split
        self.near, self.relay = {}, {}
        for phase in range(3):
            for s in PARTS:
                self.near[s, phase] = [next(take) for _ in range(3 if phase else 2)]
                self.relay[s] = [next(take), next(take)] if phase == 0 else self.relay[s]
        if narrow:
            def less(ref):
                return ref.at[:, :, :, :, pl.ds(0, ref.shape[4] * wide // narrow)]

            self.near = {key: [less(ref) for ref in held] for key, held in self.near.items()}
            self.relay = {key: [less(ref) for ref in held] for key, held in self.relay.items()}
        self.fin, self.fin_o, self.staged, self.landed, self.last, self.own = last
        self.size = {s: (2, 4, 2, 16, wide) for s in PARTS}
        self.source = {s: source.at[:, :, :, s] for s in PARTS}

    def add(self, phase, s, axis, shape):
        terms = [slab_of(self.source[s], span(self.size[s], axis, self.at), shape)]
        terms += [slab_of(buf, ALL_CUT, shape) for buf in self.near[s, phase]]
        if phase < 2:
            held = self.near[s, phase][0]
            add_up(slab_to(held, shape), terms, shape)
            self.source[s], self.size[s] = held, shape
            return
        total = terms[0](0, 0, 0).astype(jnp.float32)
        for term in terms[1:]:
            total = total + term(0, 0, 0).astype(jnp.float32)
        first = self.fin.shape[1]
        self.fin[pl.ds(16 * s, 16), :] = total[:, :first]
        if self.split:
            for b in range(2):
                self.fin_o[pl.ds(32 * s + 16 * b, 16), :] = total[:, first + 384 * b:first + 384 * b + 384]

    def steps(self):
        at, links, size, source = self.at, self.links, self.size, self.source
        sent, lent = {}, {}
        for s in PARTS:
            axis = ORDERS[s][2]
            shape = without(size[s], axis)
            lent[s] = []
            for way, step in ((0, 1), (1, 3)):
                src = source[s].at[tuple(cut_half(span(size[s], axis, moved(at, axis, 2)), shape, way))]
                lent[s].append(links.copy(src, self.relay[s][way], {axis: moved(at, axis, step)[axis]}))
        for s in PARTS:
            axis = ORDERS[s][2]
            shape = without(size[s], axis)
            sent[s] = []
            for way, step in ((0, 1), (1, 3)):
                src = source[s].at[tuple(cut_half(span(size[s], axis, moved(at, axis, step)), shape, 1 - way))]
                dst = self.near[s, 0][way].at[tuple(cut_half(ALL_CUT, shape, 1 - way))]
                sent[s].append(links.copy(src, dst, {axis: moved(at, axis, step)[axis]}))
        yield
        for s in PARTS:
            axis = ORDERS[s][2]
            shape = without(size[s], axis)
            for way, step in ((0, 1), (1, 3)):
                lent[s][way].wait_recv()
                hs = half_shape(shape, way)
                cut = cut_half(span(size[s], axis, moved(at, axis, step)), shape, way)
                buf = self.relay[s][way]
                add_up(slab_to(buf, hs), [slab_of(source[s], cut, hs), slab_of(buf, ALL_CUT, hs)], hs)
                dst = self.near[s, 0][way].at[tuple(cut_half(ALL_CUT, shape, way))]
                sent[s].append(links.copy(buf, dst, {axis: moved(at, axis, step)[axis]}))
        yield
        for phase in (1, 2):
            for s in PARTS:
                for copy in sent[s]:
                    copy.wait_recv()
                axis = ORDERS[s][3 - phase]
                self.add(phase - 1, s, axis, without(size[s], axis))
                axis = ORDERS[s][2 - phase]
                sent[s] = []
                for k in (1, 3, 2):
                    src = source[s].at[tuple(span(size[s], axis, moved(at, axis, k)))]
                    sent[s].append(links.copy(src, self.near[s, phase][k - 1], {axis: moved(at, axis, k)[axis]}))
            yield
        for s in PARTS:
            for copy in sent[s]:
                copy.wait_recv()
            axis = ORDERS[s][0]
            self.add(2, s, axis, without(size[s], axis))
        z, y, x, c = (at[name] for name in ALL)
        _, _, from_z, home = targets(at)
        self.final = []
        first, staged, landed = self.fin.shape[1], self.staged, self.landed
        for k in range(4):
            sx, sc = 2 * lax.rem(z, 2) + k // 2, k % 2
            staged[k] = jnp.zeros(staged.shape[1:], jnp.float32)
            staged[k, :12, :first] = self.fin[pl.ds(12 * k, 12), :]
            for b in range(2 if self.split else 0):
                staged[k, :12, first + 384 * b:first + 384 * b + 384] = self.fin_o[pl.ds(24 * k + 12 * b, 12), :]
            mine = jnp.logical_and(home, jnp.logical_and(sx == x, sc == c))
            remote = pltpu.make_async_remote_copy(
                src_ref=staged.at[k], dst_ref=landed.at[x], send_sem=self.own.at[k], recv_sem=self.last.at[x],
                device_id=(from_z, y, sx, jnp.int32(sc)), device_id_type=MESH)
            local = pltpu.make_async_copy(staged.at[k], landed.at[x], self.last.at[x])
            pl.when(jnp.logical_not(mine))(remote.start)
            pl.when(mine)(local.start)
            self.final.append((remote, mine))
        yield

    def finish(self, out, base, limit, out_o=None):
        first = self.fin.shape[1]
        for tx in range(4):
            pltpu.make_async_copy(self.landed.at[tx], self.landed.at[tx], self.last.at[tx]).wait()
            count = min(first, limit - tx * first)
            out[:, base + tx * first:base + tx * first + count] = self.landed[tx, :12, :count]
            for b in range(2 if self.split else 0):
                out_o[pl.ds(12 * b, 12), pl.ds(tx * 384, 384)] = self.landed[tx, :12, first + 384 * b:first + 384 * b + 384]
        for remote, mine in self.final:
            pl.when(jnp.logical_not(mine))(remote.wait_send)


SMALL = 1792


def small_steps(at, links, whole, core_sum, core_other, rounds):
    c = at["c"]

    def side(core):
        return pl.ds(pl.multiple_of(SMALL * core, 128), SMALL)

    going = [links.copy(whole.at[:, side(1 - c)], core_sum, {"c": 1 - c})]
    yield
    going[0].wait_recv()
    total = core_sum[...] + whole[:, side(c)]
    for axis, held in zip(("x", "y", "z"), rounds):
        held[at[axis]] = total
        mine = held.at[at[axis]]
        going = [links.copy(mine, mine, {axis: moved(at, axis, steps)[axis]}) for steps in (1, 3, 2)]
        yield
        for copy in going:
            copy.wait_recv()
        total = held[0]
        for j in range(1, 4):
            total = total + held[j]
    whole[:, side(c)] = total
    going = [links.copy(whole.at[:, side(c)], core_other, {"c": 1 - c})]
    yield
    going[0].wait_recv()
    links.settle()
    whole[:, side(1 - c)] = core_other[...]
    yield


def own_slices(at, whole, d_taps, d_bias, d_norm_gain, d_gate_gain, d_dt_bias, d_rates, d_skip):
    index = 32 * at["z"] + 8 * at["y"] + 2 * at["x"] + at["c"]
    total = whole[...]

    def own(size, each):
        return pltpu.roll(total[:, :size], lax.rem(size - each * index, size), 1)

    value = own(CONVC, 26)
    d_taps[...] = value[0:4, :26]
    d_bias[...] = value[4:5, :26]
    d_gate_gain[...] = own(DI, 24)[5:6, :24]
    d_norm_gain[...] = own(1536, 12)[7:8, :12]
    by_head = total[:, CONVC:CONVC + 128]
    d_dt_bias[...] = by_head[0:1, :48]
    d_rates[...] = by_head[1:2, :48]
    row = lax.broadcasted_iota(jnp.int32, (128, 128), 0)
    col = lax.broadcasted_iota(jnp.int32, (128, 128), 1)
    heads = jnp.zeros((8, 128), jnp.float32)
    for b in range(2):
        ones = jnp.where(2 * row + b == col, 1.0, 0.0).astype(jnp.bfloat16)
        for part in split3(jnp.broadcast_to(by_head[2 + b:3 + b], (8, 128))):
            heads = heads + jnp.dot(part, ones, preferred_element_type=jnp.float32)
    d_skip[...] = heads[0:1, :48]


H = 48
P_SIZE = 64
KW = 4
DI = 3072
CONVC = 3328
PROJ = 6448
WIDE = 6656
PARAMS = 6528
SEQ = ("y", "x", "c")
epsilon = 1e-05


TILES = 24
BUFFERS = 3


def dot(a, b):
    return jnp.dot(a, b, preferred_element_type=jnp.float32)


def dot_nt(a, b):
    return lax.dot_general(a, b, (((1,), (1,)), ((), ())), preferred_element_type=jnp.float32)


def dot_tn(a, b):
    return lax.dot_general(a, b, (((0,), (0,)), ((), ())), preferred_element_type=jnp.float32)


def low(v):
    return v.astype(jnp.bfloat16)


def wide(v):
    return v.astype(jnp.float32)


def split3(v):
    a = low(v)
    b = low(v - wide(a))
    return a, b, low(v - wide(a) - wide(b))


def running_sums(v, backward):
    row = lax.broadcasted_iota(jnp.int32, (256, 256), 0)
    col = lax.broadcasted_iota(jnp.int32, (256, 256), 1)
    ones = low(jnp.where(row <= col if backward else row >= col, 1.0, 0.0))
    return sum(dot(ones, part) for part in split3(v))


def sigmoid(v):
    return 1.0 / (1.0 + jnp.exp(-v))


def loop(first, count, body, unroll):
    def step(k, carry):
        for u in range(unroll):
            body(first + k * unroll + u, u)
        return carry
    lax.fori_loop(0, count // unroll, step, 0)


def mixer_kernel(normed, given_out, taps, gain, norm_gain, dt_bias, rates, d_skip, hidden_in, w_late, part_w,
                 out, d_hidden, g_in, g_o, o_taps, o_bias, o_norm, o_gate, o_dt, o_rates, o_skip, weights_,
                 skip, heads,
                 conv_in, dt_in, dproj, sums, headsums,
                 gates, db, branch, dz, sib_normed, sib_given, sib_branch, sib_dz, src, chunk, chunk_sem, flipped, out_sem, ready,
                 act, ys, dys, shift, shift2, halo_out, halo_in, back_out, back_in,
                 cum, ecum, toward, steps, rows_a, scores, dscores, usum, qin, qw, prods, stat, coef, db_in, dc_in, decay,
                 skips, loc, inc, inc2, *rest):
    f32, bf16 = jnp.float32, jnp.bfloat16
    snd, rcv, ret, sib, across = rest[:5]
    (sib_send, sib_recv, a_send, a_recv, h_sem, rs_send, rs_recv, l_send, l_recv, t_send, t_recv), rest = rest[5:16], rest[16:]
    whole, core_sum, core_other, rounds, last_early, last_late, rest = rest[0], rest[1], rest[2], rest[3:6], rest[6:12], rest[12:18], rest[18:]
    at = place()
    z, core = lax.axis_index("z"), lax.axis_index("c")
    chip = 4 * lax.axis_index("y") + lax.axis_index("x")
    me = 2 * chip + core
    lane = lax.broadcasted_iota(jnp.int32, (256, 128), 1)
    first_head = lane < 64

    def device(k):
        return (z, k // 8, lax.rem(k // 2, 4), lax.rem(k, 2))

    def same_core(k):
        return (z, k // 4, lax.rem(k, 4), core)

    def others(body):
        def step(k, carry):
            body(lax.rem(chip + k, 16))
            return carry
        lax.fori_loop(1, 16, step, 0)

    barrier = pltpu.get_barrier_semaphore()
    others(lambda k: pl.semaphore_signal(barrier, inc=1, device_id=same_core(k), device_id_type=MESH))
    pl.semaphore_signal(barrier, inc=1, device_id={"c": 1 - core}, device_id_type=MESH)
    beside = jnp.where(core == 1, me + 1, me - 1)
    inner = jnp.logical_and(beside >= 0, beside < 32)

    @pl.when(inner)
    def _():
        pl.semaphore_signal(barrier, inc=1, device_id=device(beside), device_id_type=MESH)

    for steps_ in (1, 2, 3):
        pl.semaphore_signal(barrier, inc=1, device_id={"z": moved(at, "z", steps_)["z"]}, device_id_type=MESH)
    to_z, to_c, _, home = targets(at)
    for tx in range(4):
        @pl.when(jnp.logical_not(jnp.logical_and(home, at["x"] == tx)))
        def _():
            pl.semaphore_signal(barrier, inc=1, device_id=(to_z, at["y"], jnp.int32(tx), to_c), device_id_type=MESH)
    pl.semaphore_wait(barrier, 23 + inner.astype(jnp.int32) - home.astype(jnp.int32))

    def exchange(e, source, target, own):
        def go(k):
            pltpu.make_async_remote_copy(
                src_ref=source(k), dst_ref=target(chip), send_sem=a_send.at[e, k], recv_sem=a_recv.at[e, chip],
                device_id=same_core(k), device_id_type=MESH).start()
        others(go)
        own()

    def arrived(e, target):
        others(lambda k: pltpu.make_async_copy(target(k), target(k), a_recv.at[e, k]).wait())

    def left(e, source):
        others(lambda k: pltpu.make_async_copy(source(k), source(k), a_send.at[e, k]).wait())

    def to_sibling(e, src, dst):
        made = pltpu.make_async_remote_copy(
            src_ref=src, dst_ref=dst, send_sem=sib_send.at[e], recv_sem=sib_recv.at[e],
            device_id={"c": 1 - core}, device_id_type=MESH)
        made.start()
        return made

    def neighbour(k, src, dst, steps_, on):
        made = pltpu.make_async_remote_copy(
            src_ref=src, dst_ref=dst, send_sem=h_sem.at[2 * k], recv_sem=h_sem.at[2 * k + 1],
            device_id=device(lax.rem(me + steps_ + 32, 32)), device_id_type=MESH)
        pl.when(on)(made.start)
        return made

    def lanes(start, size):
        return pl.ds(pl.multiple_of(start, 128), size)

    links = Links(rs_send, rs_recv)
    ring = Ring(links, at, weights_, 2, True)
    ring.start()

    def from_late(k, slot):
        pltpu.make_async_copy(
            w_late.at[:, :, :, :, :, :, lanes(384 * k, 384)],
            chunk.at[slot].reshape(2, 2, 4, 2, 3, 16, 384), chunk_sem.at[slot]).start()

    def from_gates(k, slot):
        pltpu.make_async_copy(
            weights_.at[:, :, :, :, :, :, lanes(1536 * (k // 2) + 384 * lax.rem(k, 2), 384)],
            chunk.at[slot].reshape(2, 2, 4, 2, 3, 16, 384), chunk_sem.at[slot]).start()

    def from_out(k, slot):
        for b in range(2):
            pltpu.make_async_copy(
                weights_.at[k // 4, :, :, :, :, :, lanes(1536 * lax.rem(k, 4) + 768 + 384 * b, 384)],
                chunk.at[slot].reshape(2, 4, 2, 3, 32, 384).at[:, :, :, :, pl.ds(16 * b, 16)], chunk_sem.at[slot]).start()

    def prefetch(fetch):
        for slot in range(BUFFERS):
            fetch(jnp.int32(slot), slot)

    def stream(fetch, count, use):
        def round_(n, u):
            for slot in range(BUFFERS):
                k = BUFFERS * n + slot

                @pl.when(k < count)
                def _():
                    pltpu.make_async_copy(chunk.at[slot], chunk.at[slot], chunk_sem.at[slot]).wait()
                    use(k, chunk[slot])

                @pl.when(k + BUFFERS < count)
                def _():
                    fetch(k + BUFFERS, slot)

        loop(0, -(-count // BUFFERS), round_, 1)

    prefetch(from_late)

    def project(k, w):
        value = dot(normed[...], w)

        @pl.when(k < 8)
        def _():
            conv_in[:, lanes(384 * jnp.minimum(k, 7), 384)] = low(value)

        @pl.when(k == 8)
        def _():
            conv_in[:, 3072:CONVC] = low(value[:, :256])
            dt_in[...] = value[:, 256:]

    stream(from_late, 9, project)
    halo_out[...] = conv_in[240:256, :]
    front = neighbour(0, halo_out, halo_in, 1, me < 31)
    shared = [to_sibling(5, normed.at[:, lanes(768 * (1 - core), 768)], sib_normed), to_sibling(6, given_out, sib_given)]


    heads[...] = jnp.zeros((8, 128), f32)
    for k, ref in enumerate((dt_bias, rates, d_skip)):
        heads[k:k + 1, :H] = ref[...]
    by_head_ = heads[2:3, :]
    for j in range(TILES):
        skip[:, 128 * j:128 * j + 128] = jnp.where(
            lane[0:1] < 64, jnp.broadcast_to(by_head_[:, 2 * j:2 * j + 1], (1, 128)), jnp.broadcast_to(by_head_[:, 2 * j + 1:2 * j + 2], (1, 128)))

    raw = dt_in[...] + heads[0:1, :]
    dt = jnp.maximum(raw, 0.0) + jnp.log1p(jnp.exp(-jnp.abs(raw)))
    total = running_sums(-heads[1:2, :] * dt, False)
    last = total[255:256, :]
    steps[...] = dt
    cum[...] = total
    ecum[...] = jnp.exp(total)
    toward[...] = jnp.exp(last - total) * dt
    rows_a[...] = jnp.transpose(total - jnp.log(dt))

    @pl.when(me == 0)
    def _():
        halo_in[...] = jnp.zeros((16, CONVC), bf16)

    pl.when(me > 0)(front.wait_recv)

    def cols(j):
        return pl.ds(pl.multiple_of(128 * j, 128), 128)

    def convolved(j, u):
        shift[u, 0:8, :] = wide(halo_in[:, cols(j)])[8:16, :]
        shift[u, 8:264, :] = wide(conv_in[:, cols(j)])
        total = taps[4:5, cols(j)] + taps[0:1, cols(j)] * shift[u, 5:261, :]
        for k in range(1, 4):
            total = total + taps[k:k + 1, cols(j)] * shift[u, 5 + k:261 + k, :]
        return total

    def conv(j, u):
        total = convolved(j, u)
        act[j] = low(total * sigmoid(total))

    loop(0, TILES + 2, conv, 2)
    b_in, c_out = act[TILES], act[TILES + 1]
    scores[...] = dot_nt(c_out, b_in)

    def pick(ref, j):
        turned = pltpu.roll(ref[...], lax.rem(128 - 2 * j, 128), 1)
        return jnp.broadcast_to(turned[:, 0:1], (256, 128)), jnp.broadcast_to(turned[:, 1:2], (256, 128))

    def spread(ref, j):
        one, two = pick(ref, j)
        return jnp.where(first_head, one, two)

    def by_head(v):
        zero = jnp.zeros_like(v)
        return jnp.where(first_head[:v.shape[0]], v, zero), jnp.where(first_head[:v.shape[0]], zero, v)

    def fold(acc, prod, j):
        row = lax.broadcasted_iota(jnp.int32, (256, 128), 0)
        col = lax.broadcasted_iota(jnp.int32, (256, 128), 1)
        pickers = low(jnp.where(lax.rem(row, 128) // 64 + 2 * j == col, 1.0, 0.0))
        top = low(prod)
        both = jnp.concatenate([top, low(prod - wide(top))], axis=1)
        acc[...] += dot(both, pickers)

    def rows128(j):
        return pl.ds(pl.multiple_of(128 * j, 128), 128)

    mine, given = 12 * core, 12 * (1 - core)
    row128 = lax.broadcasted_iota(jnp.int32, (128, 128), 0)
    row16 = lax.broadcasted_iota(jnp.int32, (16, 128), 0)
    decay[0:8, :] = jnp.broadcast_to(last, (8, 128))

    def pair_factor(line, j):
        turned = pltpu.roll(jnp.broadcast_to(line, (8, 128)), lax.rem(128 - 2 * j, 128), 1)
        return jnp.where(row128 < 64, jnp.broadcast_to(turned[0:1, 0:1], (128, 128)), jnp.broadcast_to(turned[0:1, 1:2], (128, 128)))

    head_a = 24 * core + 3 * chip // 2
    edge = jnp.where(lax.rem(chip, 2) == 0, 64, 32)
    row96 = lax.broadcasted_iota(jnp.int32, (96, 128), 0)

    class Carry:
        def __init__(self, way, backward, into):
            self.e, self.backward, self.into = 2 * way, backward, into
            self.sib, self.across = sib, across
            self.snd, self.rcv, self.ret = snd, rcv, ret

        def swap(self):
            self.first = to_sibling(self.e, loc.at[pl.ds(pl.multiple_of(1536 * (1 - core), 128), 1536)], self.sib)

        def start(self):
            self.first.wait_recv()
            second = core == (0 if self.backward else 1)
            other = decay[8:9, :]
            later = jnp.exp(jnp.where(second, last, other))

            def join(j, carry):
                own, theirs = wide(loc[rows128(mine + j), :]), wide(self.sib[rows128(j), :])
                factor = pair_factor(later, mine + j)
                tile = low(factor * jnp.where(second, theirs, own) + jnp.where(second, own, theirs))
                for g in range(4):
                    q = 4 * j + g
                    self.snd[q // 3, pl.ds(pl.multiple_of(32 * lax.rem(q, 3), 32), 32), :] = tile[32 * g:32 * g + 32]
                return carry

            loop(0, 12, join, 12)
            tail = split3(last + other)
            lines = jnp.zeros((16, 128), f32)
            for k in range(3):
                lines = jnp.where(row16 == k, wide(tail[k]), lines)
            for k in range(16):
                self.snd[k, 96:112, :] = low(lines)

            def own():
                self.rcv[chip] = self.snd[chip]

            exchange(self.e, lambda k: self.snd.at[k], lambda k: self.rcv.at[k], own)

        def turn(self):
            arrived(self.e, lambda k: self.rcv.at[k])
            carry = jnp.zeros((96, 128), f32)
            for k in (range(15, -1, -1) if self.backward else range(16)):
                line = wide(self.rcv[k, 96:112, :])
                line = jnp.exp(line[0:1] + line[1:2] + line[2:3])
                line = pltpu.roll(jnp.broadcast_to(line, (8, 128)), lax.rem(128 - head_a, 128), 1)
                factor = jnp.where(row96 < edge, jnp.broadcast_to(line[0:1, 0:1], (96, 128)), jnp.broadcast_to(line[0:1, 1:2], (96, 128)))
                self.ret[k] = low(carry)
                carry = factor * carry + wide(self.rcv[k, 0:96, :])
            start = pl.multiple_of(1536 * core, 128)

            def place_(k):
                return self.into.at[pl.ds(pl.multiple_of(start + 96 * k, 32), 96)]

            def own():
                self.into[pl.ds(pl.multiple_of(start + 96 * chip, 32), 96), :] = self.ret[chip]

            self.place = place_
            exchange(self.e + 1, lambda k: self.ret.at[k], place_, own)

        def finish(self):
            arrived(self.e + 1, self.place)
            second = core == (0 if self.backward else 1)
            before = jnp.exp(jnp.where(second, decay[8:9, :], last))

            def part(j, carry):
                at_ = rows128(mine + j)
                came = self.into[at_, :]
                passed = low(pair_factor(before, mine + j) * wide(came) + wide(jnp.where(second, self.sib[rows128(j), :], loc[at_, :])))
                self.across[rows128(j), :] = jnp.where(second, came, passed)
                self.into[at_, :] = jnp.where(second, passed, came)
                return carry

            loop(0, 12, part, 12)
            half = pl.ds(pl.multiple_of(1536 * core, 128), 1536)
            self.last = to_sibling(self.e + 1, self.across, self.into.at[half])
            self.last.wait_recv()

        def end(self):
            if self.backward:
                self.first.wait_send()
            self.last.wait_send()
            left(self.e, lambda k: self.snd.at[k])
            left(self.e + 1, lambda k: self.ret.at[k])

    ahead, aback = Carry(0, False, inc), Carry(1, True, inc2)
    decays = to_sibling(4, decay.at[0:8], decay.at[8:16])

    def local_state(j, carry):
        loc[rows128(j), :] = low(dot_tn(low(spread(toward, j) * wide(act[j])), b_in))
        return carry

    loop(given, 12, local_state, 6)
    ahead.swap()
    loop(mine, 12, local_state, 6)
    decays.wait_recv()
    ahead.start()

    row = lax.broadcasted_iota(jnp.int32, (128, 128), 0)
    col = lax.broadcasted_iota(jnp.int32, (128, 128), 1)
    causal = row >= col

    def weights(j):
        out = []
        for k, own in enumerate(pick(cum, j)):
            line = rows_a[pl.ds(2 * j + k, 1), :]
            first, second = own[:128], own[128:]
            out.append((
                jnp.exp(jnp.where(causal, first - line[:, :128], -1e30)),
                jnp.exp(second - line[:, :128]),
                jnp.exp(jnp.where(causal, second - line[:, 128:], -1e30))))
        return out

    places = ((slice(0, 128), slice(0, 128)), (slice(128, 256), slice(0, 128)), (slice(128, 256), slice(128, 256)))

    def mixing(gaps):
        return [[low(scores[r, c] * gap) for (r, c), gap in zip(places, head)] for head in gaps]

    def inside(j, carry):
        m = mixing(weights(j))
        xa, xb = by_head(act[j])
        top = dot(jnp.concatenate([m[0][0], m[1][0]], axis=1), jnp.concatenate([xa[:128], xb[:128]], axis=0))
        low_ = dot(jnp.concatenate([m[0][1], m[0][2], m[1][1], m[1][2]], axis=1), jnp.concatenate([xa, xb], axis=0))
        ys[j, 0:128, :] = top
        ys[j, 128:256, :] = low_
        return carry

    loop(0, TILES // 2, inside, 3)
    ring.turn()
    ahead.turn()
    loop(TILES // 2, TILES // 2, inside, 3)
    ring.finish()
    ahead.finish()
    ring.end()

    prefetch(from_gates)
    db[...] = jnp.zeros((256, DI), f32)

    def make_gates(k, w):
        gates[:, lanes(384 * k, 384)] = dot(normed[...], w)

    def make_db(k, w):
        db[:, lanes(1536 * (k // 4), 1536)] += dot_nt(given_out[:, lanes(384 * lax.rem(k, 4), 384)], w)

    stream(from_gates, 8, make_gates)
    prefetch(from_out)
    stream(from_out, 8, make_db)

    def state(ref, j):
        return ref[pl.ds(pl.multiple_of(128 * j, 128), 128), :]

    def gate(j, y):
        gz = gates[:, cols(j)]
        sig = sigmoid(gz)
        full = y + skip[:, cols(j)] * wide(act[j])
        return gz, sig, full, full * gz * sig

    stat[...] = jnp.zeros((256, 128), f32)
    coef[...] = jnp.zeros((256, 128), f32)

    def gate_sums(j, carry):
        y = ys[j] + spread(ecum, j) * dot_nt(c_out, state(inc, j))
        ys[j] = y
        _, _, _, gated = gate(j, y)
        stat[...] += gated * gated
        coef[...] += gated * (gain[:, cols(j)] * db[:, cols(j)])
        return carry

    loop(0, TILES, gate_sums, 4)
    scale = lax.rsqrt(jnp.sum(stat[...], axis=1, keepdims=True) * (1.0 / DI) + epsilon)
    factor = scale * scale * scale * (jnp.sum(coef[...], axis=1, keepdims=True) * (1.0 / DI))
    stat[...] = jnp.broadcast_to(scale, (256, 128))
    coef[...] = jnp.broadcast_to(factor, (256, 128))
    sums[...] = jnp.zeros((8, CONVC), f32)
    skips[...] = jnp.zeros((128, 128), f32)

    def gate_back(j, carry):
        y = ys[j]
        gz, sig, full, gated = gate(j, y)
        scaled = gated * stat[...]
        branch[:, cols(j)] = low(scaled * gain[:, cols(j)])
        given = db[:, cols(j)]
        sums[5:6, cols(j)] = jnp.sum(scaled * given, axis=0, keepdims=True)
        d_gated = stat[...] * gain[:, cols(j)] * given - gated * coef[...]
        dz[:, cols(j)] = low(d_gated * full * (sig * (1.0 + gz * (1.0 - sig))))
        dy = low(d_gated * gz * sig)
        dys[j] = dy
        dyf = wide(dy)
        skips[pl.ds(j, 1), :] = jnp.sum(dyf * wide(act[j]), axis=0, keepdims=True)
        loc[rows128(j), :] = low(dot_tn(low(spread(ecum, j) * dyf), c_out))
        return carry

    ahead.first.wait_send()
    ahead.end()
    loop(given, 12, gate_back, 4)
    aback.swap()
    theirs, ours = lanes(1536 * (1 - core), 1536), lanes(1536 * core, 1536)
    shared += [to_sibling(7, branch.at[:, theirs], sib_branch), to_sibling(8, dz.at[:, theirs], sib_dz.at[:, theirs])]
    loop(mine, 12, gate_back, 4)
    shared += [to_sibling(9, dz.at[:, ours], sib_dz.at[:, ours])]
    aback.start()
    for copy in shared:
        copy.wait_recv()

    def flip(own, theirs):
        flipped[:, :256] = low(jnp.transpose(wide(own)))
        flipped[:, 256:] = low(jnp.transpose(wide(theirs)))

    def flip_normed(zh):
        flip(normed[:, lanes(768 * core + 384 * zh, 384)], sib_normed[:, 384 * zh:384 * zh + 384])

    for zh in range(2):
        flip_normed(zh)

        def d_w_gates(n, u):
            part = lanes(384 * n, 384)
            total = dot(flipped[:, :256], dz[:, part]) + dot(flipped[:, 256:], sib_dz[:, part])
            src[zh, :, :, :, :, lanes(1536 * (n // 2) + 384 * lax.rem(n, 2), 384)] = low(total).reshape(4, 2, 3, 16, 384)

        loop(0, 8, d_w_gates, 2)
    aback.turn()
    for q in range(4):
        flip(branch[:, lanes(1536 * core + 384 * q, 384)], sib_branch[:, 384 * q:384 * q + 384])

        def d_w_out(n, u):
            part = lanes(384 * n, 384)
            total = dot(flipped[:, :256], given_out[:, part]) + dot(flipped[:, 256:], sib_given[:, part])
            total = low(total).reshape(2, 2, 3, 2, 16, 384)
            for b in range(2):
                src[q // 2, 2 * (q % 2):2 * (q % 2) + 2, :, :, :, lanes(1536 * n + 768 + 384 * b, 384)] = total[:, :, :, b]

        loop(0, 4, d_w_out, 2)
    hidden = sib_given
    hidden_load = pltpu.make_async_copy(hidden_in, hidden, out_sem.at[2])
    hidden_load.start()
    prefetch(from_gates)
    work = Scatter(at, links, src, 2 * DI, True, rest, last_early)
    reduce = work.steps()
    next(reduce)
    d_norm = gates
    d_norm[:, :1536] = jnp.zeros((256, 1536), f32)
    out_sum = db

    def norm_gates(k, w):
        d_norm[:, :1536] += dot_nt(dz[:, lanes(384 * k, 384)], w)

    def make_out(k, w):
        part = lanes(384 * lax.rem(k, 4), 384)
        held = jnp.where(k < 4, wide(hidden[:, part]), out_sum[:, part])
        out_sum[:, part] = held + dot(branch[:, lanes(1536 * (k // 4), 1536)], w)

    for ref in (usum, qin, qw):
        ref[...] = jnp.zeros((256, 128), f32)
    dscores[...] = jnp.zeros((256, 256), f32)
    prods[...] = jnp.zeros((128, 128), f32)

    def inside_back(j, carry):
        gaps = weights(j)
        m = mixing(gaps)
        x = act[j]
        dya, dyb = by_head(dys[j])
        for k, dy in enumerate((dya, dyb)):
            near = dot_nt(dy[:128], x[:128])
            far = dot_nt(dy[128:], x)
            part = (near, far[:, :128], far[:, 128:])
            for (r, c), gap, value in zip(places, gaps[k], part):
                dscores[r, c] += gap * value
        top = dot_tn(jnp.concatenate([m[0][0], m[0][1], m[1][0], m[1][1]], axis=0), jnp.concatenate([dya, dyb], axis=0))
        low_ = dot_tn(jnp.concatenate([m[0][2], m[1][2]], axis=0), jnp.concatenate([dya[128:], dyb[128:]], axis=0))
        dx = jnp.concatenate([top, low_], axis=0)
        fold(usum, wide(dys[j]) * ys[j], j)
        ys[j] = dx
        fold(qin, wide(x) * dx, j)
        return carry

    loop(0, TILES, inside_back, 3)
    stream(from_gates, 8, norm_gates)
    next(reduce)
    aback.finish()
    db_in[...] = jnp.zeros((256, 128), f32)
    dc_in[...] = jnp.zeros((256, 128), f32)

    def d_mix(j, u, d_act):
        m = convolved(j, u)
        sig = sigmoid(m)
        d_m = d_act * (sig * (1.0 + m * (1.0 - sig)))
        ys[j] = d_m
        back_out[:, cols(j)] = low(d_m[0:16])

    def carry_back(j, u):
        s_in, d_s = state(inc, j), state(inc2, j)
        x, dyf = wide(act[j]), wide(dys[j])
        w = spread(toward, j)
        d_w = w * dot_nt(b_in, d_s)
        fold(qw, x * d_w, j)
        db_in[...] += dot(low(w * x), d_s)
        dc_in[...] += dot(low(spread(ecum, j) * dyf), s_in)
        pair = wide(s_in) * wide(d_s)
        prods[pl.ds(2 * j, 1), :] = jnp.sum(pair[:64], axis=0, keepdims=True)
        prods[pl.ds(2 * j + 1, 1), :] = jnp.sum(pair[64:], axis=0, keepdims=True)
        d_mix(j, u, ys[j] + d_w + skip[:, cols(j)] * dyf)

    loop(0, 15, carry_back, 3)
    next(reduce)
    loop(15, 9, carry_back, 3)
    ds = low(dscores[...])
    d_mix(TILES, 0, db_in[...] + dot_tn(ds, c_out))
    d_mix(TILES + 1, 1, dc_in[...] + dot(ds, b_in))
    behind = neighbour(1, back_out, back_in, -1, me > 0)

    q = qin[...] + qw[...]
    d_last = ecum[255:256, :] * jnp.sum(jnp.transpose(prods[...]), axis=0, keepdims=True) + jnp.sum(qw[...], axis=0, keepdims=True)
    at_end = lax.broadcasted_iota(jnp.int32, (256, 128), 0) == 255
    d_l = running_sums(usum[...] - q + jnp.where(at_end, d_last, 0.0), True)
    dt = steps[...]
    raw = dt_in[...] + heads[0:1, :]
    d_raw = (q / jnp.maximum(dt, 1e-30) - heads[1:2, :] * d_l) * sigmoid(raw)
    d_raw = jnp.where(lane < H, d_raw, 0.0)
    headsums[...] = jnp.zeros((8, 128), f32)
    by_pair = jnp.transpose(skips[...])
    headsums[2:3, :] = jnp.sum(by_pair[:64], axis=0, keepdims=True)
    headsums[3:4, :] = jnp.sum(by_pair[64:], axis=0, keepdims=True)
    headsums[0:1, :] = jnp.sum(d_raw, axis=0, keepdims=True)
    headsums[1:2, :] = -jnp.sum(d_l * dt, axis=0, keepdims=True)
    dproj[:, CONVC:CONVC + 128] = low(d_raw)
    dproj[:, CONVC + 128:] = jnp.zeros((256, 128), bf16)
    next(reduce)

    @pl.when(me == 31)
    def _():
        back_in[...] = jnp.zeros((16, CONVC), bf16)

    pl.when(me < 31)(behind.wait_recv)

    def conv_back(j, u):
        d_m = ys[j]
        shift[u, 0:8, :] = wide(halo_in[:, cols(j)])[8:16, :]
        shift[u, 8:264, :] = wide(conv_in[:, cols(j)])
        for k in range(4):
            sums[k:k + 1, cols(j)] = jnp.sum(d_m * shift[u, 5 + k:261 + k, :], axis=0, keepdims=True)
        sums[4:5, cols(j)] = jnp.sum(d_m, axis=0, keepdims=True)
        shift2[u, 0:256, :] = d_m
        shift2[u, 256:264, :] = wide(back_in[:, cols(j)])[0:8, :]
        total = taps[3:4, cols(j)] * d_m
        for k in range(3):
            total = total + taps[k:k + 1, cols(j)] * shift2[u, 3 - k:259 - k, :]
        dproj[:, cols(j)] = low(total)

    loop(0, TILES // 2, conv_back, 2)
    shared += [to_sibling(10, dproj.at[:, :1536], sib_dz.at[:, :1536])]
    loop(TILES // 2, TILES // 2 + 2, conv_back, 2)
    shared += [to_sibling(11, dproj.at[:, 1536:], sib_dz.at[:, 1536:])]
    next(reduce)
    links.settle()
    for axis in ("z", "y", "x"):
        for steps_ in (1, 2, 3):
            pl.semaphore_signal(ready, inc=1, device_id={axis: moved(at, axis, steps_)[axis]}, device_id_type=MESH)
    for copy in shared[-2:]:
        copy.wait_recv()

    prefetch(from_late)
    for zh in range(2):
        flip_normed(zh)

        def d_w_late(n, u):
            part = lanes(384 * n, 384)
            total = dot(flipped[:, :256], dproj[:, part]) + dot(flipped[:, 256:], sib_dz[:, part])
            src[zh, :, :, :, :, part] = low(total).reshape(4, 2, 3, 16, 384)

        loop(0, 9, d_w_late, 3)
    for k in range(2):
        src[k, :, :, :, :, 3456:3584] = jnp.zeros((4, 2, 3, 16, 128), bf16)
    work.finish(g_in, 0, DI, g_o)
    pl.semaphore_wait(ready, 9)
    after = Links(l_send, l_recv)
    width = WIDE - DI
    work = Scatter(at, after, src.at[:, :, :, :, :, pl.ds(0, width)], width, False, rest, last_late, 2 * DI)
    reduce = work.steps()
    next(reduce)

    def norm_late(k, w):
        d_norm[:, :1536] += dot_nt(dproj[:, lanes(384 * k, 384)], w)

    stream(from_late, 9, norm_late)
    prefetch(from_out)

    hidden_load.wait()
    stat[...] = jnp.zeros((256, 128), f32)
    coef[...] = jnp.zeros((256, 128), f32)

    def norm_sums(j, u):
        v = wide(hidden[:, cols(j)])
        stat[...] += v * v
        coef[...] += v * (norm_gain[:, cols(j)] * d_norm[:, cols(j)])

    loop(0, 12, norm_sums, 4)
    scale = lax.rsqrt(jnp.sum(stat[...], axis=1, keepdims=True) * (1.0 / 1536) + epsilon)
    factor = scale * scale * scale * (jnp.sum(coef[...], axis=1, keepdims=True) * (1.0 / 1536))
    stat[...] = jnp.broadcast_to(scale, (256, 128))
    coef[...] = jnp.broadcast_to(factor, (256, 128))

    def norm_back(j, u):
        v, dn = wide(hidden[:, cols(j)]), d_norm[:, cols(j)]
        sums[7:8, cols(j)] = jnp.sum(dn * v * stat[...], axis=0, keepdims=True)
        d_norm[:, cols(j)] = wide(given_out[:, cols(j)]) + stat[...] * norm_gain[:, cols(j)] * dn - v * coef[...]

    loop(0, 12, norm_back, 4)
    hidden_copy = pltpu.make_async_copy(d_norm.at[:, :1536], d_hidden, out_sem.at[1])
    hidden_copy.start()
    whole[:, :CONVC] = sums[...]
    whole[:, CONVC:CONVC + 128] = headsums[...]
    whole[:, CONVC + 128:] = jnp.zeros((8, 128), f32)
    tiny = Links(t_send, t_recv)
    small = small_steps(at, tiny, whole, core_sum, core_other, rounds)
    next(small)
    next(reduce)
    next(small)
    stream(from_out, 8, make_out)
    sib_branch[...] = low(out_sum[:, :1536])
    out_copy = pltpu.make_async_copy(sib_branch, out, out_sem.at[0])
    out_copy.start()
    for _ in reduce:
        next(small)
    next(small)
    own_slices(at, whole, o_taps, o_bias, o_norm, o_gate, o_dt, o_rates, o_skip)
    work.finish(g_in, DI, PROJ - DI)
    after.finish()
    tiny.finish()
    for copy in shared:
        copy.wait_send()
    out_copy.wait()
    hidden_copy.wait()
    pl.when(me < 31)(front.wait_send)
    pl.when(me > 0)(behind.wait_send)
    decays.wait_send()
    aback.end()


def mixer(normed, given_out, taps, gain, norm_gain, dt_bias, rates, d_skip, hidden, w_late, part_w):
    f32, bf16 = jnp.float32, jnp.bfloat16
    tile, half, late = (256, 128), (16, CONVC), WIDE - DI
    vm = pltpu.VMEM
    dma = pltpu.SemaphoreType.DMA
    scratch = [
        vm((1, DI), f32), vm((8, 128), f32),
        vm((256, CONVC), bf16), vm(tile, f32), vm((256, late), bf16), vm((8, CONVC), f32), vm((8, 128), f32),
        vm((256, DI), f32), vm((256, DI), f32),
        vm((256, DI), bf16), vm((256, DI), bf16), vm((256, 768), bf16), vm((256, 1536), bf16), vm((256, 1536), bf16), vm((256, late), bf16),
        vm((2, 4, 2, 3, 16, 2 * DI), bf16), vm((BUFFERS, 1536, 384), bf16), dma((BUFFERS,)), vm((384, 512), bf16), dma((3,)), pltpu.SemaphoreType.REGULAR,
        vm((TILES + 2,) + tile, bf16), vm((TILES + 2,) + tile, f32), vm((TILES,) + tile, bf16),
        vm((3, 264, 128), f32), vm((2, 264, 128), f32), vm(half, bf16), vm(half, bf16), vm(half, bf16), vm(half, bf16),
        vm(tile, f32), vm(tile, f32), vm(tile, f32), vm(tile, f32), vm((128, 256), f32), vm((256, 256), f32), vm((256, 256), f32),
        vm(tile, f32), vm(tile, f32), vm(tile, f32), vm((128, 128), f32), vm(tile, f32), vm(tile, f32), vm(tile, f32), vm(tile, f32),
        vm((16, 128), f32), vm((128, 128), f32), vm((3072, 128), bf16), vm((3072, 128), bf16), vm((3072, 128), bf16),
    ]
    scratch += [vm((16, 112, 128), bf16), vm((16, 112, 128), bf16), vm((16, 96, 128), bf16)]
    scratch += [vm((1536, 128), bf16), vm((1536, 128), bf16)]
    scratch += [dma((12,)), dma((12,)), dma((4, 16)), dma((4, 16)), dma((4,)), dma((64,)), dma((64,)), dma((40,)), dma((40,)), dma((12,)), dma((12,))]
    scratch += [vm((8, 2 * SMALL), f32), vm((8, SMALL), f32), vm((8, SMALL), f32)] + [vm((4, 8, SMALL), f32)] * 3
    scratch += last_scratch(2 * DI, 768) + last_scratch(late, late // 4) + scatter_scratch(2 * DI)
    near, far = pl.BlockSpec(memory_space=pltpu.VMEM), pl.BlockSpec(memory_space=pl.ANY)
    return pl.pallas_call(
        mixer_kernel,
        out_shape=[jax.ShapeDtypeStruct((256, 1536), bf16), jax.ShapeDtypeStruct((256, 1536), f32),
                   jax.ShapeDtypeStruct((12, PROJ), f32), jax.ShapeDtypeStruct((24, 1536), f32)]
        + [jax.ShapeDtypeStruct(size, f32) for size in ((4, 26), (1, 26), (1, 12), (1, 24), (1, H), (1, H), (1, H))]
        + [jax.ShapeDtypeStruct(part_w.shape, bf16)],
        in_specs=[near] * 8 + [far] * 3,
        out_specs=[far] * 2 + [near] * 9 + [far],
        scratch_shapes=scratch,
        input_output_aliases={10: 11},
        compiler_params=pltpu.CompilerParams(collective_id=2, has_side_effects=True, vmem_limit_bytes=63 << 20),
        name="mixer",
    )(normed, given_out, taps, gain, norm_gain, dt_bias, rates, d_skip, hidden, w_late, part_w)


def rms_scale(values, gain):
    return values * lax.rsqrt(jnp.mean(values * values, axis=-1, keepdims=True) + epsilon) * gain


def shards(
    hidden,
    cotangent,
    in_w,
    out_w,
    conv_w,
    conv_b,
    norm_gain,
    gate_gain,
    dt_bias,
    decay_rates,
    d_skip,
):
    w_late, w_early = gather(in_w, out_w, conv_w, conv_b, norm_gain, gate_gain)
    spare = w_late[:, :, :, :, :, :, PARAMS - DI:].reshape(128, 12, 128).astype(jnp.float32)
    w_conv_f = spare[:, :4, :26].transpose(1, 0, 2).reshape(KW, CONVC)
    b_conv_f = spare[:, 4, :26].reshape(CONVC)
    gain_norm_f = spare[:, 5, :12].reshape(1536)
    gain_gate_f = spare[:, 6, :24].reshape(DI)
    residual = hidden[0].astype(jnp.float32)
    normed = rms_scale(residual, gain_norm_f).astype(jnp.bfloat16)
    taps = jnp.pad(jnp.concatenate([w_conv_f, b_conv_f[None]]), ((0, 3), (0, 0)))
    result, d_hidden, g_in, g_out, d_taps, d_bias, d_norm_gain, d_gate_gain, d_dt, d_rates, d_skips, _ = mixer(
        normed, cotangent[0], taps, gain_gate_f[None], gain_norm_f[None],
        dt_bias[None], decay_rates[None], d_skip[None], hidden[0], w_late, w_early)
    return (
        result[None],
        d_hidden[None],
        g_in,
        g_out,
        d_taps,
        d_bias[0],
        d_norm_gain[0],
        d_gate_gain[0],
        d_dt[0],
        d_rates[0],
        d_skips[0],
    )


def solution(mesh):
    grid = Mesh(mesh.devices.reshape(4, 4, 4, 2), ALL)
    tokens = P("z", SEQ, None)
    placed = (
        tokens,
        tokens,
        P(ALL, None),
        P(ALL, None),
        P(None, ALL),
        P(ALL),
        P(ALL),
        P(ALL),
        P(),
        P(),
        P(),
    )
    return jax.shard_map(
        shards,
        mesh=grid,
        in_specs=placed,
        out_specs=(tokens, tokens, P(ALL, None), P(ALL, None), P(None, ALL), P(ALL), P(ALL), P(ALL), P(), P(), P()),
        check_vma=False,
    )
```

```python
import functools
import jax
import jax.numpy as jnp
from jax import lax
from jax.experimental import pallas as pl
from jax.experimental.pallas import tpu as pltpu
from jax.sharding import PartitionSpec as P, Mesh

MESH = pl.DeviceIdType.MESH
ALL = ("z", "y", "x", "c")
ORDERS = (("z", "y", "x"), ("y", "x", "z"), ("x", "z", "y"))
PARTS = range(3)


class Links:
    def __init__(self, send, recv):
        self.send, self.recv, self.used, self.sent = send, recv, 0, []

    def copy(self, src, dst, device):
        k = self.used
        self.used += 1
        made = pltpu.make_async_remote_copy(
            src_ref=src, dst_ref=dst, send_sem=self.send.at[k], recv_sem=self.recv.at[k],
            device_id=device, device_id_type=MESH)
        made.start()
        self.sent.append(made)
        return made

    def settle(self):
        for made in self.sent:
            made.wait_send()
        self.sent = []

    finish = settle


def place():
    return {name: lax.axis_index(name) for name in ALL}


def block(ref, part, core, at, have, half=None):
    z, y, x = at["z"], at["y"], at["x"]
    wide = ref.shape[-1]
    full = slice(None)
    zh, zl = (full, full) if "z" in have else (z // 2, lax.rem(z, 2))
    ys = full if "y" in have else y
    first, count = (0, wide) if "x" in have else (x * (wide // 4), wide // 4)
    if half is not None:
        if "y" in have:
            ys = pl.ds(2 * half, 2)
        elif "z" in have:
            zh = pl.ds(half, 1)
        else:
            near = -(-count // 256) * 128
            first, count = (first, near) if half == 0 else (first + near, count - near)
    cols = full if "x" in have and count == wide else pl.ds(first if isinstance(first, int) else pl.multiple_of(first, 128), count)
    return ref.at[core, zh, ys, zl, part, :, cols]


def moved(at, axis, steps):
    return {**at, axis: lax.rem(at[axis] + steps + 4, 4)}


def targets(at):
    z, x, c = at["z"], at["x"], at["c"]
    to_z, to_c = 2 * lax.rem(z, 2) + x // 2, z // 2
    return to_z, to_c, 2 * c + z // 2, jnp.logical_and(to_z == z, to_c == c)


class Ring:
    def __init__(self, links, at, full, phase, share):
        self.links, self.at, self.full, self.phase, self.share = links, at, full, phase, share
        self.c = at["c"]
        self.shared = []

    def to_sibling(self, ref):
        if self.share:
            self.shared.append(self.links.copy(ref, ref, {"c": 1 - self.c}))

    def start(self):
        self.near = {}
        for part in PARTS:
            have, axis = ORDERS[part][:self.phase], ORDERS[part][self.phase]
            mine = block(self.full, part, self.c, self.at, have)
            self.near[part] = [self.links.copy(mine, mine, {axis: moved(self.at, axis, steps)[axis]}) for steps in (1, -1)]

    def turn(self):
        self.far = {}
        for part in PARTS:
            have, axis = ORDERS[part][:self.phase], ORDERS[part][self.phase]
            self.far[part] = []
            for way, steps in ((0, 1), (1, -1)):
                self.near[part][way].wait_recv()
                piece = block(self.full, part, self.c, moved(self.at, axis, -steps), have, way)
                self.far[part].append(self.links.copy(piece, piece, {axis: moved(self.at, axis, steps)[axis]}))
        for part in PARTS:
            have, axis = ORDERS[part][:self.phase], ORDERS[part][self.phase]
            for steps in (1, -1):
                self.to_sibling(block(self.full, part, self.c, moved(self.at, axis, -steps), have))

    def finish(self):
        for part in PARTS:
            have, axis = ORDERS[part][:self.phase], ORDERS[part][self.phase]
            for way in (0, 1):
                self.far[part][way].wait_recv()
            self.to_sibling(block(self.full, part, self.c, moved(self.at, axis, 2), have))

    def share_held(self):
        for part in PARTS:
            self.to_sibling(block(self.full, part, self.c, self.at, ORDERS[part][:self.phase]))

    def end(self):
        for copy in self.shared:
            copy.wait_recv()


def gather_kernel(*refs):
    (in_w, out_w, conv_w, conv_b, norm_gain, gate_gain), fulls, shards, (late, early), refs = refs[:6], refs[6:8], refs[8:10], refs[10:12], refs[12:]
    stages, stage_o, landed, unit, (send, recv, first_recv, own) = refs[:2], refs[2], refs[3:5], refs[5:7], refs[7:]
    at = place()
    z, y, x, c = (at[name] for name in ALL)
    to_z, to_c, from_z, home = targets(at)
    slot = 2 * lax.rem(x, 2) + c
    barrier = pltpu.get_barrier_semaphore()
    for axis in ("z", "y", "x"):
        for steps in (1, 2, 3):
            pl.semaphore_signal(barrier, inc=1, device_id={axis: moved(at, axis, steps)[axis]}, device_id_type=MESH)
    pl.semaphore_signal(barrier, inc=1, device_id={"c": 1 - c}, device_id_type=MESH)
    for k in range(4):
        sx, sc = 2 * lax.rem(z, 2) + k // 2, k % 2

        @pl.when(jnp.logical_not(jnp.logical_and(home, jnp.logical_and(sx == x, sc == c))))
        def _():
            pl.semaphore_signal(barrier, inc=1, device_id=(from_z, y, sx, jnp.int32(sc)), device_id_type=MESH)

    def wide_(ref):
        return ref[...].astype(jnp.float32)

    late[...] = jnp.zeros(late.shape, jnp.float32)
    early[...] = jnp.zeros(early.shape, jnp.float32)
    late[0:12, 0:3376] = in_w[:, 3072:6448].astype(jnp.float32)
    late[0:4, 3456:3482] = wide_(conv_w)
    late[4:5, 3456:3482] = wide_(conv_b)
    late[5:6, 3456:3468] = wide_(norm_gain)
    late[6:7, 3456:3480] = wide_(gate_gain)
    held = wide_(out_w)
    for tx in range(4):
        early[0:12, 1536 * tx:1536 * tx + 768] = in_w[:, 768 * tx:768 * tx + 768].astype(jnp.float32)
        for b in range(2):
            start = 1536 * tx + 768 + 384 * b
            early[0:12, start:start + 384] = held[12 * b:12 * b + 12, 384 * tx:384 * tx + 384]
    shards[0][...] = late[...].astype(jnp.bfloat16)
    shards[1][...] = early[...].astype(jnp.bfloat16)
    pl.semaphore_wait(barrier, 14 - home.astype(jnp.int32))

    links = Links(send, recv)
    first = []
    for i in range(2):
        wide = shards[i].shape[1] // 4
        for tx in range(4):
            k = links.used
            links.used += 1
            src = shards[i].at[:, pl.ds(tx * wide, wide)]
            remote = pltpu.make_async_remote_copy(
                src_ref=src, dst_ref=landed[i].at[slot], send_sem=send.at[k], recv_sem=first_recv.at[4 * i + slot],
                device_id=(to_z, y, jnp.int32(tx), to_c), device_id_type=MESH)
            local = pltpu.make_async_copy(src, landed[i].at[slot], first_recv.at[4 * i + slot])
            mine = jnp.logical_and(home, x == tx)
            pl.when(jnp.logical_not(mine))(remote.start)
            pl.when(mine)(local.start)
            first.append((remote, mine))
    kept, direct = [], []
    for i in range(2):
        wide = stages[i].shape[1]
        for k in range(4):
            pltpu.make_async_copy(landed[i].at[k], landed[i].at[k], first_recv.at[4 * i + k]).wait()
            stages[i][pl.ds(12 * k, 12), :] = landed[i][k, :12, :wide].astype(jnp.float32)
            for b in range(2 * i):
                stage_o[pl.ds(24 * k + 12 * b, 12), :] = landed[i][k, :12, wide + 384 * b:wide + 384 * b + 384].astype(jnp.float32)
        for part in PARTS:
            unit[i][part, :, :wide] = stages[i][pl.ds(16 * part, 16), :].astype(jnp.bfloat16)
            for b in range(2 * i):
                unit[i][part, :, wide + 384 * b:wide + 384 * b + 384] = stage_o[pl.ds(32 * part + 16 * b, 16), :].astype(jnp.bfloat16)
        for part in PARTS:
            axis = ORDERS[part][0]
            there = block(fulls[i], part, c, at, ())
            for steps in (1, 3, 2):
                direct.append(links.copy(unit[i].at[part], there, {axis: moved(at, axis, steps)[axis]}))
            copy = pltpu.make_async_copy(unit[i].at[part], there, own.at[3 * i + part])
            copy.start()
            kept.append(copy)
    rings = [Ring(links, at, fulls[i], 1, False) for i in range(2)]
    for i in range(2):
        for copy in direct[9 * i:9 * i + 9]:
            copy.wait_recv()
        for copy in kept[3 * i:3 * i + 3]:
            copy.wait()
        rings[i].start()
    for ring in rings:
        ring.turn()
    last = Ring(links, at, fulls[0], 2, True)
    rings[0].finish()
    last.start()
    last.share_held()
    rings[1].finish()
    other = Ring(links, at, fulls[1], 2, True)
    other.share_held()
    last.turn()
    last.finish()
    last.end()
    other.end()
    links.finish()
    for remote, mine in first:
        pl.when(jnp.logical_not(mine))(remote.wait_send)


def gather(in_w, out_w, conv_w, conv_b, norm_gain, gate_gain):
    wides = (3584, 6144)
    vm, dma = pltpu.VMEM, pltpu.SemaphoreType.DMA
    return pl.pallas_call(
        gather_kernel,
        out_shape=[jax.ShapeDtypeStruct((2, 2, 4, 2, 3, 16, w), jnp.bfloat16) for w in wides],
        in_specs=[pl.BlockSpec(memory_space=pltpu.VMEM)] * 6,
        out_specs=[pl.BlockSpec(memory_space=pl.ANY)] * 2,
        scratch_shapes=[vm((16, w), jnp.bfloat16) for w in wides] + [vm((16, w), jnp.float32) for w in wides]
        + [vm((48, wides[0] // 4), jnp.float32), vm((48, 768), jnp.float32), vm((96, 384), jnp.float32)]
        + [vm((4, 16, w // 4), jnp.bfloat16) for w in wides]
        + [vm((3, 16, w // 4), jnp.bfloat16) for w in wides]
        + [dma((96,)), dma((96,)), dma((8,)), dma((6,))],
        compiler_params=pltpu.CompilerParams(collective_id=0, has_side_effects=True, vmem_limit_bytes=60 << 20),
        name="gather_weights",
    )(in_w, out_w, conv_w, conv_b[None], norm_gain[None], gate_gain[None])


def span(shape, axis, at):
    cut = [slice(None)] * 5
    if axis == "y":
        cut[1] = pl.ds(at["y"], 1)
    elif axis == "z":
        cut[0], cut[2] = pl.ds(at["z"] // 2, 1), pl.ds(lax.rem(at["z"], 2), 1)
    else:
        cut[4] = pl.ds(pl.multiple_of(at["x"] * (shape[4] // 4), 128), shape[4] // 4)
    return cut


def without(shape, axis):
    zh, y, zl, rows, wide = shape
    return {"y": (zh, 1, zl, rows, wide), "z": (1, y, 1, rows, wide), "x": (zh, y, zl, rows, wide // 4)}[axis]


def halves(shape):
    if shape[1] == 4:
        return 1, ((0, 2), (2, 2))
    if shape[0] == 2:
        return 0, ((0, 1), (1, 1))
    near = -(-shape[4] // 256) * 128
    return 4, ((0, near), (near, shape[4] - near))


def cut_half(cut, shape, half):
    dim, parts = halves(shape)
    start, size = parts[half]
    cut = list(cut)
    old = cut[dim]
    base = 0 if isinstance(old, slice) else old.start
    cut[dim] = pl.ds(pl.multiple_of(base + start, 128) if dim == 4 and not isinstance(base, int) else base + start, size)
    return cut


def half_shape(shape, half):
    dim, parts = halves(shape)
    return tuple(parts[half][1] if k == dim else size for k, size in enumerate(shape))


def add_up(out, terms, shape):
    na, nb, nc = shape[:3]

    def slab(k, carry):
        a, b, d = k // (nb * nc), lax.rem(k // nc, nb), lax.rem(k, nc)
        total = terms[0](a, b, d).astype(jnp.float32)
        for term in terms[1:]:
            total = total + term(a, b, d).astype(jnp.float32)
        out(a, b, d, total)
        return carry

    lax.fori_loop(0, na * nb * nc, slab, 0)


def start_of(cut):
    return 0 if isinstance(cut, slice) else cut.start


def slab_of(ref, cut, shape):
    z0, y0, l0, _, c0 = (start_of(s) for s in cut)
    lead = ref

    def read(a, b, d):
        return lead[z0 + a, y0 + b, l0 + d, :, pl.ds(c0, shape[4])]

    return read


def slab_to(ref, shape):
    def write(a, b, d, value):
        ref[a, b, d] = value.astype(ref.dtype)

    return write


ALL_CUT = [slice(None)] * 5


def scatter_scratch(wide):
    vm, f32 = pltpu.VMEM, jnp.float32
    scratch = []
    size = {part: (2, 4, 2, 16, wide) for part in PARTS}
    for phase in range(3):
        for part in PARTS:
            shape = without(size[part], ORDERS[part][2 - phase])
            scratch += [vm(shape, jnp.bfloat16)] * (3 if phase else 2)
            if phase == 0:
                scratch += [vm(half_shape(shape, way), jnp.bfloat16) for way in (0, 1)]
            size[part] = shape
    return scratch


def last_scratch(wide, first):
    vm, f32 = pltpu.VMEM, jnp.float32
    scratch = [vm((48, first), f32), vm((96, 384) if wide > 4 * first else (8, 128), f32), vm((4, 16, wide // 4), f32), vm((4, 16, wide // 4), f32)]
    return scratch + [pltpu.SemaphoreType.DMA((4,))] * 2


class Scatter:
    def __init__(self, at, links, source, wide, split, refs, last, narrow=None):
        take = iter(refs)
        self.at, self.links, self.split = at, links, split
        self.near, self.relay = {}, {}
        for phase in range(3):
            for s in PARTS:
                self.near[s, phase] = [next(take) for _ in range(3 if phase else 2)]
                self.relay[s] = [next(take), next(take)] if phase == 0 else self.relay[s]
        if narrow:
            def less(ref):
                return ref.at[:, :, :, :, pl.ds(0, ref.shape[4] * wide // narrow)]

            self.near = {key: [less(ref) for ref in held] for key, held in self.near.items()}
            self.relay = {key: [less(ref) for ref in held] for key, held in self.relay.items()}
        self.fin, self.fin_o, self.staged, self.landed, self.last, self.own = last
        self.size = {s: (2, 4, 2, 16, wide) for s in PARTS}
        self.source = {s: source.at[:, :, :, s] for s in PARTS}

    def add(self, phase, s, axis, shape):
        terms = [slab_of(self.source[s], span(self.size[s], axis, self.at), shape)]
        terms += [slab_of(buf, ALL_CUT, shape) for buf in self.near[s, phase]]
        if phase < 2:
            held = self.near[s, phase][0]
            add_up(slab_to(held, shape), terms, shape)
            self.source[s], self.size[s] = held, shape
            return
        total = terms[0](0, 0, 0).astype(jnp.float32)
        for term in terms[1:]:
            total = total + term(0, 0, 0).astype(jnp.float32)
        first = self.fin.shape[1]
        self.fin[pl.ds(16 * s, 16), :] = total[:, :first]
        if self.split:
            for b in range(2):
                self.fin_o[pl.ds(32 * s + 16 * b, 16), :] = total[:, first + 384 * b:first + 384 * b + 384]

    def steps(self):
        at, links, size, source = self.at, self.links, self.size, self.source
        sent, lent = {}, {}
        for s in PARTS:
            axis = ORDERS[s][2]
            shape = without(size[s], axis)
            lent[s] = []
            for way, step in ((0, 1), (1, 3)):
                src = source[s].at[tuple(cut_half(span(size[s], axis, moved(at, axis, 2)), shape, way))]
                lent[s].append(links.copy(src, self.relay[s][way], {axis: moved(at, axis, step)[axis]}))
        for s in PARTS:
            axis = ORDERS[s][2]
            shape = without(size[s], axis)
            sent[s] = []
            for way, step in ((0, 1), (1, 3)):
                src = source[s].at[tuple(cut_half(span(size[s], axis, moved(at, axis, step)), shape, 1 - way))]
                dst = self.near[s, 0][way].at[tuple(cut_half(ALL_CUT, shape, 1 - way))]
                sent[s].append(links.copy(src, dst, {axis: moved(at, axis, step)[axis]}))
        yield
        for s in PARTS:
            axis = ORDERS[s][2]
            shape = without(size[s], axis)
            for way, step in ((0, 1), (1, 3)):
                lent[s][way].wait_recv()
                hs = half_shape(shape, way)
                cut = cut_half(span(size[s], axis, moved(at, axis, step)), shape, way)
                buf = self.relay[s][way]
                add_up(slab_to(buf, hs), [slab_of(source[s], cut, hs), slab_of(buf, ALL_CUT, hs)], hs)
                dst = self.near[s, 0][way].at[tuple(cut_half(ALL_CUT, shape, way))]
                sent[s].append(links.copy(buf, dst, {axis: moved(at, axis, step)[axis]}))
        yield
        for phase in (1, 2):
            for s in PARTS:
                for copy in sent[s]:
                    copy.wait_recv()
                axis = ORDERS[s][3 - phase]
                self.add(phase - 1, s, axis, without(size[s], axis))
                axis = ORDERS[s][2 - phase]
                sent[s] = []
                for k in (1, 3, 2):
                    src = source[s].at[tuple(span(size[s], axis, moved(at, axis, k)))]
                    sent[s].append(links.copy(src, self.near[s, phase][k - 1], {axis: moved(at, axis, k)[axis]}))
            yield
        for s in PARTS:
            for copy in sent[s]:
                copy.wait_recv()
            axis = ORDERS[s][0]
            self.add(2, s, axis, without(size[s], axis))
        z, y, x, c = (at[name] for name in ALL)
        _, _, from_z, home = targets(at)
        self.final = []
        first, staged, landed = self.fin.shape[1], self.staged, self.landed
        for k in range(4):
            sx, sc = 2 * lax.rem(z, 2) + k // 2, k % 2
            staged[k] = jnp.zeros(staged.shape[1:], jnp.float32)
            staged[k, :12, :first] = self.fin[pl.ds(12 * k, 12), :]
            for b in range(2 if self.split else 0):
                staged[k, :12, first + 384 * b:first + 384 * b + 384] = self.fin_o[pl.ds(24 * k + 12 * b, 12), :]
            mine = jnp.logical_and(home, jnp.logical_and(sx == x, sc == c))
            remote = pltpu.make_async_remote_copy(
                src_ref=staged.at[k], dst_ref=landed.at[x], send_sem=self.own.at[k], recv_sem=self.last.at[x],
                device_id=(from_z, y, sx, jnp.int32(sc)), device_id_type=MESH)
            local = pltpu.make_async_copy(staged.at[k], landed.at[x], self.last.at[x])
            pl.when(jnp.logical_not(mine))(remote.start)
            pl.when(mine)(local.start)
            self.final.append((remote, mine))
        yield

    def finish(self, out, base, limit, out_o=None):
        first = self.fin.shape[1]
        for tx in range(4):
            pltpu.make_async_copy(self.landed.at[tx], self.landed.at[tx], self.last.at[tx]).wait()
            count = min(first, limit - tx * first)
            out[:, base + tx * first:base + tx * first + count] = self.landed[tx, :12, :count]
            for b in range(2 if self.split else 0):
                out_o[pl.ds(12 * b, 12), pl.ds(tx * 384, 384)] = self.landed[tx, :12, first + 384 * b:first + 384 * b + 384]
        for remote, mine in self.final:
            pl.when(jnp.logical_not(mine))(remote.wait_send)


SMALL = 1792


def small_steps(at, links, whole, core_sum, core_other, rounds):
    c = at["c"]

    def side(core):
        return pl.ds(pl.multiple_of(SMALL * core, 128), SMALL)

    going = [links.copy(whole.at[:, side(1 - c)], core_sum, {"c": 1 - c})]
    yield
    going[0].wait_recv()
    total = core_sum[...] + whole[:, side(c)]
    for axis, held in zip(("x", "y", "z"), rounds):
        held[at[axis]] = total
        mine = held.at[at[axis]]
        going = [links.copy(mine, mine, {axis: moved(at, axis, steps)[axis]}) for steps in (1, 3, 2)]
        yield
        for copy in going:
            copy.wait_recv()
        total = held[0]
        for j in range(1, 4):
            total = total + held[j]
    whole[:, side(c)] = total
    going = [links.copy(whole.at[:, side(c)], core_other, {"c": 1 - c})]
    yield
    going[0].wait_recv()
    links.settle()
    whole[:, side(1 - c)] = core_other[...]
    yield


def own_slices(at, whole, d_taps, d_bias, d_norm_gain, d_gate_gain, d_dt_bias, d_rates, d_skip):
    index = 32 * at["z"] + 8 * at["y"] + 2 * at["x"] + at["c"]
    total = whole[...]

    def own(size, each):
        return pltpu.roll(total[:, :size], lax.rem(size - each * index, size), 1)

    value = own(CONVC, 26)
    d_taps[...] = value[0:4, :26]
    d_bias[...] = value[4:5, :26]
    d_gate_gain[...] = own(DI, 24)[5:6, :24]
    d_norm_gain[...] = own(1536, 12)[7:8, :12]
    by_head = total[:, CONVC:CONVC + 128]
    d_dt_bias[...] = by_head[0:1, :48]
    d_rates[...] = by_head[1:2, :48]
    row = lax.broadcasted_iota(jnp.int32, (128, 128), 0)
    col = lax.broadcasted_iota(jnp.int32, (128, 128), 1)
    heads = jnp.zeros((8, 128), jnp.float32)
    for b in range(2):
        ones = jnp.where(2 * row + b == col, 1.0, 0.0).astype(jnp.bfloat16)
        for part in split3(jnp.broadcast_to(by_head[2 + b:3 + b], (8, 128))):
            heads = heads + jnp.dot(part, ones, preferred_element_type=jnp.float32)
    d_skip[...] = heads[0:1, :48]


H = 48
P_SIZE = 64
KW = 4
DI = 3072
CONVC = 3328
PROJ = 6448
WIDE = 6656
PARAMS = 6528
SEQ = ("y", "x", "c")
epsilon = 1e-05


TILES = 24
BUFFERS = 3


def dot(a, b):
    return jnp.dot(a, b, preferred_element_type=jnp.float32)


def dot_nt(a, b):
    return lax.dot_general(a, b, (((1,), (1,)), ((), ())), preferred_element_type=jnp.float32)


def dot_tn(a, b):
    return lax.dot_general(a, b, (((0,), (0,)), ((), ())), preferred_element_type=jnp.float32)


def low(v):
    return v.astype(jnp.bfloat16)


def wide(v):
    return v.astype(jnp.float32)


def split3(v):
    a = low(v)
    b = low(v - wide(a))
    return a, b, low(v - wide(a) - wide(b))


def running_sums(v, backward):
    row = lax.broadcasted_iota(jnp.int32, (256, 256), 0)
    col = lax.broadcasted_iota(jnp.int32, (256, 256), 1)
    ones = low(jnp.where(row <= col if backward else row >= col, 1.0, 0.0))
    return sum(dot(ones, part) for part in split3(v))


def sigmoid(v):
    return 1.0 / (1.0 + jnp.exp(-v))


def loop(first, count, body, unroll):
    def step(k, carry):
        for u in range(unroll):
            body(first + k * unroll + u, u)
        return carry
    lax.fori_loop(0, count // unroll, step, 0)


def mixer_kernel(normed, given_out, taps, gain, norm_gain, dt_bias, rates, d_skip, hidden_in, w_late, part_w,
                 out, d_hidden, g_in, g_o, o_taps, o_bias, o_norm, o_gate, o_dt, o_rates, o_skip, weights_,
                 skip, heads,
                 conv_in, dt_in, dproj, sums, headsums,
                 gates, db, branch, dz, sib_normed, sib_given, sib_branch, sib_dz, src, chunk, chunk_sem, flipped, out_sem, ready,
                 act, ys, dys, shift, shift2, halo_out, halo_in, back_out, back_in,
                 cum, ecum, toward, steps, rows_a, scores, dscores, usum, qin, qw, prods, stat, coef, db_in, dc_in, decay,
                 skips, loc, inc, inc2, *rest):
    f32, bf16 = jnp.float32, jnp.bfloat16
    snd, rcv, ret, sib, across = rest[:5]
    (sib_send, sib_recv, a_send, a_recv, h_sem, rs_send, rs_recv, l_send, l_recv, t_send, t_recv), rest = rest[5:16], rest[16:]
    whole, core_sum, core_other, rounds, last_early, last_late, rest = rest[0], rest[1], rest[2], rest[3:6], rest[6:12], rest[12:18], rest[18:]
    at = place()
    z, core = lax.axis_index("z"), lax.axis_index("c")
    chip = 4 * lax.axis_index("y") + lax.axis_index("x")
    me = 2 * chip + core
    lane = lax.broadcasted_iota(jnp.int32, (256, 128), 1)
    first_head = lane < 64

    def device(k):
        return (z, k // 8, lax.rem(k // 2, 4), lax.rem(k, 2))

    def same_core(k):
        return (z, k // 4, lax.rem(k, 4), core)

    def others(body):
        def step(k, carry):
            body(lax.rem(chip + k, 16))
            return carry
        lax.fori_loop(1, 16, step, 0)

    barrier = pltpu.get_barrier_semaphore()
    others(lambda k: pl.semaphore_signal(barrier, inc=1, device_id=same_core(k), device_id_type=MESH))
    pl.semaphore_signal(barrier, inc=1, device_id={"c": 1 - core}, device_id_type=MESH)
    beside = jnp.where(core == 1, me + 1, me - 1)
    inner = jnp.logical_and(beside >= 0, beside < 32)

    @pl.when(inner)
    def _():
        pl.semaphore_signal(barrier, inc=1, device_id=device(beside), device_id_type=MESH)

    for steps_ in (1, 2, 3):
        pl.semaphore_signal(barrier, inc=1, device_id={"z": moved(at, "z", steps_)["z"]}, device_id_type=MESH)
    to_z, to_c, _, home = targets(at)
    for tx in range(4):
        @pl.when(jnp.logical_not(jnp.logical_and(home, at["x"] == tx)))
        def _():
            pl.semaphore_signal(barrier, inc=1, device_id=(to_z, at["y"], jnp.int32(tx), to_c), device_id_type=MESH)

    def exchange(e, source, target, own):
        def go(k):
            pltpu.make_async_remote_copy(
                src_ref=source(k), dst_ref=target(chip), send_sem=a_send.at[e, k], recv_sem=a_recv.at[e, chip],
                device_id=same_core(k), device_id_type=MESH).start()
        others(go)
        own()

    def arrived(e, target):
        others(lambda k: pltpu.make_async_copy(target(k), target(k), a_recv.at[e, k]).wait())

    def left(e, source):
        others(lambda k: pltpu.make_async_copy(source(k), source(k), a_send.at[e, k]).wait())

    def to_sibling(e, src, dst):
        made = pltpu.make_async_remote_copy(
            src_ref=src, dst_ref=dst, send_sem=sib_send.at[e], recv_sem=sib_recv.at[e],
            device_id={"c": 1 - core}, device_id_type=MESH)
        made.start()
        return made

    def neighbour(k, src, dst, steps_, on):
        made = pltpu.make_async_remote_copy(
            src_ref=src, dst_ref=dst, send_sem=h_sem.at[2 * k], recv_sem=h_sem.at[2 * k + 1],
            device_id=device(lax.rem(me + steps_ + 32, 32)), device_id_type=MESH)
        pl.when(on)(made.start)
        return made

    def lanes(start, size):
        return pl.ds(pl.multiple_of(start, 128), size)

    def from_late(k, slot):
        pltpu.make_async_copy(
            w_late.at[:, :, :, :, :, :, lanes(384 * k, 384)],
            chunk.at[slot].reshape(2, 2, 4, 2, 3, 16, 384), chunk_sem.at[slot]).start()

    def prefetch(fetch):
        for slot in range(BUFFERS):
            fetch(jnp.int32(slot), slot)

    prefetch(from_late)
    heads[...] = jnp.zeros((8, 128), f32)
    for k, ref in enumerate((dt_bias, rates, d_skip)):
        heads[k:k + 1, :H] = ref[...]
    by_head_ = heads[2:3, :]
    for j in range(TILES):
        skip[:, 128 * j:128 * j + 128] = jnp.where(
            lane[0:1] < 64, jnp.broadcast_to(by_head_[:, 2 * j:2 * j + 1], (1, 128)), jnp.broadcast_to(by_head_[:, 2 * j + 1:2 * j + 2], (1, 128)))

    pl.semaphore_wait(barrier, 23 + inner.astype(jnp.int32) - home.astype(jnp.int32))
    links = Links(rs_send, rs_recv)
    ring = Ring(links, at, weights_, 2, True)
    ring.start()

    def from_gates(k, slot):
        pltpu.make_async_copy(
            weights_.at[:, :, :, :, :, :, lanes(1536 * (k // 2) + 384 * lax.rem(k, 2), 384)],
            chunk.at[slot].reshape(2, 2, 4, 2, 3, 16, 384), chunk_sem.at[slot]).start()

    def from_out(k, slot):
        for b in range(2):
            pltpu.make_async_copy(
                weights_.at[k // 4, :, :, :, :, :, lanes(1536 * lax.rem(k, 4) + 768 + 384 * b, 384)],
                chunk.at[slot].reshape(2, 4, 2, 3, 32, 384).at[:, :, :, :, pl.ds(16 * b, 16)], chunk_sem.at[slot]).start()

    def stream(fetch, count, use):
        def round_(n, u):
            for slot in range(BUFFERS):
                k = BUFFERS * n + slot

                @pl.when(k < count)
                def _():
                    pltpu.make_async_copy(chunk.at[slot], chunk.at[slot], chunk_sem.at[slot]).wait()
                    use(k, chunk[slot])

                @pl.when(k + BUFFERS < count)
                def _():
                    fetch(k + BUFFERS, slot)

        loop(0, -(-count // BUFFERS), round_, 1)

    def project(k, w):
        value = dot(normed[...], w)

        @pl.when(k < 8)
        def _():
            conv_in[:, lanes(384 * jnp.minimum(k, 7), 384)] = low(value)

        @pl.when(k == 8)
        def _():
            conv_in[:, 3072:CONVC] = low(value[:, :256])
            dt_in[...] = value[:, 256:]

    stream(from_late, 9, project)
    halo_out[...] = conv_in[240:256, :]
    front = neighbour(0, halo_out, halo_in, 1, me < 31)
    shared = [to_sibling(5, normed.at[:, lanes(768 * (1 - core), 768)], sib_normed), to_sibling(6, given_out, sib_given)]


    raw = dt_in[...] + heads[0:1, :]
    dt = jnp.maximum(raw, 0.0) + jnp.log1p(jnp.exp(-jnp.abs(raw)))
    total = running_sums(-heads[1:2, :] * dt, False)
    last = total[255:256, :]
    steps[...] = dt
    cum[...] = total
    ecum[...] = jnp.exp(total)
    toward[...] = jnp.exp(last - total) * dt
    rows_a[...] = jnp.transpose(total - jnp.log(dt))

    @pl.when(me == 0)
    def _():
        halo_in[...] = jnp.zeros((16, CONVC), bf16)

    pl.when(me > 0)(front.wait_recv)

    def cols(j):
        return pl.ds(pl.multiple_of(128 * j, 128), 128)

    def convolved(j, u):
        shift[u, 0:8, :] = wide(halo_in[:, cols(j)])[8:16, :]
        shift[u, 8:264, :] = wide(conv_in[:, cols(j)])
        total = taps[4:5, cols(j)] + taps[0:1, cols(j)] * shift[u, 5:261, :]
        for k in range(1, 4):
            total = total + taps[k:k + 1, cols(j)] * shift[u, 5 + k:261 + k, :]
        return total

    def conv(j, u):
        total = convolved(j, u)
        act[j] = low(total * sigmoid(total))

    loop(0, TILES + 2, conv, 2)
    b_in, c_out = act[TILES], act[TILES + 1]
    scores[...] = dot_nt(c_out, b_in)

    def pick(ref, j):
        turned = pltpu.roll(ref[...], lax.rem(128 - 2 * j, 128), 1)
        return jnp.broadcast_to(turned[:, 0:1], (256, 128)), jnp.broadcast_to(turned[:, 1:2], (256, 128))

    def spread(ref, j):
        one, two = pick(ref, j)
        return jnp.where(first_head, one, two)

    def by_head(v):
        zero = jnp.zeros_like(v)
        return jnp.where(first_head[:v.shape[0]], v, zero), jnp.where(first_head[:v.shape[0]], zero, v)

    def fold(acc, prod, j):
        row = lax.broadcasted_iota(jnp.int32, (256, 128), 0)
        col = lax.broadcasted_iota(jnp.int32, (256, 128), 1)
        pickers = low(jnp.where(lax.rem(row, 128) // 64 + 2 * j == col, 1.0, 0.0))
        top = low(prod)
        both = jnp.concatenate([top, low(prod - wide(top))], axis=1)
        acc[...] += dot(both, pickers)

    def rows128(j):
        return pl.ds(pl.multiple_of(128 * j, 128), 128)

    mine, given = 12 * core, 12 * (1 - core)
    row128 = lax.broadcasted_iota(jnp.int32, (128, 128), 0)
    row16 = lax.broadcasted_iota(jnp.int32, (16, 128), 0)
    decay[0:8, :] = jnp.broadcast_to(last, (8, 128))

    def pair_factor(line, j):
        turned = pltpu.roll(jnp.broadcast_to(line, (8, 128)), lax.rem(128 - 2 * j, 128), 1)
        return jnp.where(row128 < 64, jnp.broadcast_to(turned[0:1, 0:1], (128, 128)), jnp.broadcast_to(turned[0:1, 1:2], (128, 128)))

    head_a = 24 * core + 3 * chip // 2
    edge = jnp.where(lax.rem(chip, 2) == 0, 64, 32)
    row96 = lax.broadcasted_iota(jnp.int32, (96, 128), 0)

    class Carry:
        def __init__(self, way, backward, into):
            self.e, self.backward, self.into = 2 * way, backward, into
            self.sib, self.across = sib, across
            self.snd, self.rcv, self.ret = snd, rcv, ret

        def swap(self):
            self.first = to_sibling(self.e, loc.at[pl.ds(pl.multiple_of(1536 * (1 - core), 128), 1536)], self.sib)

        def start(self):
            self.first.wait_recv()
            second = core == (0 if self.backward else 1)
            other = decay[8:9, :]
            later = jnp.exp(jnp.where(second, last, other))

            def join(j, carry):
                own, theirs = wide(loc[rows128(mine + j), :]), wide(self.sib[rows128(j), :])
                factor = pair_factor(later, mine + j)
                tile = low(factor * jnp.where(second, theirs, own) + jnp.where(second, own, theirs))
                for g in range(4):
                    q = 4 * j + g
                    self.snd[q // 3, pl.ds(pl.multiple_of(32 * lax.rem(q, 3), 32), 32), :] = tile[32 * g:32 * g + 32]
                return carry

            loop(0, 12, join, 12)
            tail = split3(last + other)
            lines = jnp.zeros((16, 128), f32)
            for k in range(3):
                lines = jnp.where(row16 == k, wide(tail[k]), lines)
            for k in range(16):
                self.snd[k, 96:112, :] = low(lines)

            def own():
                self.rcv[chip] = self.snd[chip]

            exchange(self.e, lambda k: self.snd.at[k], lambda k: self.rcv.at[k], own)

        def turn(self):
            arrived(self.e, lambda k: self.rcv.at[k])
            carry = jnp.zeros((96, 128), f32)
            for k in (range(15, -1, -1) if self.backward else range(16)):
                line = wide(self.rcv[k, 96:112, :])
                line = jnp.exp(line[0:1] + line[1:2] + line[2:3])
                line = pltpu.roll(jnp.broadcast_to(line, (8, 128)), lax.rem(128 - head_a, 128), 1)
                factor = jnp.where(row96 < edge, jnp.broadcast_to(line[0:1, 0:1], (96, 128)), jnp.broadcast_to(line[0:1, 1:2], (96, 128)))
                self.ret[k] = low(carry)
                carry = factor * carry + wide(self.rcv[k, 0:96, :])
            start = pl.multiple_of(1536 * core, 128)

            def place_(k):
                return self.into.at[pl.ds(pl.multiple_of(start + 96 * k, 32), 96)]

            def own():
                self.into[pl.ds(pl.multiple_of(start + 96 * chip, 32), 96), :] = self.ret[chip]

            self.place = place_
            exchange(self.e + 1, lambda k: self.ret.at[k], place_, own)

        def finish(self):
            arrived(self.e + 1, self.place)
            second = core == (0 if self.backward else 1)
            before = jnp.exp(jnp.where(second, decay[8:9, :], last))

            def part(j, carry):
                at_ = rows128(mine + j)
                came = self.into[at_, :]
                passed = low(pair_factor(before, mine + j) * wide(came) + wide(jnp.where(second, self.sib[rows128(j), :], loc[at_, :])))
                self.across[rows128(j), :] = jnp.where(second, came, passed)
                self.into[at_, :] = jnp.where(second, passed, came)
                return carry

            loop(0, 12, part, 12)
            half = pl.ds(pl.multiple_of(1536 * core, 128), 1536)
            self.last = to_sibling(self.e + 1, self.across, self.into.at[half])
            self.last.wait_recv()

        def end(self):
            if self.backward:
                self.first.wait_send()
            self.last.wait_send()
            left(self.e, lambda k: self.snd.at[k])
            left(self.e + 1, lambda k: self.ret.at[k])

    ahead, aback = Carry(0, False, inc), Carry(1, True, inc2)
    decays = to_sibling(4, decay.at[0:8], decay.at[8:16])

    def local_state(j, carry):
        loc[rows128(j), :] = low(dot_tn(low(spread(toward, j) * wide(act[j])), b_in))
        return carry

    loop(given, 12, local_state, 6)
    ahead.swap()
    loop(mine, 12, local_state, 6)
    decays.wait_recv()
    ahead.start()

    row = lax.broadcasted_iota(jnp.int32, (128, 128), 0)
    col = lax.broadcasted_iota(jnp.int32, (128, 128), 1)
    causal = row >= col

    def weights(j):
        out = []
        for k, own in enumerate(pick(cum, j)):
            line = rows_a[pl.ds(2 * j + k, 1), :]
            first, second = own[:128], own[128:]
            out.append((
                jnp.exp(jnp.where(causal, first - line[:, :128], -1e30)),
                jnp.exp(second - line[:, :128]),
                jnp.exp(jnp.where(causal, second - line[:, 128:], -1e30))))
        return out

    places = ((slice(0, 128), slice(0, 128)), (slice(128, 256), slice(0, 128)), (slice(128, 256), slice(128, 256)))

    def mixing(gaps):
        return [[low(scores[r, c] * gap) for (r, c), gap in zip(places, head)] for head in gaps]

    def inside(j, carry):
        m = mixing(weights(j))
        xa, xb = by_head(act[j])
        top = dot(jnp.concatenate([m[0][0], m[1][0]], axis=1), jnp.concatenate([xa[:128], xb[:128]], axis=0))
        low_ = dot(jnp.concatenate([m[0][1], m[0][2], m[1][1], m[1][2]], axis=1), jnp.concatenate([xa, xb], axis=0))
        ys[j, 0:128, :] = top
        ys[j, 128:256, :] = low_
        return carry

    loop(0, TILES // 2, inside, 3)
    ring.turn()
    ahead.turn()
    loop(TILES // 2, TILES // 2, inside, 3)
    ring.finish()
    ahead.finish()
    ring.end()

    prefetch(from_gates)
    db[...] = jnp.zeros((256, DI), f32)

    def make_gates(k, w):
        gates[:, lanes(384 * k, 384)] = dot(normed[...], w)

    def make_db(k, w):
        db[:, lanes(1536 * (k // 4), 1536)] += dot_nt(given_out[:, lanes(384 * lax.rem(k, 4), 384)], w)

    stream(from_gates, 8, make_gates)
    prefetch(from_out)
    stream(from_out, 8, make_db)

    def state(ref, j):
        return ref[pl.ds(pl.multiple_of(128 * j, 128), 128), :]

    def gate(j, y):
        gz = gates[:, cols(j)]
        sig = sigmoid(gz)
        full = y + skip[:, cols(j)] * wide(act[j])
        return gz, sig, full, full * gz * sig

    stat[...] = jnp.zeros((256, 128), f32)
    coef[...] = jnp.zeros((256, 128), f32)

    def gate_sums(j, carry):
        y = ys[j] + spread(ecum, j) * dot_nt(c_out, state(inc, j))
        ys[j] = y
        _, _, _, gated = gate(j, y)
        stat[...] += gated * gated
        coef[...] += gated * (gain[:, cols(j)] * db[:, cols(j)])
        return carry

    loop(0, TILES, gate_sums, 6)
    scale = lax.rsqrt(jnp.sum(stat[...], axis=1, keepdims=True) * (1.0 / DI) + epsilon)
    factor = scale * scale * scale * (jnp.sum(coef[...], axis=1, keepdims=True) * (1.0 / DI))
    stat[...] = jnp.broadcast_to(scale, (256, 128))
    coef[...] = jnp.broadcast_to(factor, (256, 128))
    sums[...] = jnp.zeros((8, CONVC), f32)
    skips[...] = jnp.zeros((128, 128), f32)

    def gate_back(j, carry):
        y = ys[j]
        gz, sig, full, gated = gate(j, y)
        scaled = gated * stat[...]
        branch[:, cols(j)] = low(scaled * gain[:, cols(j)])
        given = db[:, cols(j)]
        sums[5:6, cols(j)] = jnp.sum(scaled * given, axis=0, keepdims=True)
        d_gated = stat[...] * gain[:, cols(j)] * given - gated * coef[...]
        dz[:, cols(j)] = low(d_gated * full * (sig * (1.0 + gz * (1.0 - sig))))
        dy = low(d_gated * gz * sig)
        dys[j] = dy
        dyf = wide(dy)
        skips[pl.ds(j, 1), :] = jnp.sum(dyf * wide(act[j]), axis=0, keepdims=True)
        loc[rows128(j), :] = low(dot_tn(low(spread(ecum, j) * dyf), c_out))
        return carry

    ahead.first.wait_send()
    ahead.end()
    loop(given, 12, gate_back, 4)
    aback.swap()
    theirs, ours = lanes(1536 * (1 - core), 1536), lanes(1536 * core, 1536)
    shared += [to_sibling(7, branch.at[:, theirs], sib_branch), to_sibling(8, dz.at[:, theirs], sib_dz.at[:, theirs])]
    loop(mine, 12, gate_back, 4)
    shared += [to_sibling(9, dz.at[:, ours], sib_dz.at[:, ours])]
    aback.start()
    for copy in shared:
        copy.wait_recv()

    def flip(own, theirs):
        flipped[:, :256] = low(jnp.transpose(wide(own)))
        flipped[:, 256:] = low(jnp.transpose(wide(theirs)))

    def flip_normed(zh):
        flip(normed[:, lanes(768 * core + 384 * zh, 384)], sib_normed[:, 384 * zh:384 * zh + 384])

    for zh in range(2):
        flip_normed(zh)

        def d_w_gates(n, u):
            part = lanes(384 * n, 384)
            total = dot(flipped[:, :256], dz[:, part]) + dot(flipped[:, 256:], sib_dz[:, part])
            src[zh, :, :, :, :, lanes(1536 * (n // 2) + 384 * lax.rem(n, 2), 384)] = low(total).reshape(4, 2, 3, 16, 384)

        loop(0, 8, d_w_gates, 2)
    aback.turn()
    for q in range(4):
        flip(branch[:, lanes(1536 * core + 384 * q, 384)], sib_branch[:, 384 * q:384 * q + 384])

        def d_w_out(n, u):
            part = lanes(384 * n, 384)
            total = dot(flipped[:, :256], given_out[:, part]) + dot(flipped[:, 256:], sib_given[:, part])
            total = low(total).reshape(2, 2, 3, 2, 16, 384)
            for b in range(2):
                src[q // 2, 2 * (q % 2):2 * (q % 2) + 2, :, :, :, lanes(1536 * n + 768 + 384 * b, 384)] = total[:, :, :, b]

        loop(0, 4, d_w_out, 2)
    hidden = sib_given
    hidden_load = pltpu.make_async_copy(hidden_in, hidden, out_sem.at[2])
    hidden_load.start()
    prefetch(from_gates)
    work = Scatter(at, links, src, 2 * DI, True, rest, last_early)
    reduce = work.steps()
    next(reduce)
    d_norm = gates
    d_norm[:, :1536] = jnp.zeros((256, 1536), f32)
    out_sum = db

    def norm_gates(k, w):
        d_norm[:, :1536] += dot_nt(dz[:, lanes(384 * k, 384)], w)

    def make_out(k, w):
        part = lanes(384 * lax.rem(k, 4), 384)
        held = jnp.where(k < 4, wide(hidden[:, part]), out_sum[:, part])
        out_sum[:, part] = held + dot(branch[:, lanes(1536 * (k // 4), 1536)], w)

    for ref in (usum, qin, qw):
        ref[...] = jnp.zeros((256, 128), f32)
    dscores[...] = jnp.zeros((256, 256), f32)
    prods[...] = jnp.zeros((128, 128), f32)

    def inside_back(j, carry):
        gaps = weights(j)
        m = mixing(gaps)
        x = act[j]
        dya, dyb = by_head(dys[j])
        for k, dy in enumerate((dya, dyb)):
            near = dot_nt(dy[:128], x[:128])
            far = dot_nt(dy[128:], x)
            part = (near, far[:, :128], far[:, 128:])
            for (r, c), gap, value in zip(places, gaps[k], part):
                dscores[r, c] += gap * value
        top = dot_tn(jnp.concatenate([m[0][0], m[0][1], m[1][0], m[1][1]], axis=0), jnp.concatenate([dya, dyb], axis=0))
        low_ = dot_tn(jnp.concatenate([m[0][2], m[1][2]], axis=0), jnp.concatenate([dya[128:], dyb[128:]], axis=0))
        dx = jnp.concatenate([top, low_], axis=0)
        fold(usum, wide(dys[j]) * ys[j], j)
        ys[j] = dx
        fold(qin, wide(x) * dx, j)
        return carry

    loop(0, TILES, inside_back, 3)
    stream(from_gates, 8, norm_gates)
    next(reduce)
    aback.finish()
    db_in[...] = jnp.zeros((256, 128), f32)
    dc_in[...] = jnp.zeros((256, 128), f32)

    def d_mix(j, u, d_act):
        m = convolved(j, u)
        sig = sigmoid(m)
        d_m = d_act * (sig * (1.0 + m * (1.0 - sig)))
        ys[j] = d_m
        back_out[:, cols(j)] = low(d_m[0:16])

    def carry_back(j, u):
        s_in, d_s = state(inc, j), state(inc2, j)
        x, dyf = wide(act[j]), wide(dys[j])
        w = spread(toward, j)
        d_w = w * dot_nt(b_in, d_s)
        fold(qw, x * d_w, j)
        db_in[...] += dot(low(w * x), d_s)
        dc_in[...] += dot(low(spread(ecum, j) * dyf), s_in)
        pair = wide(s_in) * wide(d_s)
        prods[pl.ds(2 * j, 1), :] = jnp.sum(pair[:64], axis=0, keepdims=True)
        prods[pl.ds(2 * j + 1, 1), :] = jnp.sum(pair[64:], axis=0, keepdims=True)
        d_mix(j, u, ys[j] + d_w + skip[:, cols(j)] * dyf)

    loop(0, 15, carry_back, 3)
    next(reduce)
    loop(15, 9, carry_back, 3)
    ds = low(dscores[...])
    d_mix(TILES, 0, db_in[...] + dot_tn(ds, c_out))
    d_mix(TILES + 1, 1, dc_in[...] + dot(ds, b_in))
    behind = neighbour(1, back_out, back_in, -1, me > 0)

    q = qin[...] + qw[...]
    d_last = ecum[255:256, :] * jnp.sum(jnp.transpose(prods[...]), axis=0, keepdims=True) + jnp.sum(qw[...], axis=0, keepdims=True)
    at_end = lax.broadcasted_iota(jnp.int32, (256, 128), 0) == 255
    d_l = running_sums(usum[...] - q + jnp.where(at_end, d_last, 0.0), True)
    dt = steps[...]
    raw = dt_in[...] + heads[0:1, :]
    d_raw = (q / jnp.maximum(dt, 1e-30) - heads[1:2, :] * d_l) * sigmoid(raw)
    d_raw = jnp.where(lane < H, d_raw, 0.0)
    headsums[...] = jnp.zeros((8, 128), f32)
    by_pair = jnp.transpose(skips[...])
    headsums[2:3, :] = jnp.sum(by_pair[:64], axis=0, keepdims=True)
    headsums[3:4, :] = jnp.sum(by_pair[64:], axis=0, keepdims=True)
    headsums[0:1, :] = jnp.sum(d_raw, axis=0, keepdims=True)
    headsums[1:2, :] = -jnp.sum(d_l * dt, axis=0, keepdims=True)
    dproj[:, CONVC:CONVC + 128] = low(d_raw)
    dproj[:, CONVC + 128:] = jnp.zeros((256, 128), bf16)
    next(reduce)

    @pl.when(me == 31)
    def _():
        back_in[...] = jnp.zeros((16, CONVC), bf16)

    pl.when(me < 31)(behind.wait_recv)

    def conv_back(j, u):
        d_m = ys[j]
        shift[u, 0:8, :] = wide(halo_in[:, cols(j)])[8:16, :]
        shift[u, 8:264, :] = wide(conv_in[:, cols(j)])
        for k in range(4):
            sums[k:k + 1, cols(j)] = jnp.sum(d_m * shift[u, 5 + k:261 + k, :], axis=0, keepdims=True)
        sums[4:5, cols(j)] = jnp.sum(d_m, axis=0, keepdims=True)
        shift2[u, 0:256, :] = d_m
        shift2[u, 256:264, :] = wide(back_in[:, cols(j)])[0:8, :]
        total = taps[3:4, cols(j)] * d_m
        for k in range(3):
            total = total + taps[k:k + 1, cols(j)] * shift2[u, 3 - k:259 - k, :]
        dproj[:, cols(j)] = low(total)

    loop(0, TILES // 2, conv_back, 2)
    shared += [to_sibling(10, dproj.at[:, :1536], sib_dz.at[:, :1536])]
    loop(TILES // 2, TILES // 2 + 2, conv_back, 2)
    shared += [to_sibling(11, dproj.at[:, 1536:], sib_dz.at[:, 1536:])]
    next(reduce)
    links.settle()
    for axis in ("z", "y", "x"):
        for steps_ in (1, 2, 3):
            pl.semaphore_signal(ready, inc=1, device_id={axis: moved(at, axis, steps_)[axis]}, device_id_type=MESH)
    for copy in shared[-2:]:
        copy.wait_recv()

    prefetch(from_late)
    for zh in range(2):
        flip_normed(zh)

        def d_w_late(n, u):
            part = lanes(384 * n, 384)
            total = dot(flipped[:, :256], dproj[:, part]) + dot(flipped[:, 256:], sib_dz[:, part])
            src[zh, :, :, :, :, part] = low(total).reshape(4, 2, 3, 16, 384)

        loop(0, 9, d_w_late, 3)
    for k in range(2):
        src[k, :, :, :, :, 3456:3584] = jnp.zeros((4, 2, 3, 16, 128), bf16)
    work.finish(g_in, 0, DI, g_o)
    pl.semaphore_wait(ready, 9)
    after = Links(l_send, l_recv)
    width = WIDE - DI
    work = Scatter(at, after, src.at[:, :, :, :, :, pl.ds(0, width)], width, False, rest, last_late, 2 * DI)
    reduce = work.steps()
    next(reduce)

    def norm_late(k, w):
        d_norm[:, :1536] += dot_nt(dproj[:, lanes(384 * k, 384)], w)

    stream(from_late, 9, norm_late)
    prefetch(from_out)

    hidden_load.wait()
    stat[...] = jnp.zeros((256, 128), f32)
    coef[...] = jnp.zeros((256, 128), f32)

    def norm_sums(j, u):
        v = wide(hidden[:, cols(j)])
        stat[...] += v * v
        coef[...] += v * (norm_gain[:, cols(j)] * d_norm[:, cols(j)])

    loop(0, 12, norm_sums, 4)
    scale = lax.rsqrt(jnp.sum(stat[...], axis=1, keepdims=True) * (1.0 / 1536) + epsilon)
    factor = scale * scale * scale * (jnp.sum(coef[...], axis=1, keepdims=True) * (1.0 / 1536))
    stat[...] = jnp.broadcast_to(scale, (256, 128))
    coef[...] = jnp.broadcast_to(factor, (256, 128))

    def norm_back(j, u):
        v, dn = wide(hidden[:, cols(j)]), d_norm[:, cols(j)]
        sums[7:8, cols(j)] = jnp.sum(dn * v * stat[...], axis=0, keepdims=True)
        d_norm[:, cols(j)] = wide(given_out[:, cols(j)]) + stat[...] * norm_gain[:, cols(j)] * dn - v * coef[...]

    loop(0, 12, norm_back, 4)
    hidden_copy = pltpu.make_async_copy(d_norm.at[:, :1536], d_hidden, out_sem.at[1])
    hidden_copy.start()
    whole[:, :CONVC] = sums[...]
    whole[:, CONVC:CONVC + 128] = headsums[...]
    whole[:, CONVC + 128:] = jnp.zeros((8, 128), f32)
    tiny = Links(t_send, t_recv)
    small = small_steps(at, tiny, whole, core_sum, core_other, rounds)
    next(small)
    next(reduce)
    next(small)
    stream(from_out, 8, make_out)
    sib_branch[...] = low(out_sum[:, :1536])
    out_copy = pltpu.make_async_copy(sib_branch, out, out_sem.at[0])
    out_copy.start()
    for _ in reduce:
        next(small)
    next(small)
    own_slices(at, whole, o_taps, o_bias, o_norm, o_gate, o_dt, o_rates, o_skip)
    work.finish(g_in, DI, PROJ - DI)
    after.finish()
    tiny.finish()
    for copy in shared:
        copy.wait_send()
    out_copy.wait()
    hidden_copy.wait()
    pl.when(me < 31)(front.wait_send)
    pl.when(me > 0)(behind.wait_send)
    decays.wait_send()
    aback.end()


def mixer(normed, given_out, taps, gain, norm_gain, dt_bias, rates, d_skip, hidden, w_late, part_w):
    f32, bf16 = jnp.float32, jnp.bfloat16
    tile, half, late = (256, 128), (16, CONVC), WIDE - DI
    vm = pltpu.VMEM
    dma = pltpu.SemaphoreType.DMA
    scratch = [
        vm((1, DI), f32), vm((8, 128), f32),
        vm((256, CONVC), bf16), vm(tile, f32), vm((256, late), bf16), vm((8, CONVC), f32), vm((8, 128), f32),
        vm((256, DI), f32), vm((256, DI), f32),
        vm((256, DI), bf16), vm((256, DI), bf16), vm((256, 768), bf16), vm((256, 1536), bf16), vm((256, 1536), bf16), vm((256, late), bf16),
        vm((2, 4, 2, 3, 16, 2 * DI), bf16), vm((BUFFERS, 1536, 384), bf16), dma((BUFFERS,)), vm((384, 512), bf16), dma((3,)), pltpu.SemaphoreType.REGULAR,
        vm((TILES + 2,) + tile, bf16), vm((TILES + 2,) + tile, f32), vm((TILES,) + tile, bf16),
        vm((3, 264, 128), f32), vm((2, 264, 128), f32), vm(half, bf16), vm(half, bf16), vm(half, bf16), vm(half, bf16),
        vm(tile, f32), vm(tile, f32), vm(tile, f32), vm(tile, f32), vm((128, 256), f32), vm((256, 256), f32), vm((256, 256), f32),
        vm(tile, f32), vm(tile, f32), vm(tile, f32), vm((128, 128), f32), vm(tile, f32), vm(tile, f32), vm(tile, f32), vm(tile, f32),
        vm((16, 128), f32), vm((128, 128), f32), vm((3072, 128), bf16), vm((3072, 128), bf16), vm((3072, 128), bf16),
    ]
    scratch += [vm((16, 112, 128), bf16), vm((16, 112, 128), bf16), vm((16, 96, 128), bf16)]
    scratch += [vm((1536, 128), bf16), vm((1536, 128), bf16)]
    scratch += [dma((12,)), dma((12,)), dma((4, 16)), dma((4, 16)), dma((4,)), dma((64,)), dma((64,)), dma((40,)), dma((40,)), dma((12,)), dma((12,))]
    scratch += [vm((8, 2 * SMALL), f32), vm((8, SMALL), f32), vm((8, SMALL), f32)] + [vm((4, 8, SMALL), f32)] * 3
    scratch += last_scratch(2 * DI, 768) + last_scratch(late, late // 4) + scatter_scratch(2 * DI)
    near, far = pl.BlockSpec(memory_space=pltpu.VMEM), pl.BlockSpec(memory_space=pl.ANY)
    return pl.pallas_call(
        mixer_kernel,
        out_shape=[jax.ShapeDtypeStruct((256, 1536), bf16), jax.ShapeDtypeStruct((256, 1536), f32),
                   jax.ShapeDtypeStruct((12, PROJ), f32), jax.ShapeDtypeStruct((24, 1536), f32)]
        + [jax.ShapeDtypeStruct(size, f32) for size in ((4, 26), (1, 26), (1, 12), (1, 24), (1, H), (1, H), (1, H))]
        + [jax.ShapeDtypeStruct(part_w.shape, bf16)],
        in_specs=[near] * 8 + [far] * 3,
        out_specs=[far] * 2 + [near] * 9 + [far],
        scratch_shapes=scratch,
        input_output_aliases={10: 11},
        compiler_params=pltpu.CompilerParams(collective_id=2, has_side_effects=True, vmem_limit_bytes=63 << 20),
        name="mixer",
    )(normed, given_out, taps, gain, norm_gain, dt_bias, rates, d_skip, hidden, w_late, part_w)


def rms_scale(values, gain):
    return values * lax.rsqrt(jnp.mean(values * values, axis=-1, keepdims=True) + epsilon) * gain


def shards(
    hidden,
    cotangent,
    in_w,
    out_w,
    conv_w,
    conv_b,
    norm_gain,
    gate_gain,
    dt_bias,
    decay_rates,
    d_skip,
):
    w_late, w_early = gather(in_w, out_w, conv_w, conv_b, norm_gain, gate_gain)
    spare = w_late[:, :, :, :, :, :, PARAMS - DI:].reshape(128, 12, 128).astype(jnp.float32)
    w_conv_f = spare[:, :4, :26].transpose(1, 0, 2).reshape(KW, CONVC)
    b_conv_f = spare[:, 4, :26].reshape(CONVC)
    gain_norm_f = spare[:, 5, :12].reshape(1536)
    gain_gate_f = spare[:, 6, :24].reshape(DI)
    residual = hidden[0].astype(jnp.float32)
    normed = rms_scale(residual, gain_norm_f).astype(jnp.bfloat16)
    taps = jnp.pad(jnp.concatenate([w_conv_f, b_conv_f[None]]), ((0, 3), (0, 0)))
    result, d_hidden, g_in, g_out, d_taps, d_bias, d_norm_gain, d_gate_gain, d_dt, d_rates, d_skips, _ = mixer(
        normed, cotangent[0], taps, gain_gate_f[None], gain_norm_f[None],
        dt_bias[None], decay_rates[None], d_skip[None], hidden[0], w_late, w_early)
    return (
        result[None],
        d_hidden[None],
        g_in,
        g_out,
        d_taps,
        d_bias[0],
        d_norm_gain[0],
        d_gate_gain[0],
        d_dt[0],
        d_rates[0],
        d_skips[0],
    )


def solution(mesh):
    grid = Mesh(mesh.devices.reshape(4, 4, 4, 2), ALL)
    tokens = P("z", SEQ, None)
    placed = (
        tokens,
        tokens,
        P(ALL, None),
        P(ALL, None),
        P(None, ALL),
        P(ALL),
        P(ALL),
        P(ALL),
        P(),
        P(),
        P(),
    )
    return jax.shard_map(
        shards,
        mesh=grid,
        in_specs=placed,
        out_specs=(tokens, tokens, P(ALL, None), P(ALL, None), P(None, ALL), P(ALL), P(ALL), P(ALL), P(), P(), P()),
        check_vma=False,
    )
```
